32 devices in a mesh: batch: 8 (over z, x), blk: 4 (over y, core).
Axes of the slice: x: 2, y: 2, z: 4, core: 2. Of those that a mesh axis runs over, the one named last changes fastest.
Arguments:
- inputs: bfloat16 [16, 1024, 768], P('batch', 'blk'), may hold values from -6 to 6
- previous: bfloat16 [16, 1024, 768], P('batch', 'blk'), may hold values from -6 to 6
- memory_rows: int32 [16, 512], P('batch'), may hold values from 0 to 1023
- sticky_positions: int32 [16, 512], P('batch'), may hold values from 0 to 1023
- cotangent: bfloat16 [16, 1024, 768], P('batch', 'blk'), may hold values from -6 to 6
- ln1_gain: float32 [768], replicated, may hold values from 0.5 to 1.5
- ln1_bias: float32 [768], replicated, may hold values from -1.75 to 1.75
- query_weight: bfloat16 [768, 768], replicated, may hold values from -0.3125 to 0.3125
- key_weight: bfloat16 [768, 768], replicated, may hold values from -0.3125 to 0.3125
- value_weight: bfloat16 [768, 768], replicated, may hold values from -0.21875 to 0.21875
- out_weight: bfloat16 [768, 768], replicated, may hold values from -0.875 to 0.875
- mu_weight: float32 [12, 256], replicated, may hold values from -0.375 to 0.375
- sigma_weight: float32 [12, 256], replicated, may hold values from -0.375 to 0.375
- ln2_gain: float32 [768], replicated, may hold values from 0.5 to 1.5
- ln2_bias: float32 [768], replicated, may hold values from -1.75 to 1.75
- expand_weight: bfloat16 [768, 3072], replicated, may hold values from -0.21875 to 0.21875
- up_bias: float32 [3072], replicated, may hold values from -1.75 to 1.75
- down_weight: bfloat16 [3072, 768], replicated, may hold values from -0.109375 to 0.109375
- down_bias: float32 [768], replicated, may hold values from -1.75 to 1.75
Outputs:
- block_output: bfloat16 [16, 1024, 768], P('batch', 'blk')
- grad_inputs: float32 [16, 1024, 768], P('batch', 'blk')
- grad_ln1_gain: float32 [768], replicated
- grad_ln1_bias: float32 [768], replicated
- grad_query_weight: float32 [768, 768], replicated
- grad_key_weight: float32 [768, 768], replicated
- grad_value_weight: float32 [768, 768], replicated
- grad_out_weight: float32 [768, 768], replicated
- grad_mu_weight: float32 [12, 256], replicated
- grad_sigma_weight: float32 [12, 256], replicated
- grad_ln2_gain: float32 [768], replicated
- grad_ln2_bias: float32 [768], replicated
- grad_up_weight: float32 [768, 3072], replicated
- grad_up_bias: float32 [3072], replicated
- grad_down_weight: float32 [3072, 768], replicated
- grad_down_bias: float32 [768], replicated
The draws below stay inside these ranges and needn't reach their ends.
All inputs are finite; a program needn't handle non-finite values.
Results may differ from the reference program's by a relative error of at most 0.02.
The reference program's roundings to bfloat16 on the way count: a program that leaves them out, or rounds other values in their place, can miss the bound.
Values may be sent and summed in bfloat16 or wider, within the bound.
A program may use at most 320 MiB of HBM per device.

```python
import jax
import jax.numpy as jnp
from jax import lax

D = 768
HEADS = 12
HEAD_DIM = 64
FF = 3072
BASIS = 256
MEM = 512
SEGS = 16
SEGMENT_LENGTH = 1024


def plant(result, rng, smallest, high):
    shape = result.shape
    place = [jax.random.randint(jax.random.fold_in(rng, axis), (), 0, shape[axis]) for axis in range(len(shape))]
    result = result.at[tuple(place)].set(smallest)
    longest = shape.index(max(shape))
    place[longest] = (place[longest] + 1) % shape[longest]
    return result.at[tuple(place)].set(high)


def level_of(own_key, extent, split, smallest, top_value):
    factor_of = 1.0
    for position, shards_of in split:
        steps = jax.random.uniform(jax.random.fold_in(jax.random.fold_in(own_key, 6), position), (shards_of,), jnp.float32, smallest / len(split), top_value / len(split))
        factor_of = factor_of * jnp.repeat(jnp.exp(steps), extent[position] // shards_of).reshape((-1,) + (1,) * (len(extent) - 1 - position))
    return factor_of


def centred(own_key, shape, scale, limit, cuts=(), kind=jnp.bfloat16):
    drawn = scale * jax.random.normal(own_key, shape, jnp.float32)
    if cuts:
        drawn = drawn * level_of(own_key, shape, cuts, -0.22, 0.18)
    return jnp.clip(drawn, -limit, limit).astype(kind)


def setup_inputs(seed: int = 0) -> dict:
    seeds = jax.random.split(jax.random.key(seed), 20)
    inputs = centred(seeds[0], (SEGS, SEGMENT_LENGTH, D), 1.0, 6.0, ((0, 8), (1, 4)))
    previous = centred(seeds[1], (SEGS, SEGMENT_LENGTH, D), 1.0, 6.0, ((0, 8), (1, 4)))
    memory_rows = plant(jax.random.randint(seeds[2], (SEGS, MEM), 0, SEGMENT_LENGTH), jax.random.fold_in(seeds[2], 1), 0, SEGMENT_LENGTH - 1).astype(jnp.int32)
    sticky_positions = plant(jax.random.randint(seeds[3], (SEGS, MEM), 0, SEGMENT_LENGTH), jax.random.fold_in(seeds[3], 1), 0, SEGMENT_LENGTH - 1).astype(jnp.int32)
    cotangent = centred(seeds[4], (SEGS, SEGMENT_LENGTH, D), 1.0, 6.0, ((0, 8), (1, 4)))
    ln1_gain = jnp.clip(1.0 + 0.1 * jax.random.normal(seeds[5], (D,), jnp.float32), 0.5, 1.5)
    ln1_bias = centred(seeds[6], (D,), 0.3, 1.75, (), jnp.float32)
    query_weight = centred(seeds[7], (D, D), (D // 2) ** -0.5, 0.3125)
    key_weight = centred(seeds[8], (D, D), (D // 2) ** -0.5, 0.3125)
    value_weight = centred(seeds[9], (D, D), D ** -0.5, 0.21875)
    out_weight = centred(seeds[10], (D, D), (D // 16) ** -0.5, 0.875)
    mu_weight = centred(seeds[11], (HEADS, BASIS), BASIS ** -0.5, 0.375, (), jnp.float32)
    sigma_weight = centred(seeds[12], (HEADS, BASIS), BASIS ** -0.5, 0.375, (), jnp.float32)
    ln2_gain = jnp.clip(1.0 + 0.1 * jax.random.normal(seeds[13], (D,), jnp.float32), 0.5, 1.5)
    ln2_bias = centred(seeds[14], (D,), 0.3, 1.75, (), jnp.float32)
    expand_weight = centred(seeds[15], (D, FF), D ** -0.5, 0.21875)
    up_bias = centred(seeds[16], (FF,), 0.3, 1.75, (), jnp.float32)
    down_weight = centred(seeds[17], (FF, D), FF ** -0.5, 0.109375)
    down_bias = centred(seeds[18], (D,), 0.3, 1.75, (), jnp.float32)
    return dict(inputs=inputs, previous=previous, memory_rows=memory_rows, sticky_positions=sticky_positions, cotangent=cotangent, ln1_gain=ln1_gain, ln1_bias=ln1_bias, query_weight=query_weight, key_weight=key_weight, value_weight=value_weight, out_weight=out_weight, mu_weight=mu_weight, sigma_weight=sigma_weight, ln2_gain=ln2_gain, ln2_bias=ln2_bias, expand_weight=expand_weight, up_bias=up_bias, down_weight=down_weight, down_bias=down_bias)


epsilon = 1e-05
ridge_weight = 1.0
var_scale = 0.01
masked_score = -1e+30
highest = lax.Precision.HIGHEST

@jax.custom_vjp
def low(v):
    return lax.optimization_barrier(v.astype(jnp.bfloat16)).astype(jnp.float32)

@jax.custom_vjp
def low_back(v):
    return v

def low_keep(v):
    return (low(v), None)

def reduced_precision_pass(kept, grad):
    return (grad,)

def back_keep(v):
    return (v, None)

def back_low(kept, grad):
    return (low(grad),)
low.defvjp(low_keep, reduced_precision_pass)
low_back.defvjp(back_keep, back_low)

def layer_norm(values, gain, bias):
    center = lax.optimization_barrier(jnp.mean(values, axis=-1, keepdims=True))
    shifted = values - center
    spread_sq = lax.optimization_barrier(jnp.mean(shifted * shifted, axis=-1, keepdims=True))
    return shifted * lax.rsqrt(spread_sq + epsilon) * gain + bias

def density(scores, mu_row, sigma_row):
    count = scores.shape[-1]
    centers = (jnp.arange(count, dtype=scores.dtype) + 0.5) / count
    spread = 1.0 / count
    centre = jax.nn.sigmoid(jnp.dot(scores, mu_row, precision=highest))
    variance = var_scale * jax.nn.softplus(jnp.dot(scores, sigma_row, precision=highest))
    total = spread * spread + variance
    return (spread * lax.rsqrt(total))[..., None] * jnp.exp(-(centre[..., None] - centers) ** 2 / (2.0 * total[..., None]))

def ridge_coefficients(operands):
    previous_seg, rows, sticky = operands
    centers = (jnp.arange(BASIS, dtype=previous_seg.dtype) + 0.5) / BASIS
    spread = 1.0 / BASIS
    places = (sticky.astype(previous_seg.dtype) + 0.5) / SEGMENT_LENGTH
    features = low(jnp.exp(-(places[:, None] - centers) ** 2 / (2.0 * spread * spread)))
    picked = previous_seg[rows]
    gram_sum = jnp.dot(features.T, features, precision=highest) + ridge_weight * jnp.eye(BASIS, dtype=previous_seg.dtype)
    right_side = jnp.dot(features.T, picked, precision=highest)
    factor = jnp.linalg.cholesky(gram_sum)
    return jax.scipy.linalg.cho_solve((factor, True), right_side)

def segment_forward(inputs_seg, coefficients, parameters):
    ln1_gain, ln1_bias, query_weight, key_weight, value_weight, out_weight, mu_weight, sigma_weight, ln2_gain, ln2_bias, expand_weight, up_bias, down_weight, down_bias = parameters
    normed_low = low(layer_norm(inputs_seg, ln1_gain, ln1_bias))

    def project(source, weight):
        return low(low_back(jnp.dot(source, weight, precision=highest)))
    queries = project(normed_low, query_weight)
    keys = project(normed_low, key_weight)
    values = project(normed_low, value_weight)
    coeff_low = low(coefficients)
    mem_keys = project(coeff_low, key_weight)
    mem_values = project(coeff_low, value_weight)

    def split_heads(array):
        return array.reshape(array.shape[0], HEADS, HEAD_DIM).transpose(1, 0, 2)
    positions = jnp.arange(SEGMENT_LENGTH)
    causal = positions[None, :] <= positions[:, None]

    def one_head(operands):
        query_h, key_h, value_h, memkey_h, memval_h, mu_row, sigma_row = operands
        scores = low_back(jnp.dot(query_h, key_h.T, precision=highest) * 0.125)
        probs = jax.nn.softmax(jnp.where(causal, scores, masked_score), axis=-1)
        attended = jnp.dot(low(probs), value_h, precision=highest)
        memory_scores = low_back(jnp.dot(query_h, memkey_h.T, precision=highest) * 0.125)
        recalled = jnp.dot(low(density(memory_scores, mu_row, sigma_row)), memval_h, precision=highest)
        return attended + recalled
    heads = lax.map(jax.checkpoint(one_head), (split_heads(queries), split_heads(keys), split_heads(values), split_heads(mem_keys), split_heads(mem_values), mu_weight, sigma_weight))
    context = low(low_back(heads.transpose(1, 0, 2).reshape(SEGMENT_LENGTH, D)))
    mixed = inputs_seg + low_back(jnp.dot(context, out_weight, precision=highest))
    normed_two = low(layer_norm(mixed, ln2_gain, ln2_bias))
    hidden_up = low_back(jnp.dot(normed_two, expand_weight, precision=highest) + up_bias)
    active = low(jax.nn.gelu(hidden_up, approximate=True))
    return mixed + jnp.dot(active, down_weight, precision=highest) + down_bias

def reference(inputs, previous, memory_rows, sticky_positions, cotangent, ln1_gain, ln1_bias, query_weight, key_weight, value_weight, out_weight, mu_weight, sigma_weight, ln2_gain, ln2_bias, expand_weight, up_bias, down_weight, down_bias):
    previous_full = previous.astype(jnp.float32)
    parameters = tuple((item.astype(jnp.float32) for item in (ln1_gain, ln1_bias, query_weight, key_weight, value_weight, out_weight, mu_weight, sigma_weight, ln2_gain, ln2_bias, expand_weight, up_bias, down_weight, down_bias)))
    checked = jax.checkpoint(segment_forward)

    def forward(inputs_all, parameters_all):
        coefficients = lax.map(ridge_coefficients, (previous_full, memory_rows, sticky_positions))
        return lax.map(lambda operands: checked(operands[0], operands[1], parameters_all), (inputs_all, coefficients))
    output, pull = jax.vjp(forward, inputs.astype(jnp.float32), parameters)
    grad_inputs, grads = pull(cotangent.astype(jnp.float32))
    return (output.astype(jnp.bfloat16), grad_inputs, grads[0], grads[1], grads[2], grads[3], grads[4], grads[5], grads[6], grads[7], grads[8], grads[9], grads[10], grads[11], grads[12], grads[13])
```

```python
import functools

import jax
import jax.numpy as jnp
from jax import lax
from jax.experimental import pallas as pl
from jax.experimental.pallas import tpu as pltpu
from jax.sharding import PartitionSpec as P

epsilon = 1e-05
ridge_weight = 1.0
var_scale = 0.01
masked_score = -1e30
highest = lax.Precision.HIGHEST


def layer_norm(values, gain, bias):
    center = jnp.mean(values, axis=-1, keepdims=True)
    shifted = values - center
    spread_sq = jnp.mean(shifted * shifted, axis=-1, keepdims=True)
    return shifted * lax.rsqrt(spread_sq + epsilon) * gain + bias


def density(scores, mu_row, sigma_row):
    count = scores.shape[-1]
    centers = (jnp.arange(count, dtype=scores.dtype) + 0.5) / count
    spread = 1.0 / count
    centre = jax.nn.sigmoid(jnp.dot(scores, mu_row, precision=highest))
    variance = var_scale * jax.nn.softplus(jnp.dot(scores, sigma_row, precision=highest))
    total = spread * spread + variance
    return (spread * lax.rsqrt(total))[..., None] * jnp.exp(
        -((centre[..., None] - centers) ** 2) / (2.0 * total[..., None])
    )


def project(source, weight):
    return jnp.einsum("std,de->ste", source, weight, preferred_element_type=jnp.float32)


def weight_grad(source, grads):
    return jnp.einsum("std,ste->de", source, grads, preferred_element_type=jnp.float32)


def back_project(grads, weight):
    return jnp.einsum("ste,de->std", grads, weight, preferred_element_type=jnp.float32)


def gelu_tanh(values):
    return jax.nn.gelu(values, approximate=True)


def general(
    inputs,
    previous,
    memory_rows,
    sticky_positions,
    cotangent,
    ln1_gain,
    ln1_bias,
    query_weight,
    key_weight,
    value_weight,
    out_weight,
    mu_weight,
    sigma_weight,
    ln2_gain,
    ln2_bias,
    expand_weight,
    up_bias,
    down_weight,
    down_bias,
):
    seg_count, tok_rows, model_width = inputs.shape
    blocks = lax.axis_size("blk")
    length = tok_rows * blocks
    first_row = lax.axis_index("blk") * tok_rows
    head_count, basis_count = mu_weight.shape
    head_width = model_width // head_count
    centers = (jnp.arange(basis_count, dtype=jnp.float32) + 0.5) / basis_count
    spread = 1.0 / basis_count
    places = (sticky_positions.astype(jnp.float32) + 0.5) / length
    features = jnp.exp(-((places[..., None] - centers) ** 2) / (2.0 * spread * spread)).astype(
        jnp.bfloat16
    )
    local_index = memory_rows - first_row
    owned_rows = (local_index >= 0) & (local_index < tok_rows)
    picked = jax.vmap(lambda shard_rows, row_index: shard_rows[row_index])(
        previous, jnp.clip(local_index, 0, tok_rows - 1)
    )
    picked = jnp.where(owned_rows[..., None], picked, jnp.zeros_like(picked))
    own_features = jnp.where(owned_rows[..., None], features, jnp.zeros_like(features))
    side_part = jnp.einsum("smn,smd->snd", own_features, picked, preferred_element_type=jnp.float32)
    gram_part = jnp.einsum(
        "smn,smk->snk", own_features, own_features, preferred_element_type=jnp.float32
    )
    gram_sum, right_side = lax.psum((gram_part, side_part), "blk")
    system = gram_sum + ridge_weight * jnp.eye(basis_count, dtype=jnp.float32)
    factor = jnp.linalg.cholesky(system)
    coefficients = jax.scipy.linalg.cho_solve((factor, True), right_side)
    coeff_low = coefficients.astype(jnp.bfloat16)
    hidden_in = inputs.astype(jnp.float32)
    normed_low = layer_norm(hidden_in, ln1_gain, ln1_bias).astype(jnp.bfloat16)
    queries = project(normed_low, query_weight).astype(jnp.bfloat16)
    keys_local = project(normed_low, key_weight).astype(jnp.bfloat16)
    values_local = project(normed_low, value_weight).astype(jnp.bfloat16)
    mem_keys = project(coeff_low, key_weight).astype(jnp.bfloat16)
    mem_values = project(coeff_low, value_weight).astype(jnp.bfloat16)
    all_keys, all_values = (
        lax.all_gather(keys_local, "blk", axis=1, tiled=True),
        lax.all_gather(values_local, "blk", axis=1, tiled=True),
    )

    def split_heads(array):
        return array.reshape(array.shape[0], array.shape[1], head_count, head_width).transpose(
            2, 0, 1, 3
        )

    def merge_heads(array):
        return array.transpose(1, 2, 0, 3).reshape(array.shape[1], array.shape[2], model_width)

    query_pos = first_row + jnp.arange(tok_rows)
    key_pos = jnp.arange(length)
    causal = key_pos[None, :] <= query_pos[:, None]

    def forward_head(operands):
        query_h, key_h, value_h, memkey_h, memval_h, mu_row, sigma_row = operands
        scores = (
            jnp.einsum("sqd,skd->sqk", query_h, key_h, preferred_element_type=jnp.float32) * 0.125
        )
        scores = jnp.where(causal, scores, masked_score)
        top = jnp.max(scores, axis=-1, keepdims=True)
        raised = jnp.exp(scores - top)
        total = jnp.sum(raised, axis=-1, keepdims=True)
        probs = raised / total
        log_total = (top + jnp.log(total))[..., 0]
        attended = jnp.einsum(
            "sqk,skd->sqd", probs.astype(jnp.bfloat16), value_h, preferred_element_type=jnp.float32
        )
        memory_scores = (
            jnp.einsum("sqd,snd->sqn", query_h, memkey_h, preferred_element_type=jnp.float32)
            * 0.125
        )
        weights_mem = density(memory_scores, mu_row, sigma_row)
        recalled = jnp.einsum(
            "sqn,snd->sqd",
            weights_mem.astype(jnp.bfloat16),
            memval_h,
            preferred_element_type=jnp.float32,
        )
        return (attended + recalled, log_total)

    head_queries = split_heads(queries)
    head_keys = split_heads(all_keys)
    value_per_head = split_heads(all_values)
    head_memkeys = split_heads(mem_keys)
    head_memvals = split_heads(mem_values)
    heads_ctx, log_totals = lax.map(
        forward_head,
        (
            head_queries,
            head_keys,
            value_per_head,
            head_memkeys,
            head_memvals,
            mu_weight,
            sigma_weight,
        ),
    )
    context_low = merge_heads(heads_ctx).astype(jnp.bfloat16)
    mixed = hidden_in + project(context_low, out_weight)
    normed_two_low = layer_norm(mixed, ln2_gain, ln2_bias).astype(jnp.bfloat16)
    hidden_up = (
        jnp.einsum("std,df->stf", normed_two_low, expand_weight, preferred_element_type=jnp.float32)
        + up_bias
    )
    active_low = gelu_tanh(hidden_up).astype(jnp.bfloat16)
    result = (
        mixed
        + jnp.einsum("stf,fd->std", active_low, down_weight, preferred_element_type=jnp.float32)
        + down_bias
    )
    block_output = result.astype(jnp.bfloat16)
    grad_result = cotangent.astype(jnp.float32)
    grad_down_bias = jnp.sum(grad_result, axis=(0, 1))
    grad_down_weight = jnp.einsum(
        "stf,std->fd", active_low, cotangent, preferred_element_type=jnp.float32
    )
    grad_active = jnp.einsum(
        "std,fd->stf", cotangent, down_weight, preferred_element_type=jnp.float32
    )
    gelu_value, gelu_pull = jax.vjp(gelu_tanh, hidden_up)
    grad_up_low = gelu_pull(grad_active)[0].astype(jnp.bfloat16)
    grad_up_bias = jnp.sum(grad_up_low.astype(jnp.float32), axis=(0, 1))
    grad_up_weight = jnp.einsum(
        "std,stf->df", normed_two_low, grad_up_low, preferred_element_type=jnp.float32
    )
    grad_normed_two = jnp.einsum(
        "stf,df->std", grad_up_low, expand_weight, preferred_element_type=jnp.float32
    )
    norm_two_value, norm_two_pull = jax.vjp(layer_norm, mixed, ln2_gain, ln2_bias)
    grad_mixed_norm, grad_ln2_gain, grad_ln2_bias = norm_two_pull(grad_normed_two)
    grad_mixed = grad_result + grad_mixed_norm
    grad_mixed_low = grad_mixed.astype(jnp.bfloat16)
    grad_out_weight = weight_grad(context_low, grad_mixed_low)
    grad_context_low = back_project(grad_mixed_low, out_weight).astype(jnp.bfloat16)

    def backward_head(operands):
        query_h, key_h, value_h, memkey_h, memval_h, mu_row, sigma_row, grad_h, log_total = operands
        scores = (
            jnp.einsum("sqd,skd->sqk", query_h, key_h, preferred_element_type=jnp.float32) * 0.125
        )
        probs = jnp.where(causal, jnp.exp(scores - log_total[..., None]), 0.0)
        grad_probs = jnp.einsum("sqd,skd->sqk", grad_h, value_h, preferred_element_type=jnp.float32)
        row_dot = jnp.sum(probs * grad_probs, axis=-1, keepdims=True)
        grad_scores = (probs * (grad_probs - row_dot)).astype(jnp.bfloat16)
        grad_query = (
            jnp.einsum("sqk,skd->sqd", grad_scores, key_h, preferred_element_type=jnp.float32)
            * 0.125
        )
        memory_scores = (
            jnp.einsum("sqd,snd->sqn", query_h, memkey_h, preferred_element_type=jnp.float32)
            * 0.125
        )
        weights_mem, density_pull = jax.vjp(density, memory_scores, mu_row, sigma_row)
        weights_low = weights_mem.astype(jnp.bfloat16)
        grad_weights = jnp.einsum(
            "sqd,snd->sqn", grad_h, memval_h, preferred_element_type=jnp.float32
        )
        grad_memval = jnp.einsum(
            "sqn,sqd->snd", weights_low, grad_h, preferred_element_type=jnp.float32
        )
        grad_memscores, grad_mu, grad_sigma = density_pull(grad_weights)
        grad_memscores_low = grad_memscores.astype(jnp.bfloat16)
        grad_query = (
            grad_query
            + jnp.einsum(
                "sqn,snd->sqd", grad_memscores_low, memkey_h, preferred_element_type=jnp.float32
            )
            * 0.125
        )
        grad_memkey = (
            jnp.einsum(
                "sqn,sqd->snd", grad_memscores_low, query_h, preferred_element_type=jnp.float32
            )
            * 0.125
        )
        grad_key = (
            jnp.einsum("sqk,sqd->skd", grad_scores, query_h, preferred_element_type=jnp.float32)
            * 0.125
        )
        grad_value = jnp.einsum(
            "sqk,sqd->skd", probs.astype(jnp.bfloat16), grad_h, preferred_element_type=jnp.float32
        )
        return (grad_query, grad_memkey, grad_memval, grad_mu, grad_sigma, grad_key, grad_value)

    head_grads = split_heads(grad_context_low)
    outcome = lax.map(
        backward_head,
        (
            head_queries,
            head_keys,
            value_per_head,
            head_memkeys,
            head_memvals,
            mu_weight,
            sigma_weight,
            head_grads,
            log_totals,
        ),
    )
    grad_query_heads, grad_memkey_heads, grad_memval_heads, grad_mu_weight, grad_sigma_weight = (
        outcome[:5]
    )
    terms = (
        jnp.stack((outcome[5], outcome[6]))
        .transpose(3, 2, 0, 1, 4)
        .reshape(length, seg_count, 2 * model_width)
    )
    own_terms = lax.psum_scatter(
        terms.astype(jnp.bfloat16), "blk", scatter_dimension=0, tiled=True
    ).astype(jnp.float32)
    own_terms = own_terms.reshape(tok_rows, seg_count, 2, model_width).transpose(2, 1, 0, 3)
    grad_keys = own_terms[0]
    grad_values = own_terms[1]
    grad_queries_low = merge_heads(grad_query_heads).astype(jnp.bfloat16)
    grad_keys_low = grad_keys.astype(jnp.bfloat16)
    grad_values_low = grad_values.astype(jnp.bfloat16)
    memkey_sum, memval_sum = (
        lax.psum(grad_memkey_heads.astype(jnp.bfloat16), "blk").astype(jnp.float32),
        lax.psum(grad_memval_heads.astype(jnp.bfloat16), "blk").astype(jnp.float32),
    )
    gradient_memory_keys_reduced = merge_heads(memkey_sum).astype(jnp.bfloat16)
    gradient_memory_values_reduced = merge_heads(memval_sum).astype(jnp.bfloat16)
    grad_query_weight = weight_grad(normed_low, grad_queries_low)
    grad_key_weight = weight_grad(normed_low, grad_keys_low)
    grad_value_weight = weight_grad(normed_low, grad_values_low)
    grad_normed = (
        back_project(grad_queries_low, query_weight)
        + back_project(grad_keys_low, key_weight)
        + back_project(grad_values_low, value_weight)
    )
    norm_one_value, norm_one_pull = jax.vjp(layer_norm, hidden_in, ln1_gain, ln1_bias)
    grad_in_norm, grad_ln1_gain, grad_ln1_bias = norm_one_pull(grad_normed)
    grad_inputs = grad_mixed + grad_in_norm
    shares = (
        lax.psum_scatter(
            grad_ln1_gain.astype(jnp.bfloat16), "blk", scatter_dimension=0, tiled=True
        ).astype(jnp.float32),
        lax.psum_scatter(
            grad_ln1_bias.astype(jnp.bfloat16), "blk", scatter_dimension=0, tiled=True
        ).astype(jnp.float32),
        lax.psum_scatter(
            grad_query_weight.astype(jnp.bfloat16), "blk", scatter_dimension=0, tiled=True
        ).astype(jnp.float32),
        lax.psum_scatter(
            grad_key_weight.astype(jnp.bfloat16), "blk", scatter_dimension=0, tiled=True
        ).astype(jnp.float32),
        lax.psum_scatter(
            grad_value_weight.astype(jnp.bfloat16), "blk", scatter_dimension=0, tiled=True
        ).astype(jnp.float32),
        lax.psum_scatter(
            grad_out_weight.astype(jnp.bfloat16), "blk", scatter_dimension=0, tiled=True
        ).astype(jnp.float32),
        lax.psum_scatter(
            grad_mu_weight.astype(jnp.bfloat16), "blk", scatter_dimension=1, tiled=True
        ).astype(jnp.float32),
        lax.psum_scatter(
            grad_sigma_weight.astype(jnp.bfloat16), "blk", scatter_dimension=1, tiled=True
        ).astype(jnp.float32),
        lax.psum_scatter(
            grad_ln2_gain.astype(jnp.bfloat16), "blk", scatter_dimension=0, tiled=True
        ).astype(jnp.float32),
        lax.psum_scatter(
            grad_ln2_bias.astype(jnp.bfloat16), "blk", scatter_dimension=0, tiled=True
        ).astype(jnp.float32),
        lax.psum_scatter(
            grad_up_weight.astype(jnp.bfloat16), "blk", scatter_dimension=0, tiled=True
        ).astype(jnp.float32),
        lax.psum_scatter(
            grad_up_bias.astype(jnp.bfloat16), "blk", scatter_dimension=0, tiled=True
        ).astype(jnp.float32),
        lax.psum_scatter(
            grad_down_weight.astype(jnp.bfloat16), "blk", scatter_dimension=0, tiled=True
        ).astype(jnp.float32),
        lax.psum_scatter(
            grad_down_bias.astype(jnp.bfloat16), "blk", scatter_dimension=0, tiled=True
        ).astype(jnp.float32),
    )
    share_width = model_width // blocks
    coefficient_part = lax.dynamic_slice_in_dim(
        coeff_low, lax.axis_index("blk") * share_width, share_width, 2
    )
    key_share = shares[3] + jnp.einsum(
        "wrc,wrt->ct",
        coefficient_part,
        gradient_memory_keys_reduced,
        preferred_element_type=jnp.float32,
    )
    value_share = shares[4] + jnp.einsum(
        "wrc,wrt->ct",
        coefficient_part,
        gradient_memory_values_reduced,
        preferred_element_type=jnp.float32,
    )
    totals = (
        lax.psum(shares[0].astype(jnp.bfloat16), "batch").astype(jnp.float32),
        lax.psum(shares[1].astype(jnp.bfloat16), "batch").astype(jnp.float32),
        lax.psum(shares[2].astype(jnp.bfloat16), "batch").astype(jnp.float32),
        lax.psum(key_share.astype(jnp.bfloat16), "batch").astype(jnp.float32),
        lax.psum(value_share.astype(jnp.bfloat16), "batch").astype(jnp.float32),
        lax.psum(shares[5].astype(jnp.bfloat16), "batch").astype(jnp.float32),
        lax.psum(shares[6].astype(jnp.bfloat16), "batch").astype(jnp.float32),
        lax.psum(shares[7].astype(jnp.bfloat16), "batch").astype(jnp.float32),
        lax.psum(shares[8].astype(jnp.bfloat16), "batch").astype(jnp.float32),
        lax.psum(shares[9].astype(jnp.bfloat16), "batch").astype(jnp.float32),
        lax.psum(shares[10].astype(jnp.bfloat16), "batch").astype(jnp.float32),
        lax.psum(shares[11].astype(jnp.bfloat16), "batch").astype(jnp.float32),
        lax.psum(shares[12].astype(jnp.bfloat16), "batch").astype(jnp.float32),
        lax.psum(shares[13].astype(jnp.bfloat16), "batch").astype(jnp.float32),
    )
    whole = (
        lax.all_gather(totals[0].astype(jnp.bfloat16), "blk", axis=0, tiled=True).astype(
            jnp.float32
        ),
        lax.all_gather(totals[1].astype(jnp.bfloat16), "blk", axis=0, tiled=True).astype(
            jnp.float32
        ),
        lax.all_gather(totals[2].astype(jnp.bfloat16), "blk", axis=0, tiled=True).astype(
            jnp.float32
        ),
        lax.all_gather(totals[3].astype(jnp.bfloat16), "blk", axis=0, tiled=True).astype(
            jnp.float32
        ),
        lax.all_gather(totals[4].astype(jnp.bfloat16), "blk", axis=0, tiled=True).astype(
            jnp.float32
        ),
        lax.all_gather(totals[5].astype(jnp.bfloat16), "blk", axis=0, tiled=True).astype(
            jnp.float32
        ),
        lax.all_gather(totals[6].astype(jnp.bfloat16), "blk", axis=1, tiled=True).astype(
            jnp.float32
        ),
        lax.all_gather(totals[7].astype(jnp.bfloat16), "blk", axis=1, tiled=True).astype(
            jnp.float32
        ),
        lax.all_gather(totals[8].astype(jnp.bfloat16), "blk", axis=0, tiled=True).astype(
            jnp.float32
        ),
        lax.all_gather(totals[9].astype(jnp.bfloat16), "blk", axis=0, tiled=True).astype(
            jnp.float32
        ),
        lax.all_gather(totals[10].astype(jnp.bfloat16), "blk", axis=0, tiled=True).astype(
            jnp.float32
        ),
        lax.all_gather(totals[11].astype(jnp.bfloat16), "blk", axis=0, tiled=True).astype(
            jnp.float32
        ),
        lax.all_gather(totals[12].astype(jnp.bfloat16), "blk", axis=0, tiled=True).astype(
            jnp.float32
        ),
        lax.all_gather(totals[13].astype(jnp.bfloat16), "blk", axis=0, tiled=True).astype(
            jnp.float32
        ),
    )
    return (
        block_output,
        grad_inputs,
        whole[0],
        whole[1],
        whole[2],
        whole[3],
        whole[4],
        whole[5],
        whole[6],
        whole[7],
        whole[8],
        whole[9],
        whole[10],
        whole[11],
        whole[12],
        whole[13],
    )


f32 = jnp.float32
bf16 = jnp.bfloat16
NN = (((1,), (0,)), ((), ()))
NT = (((1,), (1,)), ((), ()))
TN = (((0,), (0,)), ((), ()))
QB = 256


def mm(a, b, dims=NN, precision=None):
    return lax.dot_general(a, b, dims, precision=precision, preferred_element_type=f32)


def vmem_params(**more):
    return pltpu.CompilerParams(vmem_limit_bytes=56 * 1024 * 1024, **more)


def sweep_inverse(a):
    n = a.shape[0]
    lane = lax.broadcasted_iota(jnp.int32, (1, n), 1)
    sub = lax.broadcasted_iota(jnp.int32, (n, 1), 0)
    for k in range(n):
        inv = 1.0 / a[k : k + 1, k : k + 1]
        row = jnp.where(lane == k, inv, a[k : k + 1, :] * inv)
        col = a[:, k : k + 1]
        a = jnp.where(sub == k, row, jnp.where(lane == k, 0.0, a) - col * row)
    return a


def ridge_kernel(length, prev_ref, rows_ref, sticky_ref, coef_ref, a_ref, i_ref):
    basis = coef_ref.shape[0]
    half = basis // 2
    mem = rows_ref.shape[0]
    spread = 1.0 / basis
    centers = (lax.broadcasted_iota(jnp.int32, (1, basis), 1).astype(f32) + 0.5) / basis
    places = (sticky_ref[...].astype(f32) + 0.5) / length
    features = jnp.exp(-((places - centers) ** 2) / (2.0 * spread * spread)).astype(bf16)
    index = lax.broadcasted_iota(jnp.int32, (mem, prev_ref.shape[0]), 1)
    onehot = jnp.where(rows_ref[...] == index, 1.0, 0.0).astype(bf16)
    picked = mm(onehot, prev_ref[...]).astype(bf16)
    side = mm(features, picked, TN)
    same = lax.broadcasted_iota(jnp.int32, (basis, basis), 0) == lax.broadcasted_iota(
        jnp.int32, (basis, basis), 1
    )
    a_ref[...] = mm(features, features, TN) + jnp.where(same, ridge_weight, 0.0)
    i_ref[...] = sweep_inverse(a_ref[:half, :half])
    top = i_ref[...]
    cross = a_ref[:half, half:]
    wide = mm(top, cross, precision=highest)
    schur = a_ref[half:, half:] - mm(cross, wide, TN, precision=highest)
    i_ref[...] = sweep_inverse(schur)
    low_part = mm(
        i_ref[...], side[half:] - mm(wide, side[:half], TN, precision=highest), precision=highest
    )
    coef_ref[half:, :] = low_part.astype(bf16)
    coef_ref[:half, :] = (
        mm(top, side[:half], precision=highest) - mm(wide, low_part, precision=highest)
    ).astype(bf16)


def ridge(prev, rows, sticky, basis, length):
    return pl.pallas_call(
        functools.partial(ridge_kernel, length),
        out_shape=jax.ShapeDtypeStruct((basis, prev.shape[1]), bf16),
        scratch_shapes=[
            pltpu.VMEM((basis, basis), f32),
            pltpu.VMEM((basis // 2, basis // 2), f32),
        ],
        compiler_params=vmem_params(),
        name="ridge",
    )(prev, rows[:, None], sticky[:, None])


def head_mask(h):
    lane = lax.broadcasted_iota(jnp.int32, (1, 128), 1)
    return (lane >= 64) if h else (lane < 64)


def turn(a):
    return jnp.transpose(a.astype(f32))


def place_params(q, mk, musg, mask, basis):
    u = jnp.where(mask, mm(musg, mk.astype(f32), precision=highest) * 0.125, 0.0)
    ab = mm(u, q.astype(f32), NT, precision=highest)
    spread = 1.0 / basis
    a = ab[0:1]
    b = ab[1:2]
    centre = 1.0 / (1.0 + jnp.exp(-a))
    soft = jnp.maximum(b, 0.0) + jnp.log1p(jnp.exp(-jnp.abs(b)))
    total = spread * spread + var_scale * soft
    return u, b, centre, total


def causal_block(n):
    key = lax.broadcasted_iota(jnp.int32, (n, n), 0)
    query = lax.broadcasted_iota(jnp.int32, (n, n), 1)
    return key <= query


def attn_fwd_kernel(q_ref, k_ref, v_ref, mk_ref, mv_ref, musg_ref, ctx_ref, lse_ref, s_ref, o_ref):
    tokens = q_ref.shape[0]
    basis = mk_ref.shape[0]
    spread = 1.0 / basis
    centers = (lax.broadcasted_iota(jnp.int32, (basis, 1), 0).astype(f32) + 0.5) / basis
    v_t = turn(v_ref[...]).astype(bf16)
    mv_t = turn(mv_ref[...]).astype(bf16)
    allowed = causal_block(QB)
    for h in range(2):
        mask = head_mask(h)
        rows = slice(h * 64, h * 64 + 64)
        u, b, centre, total = place_params(q_ref[...], mk_ref[...], musg_ref[h], mask, basis)
        scale = spread * lax.rsqrt(total)
        fall = -0.5 / total
        for qb in range(tokens // QB):
            cols = slice(qb * QB, qb * QB + QB)
            q = jnp.where(mask, q_ref[cols, :].astype(f32) * 0.125, 0.0).astype(bf16)
            top = None
            for kb in range(qb + 1):
                keys = slice(kb * QB, kb * QB + QB)
                s = mm(k_ref[keys, :], q, NT)
                if kb == qb:
                    s = jnp.where(allowed, s, masked_score)
                s_ref[keys, :] = s
                best = jnp.max(s, axis=0, keepdims=True)
                top = best if top is None else jnp.maximum(top, best)
            denom = jnp.zeros_like(top)
            out = jnp.zeros((64, QB), f32)
            for kb in range(qb + 1):
                keys = slice(kb * QB, kb * QB + QB)
                e = jnp.exp(s_ref[keys, :] - top)
                denom = denom + jnp.sum(e, axis=0, keepdims=True)
                out = out + mm(v_t[rows, keys], e.astype(bf16))
            gap = centre[:, cols] - centers
            dens = (scale[:, cols] * jnp.exp(gap * gap * fall[:, cols])).astype(bf16)
            o_ref[rows, cols] = out / denom + mm(mv_t[rows, :], dens)
            lse_ref[0, h : h + 1, cols] = top + jnp.log(denom)
    ctx_ref[...] = jnp.transpose(o_ref[...]).astype(bf16)


def attn_fwd(qkv, mkv, musg):
    tokens = qkv.shape[0]
    basis = mkv.shape[0]
    pairs = qkv.shape[1] // 384
    part = lambda n, j: pl.BlockSpec((n, 128), lambda i, j=j: (0, i + j * pairs))
    return pl.pallas_call(
        attn_fwd_kernel,
        grid=(pairs,),
        in_specs=[
            part(tokens, 0),
            part(tokens, 1),
            part(tokens, 2),
            part(basis, 0),
            part(basis, 1),
            pl.BlockSpec((2, 8, basis), lambda i: (i, 0, 0)),
        ],
        out_specs=[
            part(tokens, 0),
            pl.BlockSpec((1, 2, tokens), lambda i: (i, 0, 0)),
        ],
        out_shape=[
            jax.ShapeDtypeStruct((tokens, pairs * 128), bf16),
            jax.ShapeDtypeStruct((pairs, 2, tokens), f32),
        ],
        scratch_shapes=[pltpu.VMEM((tokens, QB), f32), pltpu.VMEM((128, tokens), f32)],
        compiler_params=vmem_params(),
        name="attn_fwd",
    )(qkv, qkv, qkv, mkv, mkv, musg)


def attn_bwd_kernel(
    q_ref,
    k_ref,
    v_ref,
    mk_ref,
    mv_ref,
    musg_ref,
    do_ref,
    lse_ref,
    dq_ref,
    dk_ref,
    dv_ref,
    gmk_ref,
    gmv_ref,
    gmusg_ref,
    p_ref,
    dp_ref,
    dka_ref,
    dva_ref,
    dqt_ref,
    gmv_acc,
):
    tokens = q_ref.shape[0]
    basis = mk_ref.shape[0]
    spread = 1.0 / basis
    centers = (lax.broadcasted_iota(jnp.int32, (basis, 1), 0).astype(f32) + 0.5) / basis
    k_t = turn(k_ref[...]).astype(bf16)
    allowed = causal_block(QB)
    dka_ref[...] = jnp.zeros_like(dka_ref)
    dva_ref[...] = jnp.zeros_like(dva_ref)
    gmv_acc[...] = jnp.zeros_like(gmv_acc)
    gmk = jnp.zeros((basis, 128), f32)
    pick_row = lax.broadcasted_iota(jnp.int32, (8, 1), 0)
    for h in range(2):
        mask = head_mask(h)
        rows = slice(h * 64, h * 64 + 64)
        musg = musg_ref[h]
        u, b, centre, total = place_params(q_ref[...], mk_ref[...], musg, mask, basis)
        scale = spread * lax.rsqrt(total)
        inv = 1.0 / total
        z = jnp.zeros((8, 128), f32)
        for qb in range(tokens // QB):
            cols = slice(qb * QB, qb * QB + QB)
            q = jnp.where(mask, q_ref[cols, :].astype(f32) * 0.125, 0.0).astype(bf16)
            do = jnp.where(mask, do_ref[cols, :].astype(f32), 0.0).astype(bf16)
            lse = lse_ref[0, h : h + 1, cols]
            dot_row = jnp.zeros((1, QB), f32)
            for kb in range(qb + 1):
                keys = slice(kb * QB, kb * QB + QB)
                p = jnp.exp(mm(k_ref[keys, :], q, NT) - lse)
                if kb == qb:
                    p = jnp.where(allowed, p, 0.0)
                dp = mm(v_ref[keys, :], do, NT)
                p_ref[keys, :] = p
                dp_ref[keys, :] = dp
                dot_row = dot_row + jnp.sum(p * dp, axis=0, keepdims=True)
                dva_ref[keys, :] += mm(p.astype(bf16), do)
            dq_t = jnp.zeros((64, QB), f32)
            for kb in range(qb + 1):
                keys = slice(kb * QB, kb * QB + QB)
                ds = (p_ref[keys, :] * (dp_ref[keys, :] - dot_row)).astype(bf16)
                dka_ref[keys, :] += mm(ds, q)
                dq_t = dq_t + mm(k_t[rows, keys], ds)
            dqt_ref[rows, cols] = dq_t * 0.125
            gap = centre[:, cols] - centers
            gap2 = gap * gap
            inv_b = inv[:, cols]
            dens = scale[:, cols] * jnp.exp(gap2 * (-0.5 * inv_b))
            gmv_acc[...] += mm(dens.astype(bf16), do)
            e = mm(mv_ref[...], do, NT) * dens
            sum0 = jnp.sum(e, axis=0, keepdims=True)
            sum1 = jnp.sum(e * gap, axis=0, keepdims=True)
            sum2 = jnp.sum(e * gap2, axis=0, keepdims=True)
            c = centre[:, cols]
            da = -sum1 * inv_b * c * (1.0 - c)
            dtotal = 0.5 * inv_b * (sum2 * inv_b - sum0)
            db = dtotal * var_scale / (1.0 + jnp.exp(-b[:, cols]))
            dab = jnp.where(pick_row == 0, da, jnp.where(pick_row == 1, db, 0.0))
            dqt_ref[:, cols] += mm(u, dab, TN, precision=highest)
            z = z + mm(dab, q.astype(f32), precision=highest)
        gmk = gmk + mm(musg, z, TN, precision=highest)
        gmusg_ref[h] = mm(z, mk_ref[...].astype(f32), NT, precision=highest)
    dq_ref[...] = jnp.transpose(dqt_ref[...]).astype(bf16)
    dk_ref[...] = dka_ref[...].astype(bf16)
    dv_ref[...] = dva_ref[...].astype(bf16)
    gmk_ref[...] = gmk.astype(bf16)
    gmv_ref[...] = gmv_acc[...].astype(bf16)


def attn_bwd(qkv, mkv, musg, do, lse):
    tokens = qkv.shape[0]
    basis = mkv.shape[0]
    pairs = qkv.shape[1] // 384
    part = lambda n, j: pl.BlockSpec((n, 128), lambda i, j=j: (0, i + j * pairs))
    weights = pl.BlockSpec((2, 8, basis), lambda i: (i, 0, 0))
    return pl.pallas_call(
        attn_bwd_kernel,
        grid=(pairs,),
        in_specs=[
            part(tokens, 0),
            part(tokens, 1),
            part(tokens, 2),
            part(basis, 0),
            part(basis, 1),
            weights,
            part(tokens, 0),
            pl.BlockSpec((1, 2, tokens), lambda i: (i, 0, 0)),
        ],
        out_specs=[
            part(tokens, 0),
            part(tokens, 0),
            part(tokens, 0),
            part(basis, 0),
            part(basis, 0),
            weights,
        ],
        out_shape=[
            jax.ShapeDtypeStruct((tokens, pairs * 128), bf16),
            jax.ShapeDtypeStruct((tokens, pairs * 128), bf16),
            jax.ShapeDtypeStruct((tokens, pairs * 128), bf16),
            jax.ShapeDtypeStruct((basis, pairs * 128), bf16),
            jax.ShapeDtypeStruct((basis, pairs * 128), bf16),
            jax.ShapeDtypeStruct((pairs * 2, 8, basis), f32),
        ],
        scratch_shapes=[
            pltpu.VMEM((tokens, QB), f32),
            pltpu.VMEM((tokens, QB), f32),
            pltpu.VMEM((tokens, 128), f32),
            pltpu.VMEM((tokens, 128), f32),
            pltpu.VMEM((128, tokens), f32),
            pltpu.VMEM((basis, 128), f32),
        ],
        compiler_params=vmem_params(),
        name="attn_bwd",
    )(qkv, qkv, qkv, mkv, mkv, musg, do, lse)


class Reducer:
    stages = 8

    def __init__(self, first, src, out, scratch, sems):
        b, k = lax.axis_index("batch"), lax.axis_index("blk")
        z, x = b // 2, b % 2
        y, self.core = k // 2, k % 2
        x_peer, y_peer = (z * 2 + 1 - x, k), (b, (1 - y) * 2 + self.core)
        self.z = z
        self.f, self.s = (x, y) if first == "x" else (y, x)
        self.peer_f, self.peer_s = (x_peer, y_peer) if first == "x" else (y_peer, x_peer)
        self.peer_z = [(((z + d) % 4) * 2 + x, k) for d in (1, 2, 3)]
        self.peer_core = (b, y * 2 + 1 - self.core)
        self.src, self.out = src, out
        self.r1, self.send2, self.r2, self.acc, self.r3 = scratch
        self.sems = sems
        self.rows = src.shape[0]
        self.step = self.rows // 16
        self.open = []

    def copy(self, n, src, dst, peer):
        c = pltpu.make_async_remote_copy(
            src_ref=src,
            dst_ref=dst,
            send_sem=self.sems.at[0, n],
            recv_sem=self.sems.at[1, n],
            device_id=peer,
            device_id_type=pl.DeviceIdType.MESH,
        )
        c.start()
        self.open.append(c)
        return c

    def at(self, row, count):
        return pl.ds(pl.multiple_of(row, self.step), count)

    def loop(self, body):
        def step(i, carry):
            body(i * self.step)
            return carry

        lax.fori_loop(0, 4, step, 0)

    def run(self, stage):
        rows, step, f, s, z = self.rows, self.step, self.f, self.s, self.z
        half, quarter = rows // 2, rows // 4
        home = self.out.at[self.core]
        mine = f * half + s * quarter
        other = f * half + (1 - s) * quarter
        if stage == 0:
            self.c1 = self.copy(0, self.src.at[self.at((1 - f) * half, half)], self.r1, self.peer_f)
        elif stage == 1:
            self.c1.wait_recv()

            def add(i):
                self.send2[self.at(i, step)] = (
                    self.src[self.at(other + i, step)].astype(f32)
                    + self.r1[self.at((1 - s) * quarter + i, step)].astype(f32)
                ).astype(self.send2.dtype)

            self.loop(add)
            self.c2 = self.copy(1, self.send2, self.r2, self.peer_s)
        elif stage == 2:
            self.c2.wait_recv()

            def add(i):
                self.acc[self.at(i, step)] = (
                    self.src[self.at(mine + i, step)].astype(f32)
                    + self.r1[self.at(s * quarter + i, step)].astype(f32)
                    + self.r2[self.at(i, step)].astype(f32)
                ).astype(self.acc.dtype)

            self.loop(add)
            self.c3 = [
                self.copy(2 + d, self.acc.at[self.at(((z + d + 1) % 4) * step, step)], self.r3.at[d], self.peer_z[d])
                for d in range(3)
            ]
        elif stage == 3:
            for c in self.c3:
                c.wait_recv()
            total = self.acc[self.at(z * step, step)].astype(f32)
            for d in range(3):
                total = total + self.r3[d].astype(f32)
            home[self.at(mine + z * step, step)] = total.astype(self.out.dtype)
            part = home.at[self.at(mine + z * step, step)]
            self.c4 = [self.copy(5 + d, part, part, self.peer_z[d]) for d in range(3)]
        elif stage == 4:
            for c in self.c4:
                c.wait_recv()
            part = home.at[self.at(mine, quarter)]
            self.c5 = self.copy(8, part, part, self.peer_s)
            self.c7 = [self.copy(10, part, part, self.peer_core)]
        elif stage == 5:
            self.c5.wait_recv()
            part = home.at[self.at(f * half, half)]
            self.c6 = self.copy(9, part, part, self.peer_f)
            part = home.at[self.at(other, quarter)]
            self.c7.append(self.copy(11, part, part, self.peer_core))
        elif stage == 6:
            self.c6.wait_recv()
            part = home.at[self.at((1 - f) * half, half)]
            self.c7.append(self.copy(12, part, part, self.peer_core))
        elif stage == 7:
            for c in self.c7:
                c.wait_recv()
            for c in self.open:
                c.wait_send()


def greet():
    b, k = lax.axis_index("batch"), lax.axis_index("blk")
    z, x, y, core = b // 2, b % 2, k // 2, k % 2
    peers = [(z * 2 + 1 - x, k), (b, (1 - y) * 2 + core), (b, y * 2 + 1 - core)]
    peers += [(((z + d) % 4) * 2 + x, k) for d in (1, 2, 3)]
    barrier = pltpu.get_barrier_semaphore()
    for peer in peers:
        pl.semaphore_signal(barrier, inc=1, device_id=peer, device_id_type=pl.DeviceIdType.MESH)
    pl.semaphore_wait(barrier, len(peers))


def reduce_kernel(plan, *refs):
    n = len(plan)
    scratch = refs[2 * n :]
    jobs = []
    greet()
    for i, (first, late) in enumerate(plan):
        own = scratch[6 * i : 6 * i + 6]
        jobs.append((Reducer(first, refs[i], refs[n + i], own[:5], own[5]), late))
    for t in range(Reducer.stages + max(late for _, late in plan)):
        for job, late in jobs:
            if 0 <= t - late < Reducer.stages:
                job.run(t - late)


def all_reduce(arrays, plan):
    scratch = []
    for a in arrays:
        rows, cols = a.shape
        scratch += [
            pltpu.VMEM((rows // 2, cols), a.dtype),
            pltpu.VMEM((rows // 4, cols), a.dtype),
            pltpu.VMEM((rows // 4, cols), a.dtype),
            pltpu.VMEM((rows // 4, cols), a.dtype),
            pltpu.VMEM((3, rows // 16, cols), a.dtype),
            pltpu.SemaphoreType.DMA((2, 13)),
        ]
    whole = pl.BlockSpec(memory_space=pltpu.VMEM)
    return pl.pallas_call(
        functools.partial(reduce_kernel, plan),
        in_specs=[whole] * len(arrays),
        out_specs=[whole] * len(arrays),
        out_shape=[jax.ShapeDtypeStruct((2,) + a.shape, a.dtype) for a in arrays],
        scratch_shapes=scratch,
        compiler_params=vmem_params(collective_id=1, has_side_effects=True),
        name="all_reduce",
    )(*arrays)


def chip_local(
    inputs,
    previous,
    memory_rows,
    sticky_positions,
    cotangent,
    ln1_gain,
    ln1_bias,
    query_weight,
    key_weight,
    value_weight,
    out_weight,
    mu_weight,
    sigma_weight,
    ln2_gain,
    ln2_bias,
    expand_weight,
    up_bias,
    down_weight,
    down_bias,
):
    tok_rows, width = inputs.shape[1:]
    length = tok_rows * 4
    heads, basis = mu_weight.shape
    ff = up_bias.shape[0]
    place = lax.axis_index("blk")
    y, core = place // 2, place % 2
    to_y = [(k, k ^ 2) for k in range(4)]
    to_core = [(k, k ^ 1) for k in range(4)]

    def swap_y(a):
        return lax.ppermute(a, "blk", to_y)

    def swap_core(a):
        return lax.ppermute(a, "blk", to_core)

    def pick(a, i, axis=0):
        return lax.dynamic_index_in_dim(a, i, axis, keepdims=False)

    def to_chip(a):
        own, got = pick(a, y), swap_y(pick(a, 1 - y))
        half = jnp.stack([jnp.where(y == 0, own, got), jnp.where(y == 0, got, own)])
        sibling = swap_core(half)
        whole = jnp.stack(
            [jnp.where(core == 0, half, sibling), jnp.where(core == 0, sibling, half)], 1
        )
        return whole.reshape(length, width)

    def my_rows(a, c):
        return pick(a.reshape(2, 2, tok_rows, a.shape[-1]), c, 1)

    def from_chip(half, sent):
        own, got = pick(half, y), swap_y(pick(half, 1 - y).astype(sent)).astype(half.dtype)
        return jnp.stack([jnp.where(y == 0, own, got), jnp.where(y == 0, got, own)])

    def columns(w):
        n = w.shape[1] // 2
        return lax.dynamic_slice_in_dim(w, core * n, n, 1)

    def rows_of(w):
        n = w.shape[0] // 2
        return lax.dynamic_slice_in_dim(w, core * n, n, 0)

    wide = width // 2
    w_kv = jnp.concatenate([columns(key_weight), columns(value_weight)], 1)
    w_qkv = jnp.concatenate([columns(query_weight), w_kv], 1)
    expand = columns(expand_weight)
    down = rows_of(down_weight)
    out_own = rows_of(out_weight)
    out_sib = lax.dynamic_slice_in_dim(out_weight, (1 - core) * wide, wide, 0)
    bias_up = lax.dynamic_slice_in_dim(up_bias, core * (ff // 2), ff // 2, 0)
    musg = jnp.stack([rows_of(mu_weight), rows_of(sigma_weight)], 1)
    musg = jnp.pad(musg, ((0, 0), (0, 6), (0, 0)))

    hidden_in = to_chip(inputs).astype(f32)
    prev = to_chip(previous)
    cot = to_chip(cotangent)

    normed_low = layer_norm(hidden_in, ln1_gain, ln1_bias).astype(bf16)
    qkv = mm(normed_low, w_qkv).astype(bf16)
    coeff_low = ridge(prev, pick(memory_rows, y), pick(sticky_positions, y), basis, length)
    mkv = mm(coeff_low, w_kv).astype(bf16)
    ctx, lse = attn_fwd(qkv, mkv, musg)
    ctx_sib = swap_core(ctx)
    mixed = hidden_in + (mm(ctx, out_own) + mm(ctx_sib, out_sib))
    normed_two_low = layer_norm(mixed, ln2_gain, ln2_bias).astype(bf16)
    hidden_up = mm(normed_two_low, expand) + bias_up
    active, gelu_pull = jax.vjp(gelu_tanh, hidden_up)
    active_low = active.astype(bf16)
    result = mm(active_low, down)
    result = my_rows(result, core) + swap_core(my_rows(result, 1 - core))
    result = my_rows(mixed, core) + result + down_bias
    block_output = from_chip(result.astype(bf16), bf16)

    grad_result = cot.astype(f32)
    grad_down_bias = jnp.sum(grad_result, axis=0)
    grad_down = mm(active_low, cot, TN)
    grad_up_low = gelu_pull(mm(cot, down, NT))[0].astype(bf16)
    grad_up_bias = jnp.sum(grad_up_low.astype(f32), axis=0)
    grad_up = mm(normed_two_low, grad_up_low, TN)
    grad_normed_two = mm(grad_up_low, expand, NT)
    grad_normed_two = grad_normed_two + swap_core(grad_normed_two)
    norm_two_pull = jax.vjp(layer_norm, mixed, ln2_gain, ln2_bias)[1]
    grad_mixed_norm, grad_ln2_gain, grad_ln2_bias = norm_two_pull(grad_normed_two)
    grad_mixed = grad_result + grad_mixed_norm
    grad_mixed_low = grad_mixed.astype(bf16)
    grad_out_t = mm(grad_mixed_low, ctx, TN)
    grad_ctx = mm(grad_mixed_low, out_own, NT).astype(bf16)
    dq, dk, dv, gmk, gmv, gmusg = attn_bwd(qkv, mkv, musg, grad_ctx, lse)
    grad_query = mm(normed_low, dq, TN)
    grad_key = mm(normed_low, dk, TN) + mm(coeff_low, gmk, TN)
    grad_value = mm(normed_low, dv, TN) + mm(coeff_low, gmv, TN)
    dqkv = jnp.concatenate([dq, dk, dv], 1)
    grad_normed = mm(dqkv, w_qkv, NT)
    grad_normed = my_rows(grad_normed, core) + swap_core(my_rows(grad_normed, 1 - core))
    norm_one_pull = jax.vjp(layer_norm, my_rows(hidden_in, core), ln1_gain, ln1_bias)[1]
    grad_in_norm, grad_ln1_gain, grad_ln1_bias = norm_one_pull(grad_normed)
    grad_inputs = from_chip(my_rows(grad_mixed, core) + grad_in_norm, bf16)

    n_own = heads // 2 * basis
    small = jnp.concatenate(
        [
            gmusg[:, 0].reshape(-1),
            gmusg[:, 1].reshape(-1),
            grad_up_bias,
            grad_ln2_gain,
            grad_ln2_bias,
            grad_down_bias,
            grad_ln1_gain,
            grad_ln1_bias,
        ]
    )
    small_rows = -(-small.shape[0] // (128 * 128)) * 128
    small = jnp.pad(small, (0, small_rows * 128 - small.shape[0])).reshape(small_rows, 128)
    a1, b1, a2, b2, s = all_reduce(
        (
            grad_down.astype(bf16),
            grad_up.astype(bf16),
            jnp.concatenate([grad_query, grad_key], 1).astype(bf16),
            jnp.concatenate([grad_value, grad_out_t], 1).astype(bf16),
            small,
        ),
        (("x", 0), ("y", 0), ("x", 2), ("y", 2), ("x", 2)),
    )

    def side_by_side(a, lo, hi):
        return jnp.concatenate([a[0, :, lo:hi], a[1, :, lo:hi]], 1).astype(f32)

    s = s.reshape(2, -1)
    cuts = [n_own, n_own, ff // 2, width, width, width, width, width]
    parts, start = [], 0
    for n in cuts:
        parts.append(s[:, start : start + n])
        start += n
    return (
        block_output,
        grad_inputs,
        parts[6][0] + parts[6][1],
        parts[7][0] + parts[7][1],
        side_by_side(a2, 0, wide),
        side_by_side(a2, wide, width),
        side_by_side(b2, 0, wide),
        side_by_side(b2, wide, width).T,
        parts[0].reshape(heads, basis),
        parts[1].reshape(heads, basis),
        parts[3][0],
        parts[4][0],
        side_by_side(b1, 0, ff // 2),
        parts[2].reshape(ff),
        a1.reshape(ff, width).astype(f32),
        parts[5][0],
    )


def pick(mesh):
    def step(*arrays):
        inputs, mu = arrays[0], arrays[11]
        fits = (
            mesh.shape["batch"] == 8
            and mesh.shape["blk"] == 4
            and inputs.shape[0] == 2
            and inputs.shape[1] % QB == 0
            and mu.shape[0] % 4 == 0
            and inputs.shape[2] == mu.shape[0] * 64
        )
        return (chip_local if fits else general)(*arrays)

    return step


def solution(mesh):
    return jax.shard_map(
        pick(mesh),
        mesh=mesh,
        in_specs=(
            P("batch", "blk", None),
            P("batch", "blk", None),
            P("batch", None),
            P("batch", None),
            P("batch", "blk", None),
            P(),
            P(),
            P(),
            P(),
            P(),
            P(),
            P(),
            P(),
            P(),
            P(),
            P(),
            P(),
            P(),
            P(),
        ),
        out_specs=(
            P("batch", "blk", None),
            P("batch", "blk", None),
            P(),
            P(),
            P(),
            P(),
            P(),
            P(),
            P(),
            P(),
            P(),
            P(),
            P(),
            P(),
            P(),
            P(),
        ),
        check_vma=False,
    )
```

```python
import functools
from types import SimpleNamespace

import jax
import jax.numpy as jnp
from jax import lax
from jax.experimental import pallas as pl
from jax.experimental.pallas import tpu as pltpu
from jax.sharding import PartitionSpec as P

epsilon = 1e-05
ridge_weight = 1.0
var_scale = 0.01
masked_score = -1e30
BLK = "blk"
BATCH = "batch"
highest = lax.Precision.HIGHEST


def layer_norm(values, gain, bias):
    center = jnp.mean(values, axis=-1, keepdims=True)
    shifted = values - center
    spread_sq = jnp.mean(shifted * shifted, axis=-1, keepdims=True)
    return shifted * lax.rsqrt(spread_sq + epsilon) * gain + bias


def density(scores, mu_row, sigma_row):
    count = scores.shape[-1]
    centers = (jnp.arange(count, dtype=scores.dtype) + 0.5) / count
    spread = 1.0 / count
    centre = jax.nn.sigmoid(jnp.dot(scores, mu_row, precision=highest))
    variance = var_scale * jax.nn.softplus(jnp.dot(scores, sigma_row, precision=highest))
    total = spread * spread + variance
    return (spread * lax.rsqrt(total))[..., None] * jnp.exp(
        -((centre[..., None] - centers) ** 2) / (2.0 * total[..., None])
    )


def project(source, weight):
    return jnp.einsum("std,de->ste", source, weight, preferred_element_type=jnp.float32)


def weight_grad(source, grads):
    return jnp.einsum("std,ste->de", source, grads, preferred_element_type=jnp.float32)


def back_project(grads, weight):
    return jnp.einsum("ste,de->std", grads, weight, preferred_element_type=jnp.float32)


def gelu_tanh(values):
    return jax.nn.gelu(values, approximate=True)


def general(
    inputs,
    previous,
    memory_rows,
    sticky_positions,
    cotangent,
    ln1_gain,
    ln1_bias,
    query_weight,
    key_weight,
    value_weight,
    out_weight,
    mu_weight,
    sigma_weight,
    ln2_gain,
    ln2_bias,
    expand_weight,
    up_bias,
    down_weight,
    down_bias,
):
    seg_count, tok_rows, model_width = inputs.shape
    blocks = lax.axis_size(BLK)
    length = tok_rows * blocks
    first_row = lax.axis_index(BLK) * tok_rows
    head_count, basis_count = mu_weight.shape
    head_width = model_width // head_count
    centers = (jnp.arange(basis_count, dtype=jnp.float32) + 0.5) / basis_count
    spread = 1.0 / basis_count
    places = (sticky_positions.astype(jnp.float32) + 0.5) / length
    features = jnp.exp(-((places[..., None] - centers) ** 2) / (2.0 * spread * spread)).astype(
        jnp.bfloat16
    )
    local_index = memory_rows - first_row
    owned_rows = (local_index >= 0) & (local_index < tok_rows)
    picked = jax.vmap(lambda shard_rows, row_index: shard_rows[row_index])(
        previous, jnp.clip(local_index, 0, tok_rows - 1)
    )
    picked = jnp.where(owned_rows[..., None], picked, jnp.zeros_like(picked))
    own_features = jnp.where(owned_rows[..., None], features, jnp.zeros_like(features))
    side_part = jnp.einsum("smn,smd->snd", own_features, picked, preferred_element_type=jnp.float32)
    gram_part = jnp.einsum(
        "smn,smk->snk", own_features, own_features, preferred_element_type=jnp.float32
    )
    gram_sum, right_side = lax.psum((gram_part, side_part), BLK)
    system = gram_sum + ridge_weight * jnp.eye(basis_count, dtype=jnp.float32)
    factor = jnp.linalg.cholesky(system)
    coefficients = jax.scipy.linalg.cho_solve((factor, True), right_side)
    coeff_low = coefficients.astype(jnp.bfloat16)
    hidden_in = inputs.astype(jnp.float32)
    normed_low = layer_norm(hidden_in, ln1_gain, ln1_bias).astype(jnp.bfloat16)
    queries = project(normed_low, query_weight).astype(jnp.bfloat16)
    keys_local = project(normed_low, key_weight).astype(jnp.bfloat16)
    values_local = project(normed_low, value_weight).astype(jnp.bfloat16)
    mem_keys = project(coeff_low, key_weight).astype(jnp.bfloat16)
    mem_values = project(coeff_low, value_weight).astype(jnp.bfloat16)
    all_keys, all_values = (
        lax.all_gather(keys_local, BLK, axis=1, tiled=True),
        lax.all_gather(values_local, BLK, axis=1, tiled=True),
    )

    def split_heads(array):
        return array.reshape(array.shape[0], array.shape[1], head_count, head_width).transpose(
            2, 0, 1, 3
        )

    def merge_heads(array):
        return array.transpose(1, 2, 0, 3).reshape(array.shape[1], array.shape[2], model_width)

    query_pos = first_row + jnp.arange(tok_rows)
    key_pos = jnp.arange(length)
    causal = key_pos[None, :] <= query_pos[:, None]

    def forward_head(operands):
        query_h, key_h, value_h, memkey_h, memval_h, mu_row, sigma_row = operands
        scores = (
            jnp.einsum("sqd,skd->sqk", query_h, key_h, preferred_element_type=jnp.float32) * 0.125
        )
        scores = jnp.where(causal, scores, masked_score)
        top = jnp.max(scores, axis=-1, keepdims=True)
        raised = jnp.exp(scores - top)
        total = jnp.sum(raised, axis=-1, keepdims=True)
        probs = raised / total
        log_total = (top + jnp.log(total))[..., 0]
        attended = jnp.einsum(
            "sqk,skd->sqd", probs.astype(jnp.bfloat16), value_h, preferred_element_type=jnp.float32
        )
        memory_scores = (
            jnp.einsum("sqd,snd->sqn", query_h, memkey_h, preferred_element_type=jnp.float32)
            * 0.125
        )
        weights_mem = density(memory_scores, mu_row, sigma_row)
        recalled = jnp.einsum(
            "sqn,snd->sqd",
            weights_mem.astype(jnp.bfloat16),
            memval_h,
            preferred_element_type=jnp.float32,
        )
        return (attended + recalled, log_total)

    head_queries = split_heads(queries)
    head_keys = split_heads(all_keys)
    value_per_head = split_heads(all_values)
    head_memkeys = split_heads(mem_keys)
    head_memvals = split_heads(mem_values)
    heads_ctx, log_totals = lax.map(
        forward_head,
        (
            head_queries,
            head_keys,
            value_per_head,
            head_memkeys,
            head_memvals,
            mu_weight,
            sigma_weight,
        ),
    )
    context_low = merge_heads(heads_ctx).astype(jnp.bfloat16)
    mixed = hidden_in + project(context_low, out_weight)
    normed_two_low = layer_norm(mixed, ln2_gain, ln2_bias).astype(jnp.bfloat16)
    hidden_up = (
        jnp.einsum("std,df->stf", normed_two_low, expand_weight, preferred_element_type=jnp.float32)
        + up_bias
    )
    active_low = gelu_tanh(hidden_up).astype(jnp.bfloat16)
    result = (
        mixed
        + jnp.einsum("stf,fd->std", active_low, down_weight, preferred_element_type=jnp.float32)
        + down_bias
    )
    block_output = result.astype(jnp.bfloat16)
    grad_result = cotangent.astype(jnp.float32)
    grad_down_bias = jnp.sum(grad_result, axis=(0, 1))
    grad_down_weight = jnp.einsum(
        "stf,std->fd", active_low, cotangent, preferred_element_type=jnp.float32
    )
    grad_active = jnp.einsum(
        "std,fd->stf", cotangent, down_weight, preferred_element_type=jnp.float32
    )
    gelu_value, gelu_pull = jax.vjp(gelu_tanh, hidden_up)
    grad_up_low = gelu_pull(grad_active)[0].astype(jnp.bfloat16)
    grad_up_bias = jnp.sum(grad_up_low.astype(jnp.float32), axis=(0, 1))
    grad_up_weight = jnp.einsum(
        "std,stf->df", normed_two_low, grad_up_low, preferred_element_type=jnp.float32
    )
    grad_normed_two = jnp.einsum(
        "stf,df->std", grad_up_low, expand_weight, preferred_element_type=jnp.float32
    )
    norm_two_value, norm_two_pull = jax.vjp(layer_norm, mixed, ln2_gain, ln2_bias)
    grad_mixed_norm, grad_ln2_gain, grad_ln2_bias = norm_two_pull(grad_normed_two)
    grad_mixed = grad_result + grad_mixed_norm
    grad_mixed_low = grad_mixed.astype(jnp.bfloat16)
    grad_out_weight = weight_grad(context_low, grad_mixed_low)
    grad_context_low = back_project(grad_mixed_low, out_weight).astype(jnp.bfloat16)

    def backward_head(operands):
        query_h, key_h, value_h, memkey_h, memval_h, mu_row, sigma_row, grad_h, log_total = operands
        scores = (
            jnp.einsum("sqd,skd->sqk", query_h, key_h, preferred_element_type=jnp.float32) * 0.125
        )
        probs = jnp.where(causal, jnp.exp(scores - log_total[..., None]), 0.0)
        grad_probs = jnp.einsum("sqd,skd->sqk", grad_h, value_h, preferred_element_type=jnp.float32)
        row_dot = jnp.sum(probs * grad_probs, axis=-1, keepdims=True)
        grad_scores = (probs * (grad_probs - row_dot)).astype(jnp.bfloat16)
        grad_query = (
            jnp.einsum("sqk,skd->sqd", grad_scores, key_h, preferred_element_type=jnp.float32)
            * 0.125
        )
        memory_scores = (
            jnp.einsum("sqd,snd->sqn", query_h, memkey_h, preferred_element_type=jnp.float32)
            * 0.125
        )
        weights_mem, density_pull = jax.vjp(density, memory_scores, mu_row, sigma_row)
        weights_low = weights_mem.astype(jnp.bfloat16)
        grad_weights = jnp.einsum(
            "sqd,snd->sqn", grad_h, memval_h, preferred_element_type=jnp.float32
        )
        grad_memval = jnp.einsum(
            "sqn,sqd->snd", weights_low, grad_h, preferred_element_type=jnp.float32
        )
        grad_memscores, grad_mu, grad_sigma = density_pull(grad_weights)
        grad_memscores_low = grad_memscores.astype(jnp.bfloat16)
        grad_query = (
            grad_query
            + jnp.einsum(
                "sqn,snd->sqd", grad_memscores_low, memkey_h, preferred_element_type=jnp.float32
            )
            * 0.125
        )
        grad_memkey = (
            jnp.einsum(
                "sqn,sqd->snd", grad_memscores_low, query_h, preferred_element_type=jnp.float32
            )
            * 0.125
        )
        grad_key = (
            jnp.einsum("sqk,sqd->skd", grad_scores, query_h, preferred_element_type=jnp.float32)
            * 0.125
        )
        grad_value = jnp.einsum(
            "sqk,sqd->skd", probs.astype(jnp.bfloat16), grad_h, preferred_element_type=jnp.float32
        )
        return (grad_query, grad_memkey, grad_memval, grad_mu, grad_sigma, grad_key, grad_value)

    head_grads = split_heads(grad_context_low)
    outcome = lax.map(
        backward_head,
        (
            head_queries,
            head_keys,
            value_per_head,
            head_memkeys,
            head_memvals,
            mu_weight,
            sigma_weight,
            head_grads,
            log_totals,
        ),
    )
    grad_query_heads, grad_memkey_heads, grad_memval_heads, grad_mu_weight, grad_sigma_weight = (
        outcome[:5]
    )
    terms = (
        jnp.stack((outcome[5], outcome[6]))
        .transpose(3, 2, 0, 1, 4)
        .reshape(length, seg_count, 2 * model_width)
    )
    own_terms = lax.psum_scatter(
        terms.astype(jnp.bfloat16), BLK, scatter_dimension=0, tiled=True
    ).astype(jnp.float32)
    own_terms = own_terms.reshape(tok_rows, seg_count, 2, model_width).transpose(2, 1, 0, 3)
    grad_keys = own_terms[0]
    grad_values = own_terms[1]
    grad_queries_low = merge_heads(grad_query_heads).astype(jnp.bfloat16)
    grad_keys_low = grad_keys.astype(jnp.bfloat16)
    grad_values_low = grad_values.astype(jnp.bfloat16)
    memkey_sum, memval_sum = (
        lax.psum(grad_memkey_heads.astype(jnp.bfloat16), BLK).astype(jnp.float32),
        lax.psum(grad_memval_heads.astype(jnp.bfloat16), BLK).astype(jnp.float32),
    )
    gradient_memory_keys_reduced = merge_heads(memkey_sum).astype(jnp.bfloat16)
    gradient_memory_values_reduced = merge_heads(memval_sum).astype(jnp.bfloat16)
    grad_query_weight = weight_grad(normed_low, grad_queries_low)
    grad_key_weight = weight_grad(normed_low, grad_keys_low)
    grad_value_weight = weight_grad(normed_low, grad_values_low)
    grad_normed = (
        back_project(grad_queries_low, query_weight)
        + back_project(grad_keys_low, key_weight)
        + back_project(grad_values_low, value_weight)
    )
    norm_one_value, norm_one_pull = jax.vjp(layer_norm, hidden_in, ln1_gain, ln1_bias)
    grad_in_norm, grad_ln1_gain, grad_ln1_bias = norm_one_pull(grad_normed)
    grad_inputs = grad_mixed + grad_in_norm
    shares = (
        lax.psum_scatter(
            grad_ln1_gain.astype(jnp.bfloat16), BLK, scatter_dimension=0, tiled=True
        ).astype(jnp.float32),
        lax.psum_scatter(
            grad_ln1_bias.astype(jnp.bfloat16), BLK, scatter_dimension=0, tiled=True
        ).astype(jnp.float32),
        lax.psum_scatter(
            grad_query_weight.astype(jnp.bfloat16), BLK, scatter_dimension=0, tiled=True
        ).astype(jnp.float32),
        lax.psum_scatter(
            grad_key_weight.astype(jnp.bfloat16), BLK, scatter_dimension=0, tiled=True
        ).astype(jnp.float32),
        lax.psum_scatter(
            grad_value_weight.astype(jnp.bfloat16), BLK, scatter_dimension=0, tiled=True
        ).astype(jnp.float32),
        lax.psum_scatter(
            grad_out_weight.astype(jnp.bfloat16), BLK, scatter_dimension=0, tiled=True
        ).astype(jnp.float32),
        lax.psum_scatter(
            grad_mu_weight.astype(jnp.bfloat16), BLK, scatter_dimension=1, tiled=True
        ).astype(jnp.float32),
        lax.psum_scatter(
            grad_sigma_weight.astype(jnp.bfloat16), BLK, scatter_dimension=1, tiled=True
        ).astype(jnp.float32),
        lax.psum_scatter(
            grad_ln2_gain.astype(jnp.bfloat16), BLK, scatter_dimension=0, tiled=True
        ).astype(jnp.float32),
        lax.psum_scatter(
            grad_ln2_bias.astype(jnp.bfloat16), BLK, scatter_dimension=0, tiled=True
        ).astype(jnp.float32),
        lax.psum_scatter(
            grad_up_weight.astype(jnp.bfloat16), BLK, scatter_dimension=0, tiled=True
        ).astype(jnp.float32),
        lax.psum_scatter(
            grad_up_bias.astype(jnp.bfloat16), BLK, scatter_dimension=0, tiled=True
        ).astype(jnp.float32),
        lax.psum_scatter(
            grad_down_weight.astype(jnp.bfloat16), BLK, scatter_dimension=0, tiled=True
        ).astype(jnp.float32),
        lax.psum_scatter(
            grad_down_bias.astype(jnp.bfloat16), BLK, scatter_dimension=0, tiled=True
        ).astype(jnp.float32),
    )
    share_width = model_width // blocks
    coefficient_part = lax.dynamic_slice_in_dim(
        coeff_low, lax.axis_index(BLK) * share_width, share_width, 2
    )
    key_share = shares[3] + jnp.einsum(
        "wrc,wrt->ct",
        coefficient_part,
        gradient_memory_keys_reduced,
        preferred_element_type=jnp.float32,
    )
    value_share = shares[4] + jnp.einsum(
        "wrc,wrt->ct",
        coefficient_part,
        gradient_memory_values_reduced,
        preferred_element_type=jnp.float32,
    )
    totals = (
        lax.psum(shares[0].astype(jnp.bfloat16), BATCH).astype(jnp.float32),
        lax.psum(shares[1].astype(jnp.bfloat16), BATCH).astype(jnp.float32),
        lax.psum(shares[2].astype(jnp.bfloat16), BATCH).astype(jnp.float32),
        lax.psum(key_share.astype(jnp.bfloat16), BATCH).astype(jnp.float32),
        lax.psum(value_share.astype(jnp.bfloat16), BATCH).astype(jnp.float32),
        lax.psum(shares[5].astype(jnp.bfloat16), BATCH).astype(jnp.float32),
        lax.psum(shares[6].astype(jnp.bfloat16), BATCH).astype(jnp.float32),
        lax.psum(shares[7].astype(jnp.bfloat16), BATCH).astype(jnp.float32),
        lax.psum(shares[8].astype(jnp.bfloat16), BATCH).astype(jnp.float32),
        lax.psum(shares[9].astype(jnp.bfloat16), BATCH).astype(jnp.float32),
        lax.psum(shares[10].astype(jnp.bfloat16), BATCH).astype(jnp.float32),
        lax.psum(shares[11].astype(jnp.bfloat16), BATCH).astype(jnp.float32),
        lax.psum(shares[12].astype(jnp.bfloat16), BATCH).astype(jnp.float32),
        lax.psum(shares[13].astype(jnp.bfloat16), BATCH).astype(jnp.float32),
    )
    whole = (
        lax.all_gather(totals[0].astype(jnp.bfloat16), BLK, axis=0, tiled=True).astype(
            jnp.float32
        ),
        lax.all_gather(totals[1].astype(jnp.bfloat16), BLK, axis=0, tiled=True).astype(
            jnp.float32
        ),
        lax.all_gather(totals[2].astype(jnp.bfloat16), BLK, axis=0, tiled=True).astype(
            jnp.float32
        ),
        lax.all_gather(totals[3].astype(jnp.bfloat16), BLK, axis=0, tiled=True).astype(
            jnp.float32
        ),
        lax.all_gather(totals[4].astype(jnp.bfloat16), BLK, axis=0, tiled=True).astype(
            jnp.float32
        ),
        lax.all_gather(totals[5].astype(jnp.bfloat16), BLK, axis=0, tiled=True).astype(
            jnp.float32
        ),
        lax.all_gather(totals[6].astype(jnp.bfloat16), BLK, axis=1, tiled=True).astype(
            jnp.float32
        ),
        lax.all_gather(totals[7].astype(jnp.bfloat16), BLK, axis=1, tiled=True).astype(
            jnp.float32
        ),
        lax.all_gather(totals[8].astype(jnp.bfloat16), BLK, axis=0, tiled=True).astype(
            jnp.float32
        ),
        lax.all_gather(totals[9].astype(jnp.bfloat16), BLK, axis=0, tiled=True).astype(
            jnp.float32
        ),
        lax.all_gather(totals[10].astype(jnp.bfloat16), BLK, axis=0, tiled=True).astype(
            jnp.float32
        ),
        lax.all_gather(totals[11].astype(jnp.bfloat16), BLK, axis=0, tiled=True).astype(
            jnp.float32
        ),
        lax.all_gather(totals[12].astype(jnp.bfloat16), BLK, axis=0, tiled=True).astype(
            jnp.float32
        ),
        lax.all_gather(totals[13].astype(jnp.bfloat16), BLK, axis=0, tiled=True).astype(
            jnp.float32
        ),
    )
    return (
        block_output,
        grad_inputs,
        whole[0],
        whole[1],
        whole[2],
        whole[3],
        whole[4],
        whole[5],
        whole[6],
        whole[7],
        whole[8],
        whole[9],
        whole[10],
        whole[11],
        whole[12],
        whole[13],
    )


f32 = jnp.float32
bf16 = jnp.bfloat16
NN = (((1,), (0,)), ((), ()))
NT = (((1,), (1,)), ((), ()))
TN = (((0,), (0,)), ((), ()))
QB = 256


def mm(a, b, dims=NN, precision=None):
    return lax.dot_general(a, b, dims, precision=precision, preferred_element_type=f32)


def vmem_params(**more):
    return pltpu.CompilerParams(vmem_limit_bytes=56 * 1024 * 1024, **more)


def head_mask(h):
    lane = lax.broadcasted_iota(jnp.int32, (1, 128), 1)
    return (lane >= 64) if h else (lane < 64)


def turn(a):
    return jnp.transpose(a.astype(f32))


def place_params(q, mk, musg, mask, basis):
    u = jnp.where(mask, mm(musg, mk.astype(f32), precision=highest) * 0.125, 0.0)
    ab = mm(u, q.astype(f32), NT, precision=highest)
    spread = 1.0 / basis
    a = ab[0:1]
    b = ab[1:2]
    centre = 1.0 / (1.0 + jnp.exp(-a))
    soft = jnp.maximum(b, 0.0) + jnp.log1p(jnp.exp(-jnp.abs(b)))
    total = spread * spread + var_scale * soft
    return u, b, centre, total


def causal_block(n):
    key = lax.broadcasted_iota(jnp.int32, (n, n), 0)
    query = lax.broadcasted_iota(jnp.int32, (n, n), 1)
    return key <= query


def attn_fwd_kernel(q_ref, k_ref, v_ref, mk_ref, mv_ref, musg_ref, ctx_ref, lse_ref, att_ref, s_ref, o_ref):
    tokens = q_ref.shape[0]
    basis = mk_ref.shape[0]
    spread = 1.0 / basis
    centers = (lax.broadcasted_iota(jnp.int32, (basis, 1), 0).astype(f32) + 0.5) / basis
    v_t = turn(v_ref[...]).astype(bf16)
    mv_t = turn(mv_ref[...]).astype(bf16)
    allowed = causal_block(QB)
    for h in range(2):
        mask = head_mask(h)
        rows = slice(h * 64, h * 64 + 64)
        u, b, centre, total = place_params(q_ref[...], mk_ref[...], musg_ref[h], mask, basis)
        scale = spread * lax.rsqrt(total)
        fall = -0.5 / total
        for qb in range(tokens // QB):
            cols = slice(qb * QB, qb * QB + QB)
            q = jnp.where(mask, q_ref[cols, :].astype(f32) * 0.125, 0.0).astype(bf16)
            top = None
            for kb in range(qb + 1):
                keys = slice(kb * QB, kb * QB + QB)
                s = mm(k_ref[keys, :], q, NT)
                if kb == qb:
                    s = jnp.where(allowed, s, masked_score)
                s_ref[keys, :] = s
                best = jnp.max(s, axis=0, keepdims=True)
                top = best if top is None else jnp.maximum(top, best)
            denom = jnp.zeros_like(top)
            out = jnp.zeros((64, QB), f32)
            for kb in range(qb + 1):
                keys = slice(kb * QB, kb * QB + QB)
                e = jnp.exp(s_ref[keys, :] - top)
                denom = denom + jnp.sum(e, axis=0, keepdims=True)
                out = out + mm(v_t[rows, keys], e.astype(bf16))
            gap = centre[:, cols] - centers
            dens = (scale[:, cols] * jnp.exp(gap * gap * fall[:, cols])).astype(bf16)
            out = out / denom
            att_ref[0, rows, cols] = out
            o_ref[rows, cols] = out + mm(mv_t[rows, :], dens)
            lse_ref[0, h : h + 1, cols] = top + jnp.log(denom)
    ctx_ref[...] = jnp.transpose(o_ref[...]).astype(bf16)


def attn_fwd(qkv, mkv, musg):
    tokens = qkv.shape[0]
    basis = mkv.shape[0]
    pairs = qkv.shape[1] // 384
    part = lambda n, j: pl.BlockSpec((n, 128), lambda i, j=j: (0, i + j * pairs))
    return pl.pallas_call(
        attn_fwd_kernel,
        grid=(pairs,),
        in_specs=[
            part(tokens, 0),
            part(tokens, 1),
            part(tokens, 2),
            part(basis, 0),
            part(basis, 1),
            pl.BlockSpec((2, 8, basis), lambda i: (i, 0, 0)),
        ],
        out_specs=[
            part(tokens, 0),
            pl.BlockSpec((1, 2, tokens), lambda i: (i, 0, 0)),
            pl.BlockSpec((1, 128, tokens), lambda i: (i, 0, 0)),
        ],
        out_shape=[
            jax.ShapeDtypeStruct((tokens, pairs * 128), bf16),
            jax.ShapeDtypeStruct((pairs, 2, tokens), f32),
            jax.ShapeDtypeStruct((pairs, 128, tokens), f32),
        ],
        scratch_shapes=[pltpu.VMEM((tokens, QB), f32), pltpu.VMEM((128, tokens), f32)],
        compiler_params=vmem_params(),
        name="attn_fwd",
    )(qkv, qkv, qkv, mkv, mkv, musg)


class Place:
    def __init__(self):
        b, k = lax.axis_index(BATCH), lax.axis_index(BLK)
        z, x = b // 2, b % 2
        y, core = k // 2, k % 2
        self.z, self.x, self.y, self.core = z, x, y, core
        self.peer_x = (z * 2 + 1 - x, k)
        self.peer_y = (b, (1 - y) * 2 + core)
        self.peer_core = (b, y * 2 + 1 - core)
        self.peer_z = [(((z + d) % 4) * 2 + x, k) for d in (1, 2, 3)]

    def greet(self):
        peers = [self.peer_x, self.peer_y, self.peer_core] + self.peer_z
        barrier = pltpu.get_barrier_semaphore()
        for peer in peers:
            pl.semaphore_signal(barrier, inc=1, device_id=peer, device_id_type=pl.DeviceIdType.MESH)
        pl.semaphore_wait(barrier, len(peers))


def remote(src, dst, sems, n, peer):
    return pltpu.make_async_remote_copy(
        src_ref=src,
        dst_ref=dst,
        send_sem=sems.at[0, n],
        recv_sem=sems.at[1, n],
        device_id=peer,
        device_id_type=pl.DeviceIdType.MESH,
    )


class Reducer:
    copies = 13

    def __init__(self, place, first, src, out, scratch, row0=0, col0=0):
        self.place = place
        self.f, self.s = (place.x, place.y) if first == "x" else (place.y, place.x)
        x, y = place.peer_x, place.peer_y
        self.peer_f, self.peer_s = (x, y) if first == "x" else (y, x)
        self.src, self.out = src, out
        self.r1, self.send2, self.r2, self.acc, self.r3, self.done, self.sems, self.own = scratch
        self.rows, self.cols = self.r1.shape[0] * 2, self.r1.shape[1]
        self.step = self.rows // 16
        self.row0, self.col0 = row0, col0

    @staticmethod
    def scratch(rows, cols, dtype):
        return [
            pltpu.VMEM((rows // 2, cols), dtype),
            pltpu.VMEM((rows // 4, cols), dtype),
            pltpu.VMEM((rows // 4, cols), dtype),
            pltpu.VMEM((rows // 4, cols), dtype),
            pltpu.VMEM((3, rows // 16, cols), dtype),
            pltpu.VMEM((rows // 16, cols), dtype),
            pltpu.SemaphoreType.DMA((2, Reducer.copies)),
            pltpu.SemaphoreType.DMA((1,)),
        ]

    def at(self, row, count):
        return pl.ds(pl.multiple_of(row, self.step), count)

    def taken(self, row, count):
        return self.at(self.row0 + row, count), pl.ds(self.col0, self.cols)

    def home(self, row, count):
        return self.out.at[self.place.core, *self.taken(row, count)]

    def copy(self, n):
        f, s, z = self.f, self.s, self.place.z
        half, quarter, step = self.rows // 2, self.rows // 4, self.step
        mine = f * half + s * quarter
        if n == 0:
            return remote(self.src.at[*self.taken((1 - f) * half, half)], self.r1, self.sems, n, self.peer_f)
        if n == 1:
            return remote(self.send2, self.r2, self.sems, n, self.peer_s)
        if n < 5:
            d = n - 2
            part = self.acc.at[self.at(((z + d + 1) % 4) * step, step)]
            return remote(part, self.r3.at[d], self.sems, n, self.place.peer_z[d])
        if n < 8:
            part = self.home(mine + z * step, step)
            return remote(self.done, part, self.sems, n, self.place.peer_z[n - 5])
        if n == 8:
            part, peer = self.home(mine, quarter), self.peer_s
        elif n == 9:
            part, peer = self.home(f * half, half), self.peer_f
        elif n == 10:
            part, peer = self.home(mine, quarter), self.place.peer_core
        elif n == 11:
            part, peer = self.home(f * half + (1 - s) * quarter, quarter), self.place.peer_core
        else:
            part, peer = self.home((1 - f) * half, half), self.place.peer_core
        return remote(part, part, self.sems, n, peer)

    def keep(self):
        mine = self.f * (self.rows // 2) + self.s * (self.rows // 4)
        part = self.home(mine + self.place.z * self.step, self.step)
        return pltpu.make_async_copy(self.done, part, self.own.at[0])

    def start(self, *numbers):
        for n in numbers:
            self.copy(n).start()

    def arrive(self, *numbers):
        for n in numbers:
            self.copy(n).wait_recv()

    def sum_into(self, dst, row, *more):
        def body(i, carry):
            at = i * self.step
            total = self.src[self.taken(row + at, self.step)].astype(f32)
            for ref, start in more:
                total = total + ref[self.at(start + at, self.step)].astype(f32)
            dst[self.at(at, self.step)] = total.astype(dst.dtype)
            return carry

        lax.fori_loop(0, 4, body, 0)

    def run(self, stage):
        f, s, z = self.f, self.s, self.place.z
        half, quarter, step = self.rows // 2, self.rows // 4, self.step
        if stage == 0:
            self.start(0)
        elif stage == 1:
            self.arrive(0)
            self.sum_into(self.send2, f * half + (1 - s) * quarter, (self.r1, (1 - s) * quarter))
            self.start(1)
        elif stage == 2:
            self.arrive(1)
            self.sum_into(self.acc, f * half + s * quarter, (self.r1, s * quarter), (self.r2, 0))
            self.start(2, 3, 4)
        elif stage == 3:
            self.arrive(2, 3, 4)
            total = self.acc[self.at(z * step, step)].astype(f32)
            for d in range(3):
                total = total + self.r3[d].astype(f32)
            self.done[...] = total.astype(self.done.dtype)
            self.start(5, 6, 7)
            self.keep().start()
        elif stage == 4:
            self.arrive(5, 6, 7)
            self.keep().wait()
            self.start(8, 10)
        elif stage == 5:
            self.arrive(8)
            self.start(9, 11)
        elif stage == 6:
            self.arrive(9)
            self.start(12)
        elif stage == 7:
            self.arrive(10, 11, 12)
            for n in range(self.copies):
                self.copy(n).wait_send()


def norm_back(x, gy, gain):
    center = jnp.mean(x, axis=-1, keepdims=True)
    shifted = x - center
    rstd = lax.rsqrt(jnp.mean(shifted * shifted, axis=-1, keepdims=True) + epsilon)
    hat = shifted * rstd
    g = gy * gain
    mean_g = jnp.mean(g, axis=-1, keepdims=True)
    mean_gh = jnp.mean(g * hat, axis=-1, keepdims=True)
    gx = rstd * (g - mean_g - hat * mean_gh)
    return gx, jnp.sum(gy * hat, axis=0, keepdims=True), jnp.sum(gy, axis=0, keepdims=True)


def tail_kernel(names, *refs):
    r = SimpleNamespace(**dict(zip(names, refs)))
    jobs_scratch = refs[len(names) :]
    place = Place()
    y, core = place.y, place.core
    tokens = r.qkv.shape[0]
    width = r.mixed.shape[1]
    wide = width // 2
    pairs = wide // 128
    basis = r.mkv.shape[0]
    spread = 1.0 / basis
    block = tokens // 4
    n_sem = 8
    take = lambda i: jobs_scratch[n_sem * i : n_sem * i + n_sem]
    ex, loc = r.ex, r.loc
    small_rows = pairs * 2 * basis // 128
    up_rows = r.small.shape[0]
    base = 2 * small_rows
    base_ln2 = base + up_rows
    base_ln1 = base_ln2 + 2 * (width // 128)
    jobs = [
        Reducer(place, "x", r.g_down, r.o_down, take(0), 0, 0),
        Reducer(place, "y", r.g_up, r.o_up, take(1), 0, 0),
        Reducer(place, "x", r.g_down, r.o_down, take(2), width, 0),
        Reducer(place, "y", r.g_up, r.o_up, take(3), 0, width),
        Reducer(place, "x", r.a2, r.o_a, take(4)),
        Reducer(place, "y", r.b2, r.o_b, take(5)),
        Reducer(place, "x", r.sv, r.o_s, take(6)),
    ]

    def both(pair, stage):
        jobs[2 * pair].run(stage)
        jobs[2 * pair + 1].run(stage)

    def rows_at(j, c):
        return pl.ds(pl.multiple_of((2 * j + c) * block, block), block)

    def half_at(j):
        return pl.ds(j * block, block)

    def local(j, n, src, dst):
        return pltpu.make_async_copy(src.at[rows_at(j, core)], dst.at[half_at(j)], loc.at[n, j])

    loads = [
        (r.gn2, r.gn2_own),
        (r.mixed, r.mixed_own),
        (r.cot, r.cot_own),
        (r.hidden, r.hid_own),
        (r.res, r.res_own),
    ]

    def to_sibling(n, j):
        src, dst = (r.gn2, r.gn2_rx) if n == 0 else (r.res, r.res_rx)
        return remote(src.at[rows_at(j, 1 - core)], dst.at[half_at(j)], ex, n + j, place.peer_core)

    place.greet()
    for j in range(2):
        to_sibling(0, j).start()
    for n, (a, b) in enumerate(loads):
        for j in range(2):
            local(j, n, a, b).start()
    both(0, 0)
    for j in range(2):
        to_sibling(4, j).start()
    r.sv[...] = jnp.zeros_like(r.sv)
    r.sv[base : base + up_rows, :] = r.small[...]

    def put(row, vec):
        for t in range(vec.shape[1] // 128):
            r.sv[pl.ds(row + t, 1), :] = vec[:, t * 128 : t * 128 + 128]

    def low_copy(j):
        part = r.gml.at[rows_at(j, core)]
        return remote(part, part, ex, 2 + j, place.peer_core)

    chunk = 64

    def norm_two(j, carry):
        def body(i, carry):
            at = pl.ds(pl.multiple_of(j * block + i * chunk, chunk), chunk)
            gy = r.gn2_own[at, :] + r.gn2_rx[at, :]
            gx, dg, db = norm_back(r.mixed_own[at, :], gy, r.gain2[...])
            gm = r.cot_own[at, :].astype(f32) + gx
            r.gm[at, :] = gm
            there = pl.ds(pl.multiple_of((2 * j + core) * block + i * chunk, chunk), chunk)
            r.gml[there, :] = gm.astype(bf16)
            return carry[0] + dg, carry[1] + db

        return lax.fori_loop(0, block // chunk, body, carry)

    sums = (jnp.zeros((1, width), f32), jnp.zeros((1, width), f32))
    for j in range(2):
        to_sibling(0, j).wait_recv()
        for n in range(3):
            local(j, n, *loads[n]).wait()
        sums = norm_two(j, sums)
        low_copy(j).start()
    put(base_ln2, sums[0])
    put(base_ln2 + width // 128, sums[1])

    for c in (0, 1):
        for j in range(2):
            if c:
                low_copy(j).wait_recv()
            there = rows_at(j, core if c == 0 else 1 - core)
            r.do[there, :] = mm(r.gml[there, :], r.w_out[...], NT).astype(bf16)
    both(0, 1)
    both(1, 0)
    for m in range(width // 256):
        cols = slice(m * 256, m * 256 + 256)
        r.b2[cols, wide:] = mm(r.gml[:, cols], r.ctx[...], TN).astype(bf16)

    centers = (lax.broadcasted_iota(jnp.int32, (basis, 1), 0).astype(f32) + 0.5) / basis
    allowed = causal_block(QB)
    pick_row = lax.broadcasted_iota(jnp.int32, (8, 1), 0)
    blocks = tokens // QB
    per_pair = 2 * blocks

    def finish_output():
        for j in range(2):
            to_sibling(4, j).wait_recv()
            local(j, 4, r.res, r.res_own).wait()

        def body(i, carry):
            at = pl.ds(pl.multiple_of(i * chunk, chunk), chunk)
            total = r.mixed_own[at, :] + (r.res_own[at, :] + r.res_rx[at, :]) + r.bias_d[...]
            r.bo[at, :] = total.astype(bf16)
            return carry

        lax.fori_loop(0, 2 * block // chunk, body, 0)
        out_copy().start()
        out_keep().start()

    def half_dyn(j):
        return pl.ds(pl.multiple_of(j * block, block), block)

    def out_copy():
        return remote(r.bo.at[half_dyn(1 - y)], r.out.at[y], ex, 6, place.peer_y)

    def out_keep():
        return pltpu.make_async_copy(r.bo.at[half_dyn(y)], r.out.at[y], loc.at[5, 0])

    events = {
        6: [lambda: both(0, 2)],
        17: [lambda: both(1, 1), lambda: both(0, 3)],
        23: [lambda: both(1, 2), finish_output],
    }

    def pair_step(i, carry):
        lanes = pl.ds(pl.multiple_of(i * 128, 128), 128)

        def lanes_of(j):
            return pl.ds(pl.multiple_of(i * 128 + j * wide, 128), 128)

        q_ref, k_ref, v_ref = (r.qkv.at[:, lanes_of(j)] for j in range(3))
        mk_ref, mv_ref = (r.mkv.at[:, lanes_of(j)] for j in range(2))
        do_ref = r.do.at[:, lanes]
        dka, dva, dqt, gmva, k_t, do_t = (r.dka, r.dva, r.dqt, r.gmva, r.k_t, r.do_t)
        k_t[...] = turn(k_ref[...]).astype(bf16)
        do_t[...] = turn(do_ref[...])
        dka[...] = jnp.zeros_like(dka)
        dva[...] = jnp.zeros_like(dva)
        gmva[...] = jnp.zeros_like(gmva)
        gmk = jnp.zeros((basis, 128), f32)
        for h in range(2):
            mask = head_mask(h)
            rows = slice(h * 64, h * 64 + 64)
            musg = r.musg[2 * i + h]
            u, b, centre, total = place_params(q_ref[...], mk_ref[...], musg, mask, basis)
            scale = spread * lax.rsqrt(total)
            inv = 1.0 / total
            dot_rows = jnp.sum(do_t[rows, :] * r.att[i, rows, :], axis=0, keepdims=True)
            z = jnp.zeros((8, 128), f32)
            for qb in range(blocks):
                cols = slice(qb * QB, qb * QB + QB)
                q = jnp.where(mask, q_ref[cols, :].astype(f32) * 0.125, 0.0).astype(bf16)
                do = jnp.where(mask, do_ref[cols, :].astype(f32), 0.0).astype(bf16)
                lse = r.lse[i, h : h + 1, cols]
                dot_row = dot_rows[:, cols]
                dq_t = jnp.zeros((64, QB), f32)
                for kb in range(qb + 1):
                    keys = slice(kb * QB, kb * QB + QB)
                    p = jnp.exp(mm(k_ref[keys, :], q, NT) - lse)
                    if kb == qb:
                        p = jnp.where(allowed, p, 0.0)
                    dva[keys, :] += mm(p.astype(bf16), do)
                    ds = (p * (mm(v_ref[keys, :], do, NT) - dot_row)).astype(bf16)
                    dka[keys, :] += mm(ds, q)
                    dq_t = dq_t + mm(k_t[rows, keys], ds)
                dqt[rows, cols] = dq_t * 0.125
                gap = centre[:, cols] - centers
                gap2 = gap * gap
                inv_b = inv[:, cols]
                dens = scale[:, cols] * jnp.exp(gap2 * (-0.5 * inv_b))
                gmva[...] += mm(dens.astype(bf16), do)
                e = mm(mv_ref[...], do, NT) * dens
                sum0 = jnp.sum(e, axis=0, keepdims=True)
                sum1 = jnp.sum(e * gap, axis=0, keepdims=True)
                sum2 = jnp.sum(e * gap2, axis=0, keepdims=True)
                c = centre[:, cols]
                da = -sum1 * inv_b * c * (1.0 - c)
                dtotal = 0.5 * inv_b * (sum2 * inv_b - sum0)
                db = dtotal * var_scale / (1.0 + jnp.exp(-b[:, cols]))
                dab = jnp.where(pick_row == 0, da, jnp.where(pick_row == 1, db, 0.0))
                dqt[:, cols] += mm(u, dab, TN, precision=highest)
                z = z + mm(dab, q.astype(f32), precision=highest)
                unit = h * blocks + qb
                for when, acts in events.items():
                    if when % per_pair == unit:

                        @pl.when(i == when // per_pair)
                        def _(acts=acts):
                            for act in acts:
                                act()

            gmk = gmk + mm(musg, z, TN, precision=highest)
            grads = mm(z, mk_ref[...].astype(f32), NT, precision=highest)
            at = (2 * i + h) * (basis // 128)
            put(at, grads[0:1])
            put(small_rows + at, grads[1:2])
        r.dqkv[:, lanes] = jnp.transpose(dqt[...]).astype(bf16)
        r.dqkv[:, lanes_of(1)] = dka[...].astype(bf16)
        r.dqkv[:, lanes_of(2)] = dva[...].astype(bf16)
        r.gmkv[:, lanes] = gmk.astype(bf16)
        r.gmkv[:, lanes_of(1)] = gmva[...].astype(bf16)
        return carry

    lax.fori_loop(0, pairs, pair_step, 0)

    for m in range(width // 256):
        cols = slice(m * 256, m * 256 + 256)
        g = mm(r.normed[:, cols], r.dqkv[...], TN)
        cg = mm(r.coeff[:, cols], r.gmkv[...], TN)
        r.a2[cols, :wide] = g[:, :wide].astype(bf16)
        r.a2[cols, wide:] = (g[:, wide:width] + cg[:, :wide]).astype(bf16)
        r.b2[cols, :wide] = (g[:, width:] + cg[:, wide:]).astype(bf16)
    both(2, 0)

    def norm_copy(j):
        return remote(r.gn1_tx.at[half_at(j)], r.gn1_rx.at[half_at(j)], ex, 7 + j, place.peer_core)

    for j in range(2):
        r.gn1_tx[half_at(j), :] = mm(r.dqkv[rows_at(j, 1 - core), :], r.w_qkv[...], NT)
        norm_copy(j).start()
    for j in range(2):
        r.gn1_own[half_at(j), :] = mm(r.dqkv[rows_at(j, core), :], r.w_qkv[...], NT)

    def norm_one(i, carry):
        at = pl.ds(pl.multiple_of(i * chunk, chunk), chunk)
        gy = r.gn1_own[at, :] + r.gn1_rx[at, :]
        gx, dg, db = norm_back(r.hid_own[at, :].astype(f32), gy, r.gain1[...])
        total = r.gm[at, :] + gx
        r.gm[at, :] = total
        r.gi_low[at, :] = total.astype(bf16)
        return carry[0] + dg, carry[1] + db

    def gin_copy():
        return remote(r.gi_low.at[half_dyn(1 - y)], r.gi_rx, ex, 9, place.peer_y)

    def gin_keep():
        return pltpu.make_async_copy(r.gm.at[half_dyn(y)], r.gin.at[y], loc.at[5, 1])

    def gin_place():
        return pltpu.make_async_copy(r.gi_wide, r.gin.at[1 - y], loc.at[5, 0])

    for j in range(2):
        norm_copy(j).wait_recv()
        local(j, 3, r.hidden, r.hid_own).wait()
    sums = lax.fori_loop(
        0, 2 * block // chunk, norm_one, (jnp.zeros((1, width), f32), jnp.zeros((1, width), f32))
    )
    put(base_ln1, sums[0])
    put(base_ln1 + width // 128, sums[1])
    jobs[6].run(0)
    gin_keep().start()
    both(0, 4)
    both(1, 3)
    jobs[6].run(1)
    both(0, 5)
    both(2, 1)
    jobs[6].run(2)
    both(1, 4)
    both(0, 6)
    both(2, 2)
    jobs[6].run(3)
    gin_copy().start()
    both(1, 5)
    jobs[6].run(4)
    both(2, 3)
    both(1, 6)
    jobs[6].run(5)
    both(2, 4)
    jobs[6].run(6)
    both(2, 5)
    both(0, 7)
    both(2, 6)
    both(1, 7)
    both(2, 7)
    jobs[6].run(7)
    out_copy().wait()
    out_keep().wait()
    gin_copy().wait()
    r.gi_wide[...] = r.gi_rx[...].astype(f32)
    gin_place().start()
    gin_keep().wait()
    gin_place().wait()
    for j in range(2):
        to_sibling(0, j).wait_send()
        to_sibling(4, j).wait_send()
        low_copy(j).wait_send()
        norm_copy(j).wait_send()


def tail_call(given, held):
    g = SimpleNamespace(**given, **held)
    width = g.mixed.shape[1]
    tokens, wide3 = g.qkv.shape
    wide = wide3 // 3
    basis = g.mkv.shape[0]
    half, block = tokens // 2, tokens // 4
    used = 2 * (wide // 64) * basis // 128 + g.small.shape[0] + 4 * (width // 128)
    sv_rows = -(-used // 128) * 128
    shape = jax.ShapeDtypeStruct
    g_down, g_up = g.g_down, g.g_up
    outs = dict(
        o_down=shape((2,) + g_down.shape, bf16),
        o_up=shape((2,) + g_up.shape, bf16),
        o_a=shape((2, width, width), bf16),
        o_b=shape((2, width, width), bf16),
        o_s=shape((2, sv_rows, 128), f32),
        out=shape((2, block, width), bf16),
        gin=shape((2, block, width), f32),
    )
    scratch = dict(
        ex=pltpu.SemaphoreType.DMA((2, 10)),
        loc=pltpu.SemaphoreType.DMA((6, 2)),
        gn2_own=pltpu.VMEM((half, width), f32),
        gn2_rx=pltpu.VMEM((half, width), f32),
        mixed_own=pltpu.VMEM((half, width), f32),
        cot_own=pltpu.VMEM((half, width), bf16),
        hid_own=pltpu.VMEM((half, width), bf16),
        res_own=pltpu.VMEM((half, width), f32),
        res_rx=pltpu.VMEM((half, width), f32),
        gm=pltpu.VMEM((half, width), f32),
        gml=pltpu.VMEM((tokens, width), bf16),
        bo=pltpu.VMEM((half, width), bf16),
        gi_low=pltpu.VMEM((half, width), bf16),
        gi_rx=pltpu.VMEM((block, width), bf16),
        gi_wide=pltpu.VMEM((block, width), f32),
        do=pltpu.VMEM((tokens, wide), bf16),
        dqkv=pltpu.VMEM((tokens, wide3), bf16),
        gmkv=pltpu.VMEM((basis, 2 * wide), bf16),
        gn1_tx=pltpu.VMEM((half, width), f32),
        gn1_rx=pltpu.VMEM((half, width), f32),
        gn1_own=pltpu.VMEM((half, width), f32),
        dka=pltpu.VMEM((tokens, 128), f32),
        dva=pltpu.VMEM((tokens, 128), f32),
        dqt=pltpu.VMEM((128, tokens), f32),
        gmva=pltpu.VMEM((basis, 128), f32),
        k_t=pltpu.VMEM((128, tokens), bf16),
        do_t=pltpu.VMEM((128, tokens), f32),
        a2=pltpu.VMEM((width, width), bf16),
        b2=pltpu.VMEM((width, width), bf16),
        sv=pltpu.VMEM((sv_rows, 128), f32),
    )
    more = []
    for _ in range(6):
        more += Reducer.scratch(width, width, bf16)
    more += Reducer.scratch(sv_rows, 128, f32)
    hbm, vmem = pl.BlockSpec(memory_space=pl.ANY), pl.BlockSpec(memory_space=pltpu.VMEM)
    names = list(given) + list(held) + list(outs) + list(scratch)
    return pl.pallas_call(
        functools.partial(tail_kernel, names),
        in_specs=[vmem] * len(given) + [hbm] * len(held),
        out_specs=[hbm] * len(outs),
        out_shape=list(outs.values()),
        scratch_shapes=list(scratch.values()) + more,
        compiler_params=pltpu.CompilerParams(
            vmem_limit_bytes=60 * 1024 * 1024, collective_id=1, has_side_effects=True
        ),
        name="tail",
    )(*given.values(), *held.values())


def sweep_inverse(a):
    n = a.shape[0]
    lane = lax.broadcasted_iota(jnp.int32, (8, n), 1)
    sub = lax.broadcasted_iota(jnp.int32, (8, n), 0)
    groups = [a[8 * g : 8 * g + 8, :] for g in range(n // 8)]

    def inverse_two(p, q, t):
        inv = 1.0 / (p * t - q * q)
        return t * inv, -q * inv, p * inv

    for k in range(0, n, 4):
        own, at = groups[k // 8], k % 8
        rows = [jnp.broadcast_to(own[at + i : at + i + 1, :], (8, n)) for i in range(4)]
        d = {
            (i, j): jnp.broadcast_to(rows[i][:, k + j : k + j + 1], (8, n))
            for i in range(4)
            for j in range(i, 4)
        }
        a0, a1, a2 = inverse_two(d[0, 0], d[0, 1], d[1, 1])
        w = [
            [a0 * d[0, 2] + a1 * d[1, 2], a0 * d[0, 3] + a1 * d[1, 3]],
            [a1 * d[0, 2] + a2 * d[1, 2], a1 * d[0, 3] + a2 * d[1, 3]],
        ]
        s0 = d[2, 2] - (d[0, 2] * w[0][0] + d[1, 2] * w[1][0])
        s1 = d[2, 3] - (d[0, 2] * w[0][1] + d[1, 2] * w[1][1])
        s2 = d[3, 3] - (d[0, 3] * w[0][1] + d[1, 3] * w[1][1])
        s0, s1, s2 = inverse_two(s0, s1, s2)
        v = [[w[i][0] * s0 + w[i][1] * s1, w[i][0] * s1 + w[i][1] * s2] for i in range(2)]
        p00 = a0 + v[0][0] * w[0][0] + v[0][1] * w[0][1]
        p01 = a1 + v[0][0] * w[1][0] + v[0][1] * w[1][1]
        p11 = a2 + v[1][0] * w[1][0] + v[1][1] * w[1][1]
        p = [
            [p00, p01, -v[0][0], -v[0][1]],
            [p01, p11, -v[1][0], -v[1][1]],
            [-v[0][0], -v[1][0], s0, s1],
            [-v[0][1], -v[1][1], s1, s2],
        ]
        new = []
        for i in range(4):
            row = p[i][0] * rows[0] + p[i][1] * rows[1] + p[i][2] * rows[2] + p[i][3] * rows[3]
            for j in range(4):
                row = jnp.where(lane == k + j, p[i][j], row)
            new.append(row)
        inside = (lane >= k) & (lane < k + 4)
        for g in range(n // 8):
            old = groups[g]
            cols = [jnp.broadcast_to(old[:, k + j : k + j + 1], (8, n)) for j in range(4)]
            part = (cols[0] * new[0] + cols[1] * new[1]) + (cols[2] * new[2] + cols[3] * new[3])
            fresh = jnp.where(inside, 0.0, old) - part
            if g == k // 8:
                for i in range(4):
                    fresh = jnp.where(sub == at + i, new[i], fresh)
            groups[g] = fresh
    return jnp.concatenate(groups, 0)


def front_kernel(names, *refs):
    r = SimpleNamespace(**dict(zip(names, refs)))
    place = Place()
    y, core = place.y, place.core
    tokens, width = r.hidden.shape
    block = tokens // 4
    wide = width // 2
    basis = r.mkv.shape[0]
    half = basis // 2
    ex, loc = r.ex, r.loc
    flows = [(r.previous, r.prev), (r.inputs, r.hidden), (r.cotangent, r.cot)]

    def rows_at(yy, cc):
        return pl.ds(pl.multiple_of((2 * yy + cc) * block, block), block)

    def along(n):
        src, dst = flows[n]
        return remote(src.at[1 - y], dst.at[rows_at(y, core)], ex, n, place.peer_y)

    def across(n):
        src, dst = flows[n]
        return remote(src.at[y], dst.at[rows_at(y, core)], ex, 3 + n, place.peer_core)

    def onward(n):
        part = flows[n][1].at[rows_at(1 - y, core)]
        return remote(part, part, ex, 6 + n, place.peer_core)

    def keep(n):
        src, dst = flows[n]
        return pltpu.make_async_copy(src.at[y], dst.at[rows_at(y, core)], loc.at[n])

    def weight(n):
        src = (r.wq, r.wk, r.wv)[n].at[:, pl.ds(pl.multiple_of(core * wide, 128), wide)]
        return pltpu.make_async_copy(src, r.w_qkv.at[:, n * wide : n * wide + wide], loc.at[3 + n])

    barrier = pltpu.get_barrier_semaphore()
    for peer in (place.peer_y, place.peer_core):
        pl.semaphore_signal(barrier, inc=1, device_id=peer, device_id_type=pl.DeviceIdType.MESH)
    pl.semaphore_wait(barrier, 2)
    along(0).start()
    across(1).start()
    keep(1).start()
    for n in range(3):
        weight(n).start()
    for n in (0, 2):
        across(n).start()
        keep(n).start()

    chunk = 64

    def project(yy, cc):
        def body(i, carry):
            at = pl.ds(pl.multiple_of((2 * yy + cc) * block + i * chunk, chunk), chunk)
            normed = layer_norm(r.hidden[at, :].astype(f32), r.gain1[...], r.bias1[...])
            r.normed[at, :] = normed.astype(bf16)
            return carry

        lax.fori_loop(0, block // chunk, body, 0)
        at = rows_at(yy, cc)
        r.qkv[at, :] = mm(r.normed[at, :], r.w_qkv[...]).astype(bf16)

    keep(1).wait()
    for n in range(3):
        weight(n).wait()
    project(y, core)
    across(1).wait_recv()
    project(y, 1 - core)

    spread = 1.0 / basis
    length = tokens
    centers = (lax.broadcasted_iota(jnp.int32, (basis, 1), 0).astype(f32) + 0.5) / basis
    places = (r.sticky[pl.ds(y, 1), :].astype(f32) + 0.5) / length
    features = jnp.exp(-((places - centers) ** 2) / (2.0 * spread * spread)).astype(bf16)
    same = lax.broadcasted_iota(jnp.int32, (basis, basis), 0) == lax.broadcasted_iota(
        jnp.int32, (basis, basis), 1
    )
    a_ref, i_ref = r.a, r.i
    a_ref[...] = mm(features, features, NT) + jnp.where(same, ridge_weight, 0.0)

    along(0).wait_send()
    along(1).start()
    along(0).wait_recv()
    onward(0).start()
    i_ref[...] = sweep_inverse(a_ref[:half, :half])

    index = lax.broadcasted_iota(jnp.int32, (tokens, r.picks.shape[1]), 0)
    chosen = jnp.where(index == r.picks[pl.ds(y, 1), :], 1.0, 0.0).astype(bf16)
    shares = mm(features, chosen, NT)
    high = shares.astype(bf16)
    rest = shares - high.astype(f32)
    middle = rest.astype(bf16)
    last = (rest - middle.astype(f32)).astype(bf16)
    across(0).wait_recv()
    keep(0).wait()
    onward(0).wait_recv()
    prev = r.prev[...]
    r.side[...] = mm(high, prev) + (mm(middle, prev) + mm(last, prev))
    top = i_ref[...]
    cross = a_ref[:half, half:]
    across_top = mm(top, cross, precision=highest)
    schur = a_ref[half:, half:] - mm(cross, across_top, TN, precision=highest)
    along(1).wait_send()
    along(2).start()
    along(1).wait_recv()
    onward(1).start()
    inverse = sweep_inverse(schur)
    side_top, side_low = r.side[:half, :], r.side[half:, :]
    low_part = mm(
        inverse, side_low - mm(across_top, side_top, TN, precision=highest), precision=highest
    )
    r.coeff[half:, :] = low_part.astype(bf16)
    r.coeff[:half, :] = (
        mm(top, side_top, precision=highest) - mm(across_top, low_part, precision=highest)
    ).astype(bf16)
    r.mkv[...] = mm(r.coeff[...], r.w_qkv[:, wide:]).astype(bf16)
    project(1 - y, core)
    onward(1).wait_recv()
    project(1 - y, 1 - core)
    keep(2).wait()
    across(2).wait_recv()
    along(2).wait_recv()
    onward(2).start()
    onward(2).wait_recv()
    along(2).wait_send()
    for n in range(3):
        across(n).wait_send()
        onward(n).wait_send()


def front_call(held, given, basis):
    block, width = held[next(iter(held))].shape[1:]
    tokens = block * 4
    wide = width // 2
    shape = jax.ShapeDtypeStruct
    outs = dict(
        hidden=shape((tokens, width), bf16),
        normed=shape((tokens, width), bf16),
        qkv=shape((tokens, 3 * wide), bf16),
        mkv=shape((basis, width), bf16),
        coeff=shape((basis, width), bf16),
        w_qkv=shape((width, 3 * wide), bf16),
    )
    far = dict(cot=shape((tokens, width), bf16))
    scratch = dict(
        ex=pltpu.SemaphoreType.DMA((2, 9)),
        loc=pltpu.SemaphoreType.DMA((6,)),
        prev=pltpu.VMEM((tokens, width), bf16),
        a=pltpu.VMEM((basis, basis), f32),
        i=pltpu.VMEM((basis // 2, basis // 2), f32),
        side=pltpu.VMEM((basis, width), f32),
    )
    hbm, vmem = pl.BlockSpec(memory_space=pl.ANY), pl.BlockSpec(memory_space=pltpu.VMEM)
    names = list(held) + list(given) + list(outs) + list(far) + list(scratch)
    return pl.pallas_call(
        functools.partial(front_kernel, names),
        in_specs=[hbm] * len(held) + [vmem] * len(given),
        out_specs=[vmem] * len(outs) + [hbm] * len(far),
        out_shape=list(outs.values()) + list(far.values()),
        scratch_shapes=list(scratch.values()),
        compiler_params=vmem_params(collective_id=2, has_side_effects=True),
        name="front",
    )(*held.values(), *given.values())


def finish(down, up, a, b):
    width = a.shape[1]
    steps = width // 128
    per_core = steps // 2
    tall = down.shape[1] // per_core
    wide = width // 2

    def body(down_ref, up_ref, a_ref, v_ref, t_ref, o_down, o_up, o_q, o_k, o_v, o_o):
        o_down[...] = down_ref[0].astype(f32)
        n = up_ref.shape[2]
        for c in range(2):
            o_up[:, c * n : c * n + n] = up_ref[c].astype(f32)
            here = slice(c * wide, c * wide + wide)
            o_q[:, here] = a_ref[c, :, :wide].astype(f32)
            o_k[:, here] = a_ref[c, :, wide:].astype(f32)
            o_v[:, here] = v_ref[c].astype(f32)
        o_o[...] = jnp.transpose(t_ref[0].astype(f32))

    row = lambda n: pl.BlockSpec((128, n), lambda i: (i, 0))
    shape = jax.ShapeDtypeStruct
    return pl.pallas_call(
        body,
        grid=(steps,),
        in_specs=[
            pl.BlockSpec((1, tall, width), lambda i: (i // per_core, i % per_core, 0)),
            pl.BlockSpec((2, 128, up.shape[2]), lambda i: (0, i, 0)),
            pl.BlockSpec((2, 128, width), lambda i: (0, i, 0)),
            pl.BlockSpec((2, 128, wide), lambda i: (0, i, 0)),
            pl.BlockSpec((1, width, 128), lambda i: (i // per_core, 0, per_core + i % per_core)),
        ],
        out_specs=[pl.BlockSpec((tall, width), lambda i: (i, 0)), row(2 * up.shape[2])] + [row(width)] * 4,
        out_shape=[
            shape((2 * down.shape[1], width), f32),
            shape((width, 2 * up.shape[2]), f32),
        ]
        + [shape((width, width), f32)] * 4,
        compiler_params=vmem_params(),
        name="finish",
    )(down, up, a, b, b)


def chip_local(
    inputs,
    previous,
    memory_rows,
    sticky_positions,
    cotangent,
    ln1_gain,
    ln1_bias,
    query_weight,
    key_weight,
    value_weight,
    out_weight,
    mu_weight,
    sigma_weight,
    ln2_gain,
    ln2_bias,
    expand_weight,
    up_bias,
    down_weight,
    down_bias,
):
    tok_rows, width = inputs.shape[1:]
    length = tok_rows * 4
    heads, basis = mu_weight.shape
    ff = up_bias.shape[0]
    place = lax.axis_index(BLK)
    y, core = place // 2, place % 2
    to_core = [(k, k ^ 1) for k in range(4)]

    def swap_core(a):
        return lax.ppermute(a, BLK, to_core)

    def columns(w):
        n = w.shape[1] // 2
        return lax.dynamic_slice_in_dim(w, core * n, n, 1)

    def rows_of(w):
        n = w.shape[0] // 2
        return lax.dynamic_slice_in_dim(w, core * n, n, 0)

    wide = width // 2
    expand = columns(expand_weight)
    down = rows_of(down_weight)
    out_own = rows_of(out_weight)
    out_sib = lax.dynamic_slice_in_dim(out_weight, (1 - core) * wide, wide, 0)
    bias_up = lax.dynamic_slice_in_dim(up_bias, core * (ff // 2), ff // 2, 0)
    musg = jnp.stack([rows_of(mu_weight), rows_of(sigma_weight)], 1)
    musg = jnp.pad(musg, ((0, 0), (0, 6), (0, 0)))

    hidden, normed_low, qkv, mkv, coeff_low, w_qkv, cot = front_call(
        dict(
            inputs=inputs,
            previous=previous,
            cotangent=cotangent,
            wq=query_weight,
            wk=key_weight,
            wv=value_weight,
        ),
        dict(
            picks=memory_rows,
            sticky=sticky_positions,
            gain1=ln1_gain[None],
            bias1=ln1_bias[None],
        ),
        basis,
    )
    hidden_in = hidden.astype(f32)
    ctx, lse, att = attn_fwd(qkv, mkv, musg)
    ctx_sib = swap_core(ctx)
    mixed = hidden_in + (mm(ctx, out_own) + mm(ctx_sib, out_sib))
    normed_two_low = layer_norm(mixed, ln2_gain, ln2_bias).astype(bf16)
    hidden_up = mm(normed_two_low, expand) + bias_up
    active, gelu_pull = jax.vjp(gelu_tanh, hidden_up)
    active_low = active.astype(bf16)
    result = mm(active_low, down)
    grad_down_bias = jnp.sum(cot.astype(f32), axis=0)
    grad_down = mm(active_low, cot, TN).astype(bf16)
    grad_up_low = gelu_pull(mm(cot, down, NT))[0].astype(bf16)
    grad_up_bias = jnp.sum(grad_up_low.astype(f32), axis=0)
    grad_up = mm(normed_two_low, grad_up_low, TN).astype(bf16)
    grad_normed_two = mm(grad_up_low, expand, NT)
    small = jnp.concatenate([grad_up_bias, grad_down_bias]).reshape(-1, 128)
    a1, b1, a2, b2, s, block_output, grad_inputs = tail_call(
        dict(
            g_down=grad_down,
            g_up=grad_up,
            small=small,
            gain1=ln1_gain[None],
            gain2=ln2_gain[None],
            bias_d=down_bias[None],
            w_out=out_own,
            w_qkv=w_qkv,
            ctx=ctx,
            qkv=qkv,
            mkv=mkv,
            musg=musg,
            lse=lse,
            att=att,
            normed=normed_low,
            coeff=coeff_low,
        ),
        dict(gn2=grad_normed_two, res=result, mixed=mixed, cot=cot, hidden=hidden),
    )

    n_own = heads // 2 * basis

    g_down, g_up, g_q, g_k, g_v, g_o = finish(a1, b1, a2, b2)
    s = s.reshape(2, -1)
    cuts = [n_own, n_own, ff // 2, width, width, width, width, width]
    parts, start = [], 0
    for n in cuts:
        parts.append(s[:, start : start + n])
        start += n
    return (
        block_output,
        grad_inputs,
        parts[6][0] + parts[6][1],
        parts[7][0] + parts[7][1],
        g_q,
        g_k,
        g_v,
        g_o,
        parts[0].reshape(heads, basis),
        parts[1].reshape(heads, basis),
        parts[4][0] + parts[4][1],
        parts[5][0] + parts[5][1],
        g_up,
        parts[2].reshape(ff),
        g_down,
        parts[3][0],
    )


def pick(mesh):
    def step(*arrays):
        inputs, mu = arrays[0], arrays[11]
        fits = (
            mesh.shape[BATCH] == 8
            and mesh.shape[BLK] == 4
            and inputs.shape[0] == 2
            and inputs.shape[1] % QB == 0
            and mu.shape[0] % 4 == 0
            and inputs.shape[2] == mu.shape[0] * 64
        )
        return (chip_local if fits else general)(*arrays)

    return step


def solution(mesh):
    return jax.shard_map(
        pick(mesh),
        mesh=mesh,
        in_specs=(
            P(BATCH, BLK, None),
            P(BATCH, BLK, None),
            P(BATCH, None),
            P(BATCH, None),
            P(BATCH, BLK, None),
            P(),
            P(),
            P(),
            P(),
            P(),
            P(),
            P(),
            P(),
            P(),
            P(),
            P(),
            P(),
            P(),
            P(),
        ),
        out_specs=(
            P(BATCH, BLK, None),
            P(BATCH, BLK, None),
            P(),
            P(),
            P(),
            P(),
            P(),
            P(),
            P(),
            P(),
            P(),
            P(),
            P(),
            P(),
            P(),
            P(),
        ),
        check_vma=False,
    )
```

```python
import functools
from types import SimpleNamespace

import jax
import jax.numpy as jnp
from jax import lax
from jax.experimental import pallas as pl
from jax.experimental.pallas import tpu as pltpu
from jax.sharding import PartitionSpec as P

epsilon = 1e-05
ridge_weight = 1.0
var_scale = 0.01
masked_score = -1e30
BLK = "blk"
BATCH = "batch"
highest = lax.Precision.HIGHEST


def layer_norm(values, gain, bias):
    center = jnp.mean(values, axis=-1, keepdims=True)
    shifted = values - center
    spread_sq = jnp.mean(shifted * shifted, axis=-1, keepdims=True)
    return shifted * lax.rsqrt(spread_sq + epsilon) * gain + bias


def density(scores, mu_row, sigma_row):
    count = scores.shape[-1]
    centers = (jnp.arange(count, dtype=scores.dtype) + 0.5) / count
    spread = 1.0 / count
    centre = jax.nn.sigmoid(jnp.dot(scores, mu_row, precision=highest))
    variance = var_scale * jax.nn.softplus(jnp.dot(scores, sigma_row, precision=highest))
    total = spread * spread + variance
    return (spread * lax.rsqrt(total))[..., None] * jnp.exp(
        -((centre[..., None] - centers) ** 2) / (2.0 * total[..., None])
    )


def project(source, weight):
    return jnp.einsum("std,de->ste", source, weight, preferred_element_type=jnp.float32)


def weight_grad(source, grads):
    return jnp.einsum("std,ste->de", source, grads, preferred_element_type=jnp.float32)


def back_project(grads, weight):
    return jnp.einsum("ste,de->std", grads, weight, preferred_element_type=jnp.float32)


def gelu_tanh(values):
    return jax.nn.gelu(values, approximate=True)


def general(
    inputs,
    previous,
    memory_rows,
    sticky_positions,
    cotangent,
    ln1_gain,
    ln1_bias,
    query_weight,
    key_weight,
    value_weight,
    out_weight,
    mu_weight,
    sigma_weight,
    ln2_gain,
    ln2_bias,
    expand_weight,
    up_bias,
    down_weight,
    down_bias,
):
    seg_count, tok_rows, model_width = inputs.shape
    blocks = lax.axis_size(BLK)
    length = tok_rows * blocks
    first_row = lax.axis_index(BLK) * tok_rows
    head_count, basis_count = mu_weight.shape
    head_width = model_width // head_count
    centers = (jnp.arange(basis_count, dtype=jnp.float32) + 0.5) / basis_count
    spread = 1.0 / basis_count
    places = (sticky_positions.astype(jnp.float32) + 0.5) / length
    features = jnp.exp(-((places[..., None] - centers) ** 2) / (2.0 * spread * spread)).astype(
        jnp.bfloat16
    )
    local_index = memory_rows - first_row
    owned_rows = (local_index >= 0) & (local_index < tok_rows)
    picked = jax.vmap(lambda shard_rows, row_index: shard_rows[row_index])(
        previous, jnp.clip(local_index, 0, tok_rows - 1)
    )
    picked = jnp.where(owned_rows[..., None], picked, jnp.zeros_like(picked))
    own_features = jnp.where(owned_rows[..., None], features, jnp.zeros_like(features))
    side_part = jnp.einsum("smn,smd->snd", own_features, picked, preferred_element_type=jnp.float32)
    gram_part = jnp.einsum(
        "smn,smk->snk", own_features, own_features, preferred_element_type=jnp.float32
    )
    gram_sum, right_side = lax.psum((gram_part, side_part), BLK)
    system = gram_sum + ridge_weight * jnp.eye(basis_count, dtype=jnp.float32)
    factor = jnp.linalg.cholesky(system)
    coefficients = jax.scipy.linalg.cho_solve((factor, True), right_side)
    coeff_low = coefficients.astype(jnp.bfloat16)
    hidden_in = inputs.astype(jnp.float32)
    normed_low = layer_norm(hidden_in, ln1_gain, ln1_bias).astype(jnp.bfloat16)
    queries = project(normed_low, query_weight).astype(jnp.bfloat16)
    keys_local = project(normed_low, key_weight).astype(jnp.bfloat16)
    values_local = project(normed_low, value_weight).astype(jnp.bfloat16)
    mem_keys = project(coeff_low, key_weight).astype(jnp.bfloat16)
    mem_values = project(coeff_low, value_weight).astype(jnp.bfloat16)
    all_keys, all_values = (
        lax.all_gather(keys_local, BLK, axis=1, tiled=True),
        lax.all_gather(values_local, BLK, axis=1, tiled=True),
    )

    def split_heads(array):
        return array.reshape(array.shape[0], array.shape[1], head_count, head_width).transpose(
            2, 0, 1, 3
        )

    def merge_heads(array):
        return array.transpose(1, 2, 0, 3).reshape(array.shape[1], array.shape[2], model_width)

    query_pos = first_row + jnp.arange(tok_rows)
    key_pos = jnp.arange(length)
    causal = key_pos[None, :] <= query_pos[:, None]

    def forward_head(operands):
        query_h, key_h, value_h, memkey_h, memval_h, mu_row, sigma_row = operands
        scores = (
            jnp.einsum("sqd,skd->sqk", query_h, key_h, preferred_element_type=jnp.float32) * 0.125
        )
        scores = jnp.where(causal, scores, masked_score)
        top = jnp.max(scores, axis=-1, keepdims=True)
        raised = jnp.exp(scores - top)
        total = jnp.sum(raised, axis=-1, keepdims=True)
        probs = raised / total
        log_total = (top + jnp.log(total))[..., 0]
        attended = jnp.einsum(
            "sqk,skd->sqd", probs.astype(jnp.bfloat16), value_h, preferred_element_type=jnp.float32
        )
        memory_scores = (
            jnp.einsum("sqd,snd->sqn", query_h, memkey_h, preferred_element_type=jnp.float32)
            * 0.125
        )
        weights_mem = density(memory_scores, mu_row, sigma_row)
        recalled = jnp.einsum(
            "sqn,snd->sqd",
            weights_mem.astype(jnp.bfloat16),
            memval_h,
            preferred_element_type=jnp.float32,
        )
        return (attended + recalled, log_total)

    head_queries = split_heads(queries)
    head_keys = split_heads(all_keys)
    value_per_head = split_heads(all_values)
    head_memkeys = split_heads(mem_keys)
    head_memvals = split_heads(mem_values)
    heads_ctx, log_totals = lax.map(
        forward_head,
        (
            head_queries,
            head_keys,
            value_per_head,
            head_memkeys,
            head_memvals,
            mu_weight,
            sigma_weight,
        ),
    )
    context_low = merge_heads(heads_ctx).astype(jnp.bfloat16)
    mixed = hidden_in + project(context_low, out_weight)
    normed_two_low = layer_norm(mixed, ln2_gain, ln2_bias).astype(jnp.bfloat16)
    hidden_up = (
        jnp.einsum("std,df->stf", normed_two_low, expand_weight, preferred_element_type=jnp.float32)
        + up_bias
    )
    active_low = gelu_tanh(hidden_up).astype(jnp.bfloat16)
    result = (
        mixed
        + jnp.einsum("stf,fd->std", active_low, down_weight, preferred_element_type=jnp.float32)
        + down_bias
    )
    block_output = result.astype(jnp.bfloat16)
    grad_result = cotangent.astype(jnp.float32)
    grad_down_bias = jnp.sum(grad_result, axis=(0, 1))
    grad_down_weight = jnp.einsum(
        "stf,std->fd", active_low, cotangent, preferred_element_type=jnp.float32
    )
    grad_active = jnp.einsum(
        "std,fd->stf", cotangent, down_weight, preferred_element_type=jnp.float32
    )
    gelu_value, gelu_pull = jax.vjp(gelu_tanh, hidden_up)
    grad_up_low = gelu_pull(grad_active)[0].astype(jnp.bfloat16)
    grad_up_bias = jnp.sum(grad_up_low.astype(jnp.float32), axis=(0, 1))
    grad_up_weight = jnp.einsum(
        "std,stf->df", normed_two_low, grad_up_low, preferred_element_type=jnp.float32
    )
    grad_normed_two = jnp.einsum(
        "stf,df->std", grad_up_low, expand_weight, preferred_element_type=jnp.float32
    )
    norm_two_value, norm_two_pull = jax.vjp(layer_norm, mixed, ln2_gain, ln2_bias)
    grad_mixed_norm, grad_ln2_gain, grad_ln2_bias = norm_two_pull(grad_normed_two)
    grad_mixed = grad_result + grad_mixed_norm
    grad_mixed_low = grad_mixed.astype(jnp.bfloat16)
    grad_out_weight = weight_grad(context_low, grad_mixed_low)
    grad_context_low = back_project(grad_mixed_low, out_weight).astype(jnp.bfloat16)

    def backward_head(operands):
        query_h, key_h, value_h, memkey_h, memval_h, mu_row, sigma_row, grad_h, log_total = operands
        scores = (
            jnp.einsum("sqd,skd->sqk", query_h, key_h, preferred_element_type=jnp.float32) * 0.125
        )
        probs = jnp.where(causal, jnp.exp(scores - log_total[..., None]), 0.0)
        grad_probs = jnp.einsum("sqd,skd->sqk", grad_h, value_h, preferred_element_type=jnp.float32)
        row_dot = jnp.sum(probs * grad_probs, axis=-1, keepdims=True)
        grad_scores = (probs * (grad_probs - row_dot)).astype(jnp.bfloat16)
        grad_query = (
            jnp.einsum("sqk,skd->sqd", grad_scores, key_h, preferred_element_type=jnp.float32)
            * 0.125
        )
        memory_scores = (
            jnp.einsum("sqd,snd->sqn", query_h, memkey_h, preferred_element_type=jnp.float32)
            * 0.125
        )
        weights_mem, density_pull = jax.vjp(density, memory_scores, mu_row, sigma_row)
        weights_low = weights_mem.astype(jnp.bfloat16)
        grad_weights = jnp.einsum(
            "sqd,snd->sqn", grad_h, memval_h, preferred_element_type=jnp.float32
        )
        grad_memval = jnp.einsum(
            "sqn,sqd->snd", weights_low, grad_h, preferred_element_type=jnp.float32
        )
        grad_memscores, grad_mu, grad_sigma = density_pull(grad_weights)
        grad_memscores_low = grad_memscores.astype(jnp.bfloat16)
        grad_query = (
            grad_query
            + jnp.einsum(
                "sqn,snd->sqd", grad_memscores_low, memkey_h, preferred_element_type=jnp.float32
            )
            * 0.125
        )
        grad_memkey = (
            jnp.einsum(
                "sqn,sqd->snd", grad_memscores_low, query_h, preferred_element_type=jnp.float32
            )
            * 0.125
        )
        grad_key = (
            jnp.einsum("sqk,sqd->skd", grad_scores, query_h, preferred_element_type=jnp.float32)
            * 0.125
        )
        grad_value = jnp.einsum(
            "sqk,sqd->skd", probs.astype(jnp.bfloat16), grad_h, preferred_element_type=jnp.float32
        )
        return (grad_query, grad_memkey, grad_memval, grad_mu, grad_sigma, grad_key, grad_value)

    head_grads = split_heads(grad_context_low)
    outcome = lax.map(
        backward_head,
        (
            head_queries,
            head_keys,
            value_per_head,
            head_memkeys,
            head_memvals,
            mu_weight,
            sigma_weight,
            head_grads,
            log_totals,
        ),
    )
    grad_query_heads, grad_memkey_heads, grad_memval_heads, grad_mu_weight, grad_sigma_weight = (
        outcome[:5]
    )
    terms = (
        jnp.stack((outcome[5], outcome[6]))
        .transpose(3, 2, 0, 1, 4)
        .reshape(length, seg_count, 2 * model_width)
    )
    own_terms = lax.psum_scatter(
        terms.astype(jnp.bfloat16), BLK, scatter_dimension=0, tiled=True
    ).astype(jnp.float32)
    own_terms = own_terms.reshape(tok_rows, seg_count, 2, model_width).transpose(2, 1, 0, 3)
    grad_keys = own_terms[0]
    grad_values = own_terms[1]
    grad_queries_low = merge_heads(grad_query_heads).astype(jnp.bfloat16)
    grad_keys_low = grad_keys.astype(jnp.bfloat16)
    grad_values_low = grad_values.astype(jnp.bfloat16)
    memkey_sum, memval_sum = (
        lax.psum(grad_memkey_heads.astype(jnp.bfloat16), BLK).astype(jnp.float32),
        lax.psum(grad_memval_heads.astype(jnp.bfloat16), BLK).astype(jnp.float32),
    )
    gradient_memory_keys_reduced = merge_heads(memkey_sum).astype(jnp.bfloat16)
    gradient_memory_values_reduced = merge_heads(memval_sum).astype(jnp.bfloat16)
    grad_query_weight = weight_grad(normed_low, grad_queries_low)
    grad_key_weight = weight_grad(normed_low, grad_keys_low)
    grad_value_weight = weight_grad(normed_low, grad_values_low)
    grad_normed = (
        back_project(grad_queries_low, query_weight)
        + back_project(grad_keys_low, key_weight)
        + back_project(grad_values_low, value_weight)
    )
    norm_one_value, norm_one_pull = jax.vjp(layer_norm, hidden_in, ln1_gain, ln1_bias)
    grad_in_norm, grad_ln1_gain, grad_ln1_bias = norm_one_pull(grad_normed)
    grad_inputs = grad_mixed + grad_in_norm
    shares = (
        lax.psum_scatter(
            grad_ln1_gain.astype(jnp.bfloat16), BLK, scatter_dimension=0, tiled=True
        ).astype(jnp.float32),
        lax.psum_scatter(
            grad_ln1_bias.astype(jnp.bfloat16), BLK, scatter_dimension=0, tiled=True
        ).astype(jnp.float32),
        lax.psum_scatter(
            grad_query_weight.astype(jnp.bfloat16), BLK, scatter_dimension=0, tiled=True
        ).astype(jnp.float32),
        lax.psum_scatter(
            grad_key_weight.astype(jnp.bfloat16), BLK, scatter_dimension=0, tiled=True
        ).astype(jnp.float32),
        lax.psum_scatter(
            grad_value_weight.astype(jnp.bfloat16), BLK, scatter_dimension=0, tiled=True
        ).astype(jnp.float32),
        lax.psum_scatter(
            grad_out_weight.astype(jnp.bfloat16), BLK, scatter_dimension=0, tiled=True
        ).astype(jnp.float32),
        lax.psum_scatter(
            grad_mu_weight.astype(jnp.bfloat16), BLK, scatter_dimension=1, tiled=True
        ).astype(jnp.float32),
        lax.psum_scatter(
            grad_sigma_weight.astype(jnp.bfloat16), BLK, scatter_dimension=1, tiled=True
        ).astype(jnp.float32),
        lax.psum_scatter(
            grad_ln2_gain.astype(jnp.bfloat16), BLK, scatter_dimension=0, tiled=True
        ).astype(jnp.float32),
        lax.psum_scatter(
            grad_ln2_bias.astype(jnp.bfloat16), BLK, scatter_dimension=0, tiled=True
        ).astype(jnp.float32),
        lax.psum_scatter(
            grad_up_weight.astype(jnp.bfloat16), BLK, scatter_dimension=0, tiled=True
        ).astype(jnp.float32),
        lax.psum_scatter(
            grad_up_bias.astype(jnp.bfloat16), BLK, scatter_dimension=0, tiled=True
        ).astype(jnp.float32),
        lax.psum_scatter(
            grad_down_weight.astype(jnp.bfloat16), BLK, scatter_dimension=0, tiled=True
        ).astype(jnp.float32),
        lax.psum_scatter(
            grad_down_bias.astype(jnp.bfloat16), BLK, scatter_dimension=0, tiled=True
        ).astype(jnp.float32),
    )
    share_width = model_width // blocks
    coefficient_part = lax.dynamic_slice_in_dim(
        coeff_low, lax.axis_index(BLK) * share_width, share_width, 2
    )
    key_share = shares[3] + jnp.einsum(
        "wrc,wrt->ct",
        coefficient_part,
        gradient_memory_keys_reduced,
        preferred_element_type=jnp.float32,
    )
    value_share = shares[4] + jnp.einsum(
        "wrc,wrt->ct",
        coefficient_part,
        gradient_memory_values_reduced,
        preferred_element_type=jnp.float32,
    )
    totals = (
        lax.psum(shares[0].astype(jnp.bfloat16), BATCH).astype(jnp.float32),
        lax.psum(shares[1].astype(jnp.bfloat16), BATCH).astype(jnp.float32),
        lax.psum(shares[2].astype(jnp.bfloat16), BATCH).astype(jnp.float32),
        lax.psum(key_share.astype(jnp.bfloat16), BATCH).astype(jnp.float32),
        lax.psum(value_share.astype(jnp.bfloat16), BATCH).astype(jnp.float32),
        lax.psum(shares[5].astype(jnp.bfloat16), BATCH).astype(jnp.float32),
        lax.psum(shares[6].astype(jnp.bfloat16), BATCH).astype(jnp.float32),
        lax.psum(shares[7].astype(jnp.bfloat16), BATCH).astype(jnp.float32),
        lax.psum(shares[8].astype(jnp.bfloat16), BATCH).astype(jnp.float32),
        lax.psum(shares[9].astype(jnp.bfloat16), BATCH).astype(jnp.float32),
        lax.psum(shares[10].astype(jnp.bfloat16), BATCH).astype(jnp.float32),
        lax.psum(shares[11].astype(jnp.bfloat16), BATCH).astype(jnp.float32),
        lax.psum(shares[12].astype(jnp.bfloat16), BATCH).astype(jnp.float32),
        lax.psum(shares[13].astype(jnp.bfloat16), BATCH).astype(jnp.float32),
    )
    whole = (
        lax.all_gather(totals[0].astype(jnp.bfloat16), BLK, axis=0, tiled=True).astype(
            jnp.float32
        ),
        lax.all_gather(totals[1].astype(jnp.bfloat16), BLK, axis=0, tiled=True).astype(
            jnp.float32
        ),
        lax.all_gather(totals[2].astype(jnp.bfloat16), BLK, axis=0, tiled=True).astype(
            jnp.float32
        ),
        lax.all_gather(totals[3].astype(jnp.bfloat16), BLK, axis=0, tiled=True).astype(
            jnp.float32
        ),
        lax.all_gather(totals[4].astype(jnp.bfloat16), BLK, axis=0, tiled=True).astype(
            jnp.float32
        ),
        lax.all_gather(totals[5].astype(jnp.bfloat16), BLK, axis=0, tiled=True).astype(
            jnp.float32
        ),
        lax.all_gather(totals[6].astype(jnp.bfloat16), BLK, axis=1, tiled=True).astype(
            jnp.float32
        ),
        lax.all_gather(totals[7].astype(jnp.bfloat16), BLK, axis=1, tiled=True).astype(
            jnp.float32
        ),
        lax.all_gather(totals[8].astype(jnp.bfloat16), BLK, axis=0, tiled=True).astype(
            jnp.float32
        ),
        lax.all_gather(totals[9].astype(jnp.bfloat16), BLK, axis=0, tiled=True).astype(
            jnp.float32
        ),
        lax.all_gather(totals[10].astype(jnp.bfloat16), BLK, axis=0, tiled=True).astype(
            jnp.float32
        ),
        lax.all_gather(totals[11].astype(jnp.bfloat16), BLK, axis=0, tiled=True).astype(
            jnp.float32
        ),
        lax.all_gather(totals[12].astype(jnp.bfloat16), BLK, axis=0, tiled=True).astype(
            jnp.float32
        ),
        lax.all_gather(totals[13].astype(jnp.bfloat16), BLK, axis=0, tiled=True).astype(
            jnp.float32
        ),
    )
    return (
        block_output,
        grad_inputs,
        whole[0],
        whole[1],
        whole[2],
        whole[3],
        whole[4],
        whole[5],
        whole[6],
        whole[7],
        whole[8],
        whole[9],
        whole[10],
        whole[11],
        whole[12],
        whole[13],
    )


f32 = jnp.float32
bf16 = jnp.bfloat16
NN = (((1,), (0,)), ((), ()))
NT = (((1,), (1,)), ((), ()))
TN = (((0,), (0,)), ((), ()))
QB = 256


def mm(a, b, dims=NN, precision=None):
    return lax.dot_general(a, b, dims, precision=precision, preferred_element_type=f32)


def vmem_params(**more):
    return pltpu.CompilerParams(vmem_limit_bytes=56 * 1024 * 1024, **more)


def head_mask(h):
    lane = lax.broadcasted_iota(jnp.int32, (1, 128), 1)
    return (lane >= 64) if h else (lane < 64)


def turn(a):
    return jnp.transpose(a.astype(f32))


def place_params(q, mk, musg, mask, basis):
    u = jnp.where(mask, mm(musg, mk.astype(f32), precision=highest) * 0.125, 0.0)
    ab = mm(u, q.astype(f32), NT, precision=highest)
    spread = 1.0 / basis
    a = ab[0:1]
    b = ab[1:2]
    centre = 1.0 / (1.0 + jnp.exp(-a))
    soft = jnp.maximum(b, 0.0) + jnp.log1p(jnp.exp(-jnp.abs(b)))
    total = spread * spread + var_scale * soft
    return u, b, centre, total


def causal_block(n):
    key = lax.broadcasted_iota(jnp.int32, (n, n), 0)
    query = lax.broadcasted_iota(jnp.int32, (n, n), 1)
    return key <= query


class Place:
    def __init__(self):
        b, k = lax.axis_index(BATCH), lax.axis_index(BLK)
        z, x = b // 2, b % 2
        y, core = k // 2, k % 2
        self.z, self.x, self.y, self.core = z, x, y, core
        self.peer_x = (z * 2 + 1 - x, k)
        self.peer_y = (b, (1 - y) * 2 + core)
        self.peer_core = (b, y * 2 + 1 - core)
        self.peer_z = [(((z + d) % 4) * 2 + x, k) for d in (1, 2, 3)]

    def greet(self):
        peers = [self.peer_x, self.peer_y, self.peer_core] + self.peer_z
        barrier = pltpu.get_barrier_semaphore()
        for peer in peers:
            pl.semaphore_signal(barrier, inc=1, device_id=peer, device_id_type=pl.DeviceIdType.MESH)
        pl.semaphore_wait(barrier, len(peers))


def remote(src, dst, sems, n, peer):
    return pltpu.make_async_remote_copy(
        src_ref=src,
        dst_ref=dst,
        send_sem=sems.at[0, n],
        recv_sem=sems.at[1, n],
        device_id=peer,
        device_id_type=pl.DeviceIdType.MESH,
    )


class Reducer:
    copies = 13

    def __init__(self, place, first, src, out, scratch, window=(0, 0), target=(0, 0)):
        self.place = place
        self.f, self.s = (place.x, place.y) if first == "x" else (place.y, place.x)
        x, y = place.peer_x, place.peer_y
        self.peer_f, self.peer_s = (x, y) if first == "x" else (y, x)
        self.src, self.out = src, out
        self.r1, self.send2, self.r2, self.acc, self.r3, self.done, self.sems, self.own = scratch
        self.rows, self.cols = self.r1.shape[0] * 2, self.r1.shape[1]
        self.step = self.rows // 16
        self.window, self.target = window, target

    @staticmethod
    def scratch(rows, cols, dtype):
        return [
            pltpu.VMEM((rows // 2, cols), dtype),
            pltpu.VMEM((rows // 4, cols), dtype),
            pltpu.VMEM((rows // 4, cols), dtype),
            pltpu.VMEM((rows // 4, cols), dtype),
            pltpu.VMEM((3, rows // 16, cols), dtype),
            pltpu.VMEM((rows // 16, cols), dtype),
            pltpu.SemaphoreType.DMA((2, Reducer.copies)),
            pltpu.SemaphoreType.DMA((1,)),
        ]

    def at(self, row, count):
        return pl.ds(pl.multiple_of(row, self.step), count)

    def taken(self, row, count):
        return self.at(self.window[0] + row, count), pl.ds(self.window[1], self.cols)

    def home(self, row, count):
        rows = self.at(self.target[0] + row, count)
        return self.out.at[self.place.core, rows, pl.ds(self.target[1], self.cols)]

    def copy(self, n):
        f, s, z = self.f, self.s, self.place.z
        half, quarter, step = self.rows // 2, self.rows // 4, self.step
        mine = f * half + s * quarter
        if n == 0:
            return remote(self.src.at[*self.taken((1 - f) * half, half)], self.r1, self.sems, n, self.peer_f)
        if n == 1:
            return remote(self.send2, self.r2, self.sems, n, self.peer_s)
        if n < 5:
            d = n - 2
            part = self.acc.at[self.at(((z + d + 1) % 4) * step, step)]
            return remote(part, self.r3.at[d], self.sems, n, self.place.peer_z[d])
        if n < 8:
            part = self.home(mine + z * step, step)
            return remote(self.done, part, self.sems, n, self.place.peer_z[n - 5])
        if n == 8:
            part, peer = self.home(mine, quarter), self.peer_s
        elif n == 9:
            part, peer = self.home(f * half, half), self.peer_f
        elif n == 10:
            part, peer = self.home(mine, quarter), self.place.peer_core
        elif n == 11:
            part, peer = self.home(f * half + (1 - s) * quarter, quarter), self.place.peer_core
        else:
            part, peer = self.home((1 - f) * half, half), self.place.peer_core
        return remote(part, part, self.sems, n, peer)

    def keep(self):
        mine = self.f * (self.rows // 2) + self.s * (self.rows // 4)
        part = self.home(mine + self.place.z * self.step, self.step)
        return pltpu.make_async_copy(self.done, part, self.own.at[0])

    def start(self, *numbers):
        for n in numbers:
            self.copy(n).start()

    def arrive(self, *numbers):
        for n in numbers:
            self.copy(n).wait_recv()

    def sum_into(self, dst, row, *more):
        def body(i, carry):
            at = i * self.step
            total = self.src[self.taken(row + at, self.step)].astype(f32)
            for ref, start in more:
                total = total + ref[self.at(start + at, self.step)].astype(f32)
            dst[self.at(at, self.step)] = total.astype(dst.dtype)
            return carry

        lax.fori_loop(0, 4, body, 0)

    def run(self, stage):
        f, s, z = self.f, self.s, self.place.z
        half, quarter, step = self.rows // 2, self.rows // 4, self.step
        if stage == 0:
            self.start(0)
        elif stage == 1:
            self.arrive(0)
            self.sum_into(self.send2, f * half + (1 - s) * quarter, (self.r1, (1 - s) * quarter))
            self.start(1)
        elif stage == 2:
            self.arrive(1)
            self.sum_into(self.acc, f * half + s * quarter, (self.r1, s * quarter), (self.r2, 0))
            self.start(2, 3, 4)
        elif stage == 3:
            self.arrive(2, 3, 4)
            total = self.acc[self.at(z * step, step)].astype(f32)
            for d in range(3):
                total = total + self.r3[d].astype(f32)
            self.done[...] = total.astype(self.done.dtype)
            self.start(5, 6, 7)
            self.keep().start()
        elif stage == 4:
            self.arrive(5, 6, 7)
            self.keep().wait()
            self.start(8, 10)
        elif stage == 5:
            self.arrive(8)
            self.start(9, 11)
        elif stage == 6:
            self.arrive(9)
            self.start(12)
        elif stage == 7:
            self.arrive(10, 11, 12)
            for n in range(self.copies):
                self.copy(n).wait_send()


def norm_back(x, gy, gain):
    center = jnp.mean(x, axis=-1, keepdims=True)
    shifted = x - center
    rstd = lax.rsqrt(jnp.mean(shifted * shifted, axis=-1, keepdims=True) + epsilon)
    hat = shifted * rstd
    g = gy * gain
    mean_g = jnp.mean(g, axis=-1, keepdims=True)
    mean_gh = jnp.mean(g * hat, axis=-1, keepdims=True)
    gx = rstd * (g - mean_g - hat * mean_gh)
    return gx, jnp.sum(gy * hat, axis=0, keepdims=True), jnp.sum(gy, axis=0, keepdims=True)


def gelu_both(v):
    root = 0.7978845608028654
    sq = v * v
    t = jnp.tanh(root * v * (1.0 + 0.044715 * sq))
    up = 0.5 + 0.5 * t
    slope = up + (0.5 * v) * (1.0 - t * t) * (root + (3.0 * 0.044715 * root) * sq)
    return v * up, slope


FIRST = "yxxyyxxxy"
PLAN = {
    0: [(0, 0), (1, 0)],
    1: [(3, 0)],
    2: [(1, 1), (0, 1)],
    3: [(2, 0)],
    4: [(0, 2)],
    6: [(9, 0), (3, 1)],
    9: [(1, 2)],
    10: [(0, 3)],
    11: [(4, 0)],
    12: [(5, 0)],
    13: [(2, 1)],
    15: [(1, 3)],
    16: [(4, 1)],
    17: [(3, 2), (5, 1)],
    18: [(0, 4)],
    20: [(1, 4)],
    23: [(6, 0), (2, 2)],
    24: [(0, 5)],
    27: [(1, 5)],
    28: [(6, 1), (2, 3), (3, 3), (7, 0)],
    30: [(8, 0), (2, 4), (5, 2), (3, 4), (0, 6), (5, 3), (7, 1), (6, 2), (8, 1), (2, 5), (8, 2), (5, 4), (6, 3), (8, 3), (8, 4), (6, 4), (4, 2), (3, 5), (5, 5), (7, 2), (4, 3), (4, 4), (7, 3), (5, 6), (6, 5), (7, 4), (8, 5), (2, 6), (3, 6), (4, 5), (7, 5), (8, 6), (0, 7), (8, 7), (6, 6), (6, 7), (1, 6), (1, 7), (4, 6), (3, 7), (7, 6), (4, 7), (5, 7), (2, 7), (7, 7)],
}


def tail_kernel(names, *refs):
    r = SimpleNamespace(**dict(zip(names, refs)))
    jobs_scratch = refs[len(names) :]
    place = Place()
    y, core = place.y, place.core
    tokens, width = r.cot_v.shape
    wide = width // 2
    ff = r.e_v.shape[1]
    pairs = wide // 128
    basis = r.mkv_v.shape[0]
    spread = 1.0 / basis
    block = tokens // 4
    chunk = 64
    n_sem = 8
    take = lambda i: jobs_scratch[n_sem * i : n_sem * i + n_sem]
    ex, loc = r.ex, r.loc
    small_rows = pairs * 2 * basis // 128
    up_rows = ff // 128
    width_rows = width // 128
    base_up = 2 * small_rows
    base_down = base_up + up_rows
    base_ln2 = base_down + width_rows
    base_ln1 = base_ln2 + 2 * width_rows
    third = lambda n: (0, n * wide)
    jobs = [
        Reducer(place, FIRST[0], r.g_down, r.o_down, take(0), (0, 0), (0, 0)),
        Reducer(place, FIRST[1], r.g_up, r.o_up, take(1), (0, 0), (0, 0)),
        Reducer(place, FIRST[2], r.g_down, r.o_down, take(2), (width, 0), (width, 0)),
        Reducer(place, FIRST[3], r.g_up, r.o_up, take(3), (0, width), (0, width)),
        Reducer(place, FIRST[4], r.gup, r.o_out, take(4), third(3)),
        Reducer(place, FIRST[5], r.gup, r.o_0, take(5), third(0)),
        Reducer(place, FIRST[6], r.gup, r.o_1, take(6), third(1)),
        Reducer(place, FIRST[7], r.gup, r.o_2, take(7), third(2)),
        Reducer(place, FIRST[8], r.sv, r.o_s, take(8)),
    ]

    def act(step):
        for job, stage in PLAN.get(step, ()):
            if job < len(jobs):
                jobs[job].run(stage)
            else:
                out_copy().start()

    def rows_at(j, c):
        return pl.ds(pl.multiple_of((2 * j + c) * block, block), block)

    def half_at(j):
        return pl.ds(j * block, block)

    def half_dyn(j):
        return pl.ds(pl.multiple_of(j * block, block), block)

    def small_at(j, i):
        return pl.ds(pl.multiple_of((2 * j + core) * block + i * chunk, chunk), chunk)

    def lanes_from(ref, n, c):
        return ref.at[:, pl.ds(pl.multiple_of(c * n, 128), n)]

    def rows_from(ref, n, c):
        return ref.at[pl.ds(pl.multiple_of(c * n, 128), n), :]

    loads = [
        (r.ctx, r.ctx_v),
        (rows_from(r.w_out, wide, core), r.wo_own),
        (rows_from(r.w_out, wide, 1 - core), r.wo_sib),
        (r.hidden.at[rows_at(0, core)], r.hid_own.at[half_at(0)]),
        (r.hidden.at[rows_at(1, core)], r.hid_own.at[half_at(1)]),
        (lanes_from(r.expand, ff, core), r.e_v),
        (rows_from(r.down, ff, core), r.d_v),
        (r.cot, r.cot_v),
        (r.qkv, r.qkv_v),
        (r.mkv, r.mkv_v),
        (r.att, r.att_v),
        (r.normed_t, r.normed_v),
        (r.coeff, r.coeff_v),
        (r.w_qkv, r.wqkv_v),
    ]

    def load(n):
        return pltpu.make_async_copy(*loads[n], loc.at[n])

    def ready(*numbers):
        for n in numbers:
            load(n).wait()

    def swap(n, j):
        if n == 0:
            src, dst = r.ctx.at[rows_at(j, 1 - core)], r.ctx_rx.at[half_at(j)]
        elif n == 1:
            src = dst = r.n2.at[rows_at(j, core)]
        elif n == 2 or n == 5:
            src, dst = r.tx.at[half_at(j)], r.rx.at[half_at(j)]
        elif n == 3:
            src = dst = r.gml.at[rows_at(j, core)]
        else:
            src, dst = r.tx.at[half_at(j)], r.rx_out.at[half_at(j)]
        return remote(src, dst, ex, 2 * n + j, place.peer_core)

    def out_copy():
        return remote(r.bo.at[half_dyn(1 - y)], r.out.at[y], ex, 12, place.peer_y)

    def out_keep():
        return pltpu.make_async_copy(r.bo.at[half_dyn(y)], r.out.at[y], loc.at[14])

    def gin_copy():
        return remote(r.n2.at[half_dyn(1 - y)], r.gi_rx, ex, 13, place.peer_y)

    def gin_keep():
        return pltpu.make_async_copy(r.gm.at[half_dyn(y)], r.gin.at[y], loc.at[15])

    def gin_place():
        return pltpu.make_async_copy(r.rx.at[half_at(0)], r.gin.at[1 - y], loc.at[16])

    place.greet()
    for j in range(2):
        swap(0, j).start()
    for n in range(len(loads)):
        load(n).start()
    r.sv[...] = jnp.zeros_like(r.sv)
    r.gain1[...] = as_row(r.ln1_gain)
    r.gain2[...] = as_row(r.ln2_gain)
    r.bias2[...] = as_row(r.ln2_bias)
    r.bias_d[...] = as_row(r.down_bias)
    both_up = as_row(r.up_bias)
    r.bias_u[...] = jnp.where(core == 0, both_up[:, :ff], both_up[:, ff:])
    fill_heads(r.musg, r.mu, r.sigma, core)

    def put(row, vec):
        for t in range(vec.shape[1] // 128):
            r.sv[pl.ds(row + t, 1), :] = vec[:, t * 128 : t * 128 + 128]

    ready(0, 1, 2, 3, 4)
    for j in range(2):
        swap(0, j).wait_recv()
        own = mm(r.ctx_v[rows_at(j, core), :], r.wo_own[...])
        sib = mm(r.ctx_rx[half_at(j), :], r.wo_sib[...])
        r.mixed[half_at(j), :] = r.hid_own[half_at(j), :].astype(f32) + (own + sib)

        def norm_chunk(i, carry, j=j):
            at = pl.ds(pl.multiple_of(j * block + i * chunk, chunk), chunk)
            normed = layer_norm(r.mixed[at, :], r.gain2[...], r.bias2[...])
            r.n2[small_at(j, i), :] = normed.astype(bf16)
            return carry

        lax.fori_loop(0, block // chunk, norm_chunk, 0)
        swap(1, j).start()
    for j in range(2):
        swap(1, j).wait_recv()

    ready(5, 6, 7)
    tall = tokens // 2
    for part in range(2):
        lo = part * width

        def tile(i, carry, lo=lo):
            rows = pl.ds(pl.multiple_of((i % 2) * tall, tall), tall)
            col = pl.multiple_of(lo + (i // 2) * 256, 256)
            cols = pl.ds(col, 256)
            hidden_up = mm(r.n2[rows, :], r.e_v[:, cols]) + r.bias_u[:, cols]
            value, slope = gelu_both(hidden_up)
            r.active[rows, cols] = value.astype(bf16)
            grad = (mm(r.cot_v[rows, :], r.d_v[cols, :], NT) * slope).astype(bf16)
            r.gup[rows, cols] = grad
            sums = jnp.sum(grad.astype(f32), axis=0, keepdims=True)
            at = base_up + col // 128
            for t in range(2):
                r.sv[pl.ds(at + t, 1), :] += sums[:, t * 128 : t * 128 + 128]
            return carry

        lax.fori_loop(0, 2 * (width // 256), tile, 0)
        for m in range(width // 256):
            here = slice(lo + m * 256, lo + m * 256 + 256)
            r.g_down[here, :] = mm(r.active[:, here], r.cot_v[...], TN).astype(bf16)
            cols = slice(m * 256, m * 256 + 256)
            r.g_up[cols, lo : lo + width] = mm(r.n2[:, cols], r.gup[:, lo : lo + width], TN).astype(bf16)
        act(part)

    for j in range(2):
        r.tx[half_at(j), :] = mm(r.gup[rows_at(j, 1 - core), :], r.e_v[...], NT)
        swap(2, j).start()

    def norm_two(j, carry):
        def body(i, carry):
            at = pl.ds(pl.multiple_of(j * block + i * chunk, chunk), chunk)
            gy = r.gm[at, :] + r.rx[at, :]
            gx, dg, db = norm_back(r.mixed[at, :], gy, r.gain2[...])
            cot = r.cot_v[small_at(j, i), :].astype(f32)
            gm = cot + gx
            r.gm[at, :] = gm
            r.gml[small_at(j, i), :] = gm.astype(bf16)
            return carry[0] + dg, carry[1] + db

        return lax.fori_loop(0, block // chunk, body, carry)

    sums = (jnp.zeros((1, width), f32), jnp.zeros((1, width), f32))
    for j in range(2):
        r.gm[half_at(j), :] = mm(r.gup[rows_at(j, core), :], r.e_v[...], NT)
        swap(2, j).wait_recv()
        sums = norm_two(j, sums)
        swap(3, j).start()
    put(base_ln2, sums[0])
    put(base_ln2 + width_rows, sums[1])
    put(base_down, jnp.sum(r.cot_v[...].astype(f32), axis=0, keepdims=True))
    act(2)
    for c in (0, 1):
        for j in range(2):
            if c:
                swap(3, j).wait_recv()
            there = rows_at(j, core if c == 0 else 1 - core)
            r.do[there, :] = mm(r.gml[there, :], r.wo_own[...], NT).astype(bf16)
    for m in range(width // 256):
        cols = slice(m * 256, m * 256 + 256)
        r.gup[cols, pairs * wide : pairs * wide + wide] = mm(r.gml[:, cols], r.ctx_v[...], TN).astype(bf16)
    act(3)

    for j in range(2):
        swap(2, j).wait_send()
        r.tx[half_at(j), :] = mm(r.active[rows_at(j, 1 - core), :], r.d_v[...])
        swap(4, j).start()
    for j in range(2):
        own = mm(r.active[rows_at(j, core), :], r.d_v[...])
        swap(4, j).wait_recv()
        total = r.mixed[half_at(j), :] + (own + r.rx_out[half_at(j), :]) + r.bias_d[...]
        r.bo[half_at(j), :] = total.astype(bf16)
    out_keep().start()
    act(4)

    centers = (lax.broadcasted_iota(jnp.int32, (basis, 1), 0).astype(f32) + 0.5) / basis
    allowed = causal_block(QB)
    pick_row = lax.broadcasted_iota(jnp.int32, (8, 1), 0)
    blocks = tokens // QB
    per_pair = 2 * blocks
    ready(8, 9, 10, 11, 12)

    def pair_step(i, carry):
        lanes = pl.ds(pl.multiple_of(i * 128, 128), 128)

        def lanes_of(j):
            return pl.ds(pl.multiple_of(i * 128 + j * wide, 128), 128)

        q_ref, k_ref, v_ref = (r.qkv_v.at[:, lanes_of(j)] for j in range(3))
        mk_ref, mv_ref = (r.mkv_v.at[:, lanes_of(j)] for j in range(2))
        do_ref = r.do.at[:, lanes]
        dka, dva, dqt, gmva, k_t, do_t = r.dka, r.dva, r.dqt, r.gmva, r.k_t, r.do_t
        k_t[...] = turn(k_ref[...]).astype(bf16)
        do_t[...] = turn(do_ref[...])
        dka[...] = jnp.zeros_like(dka)
        dva[...] = jnp.zeros_like(dva)
        gmva[...] = jnp.zeros_like(gmva)
        gmk = jnp.zeros((basis, 128), f32)
        for h in range(2):
            mask = head_mask(h)
            rows = slice(h * 64, h * 64 + 64)
            musg = r.musg[2 * i + h]
            u, b, centre, total = place_params(q_ref[...], mk_ref[...], musg, mask, basis)
            scale = spread * lax.rsqrt(total)
            inv = 1.0 / total
            dot_rows = jnp.sum(do_t[rows, :] * r.att_v[i, rows, :], axis=0, keepdims=True)
            z = jnp.zeros((8, 128), f32)
            for qb in range(blocks):
                cols = slice(qb * QB, qb * QB + QB)
                q = jnp.where(mask, q_ref[cols, :].astype(f32) * 0.125, 0.0).astype(bf16)
                do = jnp.where(mask, do_ref[cols, :].astype(f32), 0.0).astype(bf16)
                lse = r.lse[i, h : h + 1, cols]
                dot_row = dot_rows[:, cols]
                dq_t = jnp.zeros((64, QB), f32)
                for kb in range(qb + 1):
                    keys = slice(kb * QB, kb * QB + QB)
                    p = jnp.exp(mm(k_ref[keys, :], q, NT) - lse)
                    if kb == qb:
                        p = jnp.where(allowed, p, 0.0)
                    dva[keys, :] += mm(p.astype(bf16), do)
                    ds = (p * (mm(v_ref[keys, :], do, NT) - dot_row)).astype(bf16)
                    dka[keys, :] += mm(ds, q)
                    dq_t = dq_t + mm(k_t[rows, keys], ds)
                dqt[rows, cols] = dq_t * 0.125
                gap = centre[:, cols] - centers
                gap2 = gap * gap
                inv_b = inv[:, cols]
                dens = scale[:, cols] * jnp.exp(gap2 * (-0.5 * inv_b))
                gmva[...] += mm(dens.astype(bf16), do)
                e = mm(mv_ref[...], do, NT) * dens
                sum0 = jnp.sum(e, axis=0, keepdims=True)
                sum1 = jnp.sum(e * gap, axis=0, keepdims=True)
                sum2 = jnp.sum(e * gap2, axis=0, keepdims=True)
                c = centre[:, cols]
                da = -sum1 * inv_b * c * (1.0 - c)
                dtotal = 0.5 * inv_b * (sum2 * inv_b - sum0)
                db = dtotal * var_scale / (1.0 + jnp.exp(-b[:, cols]))
                dab = jnp.where(pick_row == 0, da, jnp.where(pick_row == 1, db, 0.0))
                dqt[:, cols] += mm(u, dab, TN, precision=highest)
                z = z + mm(dab, q.astype(f32), precision=highest)
                unit = h * blocks + qb
                if unit == per_pair - 1:
                    gmk = gmk + mm(musg, z, TN, precision=highest)
                    grads = mm(z, mk_ref[...].astype(f32), NT, precision=highest)
                    at = (2 * i + h) * (basis // 128)
                    put(at, grads[0:1])
                    put(small_rows + at, grads[1:2])
                    r.active[:, lanes] = jnp.transpose(dqt[...]).astype(bf16)
                    r.active[:, lanes_of(1)] = dka[...].astype(bf16)
                    r.active[:, lanes_of(2)] = dva[...].astype(bf16)
                    r.part[:, 0:128] = r.active[:, lanes]
                    r.part[:, 128:256] = r.active[:, lanes_of(1)]
                    r.part[:, 256:384] = r.active[:, lanes_of(2)]
                    r.part_mem[:, 0:128] = gmk.astype(bf16)
                    r.part_mem[:, 128:256] = gmva[...].astype(bf16)
                    spot = pl.multiple_of(i * wide, 128)
                    for m in range(width // 256):
                        here = slice(m * 256, m * 256 + 256)
                        g = mm(r.normed_v[here, :], r.part[...])
                        cg = mm(r.coeff_v[:, here], r.part_mem[...], TN)
                        r.gup[here, pl.ds(spot, 128)] = g[:, :128].astype(bf16)
                        r.gup[here, pl.ds(spot + 128, 256)] = (g[:, 128:] + cg).astype(bf16)
                for step in range(pairs):
                    at_step = 5 + step * per_pair + unit
                    if at_step in PLAN:

                        @pl.when(i == step)
                        def _(at_step=at_step):
                            act(at_step)

            if h == 0:
                gmk = gmk + mm(musg, z, TN, precision=highest)
                grads = mm(z, mk_ref[...].astype(f32), NT, precision=highest)
                at = (2 * i + h) * (basis // 128)
                put(at, grads[0:1])
                put(small_rows + at, grads[1:2])
        return carry

    lax.fori_loop(0, pairs, pair_step, 0)

    ready(13)
    for j in range(2):
        swap(4, j).wait_send()
        r.tx[half_at(j), :] = mm(r.active[rows_at(j, 1 - core), : 3 * wide], r.wqkv_v[...], NT)
        swap(5, j).start()
    for j in range(2):
        r.mixed[half_at(j), :] = mm(r.active[rows_at(j, core), : 3 * wide], r.wqkv_v[...], NT)

    act(29)
    for j in range(2):
        swap(1, j).wait_send()

    def norm_one(i, carry):
        at = pl.ds(pl.multiple_of(i * chunk, chunk), chunk)
        gy = r.mixed[at, :] + r.rx[at, :]
        gx, dg, db = norm_back(r.hid_own[at, :].astype(f32), gy, r.gain1[...])
        total = r.gm[at, :] + gx
        r.gm[at, :] = total
        r.n2[at, :] = total.astype(bf16)
        return carry[0] + dg, carry[1] + db

    for j in range(2):
        swap(5, j).wait_recv()
    sums = lax.fori_loop(
        0, 2 * block // chunk, norm_one, (jnp.zeros((1, width), f32), jnp.zeros((1, width), f32))
    )
    put(base_ln1, sums[0])
    put(base_ln1 + width_rows, sums[1])
    gin_keep().start()
    gin_copy().start()
    act(30)
    gin_copy().wait()
    r.rx[half_at(0), :] = r.gi_rx[...].astype(f32)
    gin_place().start()
    out_copy().wait()
    out_keep().wait()
    gin_keep().wait()
    gin_place().wait()
    for j in range(2):
        for n in (0, 3, 5):
            swap(n, j).wait_send()


def tail_call(held, given):
    g = SimpleNamespace(**held, **given)
    tokens, width = g.cot.shape
    wide = width // 2
    ff = g.expand.shape[1] // 2
    heads = wide // 64
    basis = g.mkv.shape[0]
    half, block = tokens // 2, tokens // 4
    used = 2 * (wide // 64) * basis // 128 + ff // 128 + 5 * (width // 128)
    sv_rows = -(-used // 128) * 128
    shape = jax.ShapeDtypeStruct
    like = lambda a: pltpu.VMEM(a.shape, a.dtype)
    outs = dict(
        o_down=shape((2, ff, width), bf16),
        o_up=shape((2, width, ff), bf16),
        o_out=shape((2, width, wide), bf16),
        o_0=shape((2, width, wide), bf16),
        o_1=shape((2, width, wide), bf16),
        o_2=shape((2, width, wide), bf16),
        o_s=shape((2, sv_rows, 128), f32),
        out=shape((2, block, width), bf16),
        gin=shape((2, block, width), f32),
    )
    scratch = dict(
        ex=pltpu.SemaphoreType.DMA((2, 14)),
        loc=pltpu.SemaphoreType.DMA((17,)),
        ctx_v=like(g.ctx),
        ctx_rx=pltpu.VMEM((half, wide), bf16),
        wo_own=pltpu.VMEM((wide, width), bf16),
        wo_sib=pltpu.VMEM((wide, width), bf16),
        hid_own=pltpu.VMEM((half, width), bf16),
        e_v=pltpu.VMEM((width, ff), bf16),
        d_v=pltpu.VMEM((ff, width), bf16),
        cot_v=like(g.cot),
        qkv_v=like(g.qkv),
        mkv_v=like(g.mkv),
        att_v=like(g.att),
        normed_v=like(g.normed_t),
        coeff_v=like(g.coeff),
        wqkv_v=like(g.w_qkv),
        mixed=pltpu.VMEM((half, width), f32),
        n2=pltpu.VMEM((tokens, width), bf16),
        active=pltpu.VMEM((tokens, ff), bf16),
        gup=pltpu.VMEM((tokens, ff), bf16),
        g_down=pltpu.VMEM((ff, width), bf16),
        g_up=pltpu.VMEM((width, ff), bf16),
        tx=pltpu.VMEM((half, width), f32),
        rx=pltpu.VMEM((half, width), f32),
        rx_out=pltpu.VMEM((half, width), f32),
        gm=pltpu.VMEM((half, width), f32),
        gml=pltpu.VMEM((tokens, width), bf16),
        bo=pltpu.VMEM((half, width), bf16),
        gi_rx=pltpu.VMEM((block, width), bf16),
        do=pltpu.VMEM((tokens, wide), bf16),
        part=pltpu.VMEM((tokens, 384), bf16),
        part_mem=pltpu.VMEM((basis, 256), bf16),
        dka=pltpu.VMEM((tokens, 128), f32),
        dva=pltpu.VMEM((tokens, 128), f32),
        dqt=pltpu.VMEM((128, tokens), f32),
        gmva=pltpu.VMEM((basis, 128), f32),
        k_t=pltpu.VMEM((128, tokens), bf16),
        do_t=pltpu.VMEM((128, tokens), f32),
        sv=pltpu.VMEM((sv_rows, 128), f32),
        gain1=pltpu.VMEM((1, width), f32),
        gain2=pltpu.VMEM((1, width), f32),
        bias2=pltpu.VMEM((1, width), f32),
        bias_d=pltpu.VMEM((1, width), f32),
        bias_u=pltpu.VMEM((1, ff), f32),
        musg=pltpu.VMEM((heads, 8, basis), f32),
    )
    more = []
    for _ in range(4):
        more += Reducer.scratch(width, width, bf16)
    for _ in range(4):
        more += Reducer.scratch(width, wide, bf16)
    more += Reducer.scratch(sv_rows, 128, f32)
    hbm, vmem = pl.BlockSpec(memory_space=pl.ANY), pl.BlockSpec(memory_space=pltpu.VMEM)
    names = list(held) + list(given) + list(outs) + list(scratch)
    return pl.pallas_call(
        functools.partial(tail_kernel, names),
        in_specs=[hbm] * len(held) + [vmem] * len(given),
        out_specs=[hbm] * len(outs),
        out_shape=list(outs.values()),
        scratch_shapes=list(scratch.values()) + more,
        compiler_params=pltpu.CompilerParams(
            vmem_limit_bytes=60 * 1024 * 1024, collective_id=1, has_side_effects=True
        ),
        name="tail",
    )(*held.values(), *given.values())


def as_row(ref):
    return ref[...].reshape(1, ref.shape[0])


def fill_heads(dst, mu, sigma, core):
    heads = dst.shape[0]
    dst[...] = jnp.zeros_like(dst)
    for h in range(heads):
        for n, src in enumerate((mu, sigma)):
            dst[h, n : n + 1, :] = src[pl.ds(core * heads + h, 1), :]


def sweep_inverse(a):
    n = a.shape[0]
    lane = lax.broadcasted_iota(jnp.int32, (8, n), 1)
    sub = lax.broadcasted_iota(jnp.int32, (8, n), 0)
    groups = [a[8 * g : 8 * g + 8, :] for g in range(n // 8)]

    def inverse_two(p, q, t):
        inv = 1.0 / (p * t - q * q)
        return t * inv, -q * inv, p * inv

    for k in range(0, n, 4):
        own, at = groups[k // 8], k % 8
        rows = [jnp.broadcast_to(own[at + i : at + i + 1, :], (8, n)) for i in range(4)]
        d = {
            (i, j): jnp.broadcast_to(rows[i][:, k + j : k + j + 1], (8, n))
            for i in range(4)
            for j in range(i, 4)
        }
        a0, a1, a2 = inverse_two(d[0, 0], d[0, 1], d[1, 1])
        w = [
            [a0 * d[0, 2] + a1 * d[1, 2], a0 * d[0, 3] + a1 * d[1, 3]],
            [a1 * d[0, 2] + a2 * d[1, 2], a1 * d[0, 3] + a2 * d[1, 3]],
        ]
        s0 = d[2, 2] - (d[0, 2] * w[0][0] + d[1, 2] * w[1][0])
        s1 = d[2, 3] - (d[0, 2] * w[0][1] + d[1, 2] * w[1][1])
        s2 = d[3, 3] - (d[0, 3] * w[0][1] + d[1, 3] * w[1][1])
        s0, s1, s2 = inverse_two(s0, s1, s2)
        v = [[w[i][0] * s0 + w[i][1] * s1, w[i][0] * s1 + w[i][1] * s2] for i in range(2)]
        p00 = a0 + v[0][0] * w[0][0] + v[0][1] * w[0][1]
        p01 = a1 + v[0][0] * w[1][0] + v[0][1] * w[1][1]
        p11 = a2 + v[1][0] * w[1][0] + v[1][1] * w[1][1]
        p = [
            [p00, p01, -v[0][0], -v[0][1]],
            [p01, p11, -v[1][0], -v[1][1]],
            [-v[0][0], -v[1][0], s0, s1],
            [-v[0][1], -v[1][1], s1, s2],
        ]
        new = []
        for i in range(4):
            row = p[i][0] * rows[0] + p[i][1] * rows[1] + p[i][2] * rows[2] + p[i][3] * rows[3]
            for j in range(4):
                row = jnp.where(lane == k + j, p[i][j], row)
            new.append(row)
        inside = (lane >= k) & (lane < k + 4)
        for g in range(n // 8):
            old = groups[g]
            cols = [jnp.broadcast_to(old[:, k + j : k + j + 1], (8, n)) for j in range(4)]
            part = (cols[0] * new[0] + cols[1] * new[1]) + (cols[2] * new[2] + cols[3] * new[3])
            fresh = jnp.where(inside, 0.0, old) - part
            if g == k // 8:
                for i in range(4):
                    fresh = jnp.where(sub == at + i, new[i], fresh)
            groups[g] = fresh
    return jnp.concatenate(groups, 0)


def front_kernel(names, *refs):
    r = SimpleNamespace(**dict(zip(names, refs)))
    place = Place()
    y, core = place.y, place.core
    tokens, width = r.hid_v.shape
    block = tokens // 4
    wide = width // 2
    pairs = wide // 128
    basis = r.mkv_v.shape[0]
    half = basis // 2
    ex, loc = r.ex, r.loc
    flows = [(r.inputs, r.hid_v), (r.previous, r.prev), (r.cotangent, r.cot)]

    def rows_at(yy, cc):
        return pl.ds(pl.multiple_of((2 * yy + cc) * block, block), block)

    def along(n):
        src, dst = flows[n]
        return remote(src.at[1 - y], dst.at[rows_at(y, core)], ex, n, place.peer_y)

    def across(n):
        src, dst = flows[n]
        return remote(src.at[y], dst.at[rows_at(y, core)], ex, 3 + n, place.peer_core)

    def onward(n):
        part = flows[n][1].at[rows_at(1 - y, core)]
        return remote(part, part, ex, 6 + n, place.peer_core)

    def keep(n):
        src, dst = flows[n]
        return pltpu.make_async_copy(src.at[y], dst.at[rows_at(y, core)], loc.at[n])

    def weight(n):
        src = (r.wq, r.wk, r.wv)[n].at[:, pl.ds(pl.multiple_of(core * wide, 128), wide)]
        return pltpu.make_async_copy(src, r.w_v.at[:, n * wide : n * wide + wide], loc.at[3 + n])

    results = [
        (r.w_v, r.w_qkv),
        (r.hid_v, r.hidden),
        (r.norm_t, r.normed_t),
        (r.qkv_v, r.qkv),
        (r.mkv_v, r.mkv),
        (r.coeff_v, r.coeff),
        (r.att_v, r.att),
        (r.ctx_v, r.ctx),
    ]

    def result(n):
        return pltpu.make_async_copy(*results[n], loc.at[6 + n])

    barrier = pltpu.get_barrier_semaphore()
    for peer in (place.peer_y, place.peer_core):
        pl.semaphore_signal(barrier, inc=1, device_id=peer, device_id_type=pl.DeviceIdType.MESH)
    pl.semaphore_wait(barrier, 2)
    along(0).start()
    across(0).start()
    keep(0).start()
    along(1).start()
    for n in range(3):
        weight(n).start()
    across(1).start()
    keep(1).start()
    along(2).start()
    across(2).start()
    keep(2).start()

    r.gain1[...] = as_row(r.ln1_gain)
    r.bias1[...] = as_row(r.ln1_bias)
    fill_heads(r.musg, r.mu, r.sigma, core)

    spread = 1.0 / basis
    centers = (lax.broadcasted_iota(jnp.int32, (basis, 1), 0).astype(f32) + 0.5) / basis
    places = (r.sticky[pl.ds(y, 1), :].astype(f32) + 0.5) / tokens
    features = jnp.exp(-((places - centers) ** 2) / (2.0 * spread * spread)).astype(bf16)
    same = lax.broadcasted_iota(jnp.int32, (basis, basis), 0) == lax.broadcasted_iota(
        jnp.int32, (basis, basis), 1
    )
    a_ref, i_ref = r.a, r.i
    a_ref[...] = mm(features, features, NT) + jnp.where(same, ridge_weight, 0.0)
    i_ref[0] = sweep_inverse(a_ref[:half, :half])
    cross = a_ref[:half, half:]
    r.cross[...] = mm(i_ref[0], cross, precision=highest)
    schur = a_ref[half:, half:] - mm(cross, r.cross[...], TN, precision=highest)
    i_ref[1] = sweep_inverse(schur)
    index = lax.broadcasted_iota(jnp.int32, (tokens, r.picks.shape[1]), 0)
    chosen = jnp.where(index == r.picks[pl.ds(y, 1), :], 1.0, 0.0).astype(bf16)
    shares = mm(features, chosen, NT)
    high = shares.astype(bf16)
    rest = shares - high.astype(f32)
    middle = rest.astype(bf16)
    r.shares[0] = high
    r.shares[1] = middle
    r.shares[2] = (rest - middle.astype(f32)).astype(bf16)

    chunk = 64

    def project(yy, cc):
        def body(i, carry):
            at = pl.ds(pl.multiple_of((2 * yy + cc) * block + i * chunk, chunk), chunk)
            normed = layer_norm(r.hid_v[at, :].astype(f32), r.gain1[...], r.bias1[...])
            r.normed[at, :] = normed.astype(bf16)
            return carry

        lax.fori_loop(0, block // chunk, body, 0)
        at = rows_at(yy, cc)
        r.qkv_v[at, :] = mm(r.normed[at, :], r.w_v[...]).astype(bf16)

    keep(0).wait()
    for n in range(3):
        weight(n).wait()
    result(0).start()
    project(y, core)
    across(0).wait_recv()
    project(y, 1 - core)
    along(0).wait_recv()
    onward(0).start()
    project(1 - y, core)
    onward(0).wait_recv()
    project(1 - y, 1 - core)
    result(1).start()
    result(3).start()

    allowed = causal_block(QB)
    blocks = tokens // QB

    def lanes_of(i, j):
        return pl.ds(pl.multiple_of(i * 128 + j * wide, 128), 128)

    def causal_pair(i, carry):
        q_ref, k_ref, v_ref = (r.qkv_v.at[:, lanes_of(i, j)] for j in range(3))
        r.v_t[...] = turn(v_ref[...]).astype(bf16)
        for h in range(2):
            mask = head_mask(h)
            rows = slice(h * 64, h * 64 + 64)
            for qb in range(blocks):
                cols = slice(qb * QB, qb * QB + QB)
                q = jnp.where(mask, q_ref[cols, :].astype(f32) * 0.125, 0.0).astype(bf16)
                top = None
                for kb in range(qb + 1):
                    keys = slice(kb * QB, kb * QB + QB)
                    s = mm(k_ref[keys, :], q, NT)
                    if kb == qb:
                        s = jnp.where(allowed, s, masked_score)
                    r.s[keys, :] = s
                    best = jnp.max(s, axis=0, keepdims=True)
                    top = best if top is None else jnp.maximum(top, best)
                denom = jnp.zeros_like(top)
                out = jnp.zeros((64, QB), f32)
                for kb in range(qb + 1):
                    keys = slice(kb * QB, kb * QB + QB)
                    e = jnp.exp(r.s[keys, :] - top)
                    denom = denom + jnp.sum(e, axis=0, keepdims=True)
                    out = out + mm(r.v_t[rows, keys], e.astype(bf16))
                r.att_v[i, rows, cols] = out / denom
                r.lse[i, h : h + 1, cols] = top + jnp.log(denom)
        return carry

    lax.fori_loop(0, pairs - 1, causal_pair, 0)
    along(1).wait_recv()
    onward(1).start()
    lax.fori_loop(pairs - 1, pairs, causal_pair, 0)
    result(6).start()
    for n in range(4):
        at = slice(n * block, n * block + block)
        r.norm_t[:, at] = turn(r.normed[at, :]).astype(bf16)
    result(2).start()

    across(1).wait_recv()
    keep(1).wait()
    onward(1).wait_recv()
    prev = r.prev[...]
    side = mm(r.shares[0], prev) + (mm(r.shares[1], prev) + mm(r.shares[2], prev))
    low_part = mm(
        i_ref[1], side[half:] - mm(r.cross[...], side[:half], TN, precision=highest), precision=highest
    )
    r.coeff_v[half:, :] = low_part.astype(bf16)
    r.coeff_v[:half, :] = (
        mm(i_ref[0], side[:half], precision=highest) - mm(r.cross[...], low_part, precision=highest)
    ).astype(bf16)
    r.mkv_v[...] = mm(r.coeff_v[...], r.w_v[:, wide:]).astype(bf16)
    result(4).start()
    result(5).start()
    along(2).wait_recv()
    onward(2).start()

    def memory_pair(i, carry):
        q_ref = r.qkv_v.at[:, lanes_of(i, 0)]
        mk_ref, mv_ref = (r.mkv_v.at[:, lanes_of(i, j)] for j in range(2))
        mv_t = turn(mv_ref[...]).astype(bf16)
        for h in range(2):
            rows = slice(h * 64, h * 64 + 64)
            u, b, centre, total = place_params(q_ref[...], mk_ref[...], r.musg[2 * i + h], head_mask(h), basis)
            scale = spread * lax.rsqrt(total)
            fall = -0.5 / total
            for qb in range(blocks):
                cols = slice(qb * QB, qb * QB + QB)
                gap = centre[:, cols] - centers
                dens = (scale[:, cols] * jnp.exp(gap * gap * fall[:, cols])).astype(bf16)
                r.o[rows, cols] = r.att_v[i, rows, cols] + mm(mv_t[rows, :], dens)
        r.ctx_v[:, lanes_of(i, 0)] = jnp.transpose(r.o[...]).astype(bf16)
        return carry

    lax.fori_loop(0, pairs, memory_pair, 0)
    result(7).start()
    keep(2).wait()
    across(2).wait_recv()
    onward(2).wait_recv()
    for n in range(3):
        along(n).wait_send()
        across(n).wait_send()
        onward(n).wait_send()
    for n in range(len(results)):
        result(n).wait()


def front_call(held, given, basis):
    block, width = held[next(iter(held))].shape[1:]
    tokens = block * 4
    wide = width // 2
    pairs = wide // 128
    shape = jax.ShapeDtypeStruct
    outs = dict(
        hidden=shape((tokens, width), bf16),
        normed_t=shape((width, tokens), bf16),
        qkv=shape((tokens, 3 * wide), bf16),
        mkv=shape((basis, width), bf16),
        coeff=shape((basis, width), bf16),
        w_qkv=shape((width, 3 * wide), bf16),
        cot=shape((tokens, width), bf16),
        ctx=shape((tokens, wide), bf16),
        att=shape((pairs, 128, tokens), f32),
    )
    near = dict(lse=shape((pairs, 2, tokens), f32))
    like = lambda a: pltpu.VMEM(a.shape, a.dtype)
    o = SimpleNamespace(**outs)
    scratch = dict(
        ex=pltpu.SemaphoreType.DMA((2, 9)),
        loc=pltpu.SemaphoreType.DMA((14,)),
        hid_v=like(o.hidden),
        norm_t=like(o.normed_t),
        qkv_v=like(o.qkv),
        mkv_v=like(o.mkv),
        coeff_v=like(o.coeff),
        w_v=like(o.w_qkv),
        ctx_v=like(o.ctx),
        att_v=like(o.att),
        prev=pltpu.VMEM((tokens, width), bf16),
        normed=pltpu.VMEM((tokens, width), bf16),
        a=pltpu.VMEM((basis, basis), f32),
        i=pltpu.VMEM((2, basis // 2, basis // 2), f32),
        cross=pltpu.VMEM((basis // 2, basis // 2), f32),
        shares=pltpu.VMEM((3, basis, tokens), bf16),
        gain1=pltpu.VMEM((1, width), f32),
        bias1=pltpu.VMEM((1, width), f32),
        musg=pltpu.VMEM((2 * pairs, 8, basis), f32),
        s=pltpu.VMEM((tokens, QB), f32),
        v_t=pltpu.VMEM((128, tokens), bf16),
        o=pltpu.VMEM((128, tokens), f32),
    )
    hbm, vmem = pl.BlockSpec(memory_space=pl.ANY), pl.BlockSpec(memory_space=pltpu.VMEM)
    names = list(held) + list(given) + list(outs) + list(near) + list(scratch)
    return pl.pallas_call(
        functools.partial(front_kernel, names),
        in_specs=[hbm] * len(held) + [vmem] * len(given),
        out_specs=[hbm] * len(outs) + [vmem] * len(near),
        out_shape=list(outs.values()) + list(near.values()),
        scratch_shapes=list(scratch.values()),
        compiler_params=vmem_params(collective_id=2, has_side_effects=True),
        name="front",
    )(*held.values(), *given.values())


def finish(down, up, out_t, parts, small, basis):
    width = out_t.shape[1]
    per = basis // 128
    heads = width // 64
    steps = width // 128
    per_core = steps // 2
    tall = down.shape[1] // per_core
    wide = width // 2

    def body(down_ref, up_ref, t_ref, s_ref, *refs):
        o_down, o_up, o_q, o_k, o_v, o_o, o_mu, o_sg = refs[len(parts) :]
        for n, ref in enumerate((o_mu, o_sg)):
            for h in range(heads):
                for t in range(per):
                    row = n * (heads // 2) * per + h % (heads // 2) * per + t
                    here = slice(t * 128, t * 128 + 128)
                    ref[h : h + 1, here] = s_ref[h // (heads // 2), row : row + 1, :]
        o_down[...] = down_ref[0].astype(f32)
        n = up_ref.shape[2]
        for c in range(2):
            o_up[:, c * n : c * n + n] = up_ref[c].astype(f32)
            for i, ref in enumerate(refs[: len(parts)]):
                here = slice(c * wide + i * 128, c * wide + i * 128 + 128)
                o_q[:, here] = ref[c, :, 0:128].astype(f32)
                o_k[:, here] = ref[c, :, 128:256].astype(f32)
                o_v[:, here] = ref[c, :, 256:384].astype(f32)
        o_o[...] = jnp.transpose(t_ref[0].astype(f32))

    row = lambda n: pl.BlockSpec((128, n), lambda i: (i, 0))
    shape = jax.ShapeDtypeStruct
    return pl.pallas_call(
        body,
        grid=(steps,),
        in_specs=[
            pl.BlockSpec((1, tall, width), lambda i: (i // per_core, i % per_core, 0)),
            pl.BlockSpec((2, 128, up.shape[2]), lambda i: (0, i, 0)),
            pl.BlockSpec((1, width, 128), lambda i: (i // per_core, 0, i % per_core)),
            pl.BlockSpec(small.shape, lambda i: (0, 0, 0)),
        ]
        + [pl.BlockSpec((2, 128, 384), lambda i: (0, i, 0))] * len(parts),
        out_specs=[pl.BlockSpec((tall, width), lambda i: (i, 0)), row(2 * up.shape[2])]
        + [row(width)] * 4
        + [pl.BlockSpec((heads, basis), lambda i: (0, 0))] * 2,
        out_shape=[
            shape((2 * down.shape[1], width), f32),
            shape((width, 2 * up.shape[2]), f32),
        ]
        + [shape((width, width), f32)] * 4
        + [shape((heads, basis), f32)] * 2,
        compiler_params=vmem_params(),
        name="finish",
    )(down, up, out_t, small, *parts)


def chip_local(
    inputs,
    previous,
    memory_rows,
    sticky_positions,
    cotangent,
    ln1_gain,
    ln1_bias,
    query_weight,
    key_weight,
    value_weight,
    out_weight,
    mu_weight,
    sigma_weight,
    ln2_gain,
    ln2_bias,
    expand_weight,
    up_bias,
    down_weight,
    down_bias,
):
    width = inputs.shape[2]
    heads, basis = mu_weight.shape
    ff = up_bias.shape[0]
    params = dict(ln1_gain=ln1_gain, mu=mu_weight, sigma=sigma_weight)
    hidden, normed_t, qkv, mkv, coeff, w_qkv, cot, ctx, att, lse = front_call(
        dict(
            inputs=inputs,
            previous=previous,
            cotangent=cotangent,
            wq=query_weight,
            wk=key_weight,
            wv=value_weight,
        ),
        dict(picks=memory_rows, sticky=sticky_positions, ln1_bias=ln1_bias, **params),
        basis,
    )
    o_down, o_up, o_out, o_0, o_1, o_2, o_s, block_output, grad_inputs = tail_call(
        dict(
            cot=cot,
            hidden=hidden,
            ctx=ctx,
            expand=expand_weight,
            down=down_weight,
            w_out=out_weight,
            qkv=qkv,
            mkv=mkv,
            att=att,
            normed_t=normed_t,
            coeff=coeff,
            w_qkv=w_qkv,
        ),
        dict(lse=lse, ln2_gain=ln2_gain, ln2_bias=ln2_bias, up_bias=up_bias, down_bias=down_bias, **params),
    )
    g_down, g_up, g_q, g_k, g_v, g_o, g_mu, g_sigma = finish(
        o_down, o_up, o_out, (o_0, o_1, o_2), o_s, basis
    )
    s = o_s.reshape(2, -1)
    start = heads * basis
    cuts = [ff // 2, width, width, width, width, width]
    parts = []
    for n in cuts:
        parts.append(s[:, start : start + n])
        start += n
    both = [a[0] + a[1] for a in parts[2:]]
    return (
        block_output,
        grad_inputs,
        both[2],
        both[3],
        g_q,
        g_k,
        g_v,
        g_o,
        g_mu,
        g_sigma,
        both[0],
        both[1],
        g_up,
        parts[0].reshape(ff),
        g_down,
        parts[1][0],
    )


def pick(mesh):
    def step(*arrays):
        inputs, mu = arrays[0], arrays[11]
        fits = (
            mesh.shape[BATCH] == 8
            and mesh.shape[BLK] == 4
            and inputs.shape[0] == 2
            and inputs.shape[1] % QB == 0
            and mu.shape[0] % 4 == 0
            and inputs.shape[2] == mu.shape[0] * 64
        )
        return (chip_local if fits else general)(*arrays)

    return step


def solution(mesh):
    return jax.shard_map(
        pick(mesh),
        mesh=mesh,
        in_specs=(
            P(BATCH, BLK, None),
            P(BATCH, BLK, None),
            P(BATCH, None),
            P(BATCH, None),
            P(BATCH, BLK, None),
            P(),
            P(),
            P(),
            P(),
            P(),
            P(),
            P(),
            P(),
            P(),
            P(),
            P(),
            P(),
            P(),
            P(),
        ),
        out_specs=(
            P(BATCH, BLK, None),
            P(BATCH, BLK, None),
            P(),
            P(),
            P(),
            P(),
            P(),
            P(),
            P(),
            P(),
            P(),
            P(),
            P(),
            P(),
            P(),
            P(),
        ),
        check_vma=False,
    )
```

```python
import functools
from types import SimpleNamespace

import jax
import jax.numpy as jnp
from jax import lax
from jax.experimental import pallas as pl
from jax.experimental.pallas import tpu as pltpu
from jax.sharding import PartitionSpec as P

epsilon = 1e-05
ridge_weight = 1.0
var_scale = 0.01
masked_score = -1e30
BLK = "blk"
BATCH = "batch"
highest = lax.Precision.HIGHEST


def layer_norm(values, gain, bias):
    center = jnp.mean(values, axis=-1, keepdims=True)
    shifted = values - center
    spread_sq = jnp.mean(shifted * shifted, axis=-1, keepdims=True)
    return shifted * lax.rsqrt(spread_sq + epsilon) * gain + bias


def density(scores, mu_row, sigma_row):
    count = scores.shape[-1]
    centers = (jnp.arange(count, dtype=scores.dtype) + 0.5) / count
    spread = 1.0 / count
    centre = jax.nn.sigmoid(jnp.dot(scores, mu_row, precision=highest))
    variance = var_scale * jax.nn.softplus(jnp.dot(scores, sigma_row, precision=highest))
    total = spread * spread + variance
    return (spread * lax.rsqrt(total))[..., None] * jnp.exp(
        -((centre[..., None] - centers) ** 2) / (2.0 * total[..., None])
    )


def project(source, weight):
    return jnp.einsum("std,de->ste", source, weight, preferred_element_type=jnp.float32)


def weight_grad(source, grads):
    return jnp.einsum("std,ste->de", source, grads, preferred_element_type=jnp.float32)


def back_project(grads, weight):
    return jnp.einsum("ste,de->std", grads, weight, preferred_element_type=jnp.float32)


def gelu_tanh(values):
    return jax.nn.gelu(values, approximate=True)


def general(
    inputs,
    previous,
    memory_rows,
    sticky_positions,
    cotangent,
    ln1_gain,
    ln1_bias,
    query_weight,
    key_weight,
    value_weight,
    out_weight,
    mu_weight,
    sigma_weight,
    ln2_gain,
    ln2_bias,
    expand_weight,
    up_bias,
    down_weight,
    down_bias,
):
    seg_count, tok_rows, model_width = inputs.shape
    blocks = lax.axis_size(BLK)
    length = tok_rows * blocks
    first_row = lax.axis_index(BLK) * tok_rows
    head_count, basis_count = mu_weight.shape
    head_width = model_width // head_count
    centers = (jnp.arange(basis_count, dtype=jnp.float32) + 0.5) / basis_count
    spread = 1.0 / basis_count
    places = (sticky_positions.astype(jnp.float32) + 0.5) / length
    features = jnp.exp(-((places[..., None] - centers) ** 2) / (2.0 * spread * spread)).astype(
        jnp.bfloat16
    )
    local_index = memory_rows - first_row
    owned_rows = (local_index >= 0) & (local_index < tok_rows)
    picked = jax.vmap(lambda shard_rows, row_index: shard_rows[row_index])(
        previous, jnp.clip(local_index, 0, tok_rows - 1)
    )
    picked = jnp.where(owned_rows[..., None], picked, jnp.zeros_like(picked))
    own_features = jnp.where(owned_rows[..., None], features, jnp.zeros_like(features))
    side_part = jnp.einsum("smn,smd->snd", own_features, picked, preferred_element_type=jnp.float32)
    gram_part = jnp.einsum(
        "smn,smk->snk", own_features, own_features, preferred_element_type=jnp.float32
    )
    gram_sum, right_side = lax.psum((gram_part, side_part), BLK)
    system = gram_sum + ridge_weight * jnp.eye(basis_count, dtype=jnp.float32)
    factor = jnp.linalg.cholesky(system)
    coefficients = jax.scipy.linalg.cho_solve((factor, True), right_side)
    coeff_low = coefficients.astype(jnp.bfloat16)
    hidden_in = inputs.astype(jnp.float32)
    normed_low = layer_norm(hidden_in, ln1_gain, ln1_bias).astype(jnp.bfloat16)
    queries = project(normed_low, query_weight).astype(jnp.bfloat16)
    keys_local = project(normed_low, key_weight).astype(jnp.bfloat16)
    values_local = project(normed_low, value_weight).astype(jnp.bfloat16)
    mem_keys = project(coeff_low, key_weight).astype(jnp.bfloat16)
    mem_values = project(coeff_low, value_weight).astype(jnp.bfloat16)
    all_keys, all_values = (
        lax.all_gather(keys_local, BLK, axis=1, tiled=True),
        lax.all_gather(values_local, BLK, axis=1, tiled=True),
    )

    def split_heads(array):
        return array.reshape(array.shape[0], array.shape[1], head_count, head_width).transpose(
            2, 0, 1, 3
        )

    def merge_heads(array):
        return array.transpose(1, 2, 0, 3).reshape(array.shape[1], array.shape[2], model_width)

    query_pos = first_row + jnp.arange(tok_rows)
    key_pos = jnp.arange(length)
    causal = key_pos[None, :] <= query_pos[:, None]

    def forward_head(operands):
        query_h, key_h, value_h, memkey_h, memval_h, mu_row, sigma_row = operands
        scores = (
            jnp.einsum("sqd,skd->sqk", query_h, key_h, preferred_element_type=jnp.float32) * 0.125
        )
        scores = jnp.where(causal, scores, masked_score)
        top = jnp.max(scores, axis=-1, keepdims=True)
        raised = jnp.exp(scores - top)
        total = jnp.sum(raised, axis=-1, keepdims=True)
        probs = raised / total
        log_total = (top + jnp.log(total))[..., 0]
        attended = jnp.einsum(
            "sqk,skd->sqd", probs.astype(jnp.bfloat16), value_h, preferred_element_type=jnp.float32
        )
        memory_scores = (
            jnp.einsum("sqd,snd->sqn", query_h, memkey_h, preferred_element_type=jnp.float32)
            * 0.125
        )
        weights_mem = density(memory_scores, mu_row, sigma_row)
        recalled = jnp.einsum(
            "sqn,snd->sqd",
            weights_mem.astype(jnp.bfloat16),
            memval_h,
            preferred_element_type=jnp.float32,
        )
        return (attended + recalled, log_total)

    head_queries = split_heads(queries)
    head_keys = split_heads(all_keys)
    value_per_head = split_heads(all_values)
    head_memkeys = split_heads(mem_keys)
    head_memvals = split_heads(mem_values)
    heads_ctx, log_totals = lax.map(
        forward_head,
        (
            head_queries,
            head_keys,
            value_per_head,
            head_memkeys,
            head_memvals,
            mu_weight,
            sigma_weight,
        ),
    )
    context_low = merge_heads(heads_ctx).astype(jnp.bfloat16)
    mixed = hidden_in + project(context_low, out_weight)
    normed_two_low = layer_norm(mixed, ln2_gain, ln2_bias).astype(jnp.bfloat16)
    hidden_up = (
        jnp.einsum("std,df->stf", normed_two_low, expand_weight, preferred_element_type=jnp.float32)
        + up_bias
    )
    active_low = gelu_tanh(hidden_up).astype(jnp.bfloat16)
    result = (
        mixed
        + jnp.einsum("stf,fd->std", active_low, down_weight, preferred_element_type=jnp.float32)
        + down_bias
    )
    block_output = result.astype(jnp.bfloat16)
    grad_result = cotangent.astype(jnp.float32)
    grad_down_bias = jnp.sum(grad_result, axis=(0, 1))
    grad_down_weight = jnp.einsum(
        "stf,std->fd", active_low, cotangent, preferred_element_type=jnp.float32
    )
    grad_active = jnp.einsum(
        "std,fd->stf", cotangent, down_weight, preferred_element_type=jnp.float32
    )
    gelu_value, gelu_pull = jax.vjp(gelu_tanh, hidden_up)
    grad_up_low = gelu_pull(grad_active)[0].astype(jnp.bfloat16)
    grad_up_bias = jnp.sum(grad_up_low.astype(jnp.float32), axis=(0, 1))
    grad_up_weight = jnp.einsum(
        "std,stf->df", normed_two_low, grad_up_low, preferred_element_type=jnp.float32
    )
    grad_normed_two = jnp.einsum(
        "stf,df->std", grad_up_low, expand_weight, preferred_element_type=jnp.float32
    )
    norm_two_value, norm_two_pull = jax.vjp(layer_norm, mixed, ln2_gain, ln2_bias)
    grad_mixed_norm, grad_ln2_gain, grad_ln2_bias = norm_two_pull(grad_normed_two)
    grad_mixed = grad_result + grad_mixed_norm
    grad_mixed_low = grad_mixed.astype(jnp.bfloat16)
    grad_out_weight = weight_grad(context_low, grad_mixed_low)
    grad_context_low = back_project(grad_mixed_low, out_weight).astype(jnp.bfloat16)

    def backward_head(operands):
        query_h, key_h, value_h, memkey_h, memval_h, mu_row, sigma_row, grad_h, log_total = operands
        scores = (
            jnp.einsum("sqd,skd->sqk", query_h, key_h, preferred_element_type=jnp.float32) * 0.125
        )
        probs = jnp.where(causal, jnp.exp(scores - log_total[..., None]), 0.0)
        grad_probs = jnp.einsum("sqd,skd->sqk", grad_h, value_h, preferred_element_type=jnp.float32)
        row_dot = jnp.sum(probs * grad_probs, axis=-1, keepdims=True)
        grad_scores = (probs * (grad_probs - row_dot)).astype(jnp.bfloat16)
        grad_query = (
            jnp.einsum("sqk,skd->sqd", grad_scores, key_h, preferred_element_type=jnp.float32)
            * 0.125
        )
        memory_scores = (
            jnp.einsum("sqd,snd->sqn", query_h, memkey_h, preferred_element_type=jnp.float32)
            * 0.125
        )
        weights_mem, density_pull = jax.vjp(density, memory_scores, mu_row, sigma_row)
        weights_low = weights_mem.astype(jnp.bfloat16)
        grad_weights = jnp.einsum(
            "sqd,snd->sqn", grad_h, memval_h, preferred_element_type=jnp.float32
        )
        grad_memval = jnp.einsum(
            "sqn,sqd->snd", weights_low, grad_h, preferred_element_type=jnp.float32
        )
        grad_memscores, grad_mu, grad_sigma = density_pull(grad_weights)
        grad_memscores_low = grad_memscores.astype(jnp.bfloat16)
        grad_query = (
            grad_query
            + jnp.einsum(
                "sqn,snd->sqd", grad_memscores_low, memkey_h, preferred_element_type=jnp.float32
            )
            * 0.125
        )
        grad_memkey = (
            jnp.einsum(
                "sqn,sqd->snd", grad_memscores_low, query_h, preferred_element_type=jnp.float32
            )
            * 0.125
        )
        grad_key = (
            jnp.einsum("sqk,sqd->skd", grad_scores, query_h, preferred_element_type=jnp.float32)
            * 0.125
        )
        grad_value = jnp.einsum(
            "sqk,sqd->skd", probs.astype(jnp.bfloat16), grad_h, preferred_element_type=jnp.float32
        )
        return (grad_query, grad_memkey, grad_memval, grad_mu, grad_sigma, grad_key, grad_value)

    head_grads = split_heads(grad_context_low)
    outcome = lax.map(
        backward_head,
        (
            head_queries,
            head_keys,
            value_per_head,
            head_memkeys,
            head_memvals,
            mu_weight,
            sigma_weight,
            head_grads,
            log_totals,
        ),
    )
    grad_query_heads, grad_memkey_heads, grad_memval_heads, grad_mu_weight, grad_sigma_weight = (
        outcome[:5]
    )
    terms = (
        jnp.stack((outcome[5], outcome[6]))
        .transpose(3, 2, 0, 1, 4)
        .reshape(length, seg_count, 2 * model_width)
    )
    own_terms = lax.psum_scatter(
        terms.astype(jnp.bfloat16), BLK, scatter_dimension=0, tiled=True
    ).astype(jnp.float32)
    own_terms = own_terms.reshape(tok_rows, seg_count, 2, model_width).transpose(2, 1, 0, 3)
    grad_keys = own_terms[0]
    grad_values = own_terms[1]
    grad_queries_low = merge_heads(grad_query_heads).astype(jnp.bfloat16)
    grad_keys_low = grad_keys.astype(jnp.bfloat16)
    grad_values_low = grad_values.astype(jnp.bfloat16)
    memkey_sum, memval_sum = (
        lax.psum(grad_memkey_heads.astype(jnp.bfloat16), BLK).astype(jnp.float32),
        lax.psum(grad_memval_heads.astype(jnp.bfloat16), BLK).astype(jnp.float32),
    )
    gradient_memory_keys_reduced = merge_heads(memkey_sum).astype(jnp.bfloat16)
    gradient_memory_values_reduced = merge_heads(memval_sum).astype(jnp.bfloat16)
    grad_query_weight = weight_grad(normed_low, grad_queries_low)
    grad_key_weight = weight_grad(normed_low, grad_keys_low)
    grad_value_weight = weight_grad(normed_low, grad_values_low)
    grad_normed = (
        back_project(grad_queries_low, query_weight)
        + back_project(grad_keys_low, key_weight)
        + back_project(grad_values_low, value_weight)
    )
    norm_one_value, norm_one_pull = jax.vjp(layer_norm, hidden_in, ln1_gain, ln1_bias)
    grad_in_norm, grad_ln1_gain, grad_ln1_bias = norm_one_pull(grad_normed)
    grad_inputs = grad_mixed + grad_in_norm
    shares = (
        lax.psum_scatter(
            grad_ln1_gain.astype(jnp.bfloat16), BLK, scatter_dimension=0, tiled=True
        ).astype(jnp.float32),
        lax.psum_scatter(
            grad_ln1_bias.astype(jnp.bfloat16), BLK, scatter_dimension=0, tiled=True
        ).astype(jnp.float32),
        lax.psum_scatter(
            grad_query_weight.astype(jnp.bfloat16), BLK, scatter_dimension=0, tiled=True
        ).astype(jnp.float32),
        lax.psum_scatter(
            grad_key_weight.astype(jnp.bfloat16), BLK, scatter_dimension=0, tiled=True
        ).astype(jnp.float32),
        lax.psum_scatter(
            grad_value_weight.astype(jnp.bfloat16), BLK, scatter_dimension=0, tiled=True
        ).astype(jnp.float32),
        lax.psum_scatter(
            grad_out_weight.astype(jnp.bfloat16), BLK, scatter_dimension=0, tiled=True
        ).astype(jnp.float32),
        lax.psum_scatter(
            grad_mu_weight.astype(jnp.bfloat16), BLK, scatter_dimension=1, tiled=True
        ).astype(jnp.float32),
        lax.psum_scatter(
            grad_sigma_weight.astype(jnp.bfloat16), BLK, scatter_dimension=1, tiled=True
        ).astype(jnp.float32),
        lax.psum_scatter(
            grad_ln2_gain.astype(jnp.bfloat16), BLK, scatter_dimension=0, tiled=True
        ).astype(jnp.float32),
        lax.psum_scatter(
            grad_ln2_bias.astype(jnp.bfloat16), BLK, scatter_dimension=0, tiled=True
        ).astype(jnp.float32),
        lax.psum_scatter(
            grad_up_weight.astype(jnp.bfloat16), BLK, scatter_dimension=0, tiled=True
        ).astype(jnp.float32),
        lax.psum_scatter(
            grad_up_bias.astype(jnp.bfloat16), BLK, scatter_dimension=0, tiled=True
        ).astype(jnp.float32),
        lax.psum_scatter(
            grad_down_weight.astype(jnp.bfloat16), BLK, scatter_dimension=0, tiled=True
        ).astype(jnp.float32),
        lax.psum_scatter(
            grad_down_bias.astype(jnp.bfloat16), BLK, scatter_dimension=0, tiled=True
        ).astype(jnp.float32),
    )
    share_width = model_width // blocks
    coefficient_part = lax.dynamic_slice_in_dim(
        coeff_low, lax.axis_index(BLK) * share_width, share_width, 2
    )
    key_share = shares[3] + jnp.einsum(
        "wrc,wrt->ct",
        coefficient_part,
        gradient_memory_keys_reduced,
        preferred_element_type=jnp.float32,
    )
    value_share = shares[4] + jnp.einsum(
        "wrc,wrt->ct",
        coefficient_part,
        gradient_memory_values_reduced,
        preferred_element_type=jnp.float32,
    )
    totals = (
        lax.psum(shares[0].astype(jnp.bfloat16), BATCH).astype(jnp.float32),
        lax.psum(shares[1].astype(jnp.bfloat16), BATCH).astype(jnp.float32),
        lax.psum(shares[2].astype(jnp.bfloat16), BATCH).astype(jnp.float32),
        lax.psum(key_share.astype(jnp.bfloat16), BATCH).astype(jnp.float32),
        lax.psum(value_share.astype(jnp.bfloat16), BATCH).astype(jnp.float32),
        lax.psum(shares[5].astype(jnp.bfloat16), BATCH).astype(jnp.float32),
        lax.psum(shares[6].astype(jnp.bfloat16), BATCH).astype(jnp.float32),
        lax.psum(shares[7].astype(jnp.bfloat16), BATCH).astype(jnp.float32),
        lax.psum(shares[8].astype(jnp.bfloat16), BATCH).astype(jnp.float32),
        lax.psum(shares[9].astype(jnp.bfloat16), BATCH).astype(jnp.float32),
        lax.psum(shares[10].astype(jnp.bfloat16), BATCH).astype(jnp.float32),
        lax.psum(shares[11].astype(jnp.bfloat16), BATCH).astype(jnp.float32),
        lax.psum(shares[12].astype(jnp.bfloat16), BATCH).astype(jnp.float32),
        lax.psum(shares[13].astype(jnp.bfloat16), BATCH).astype(jnp.float32),
    )
    whole = (
        lax.all_gather(totals[0].astype(jnp.bfloat16), BLK, axis=0, tiled=True).astype(
            jnp.float32
        ),
        lax.all_gather(totals[1].astype(jnp.bfloat16), BLK, axis=0, tiled=True).astype(
            jnp.float32
        ),
        lax.all_gather(totals[2].astype(jnp.bfloat16), BLK, axis=0, tiled=True).astype(
            jnp.float32
        ),
        lax.all_gather(totals[3].astype(jnp.bfloat16), BLK, axis=0, tiled=True).astype(
            jnp.float32
        ),
        lax.all_gather(totals[4].astype(jnp.bfloat16), BLK, axis=0, tiled=True).astype(
            jnp.float32
        ),
        lax.all_gather(totals[5].astype(jnp.bfloat16), BLK, axis=0, tiled=True).astype(
            jnp.float32
        ),
        lax.all_gather(totals[6].astype(jnp.bfloat16), BLK, axis=1, tiled=True).astype(
            jnp.float32
        ),
        lax.all_gather(totals[7].astype(jnp.bfloat16), BLK, axis=1, tiled=True).astype(
            jnp.float32
        ),
        lax.all_gather(totals[8].astype(jnp.bfloat16), BLK, axis=0, tiled=True).astype(
            jnp.float32
        ),
        lax.all_gather(totals[9].astype(jnp.bfloat16), BLK, axis=0, tiled=True).astype(
            jnp.float32
        ),
        lax.all_gather(totals[10].astype(jnp.bfloat16), BLK, axis=0, tiled=True).astype(
            jnp.float32
        ),
        lax.all_gather(totals[11].astype(jnp.bfloat16), BLK, axis=0, tiled=True).astype(
            jnp.float32
        ),
        lax.all_gather(totals[12].astype(jnp.bfloat16), BLK, axis=0, tiled=True).astype(
            jnp.float32
        ),
        lax.all_gather(totals[13].astype(jnp.bfloat16), BLK, axis=0, tiled=True).astype(
            jnp.float32
        ),
    )
    return (
        block_output,
        grad_inputs,
        whole[0],
        whole[1],
        whole[2],
        whole[3],
        whole[4],
        whole[5],
        whole[6],
        whole[7],
        whole[8],
        whole[9],
        whole[10],
        whole[11],
        whole[12],
        whole[13],
    )


f32 = jnp.float32
bf16 = jnp.bfloat16
NN = (((1,), (0,)), ((), ()))
NT = (((1,), (1,)), ((), ()))
TN = (((0,), (0,)), ((), ()))
QB = 256


def mm(a, b, dims=NN, precision=None):
    return lax.dot_general(a, b, dims, precision=precision, preferred_element_type=f32)


def vmem_params(**more):
    return pltpu.CompilerParams(vmem_limit_bytes=56 * 1024 * 1024, **more)


def head_mask(h):
    lane = lax.broadcasted_iota(jnp.int32, (1, 128), 1)
    return lane // 64 == h


def head_rows(h):
    return pl.ds(pl.multiple_of(h * 64, 64), 64)


def turn(a):
    return jnp.transpose(a.astype(f32))


def parts_of(rows):
    index = lax.broadcasted_iota(jnp.int32, (8, 1), 0)
    out = jnp.zeros_like(rows)
    for n in range(2):
        rest = rows[n : n + 1]
        for t in range(3):
            part = rest.astype(bf16).astype(f32)
            out = jnp.where(index == 3 * n + t, part, out)
            rest = rest - part
    return out.astype(bf16)


def gather_parts(rows):
    index = lax.broadcasted_iota(jnp.int32, (8, 1), 0)
    first = rows[2:3] + rows[1:2] + rows[0:1]
    second = rows[5:6] + rows[4:5] + rows[3:4]
    return jnp.where(index == 0, first, jnp.where(index == 1, second, 0.0))


def place_params(q, mk, musg, mask, basis):
    u = jnp.where(mask, gather_parts(mm(parts_of(musg), mk)) * 0.125, 0.0)
    ab = gather_parts(mm(parts_of(u), q, NT))
    spread = 1.0 / basis
    a = ab[0:1]
    b = ab[1:2]
    centre = 1.0 / (1.0 + jnp.exp(-a))
    soft = jnp.maximum(b, 0.0) + jnp.log1p(jnp.exp(-jnp.abs(b)))
    total = spread * spread + var_scale * soft
    return u, b, centre, total


def causal_block(n):
    key = lax.broadcasted_iota(jnp.int32, (n, n), 0)
    query = lax.broadcasted_iota(jnp.int32, (n, n), 1)
    return key <= query


class Place:
    def __init__(self):
        b, k = lax.axis_index(BATCH), lax.axis_index(BLK)
        z, x = b // 2, b % 2
        y, core = k // 2, k % 2
        self.z, self.x, self.y, self.core = z, x, y, core
        self.peer_x = (z * 2 + 1 - x, k)
        self.peer_y = (b, (1 - y) * 2 + core)
        self.peer_core = (b, y * 2 + 1 - core)
        self.peer_z = [(((z + d) % 4) * 2 + x, k) for d in (1, 2, 3)]

    def announce(self):
        peers = [self.peer_x, self.peer_y, self.peer_core] + self.peer_z
        barrier = pltpu.get_barrier_semaphore()
        for peer in peers:
            pl.semaphore_signal(barrier, inc=1, device_id=peer, device_id_type=pl.DeviceIdType.MESH)

    def wait(self):
        pl.semaphore_wait(pltpu.get_barrier_semaphore(), 6)


def remote(src, dst, sems, n, peer):
    return pltpu.make_async_remote_copy(
        src_ref=src,
        dst_ref=dst,
        send_sem=sems.at[0, n],
        recv_sem=sems.at[1, n],
        device_id=peer,
        device_id_type=pl.DeviceIdType.MESH,
    )


class Reducer:
    copies = 13

    def __init__(self, place, first, src, out, scratch, window=(0, 0), target=(0, 0)):
        self.place = place
        self.f, self.s = (place.x, place.y) if first == "x" else (place.y, place.x)
        x, y = place.peer_x, place.peer_y
        self.peer_f, self.peer_s = (x, y) if first == "x" else (y, x)
        self.src, self.out = src, out
        self.r1, self.send2, self.r2, self.acc, self.r3, self.done, self.sems, self.own = scratch
        self.rows, self.cols = self.r1.shape[0] * 2, self.r1.shape[1]
        self.step = self.rows // 16
        self.window, self.target = window, target

    @staticmethod
    def scratch(rows, cols, dtype):
        return [
            pltpu.VMEM((rows // 2, cols), dtype),
            pltpu.VMEM((rows // 4, cols), dtype),
            pltpu.VMEM((rows // 4, cols), dtype),
            pltpu.VMEM((rows // 4, cols), dtype),
            pltpu.VMEM((3, rows // 16, cols), dtype),
            pltpu.VMEM((rows // 16, cols), dtype),
            pltpu.SemaphoreType.DMA((2, Reducer.copies)),
            pltpu.SemaphoreType.DMA((1,)),
        ]

    def at(self, row, count):
        return pl.ds(pl.multiple_of(row, self.step), count)

    def taken(self, row, count):
        return self.at(self.window[0] + row, count), pl.ds(self.window[1], self.cols)

    def home(self, row, count):
        rows = self.at(self.target[0] + row, count)
        return self.out.at[self.place.core, rows, pl.ds(self.target[1], self.cols)]

    def copy(self, n):
        f, s, z = self.f, self.s, self.place.z
        half, quarter, step = self.rows // 2, self.rows // 4, self.step
        mine = f * half + s * quarter
        if n == 0:
            return remote(self.src.at[*self.taken((1 - f) * half, half)], self.r1, self.sems, n, self.peer_f)
        if n == 1:
            return remote(self.send2, self.r2, self.sems, n, self.peer_s)
        if n < 5:
            d = n - 2
            part = self.acc.at[self.at(((z + d + 1) % 4) * step, step)]
            return remote(part, self.r3.at[d], self.sems, n, self.place.peer_z[d])
        if n < 8:
            part = self.home(mine + z * step, step)
            return remote(self.done, part, self.sems, n, self.place.peer_z[n - 5])
        if n == 8:
            part, peer = self.home(mine, quarter), self.peer_s
        elif n == 9:
            part, peer = self.home(f * half, half), self.peer_f
        elif n == 10:
            part, peer = self.home(mine, quarter), self.place.peer_core
        elif n == 11:
            part, peer = self.home(f * half + (1 - s) * quarter, quarter), self.place.peer_core
        else:
            part, peer = self.home((1 - f) * half, half), self.place.peer_core
        return remote(part, part, self.sems, n, peer)

    def keep(self):
        mine = self.f * (self.rows // 2) + self.s * (self.rows // 4)
        part = self.home(mine + self.place.z * self.step, self.step)
        return pltpu.make_async_copy(self.done, part, self.own.at[0])

    def start(self, *numbers):
        for n in numbers:
            self.copy(n).start()

    def arrive(self, *numbers):
        for n in numbers:
            self.copy(n).wait_recv()

    def sum_into(self, dst, row, *more):
        def body(i, carry):
            at = i * self.step
            total = self.src[self.taken(row + at, self.step)].astype(f32)
            for ref, start in more:
                total = total + ref[self.at(start + at, self.step)].astype(f32)
            dst[self.at(at, self.step)] = total.astype(dst.dtype)
            return carry

        lax.fori_loop(0, 4, body, 0)

    def run(self, stage):
        f, s, z = self.f, self.s, self.place.z
        half, quarter, step = self.rows // 2, self.rows // 4, self.step
        if stage == 0:
            self.start(0)
        elif stage == 1:
            self.arrive(0)
            self.sum_into(self.send2, f * half + (1 - s) * quarter, (self.r1, (1 - s) * quarter))
            self.start(1)
        elif stage == 2:
            self.arrive(1)
            self.sum_into(self.acc, f * half + s * quarter, (self.r1, s * quarter), (self.r2, 0))
            self.start(2, 3, 4)
        elif stage == 3:
            self.arrive(2, 3, 4)
            total = self.acc[self.at(z * step, step)].astype(f32)
            for d in range(3):
                total = total + self.r3[d].astype(f32)
            self.done[...] = total.astype(self.done.dtype)
            self.start(5, 6, 7)
            self.keep().start()
        elif stage == 4:
            self.arrive(5, 6, 7)
            self.keep().wait()
            self.start(8, 10)
        elif stage == 5:
            self.arrive(8)
            self.start(9, 11)
        elif stage == 6:
            self.arrive(9)
            self.start(12)
        elif stage == 7:
            self.arrive(10, 11, 12)
            for n in range(self.copies):
                self.copy(n).wait_send()


def norm_back(x, gy, gain):
    center = jnp.mean(x, axis=-1, keepdims=True)
    shifted = x - center
    rstd = lax.rsqrt(jnp.mean(shifted * shifted, axis=-1, keepdims=True) + epsilon)
    hat = shifted * rstd
    g = gy * gain
    mean_g = jnp.mean(g, axis=-1, keepdims=True)
    mean_gh = jnp.mean(g * hat, axis=-1, keepdims=True)
    gx = rstd * (g - mean_g - hat * mean_gh)
    return gx, jnp.sum(gy * hat, axis=0, keepdims=True), jnp.sum(gy, axis=0, keepdims=True)


def gelu_both(v):
    root = 0.7978845608028654
    sq = v * v
    t = jnp.tanh(root * v * (1.0 + 0.044715 * sq))
    up = 0.5 + 0.5 * t
    slope = up + (0.5 * v) * (1.0 - t * t) * (root + (3.0 * 0.044715 * root) * sq)
    return v * up, slope


SPANS = (256, 512, 768)
STARTS = (0, 256, 768)
AFTER = 3
FIRST = "yyxyxxyxyxy"
PLAN = {
    0: [(1, 0), (0, 0)],
    1: [(3, 0), (2, 0)],
    2: [(1, 1), (5, 0), (0, 1), (4, 0)],
    3: [(2, 1)],
    4: [(6, 0)],
    5: [(11, 0), (1, 2)],
    7: [(0, 2), (2, 2)],
    10: [(5, 1), (1, 3)],
    11: [(6, 1), (0, 3)],
    13: [(2, 3), (1, 4), (4, 1)],
    15: [(3, 1), (5, 2)],
    17: [(2, 4), (6, 2), (7, 0)],
    20: [(1, 5), (0, 4), (4, 2)],
    22: [(2, 5)],
    23: [(8, 0)],
    25: [(5, 3)],
    26: [(7, 1)],
    29: [(8, 1), (6, 3), (0, 5), (9, 0)],
    30: [(5, 4), (4, 3), (8, 2), (6, 4)],
    31: [(9, 1), (10, 0), (5, 5), (4, 4), (7, 2), (8, 3), (3, 2), (10, 1), (7, 3), (6, 5), (8, 4), (4, 5), (3, 3), (9, 2), (10, 2), (3, 4), (7, 4), (9, 3), (8, 5), (7, 5), (5, 6), (1, 6), (9, 4), (5, 7), (0, 6), (0, 7), (2, 6), (4, 6), (10, 3), (6, 6), (3, 5), (10, 4), (1, 7), (8, 6), (9, 5), (10, 5), (7, 6), (7, 7), (2, 7), (3, 6), (6, 7), (9, 6), (10, 6), (4, 7), (10, 7), (3, 7), (8, 7), (9, 7)],
}


def tail_kernel(names, *refs):
    r = SimpleNamespace(**dict(zip(names, refs)))
    jobs_scratch = refs[len(names) :]
    place = Place()
    y, core = place.y, place.core
    tokens, width = r.cot_v.shape
    wide = width // 2
    ff = r.e_v.shape[1]
    pairs = wide // 128
    basis = r.mkv_v.shape[0]
    spread = 1.0 / basis
    block = tokens // 4
    chunk = 64
    n_sem = 8
    take = lambda i: jobs_scratch[n_sem * i : n_sem * i + n_sem]
    ex, loc = r.ex, r.loc
    small_rows = pairs * 2 * basis // 128
    up_rows = ff // 128
    width_rows = width // 128
    base_up = 2 * small_rows
    base_down = base_up + up_rows
    base_ln2 = base_down + width_rows
    base_ln1 = base_ln2 + 2 * width_rows
    third = lambda n: (0, n * wide)
    jobs = []
    for n, lo in enumerate(STARTS):
        jobs += [(r.g_down, r.o_down, (lo, 0), (lo, 0)), (r.g_up, r.o_up, (0, lo), (0, lo))]
    jobs += [(r.gup, r.o_out, third(3)), (r.gup, r.o_0, third(0)), (r.gup, r.o_1, third(1)), (r.gup, r.o_2, third(2))]
    jobs += [(r.sv, r.o_s)]
    jobs = [
        Reducer(place, FIRST[n], src, out, take(n), *windows)
        for n, (src, out, *windows) in enumerate(jobs)
    ]

    def act(step):
        for job, stage in PLAN.get(step, ()):
            if job < len(jobs):
                jobs[job].run(stage)
            else:
                out_copy().start()

    def rows_at(j, c):
        return pl.ds(pl.multiple_of((2 * j + c) * block, block), block)

    def half_at(j):
        return pl.ds(j * block, block)

    def half_dyn(j):
        return pl.ds(pl.multiple_of(j * block, block), block)

    def small_at(j, i):
        return pl.ds(pl.multiple_of((2 * j + core) * block + i * chunk, chunk), chunk)

    def lanes_from(ref, n, c):
        return ref.at[:, pl.ds(pl.multiple_of(c * n, 128), n)]

    def rows_from(ref, n, c):
        return ref.at[pl.ds(pl.multiple_of(c * n, 128), n), :]

    loads = [
        (r.n2_in, r.n2),
        (lanes_from(r.expand, ff, core), r.e_v),
        (rows_from(r.down, ff, core), r.d_v),
        (r.cot, r.cot_v),
        (r.mixed_in, r.mixed),
        (rows_from(r.w_out, wide, core), r.wo_own),
        (r.ctx, r.ctx_v),
        (r.qkv, r.qkv_v),
        (r.mkv, r.mkv_v),
        (r.att, r.att_v),
        (r.normed, r.norm_v),
        (r.coeff, r.coeff_v),
        (r.w_qkv, r.wqkv_v),
        (r.hidden.at[rows_at(0, core)], r.hid_own.at[half_at(0)]),
        (r.hidden.at[rows_at(1, core)], r.hid_own.at[half_at(1)]),
    ]

    def load(n):
        return pltpu.make_async_copy(*loads[n], loc.at[n])

    def ready(*numbers):
        for n in numbers:
            load(n).wait()

    def swap(n, j):
        if n == 2 or n == 5:
            src, dst = r.tx.at[half_at(j)], r.rx.at[half_at(j)]
        elif n == 3:
            src = dst = r.gml.at[rows_at(j, core)]
        else:
            src, dst = r.tx.at[half_at(j)], r.rx_out.at[half_at(j)]
        return remote(src, dst, ex, 2 * n + j, place.peer_core)

    def out_copy():
        return remote(r.bo.at[half_dyn(1 - y)], r.out.at[y], ex, 12, place.peer_y)

    def out_keep():
        return pltpu.make_async_copy(r.bo.at[half_dyn(y)], r.out.at[y], loc.at[15])

    def gin_copy():
        return remote(r.n2.at[half_dyn(1 - y)], r.gi_rx, ex, 13, place.peer_y)

    def gin_keep():
        return pltpu.make_async_copy(r.gm.at[half_dyn(y)], r.gin.at[y], loc.at[16])

    def gin_place():
        return pltpu.make_async_copy(r.rx.at[half_at(0)], r.gin.at[1 - y], loc.at[17])

    for n in range(len(loads)):
        load(n).start()
    place.announce()
    r.sv[...] = jnp.zeros_like(r.sv)
    r.gain1[...] = as_row(r.ln1_gain)
    r.gain2[...] = as_row(r.ln2_gain)
    r.bias_d[...] = as_row(r.down_bias)
    both_up = as_row(r.up_bias)
    r.bias_u[...] = jnp.where(core == 0, both_up[:, :ff], both_up[:, ff:])
    fill_heads(r.musg, r.mu, r.sigma, core)

    def put(row, vec):
        for t in range(vec.shape[1] // 128):
            r.sv[pl.ds(row + t, 1), :] = vec[:, t * 128 : t * 128 + 128]

    ready(0, 1, 2, 3)
    tall = tokens // 2
    for part, (lo, span) in enumerate(zip(STARTS, SPANS)):

        def tile(i, carry, lo=lo):
            rows = pl.ds(pl.multiple_of((i % 2) * tall, tall), tall)
            col = pl.multiple_of(lo + (i // 2) * 256, 256)
            cols = pl.ds(col, 256)
            hidden_up = mm(r.n2[rows, :], r.e_v[:, cols]) + r.bias_u[:, cols]
            value, slope = gelu_both(hidden_up)
            r.active[rows, cols] = value.astype(bf16)
            grad = (mm(r.cot_v[rows, :], r.d_v[cols, :], NT) * slope).astype(bf16)
            r.gup[rows, cols] = grad
            sums = jnp.sum(grad.astype(f32), axis=0, keepdims=True)
            at = base_up + col // 128
            for t in range(2):
                r.sv[pl.ds(at + t, 1), :] += sums[:, t * 128 : t * 128 + 128]
            return carry

        lax.fori_loop(0, 2 * (span // 256), tile, 0)
        for m in range(span // 256):
            here = slice(lo + m * 256, lo + m * 256 + 256)
            r.g_down[here, :] = mm(r.active[:, here], r.cot_v[...], TN).astype(bf16)
        for m in range(width // 256):
            cols = slice(m * 256, m * 256 + 256)
            r.g_up[cols, lo : lo + span] = mm(r.n2[:, cols], r.gup[:, lo : lo + span], TN).astype(bf16)
        if part == 0:
            place.wait()
        act(part)

    ready(4, 5, 6)
    for j in range(2):
        r.tx[half_at(j), :] = mm(r.gup[rows_at(j, 1 - core), :], r.e_v[...], NT)
        swap(2, j).start()

    def norm_two(j, carry):
        def body(i, carry):
            at = pl.ds(pl.multiple_of(j * block + i * chunk, chunk), chunk)
            gy = r.gm[at, :] + r.rx[at, :]
            gx, dg, db = norm_back(r.mixed[at, :], gy, r.gain2[...])
            cot = r.cot_v[small_at(j, i), :].astype(f32)
            gm = cot + gx
            r.gm[at, :] = gm
            r.gml[small_at(j, i), :] = gm.astype(bf16)
            return carry[0] + dg, carry[1] + db

        return lax.fori_loop(0, block // chunk, body, carry)

    sums = (jnp.zeros((1, width), f32), jnp.zeros((1, width), f32))
    for j in range(2):
        r.gm[half_at(j), :] = mm(r.gup[rows_at(j, core), :], r.e_v[...], NT)
        swap(2, j).wait_recv()
        sums = norm_two(j, sums)
        swap(3, j).start()
    put(base_ln2, sums[0])
    put(base_ln2 + width_rows, sums[1])
    put(base_down, jnp.sum(r.cot_v[...].astype(f32), axis=0, keepdims=True))
    act(AFTER + 0)
    for c in (0, 1):
        for j in range(2):
            if c:
                swap(3, j).wait_recv()
            there = rows_at(j, core if c == 0 else 1 - core)
            r.do[there, :] = mm(r.gml[there, :], r.wo_own[...], NT).astype(bf16)
    for m in range(width // 256):
        cols = slice(m * 256, m * 256 + 256)
        r.gup[cols, pairs * wide : pairs * wide + wide] = mm(r.gml[:, cols], r.ctx_v[...], TN).astype(bf16)
    act(AFTER + 1)

    for j in range(2):
        swap(2, j).wait_send()
        r.tx[half_at(j), :] = mm(r.active[rows_at(j, 1 - core), :], r.d_v[...])
        swap(4, j).start()
    for j in range(2):
        own = mm(r.active[rows_at(j, core), :], r.d_v[...])
        swap(4, j).wait_recv()
        total = r.mixed[half_at(j), :] + (own + r.rx_out[half_at(j), :]) + r.bias_d[...]
        r.bo[half_at(j), :] = total.astype(bf16)
    out_keep().start()
    act(AFTER + 2)

    centers = (lax.broadcasted_iota(jnp.int32, (basis, 1), 0).astype(f32) + 0.5) / basis
    allowed = causal_block(QB)
    pick_row = lax.broadcasted_iota(jnp.int32, (8, 1), 0)
    blocks = tokens // QB
    per_pair = 2 * blocks
    ready(7, 8, 9, 10, 11)
    for n in range(4):
        at = slice(n * block, n * block + block)
        r.normed_v[:, at] = turn(r.norm_v[at, :]).astype(bf16)

    def pair_step(i, carry):
        lanes = pl.ds(pl.multiple_of(i * 128, 128), 128)

        def lanes_of(j):
            return pl.ds(pl.multiple_of(i * 128 + j * wide, 128), 128)

        q_ref, k_ref, v_ref = (r.qkv_v.at[:, lanes_of(j)] for j in range(3))
        mk_ref, mv_ref = (r.mkv_v.at[:, lanes_of(j)] for j in range(2))
        do_ref = r.do.at[:, lanes]
        dka, dva, dqt, gmva, k_t, do_t = r.dka, r.dva, r.dqt, r.gmva, r.k_t, r.do_t
        k_t[...] = turn(k_ref[...]).astype(bf16)
        do_t[...] = turn(do_ref[...])
        dka[...] = jnp.zeros_like(dka)
        dva[...] = jnp.zeros_like(dva)
        gmva[...] = jnp.zeros_like(gmva)
        r.gmk[...] = jnp.zeros_like(r.gmk)

        def finish_pair():
            r.active[:, lanes] = jnp.transpose(dqt[...]).astype(bf16)
            r.active[:, lanes_of(1)] = dka[...].astype(bf16)
            r.active[:, lanes_of(2)] = dva[...].astype(bf16)
            r.part[:, 0:128] = r.active[:, lanes]
            r.part[:, 128:256] = r.active[:, lanes_of(1)]
            r.part[:, 256:384] = r.active[:, lanes_of(2)]
            r.part_mem[:, 0:128] = r.gmk[...].astype(bf16)
            r.part_mem[:, 128:256] = gmva[...].astype(bf16)
            spot = pl.multiple_of(i * wide, 128)
            for m in range(width // 256):
                here = slice(m * 256, m * 256 + 256)
                g = mm(r.normed_v[here, :], r.part[...])
                cg = mm(r.coeff_v[:, here], r.part_mem[...], TN)
                r.gup[here, pl.ds(spot, 128)] = g[:, :128].astype(bf16)
                r.gup[here, pl.ds(spot + 128, 256)] = (g[:, 128:] + cg).astype(bf16)

        def head_step(h, carry):
            mask = head_mask(h)
            rows = head_rows(h)
            musg = r.musg[2 * i + h]
            u, b, centre, total = place_params(q_ref[...], mk_ref[...], musg, mask, basis)
            scale = spread * lax.rsqrt(total)
            inv = 1.0 / total
            dot_rows = jnp.sum(do_t[rows, :] * r.att_v[i, rows, :], axis=0, keepdims=True)
            z = jnp.zeros((8, 128), f32)
            for qb in range(blocks):
                cols = slice(qb * QB, qb * QB + QB)
                q = jnp.where(mask, q_ref[cols, :].astype(f32) * 0.125, 0.0).astype(bf16)
                do = jnp.where(mask, do_ref[cols, :].astype(f32), 0.0).astype(bf16)
                lse = r.lse[i, pl.ds(h, 1), cols]
                dot_row = dot_rows[:, cols]
                dq_t = jnp.zeros((64, QB), f32)
                for kb in range(qb + 1):
                    keys = slice(kb * QB, kb * QB + QB)
                    p = jnp.exp(mm(k_ref[keys, :], q, NT) - lse)
                    if kb == qb:
                        p = jnp.where(allowed, p, 0.0)
                    dva[keys, :] += mm(p.astype(bf16), do)
                    ds = (p * (mm(v_ref[keys, :], do, NT) - dot_row)).astype(bf16)
                    dka[keys, :] += mm(ds, q)
                    dq_t = dq_t + mm(k_t[rows, keys], ds)
                dqt[rows, cols] = dq_t * 0.125
                gap = centre[:, cols] - centers
                gap2 = gap * gap
                inv_b = inv[:, cols]
                dens = scale[:, cols] * jnp.exp(gap2 * (-0.5 * inv_b))
                gmva[...] += mm(dens.astype(bf16), do)
                e = mm(mv_ref[...], do, NT) * dens
                sum0 = jnp.sum(e, axis=0, keepdims=True)
                sum1 = jnp.sum(e * gap, axis=0, keepdims=True)
                sum2 = jnp.sum(e * gap2, axis=0, keepdims=True)
                c = centre[:, cols]
                da = -sum1 * inv_b * c * (1.0 - c)
                dtotal = 0.5 * inv_b * (sum2 * inv_b - sum0)
                db = dtotal * var_scale / (1.0 + jnp.exp(-b[:, cols]))
                dab = jnp.where(pick_row == 0, da, jnp.where(pick_row == 1, db, 0.0))
                dqt[:, cols] += mm(u, dab, TN, precision=highest)
                z = z + gather_parts(mm(parts_of(dab), q))
                if qb == blocks - 1:
                    r.gmk[...] += mm(musg, z, TN, precision=highest)
                    grads = gather_parts(mm(parts_of(z), mk_ref[...], NT))
                    at = (2 * i + h) * (basis // 128)
                    put(at, grads[0:1])
                    put(small_rows + at, grads[1:2])
                    pl.when(h == 1)(finish_pair)
                for step in range(2 * pairs):
                    at_step = AFTER + 3 + step * blocks + qb
                    if at_step in PLAN:

                        @pl.when(2 * i + h == step)
                        def _(at_step=at_step):
                            act(at_step)

            return carry

        lax.fori_loop(0, 2, head_step, 0)
        return carry

    lax.fori_loop(0, pairs, pair_step, 0)

    ready(12, 13, 14)
    for j in range(2):
        swap(4, j).wait_send()
        r.tx[half_at(j), :] = mm(r.active[rows_at(j, 1 - core), : 3 * wide], r.wqkv_v[...], NT)
        swap(5, j).start()
    for j in range(2):
        r.mixed[half_at(j), :] = mm(r.active[rows_at(j, core), : 3 * wide], r.wqkv_v[...], NT)

    act(AFTER + 27)
    def norm_one(i, carry):
        at = pl.ds(pl.multiple_of(i * chunk, chunk), chunk)
        gy = r.mixed[at, :] + r.rx[at, :]
        gx, dg, db = norm_back(r.hid_own[at, :].astype(f32), gy, r.gain1[...])
        total = r.gm[at, :] + gx
        r.gm[at, :] = total
        r.n2[at, :] = total.astype(bf16)
        return carry[0] + dg, carry[1] + db

    for j in range(2):
        swap(5, j).wait_recv()
    sums = lax.fori_loop(
        0, 2 * block // chunk, norm_one, (jnp.zeros((1, width), f32), jnp.zeros((1, width), f32))
    )
    put(base_ln1, sums[0])
    put(base_ln1 + width_rows, sums[1])
    gin_keep().start()
    gin_copy().start()
    act(AFTER + 28)
    gin_copy().wait()
    r.rx[half_at(0), :] = r.gi_rx[...].astype(f32)
    gin_place().start()
    out_copy().wait()
    out_keep().wait()
    gin_keep().wait()
    gin_place().wait()
    for j in range(2):
        for n in (3, 5):
            swap(n, j).wait_send()


def tail_call(held, given):
    g = SimpleNamespace(**held, **given)
    tokens, width = g.cot.shape
    wide = width // 2
    ff = g.expand.shape[1] // 2
    heads = wide // 64
    basis = g.mkv.shape[0]
    half, block = tokens // 2, tokens // 4
    used = 2 * (wide // 64) * basis // 128 + ff // 128 + 5 * (width // 128)
    sv_rows = -(-used // 128) * 128
    shape = jax.ShapeDtypeStruct
    like = lambda a: pltpu.VMEM(a.shape, a.dtype)
    outs = dict(
        o_down=shape((2, ff, width), bf16),
        o_up=shape((2, width, ff), bf16),
        o_out=shape((2, width, wide), bf16),
        o_0=shape((2, width, wide), bf16),
        o_1=shape((2, width, wide), bf16),
        o_2=shape((2, width, wide), bf16),
        o_s=shape((2, sv_rows, 128), f32),
        out=shape((2, block, width), bf16),
        gin=shape((2, block, width), f32),
    )
    scratch = dict(
        ex=pltpu.SemaphoreType.DMA((2, 14)),
        loc=pltpu.SemaphoreType.DMA((18,)),
        ctx_v=like(g.ctx),
        wo_own=pltpu.VMEM((wide, width), bf16),
        hid_own=pltpu.VMEM((half, width), bf16),
        e_v=pltpu.VMEM((width, ff), bf16),
        d_v=pltpu.VMEM((ff, width), bf16),
        cot_v=like(g.cot),
        qkv_v=like(g.qkv),
        mkv_v=like(g.mkv),
        att_v=like(g.att),
        norm_v=like(g.normed),
        normed_v=pltpu.VMEM((width, tokens), bf16),
        coeff_v=like(g.coeff),
        wqkv_v=like(g.w_qkv),
        mixed=pltpu.VMEM((half, width), f32),
        n2=pltpu.VMEM((tokens, width), bf16),
        active=pltpu.VMEM((tokens, ff), bf16),
        gup=pltpu.VMEM((tokens, ff), bf16),
        g_down=pltpu.VMEM((ff, width), bf16),
        g_up=pltpu.VMEM((width, ff), bf16),
        tx=pltpu.VMEM((half, width), f32),
        rx=pltpu.VMEM((half, width), f32),
        rx_out=pltpu.VMEM((half, width), f32),
        gm=pltpu.VMEM((half, width), f32),
        gml=pltpu.VMEM((tokens, width), bf16),
        bo=pltpu.VMEM((half, width), bf16),
        gi_rx=pltpu.VMEM((block, width), bf16),
        do=pltpu.VMEM((tokens, wide), bf16),
        part=pltpu.VMEM((tokens, 384), bf16),
        part_mem=pltpu.VMEM((basis, 256), bf16),
        dka=pltpu.VMEM((tokens, 128), f32),
        dva=pltpu.VMEM((tokens, 128), f32),
        dqt=pltpu.VMEM((128, tokens), f32),
        gmva=pltpu.VMEM((basis, 128), f32),
        gmk=pltpu.VMEM((basis, 128), f32),
        k_t=pltpu.VMEM((128, tokens), bf16),
        do_t=pltpu.VMEM((128, tokens), f32),
        sv=pltpu.VMEM((sv_rows, 128), f32),
        gain1=pltpu.VMEM((1, width), f32),
        gain2=pltpu.VMEM((1, width), f32),
        bias_d=pltpu.VMEM((1, width), f32),
        bias_u=pltpu.VMEM((1, ff), f32),
        musg=pltpu.VMEM((heads, 8, basis), f32),
    )
    more = []
    shapes = []
    for span in SPANS:
        shapes += [(span, width, bf16), (width, span, bf16)]
    shapes += [(width, wide, bf16)] * 4 + [(sv_rows, 128, f32)]
    for item in shapes:
        more += Reducer.scratch(*item)
    hbm, vmem = pl.BlockSpec(memory_space=pl.ANY), pl.BlockSpec(memory_space=pltpu.VMEM)
    names = list(held) + list(given) + list(outs) + list(scratch)
    return pl.pallas_call(
        functools.partial(tail_kernel, names),
        in_specs=[hbm] * len(held) + [vmem] * len(given),
        out_specs=[hbm] * len(outs),
        out_shape=list(outs.values()),
        scratch_shapes=list(scratch.values()) + more,
        compiler_params=pltpu.CompilerParams(
            vmem_limit_bytes=60 * 1024 * 1024, collective_id=1, has_side_effects=True
        ),
        name="tail",
    )(*held.values(), *given.values())


def as_row(ref):
    return ref[...].reshape(1, ref.shape[0])


def fill_heads(dst, mu, sigma, core):
    heads = dst.shape[0]
    dst[...] = jnp.zeros_like(dst)
    for h in range(heads):
        for n, src in enumerate((mu, sigma)):
            dst[h, n : n + 1, :] = src[pl.ds(core * heads + h, 1), :]


def sweep_inverse(a):
    n = a.shape[0]
    lane = lax.broadcasted_iota(jnp.int32, (8, n), 1)
    sub = lax.broadcasted_iota(jnp.int32, (8, n), 0)
    groups = [a[8 * g : 8 * g + 8, :] for g in range(n // 8)]

    def inverse_two(p, q, t):
        inv = 1.0 / (p * t - q * q)
        return t * inv, -q * inv, p * inv

    for k in range(0, n, 4):
        own, at = groups[k // 8], k % 8
        rows = [jnp.broadcast_to(own[at + i : at + i + 1, :], (8, n)) for i in range(4)]
        d = {
            (i, j): jnp.broadcast_to(rows[i][:, k + j : k + j + 1], (8, n))
            for i in range(4)
            for j in range(i, 4)
        }
        a0, a1, a2 = inverse_two(d[0, 0], d[0, 1], d[1, 1])
        w = [
            [a0 * d[0, 2] + a1 * d[1, 2], a0 * d[0, 3] + a1 * d[1, 3]],
            [a1 * d[0, 2] + a2 * d[1, 2], a1 * d[0, 3] + a2 * d[1, 3]],
        ]
        s0 = d[2, 2] - (d[0, 2] * w[0][0] + d[1, 2] * w[1][0])
        s1 = d[2, 3] - (d[0, 2] * w[0][1] + d[1, 2] * w[1][1])
        s2 = d[3, 3] - (d[0, 3] * w[0][1] + d[1, 3] * w[1][1])
        s0, s1, s2 = inverse_two(s0, s1, s2)
        v = [[w[i][0] * s0 + w[i][1] * s1, w[i][0] * s1 + w[i][1] * s2] for i in range(2)]
        p00 = a0 + v[0][0] * w[0][0] + v[0][1] * w[0][1]
        p01 = a1 + v[0][0] * w[1][0] + v[0][1] * w[1][1]
        p11 = a2 + v[1][0] * w[1][0] + v[1][1] * w[1][1]
        p = [
            [p00, p01, -v[0][0], -v[0][1]],
            [p01, p11, -v[1][0], -v[1][1]],
            [-v[0][0], -v[1][0], s0, s1],
            [-v[0][1], -v[1][1], s1, s2],
        ]
        new = []
        for i in range(4):
            row = p[i][0] * rows[0] + p[i][1] * rows[1] + p[i][2] * rows[2] + p[i][3] * rows[3]
            for j in range(4):
                row = jnp.where(lane == k + j, p[i][j], row)
            new.append(row)
        inside = (lane >= k) & (lane < k + 4)
        for g in range(n // 8):
            old = groups[g]
            cols = [jnp.broadcast_to(old[:, k + j : k + j + 1], (8, n)) for j in range(4)]
            part = (cols[0] * new[0] + cols[1] * new[1]) + (cols[2] * new[2] + cols[3] * new[3])
            fresh = jnp.where(inside, 0.0, old) - part
            if g == k // 8:
                for i in range(4):
                    fresh = jnp.where(sub == at + i, new[i], fresh)
            groups[g] = fresh
    return jnp.concatenate(groups, 0)


def front_kernel(names, *refs):
    r = SimpleNamespace(**dict(zip(names, refs)))
    place = Place()
    y, core = place.y, place.core
    tokens, width = r.hid_v.shape
    block = tokens // 4
    wide = width // 2
    pairs = wide // 128
    basis = r.mkv_v.shape[0]
    half = basis // 2
    ex, loc = r.ex, r.loc
    flows = [(r.inputs, r.hid_v), (r.previous, r.prev), (r.cotangent, r.cot)]

    def rows_at(yy, cc):
        return pl.ds(pl.multiple_of((2 * yy + cc) * block, block), block)

    def along(n):
        src, dst = flows[n]
        return remote(src.at[1 - y], dst.at[rows_at(y, core)], ex, n, place.peer_y)

    def across(n):
        src, dst = flows[n]
        return remote(src.at[y], dst.at[rows_at(y, core)], ex, 3 + n, place.peer_core)

    def onward(n):
        part = flows[n][1].at[rows_at(1 - y, core)]
        return remote(part, part, ex, 6 + n, place.peer_core)

    def keep(n):
        src, dst = flows[n]
        return pltpu.make_async_copy(src.at[y], dst.at[rows_at(y, core)], loc.at[n])

    def weight(n):
        src = (r.wq, r.wk, r.wv)[n].at[:, pl.ds(pl.multiple_of(core * wide, 128), wide)]
        return pltpu.make_async_copy(src, r.w_v.at[:, n * wide : n * wide + wide], loc.at[3 + n])

    def projection(n):
        c = core if n == 0 else 1 - core
        src = r.wo.at[pl.ds(pl.multiple_of(c * wide, 128), wide)]
        return pltpu.make_async_copy(src, r.wo_v.at[n], loc.at[17 + n])

    results = [
        (r.w_v, r.w_qkv),
        (r.hid_v, r.hidden),
        (r.normed, r.normed_out),
        (r.qkv_v, r.qkv),
        (r.mkv_v, r.mkv),
        (r.coeff_v, r.coeff),
        (r.att_v, r.att),
        (r.ctx_v, r.ctx),
        (r.mix_v, r.mixed),
    ]

    def result(n):
        return pltpu.make_async_copy(*results[n], loc.at[6 + n])

    barrier = pltpu.get_barrier_semaphore()
    for peer in (place.peer_y, place.peer_core):
        pl.semaphore_signal(barrier, inc=1, device_id=peer, device_id_type=pl.DeviceIdType.MESH)
    r.gain1[...] = as_row(r.ln1_gain)
    r.bias1[...] = as_row(r.ln1_bias)
    r.gain2[...] = as_row(r.ln2_gain)
    r.bias2[...] = as_row(r.ln2_bias)
    fill_heads(r.musg, r.mu, r.sigma, core)

    spread = 1.0 / basis
    centers = (lax.broadcasted_iota(jnp.int32, (basis, 1), 0).astype(f32) + 0.5) / basis
    places = (r.sticky[pl.ds(y, 1), :].astype(f32) + 0.5) / tokens
    features = jnp.exp(-((places - centers) ** 2) / (2.0 * spread * spread)).astype(bf16)
    same = lax.broadcasted_iota(jnp.int32, (basis, basis), 0) == lax.broadcasted_iota(
        jnp.int32, (basis, basis), 1
    )
    a_ref, i_ref = r.a, r.i
    a_ref[...] = mm(features, features, NT) + jnp.where(same, ridge_weight, 0.0)
    pl.semaphore_wait(barrier, 2)
    along(0).start()
    across(0).start()
    keep(0).start()
    for n in range(3):
        weight(n).start()
    for n in range(2):
        projection(n).start()
    across(1).start()
    keep(1).start()
    across(2).start()
    keep(2).start()

    r.schur[...] = a_ref[:half, :half]

    def eliminate(n, carry):
        i_ref[n] = sweep_inverse(r.schur[...])

        @pl.when(n == 0)
        def _():
            cross = a_ref[:half, half:]
            r.cross[...] = mm(i_ref[0], cross, precision=highest)
            r.schur[...] = a_ref[half:, half:] - mm(cross, r.cross[...], TN, precision=highest)

        return carry

    lax.fori_loop(0, 2, eliminate, 0)

    chunk = 64

    def project(yy, cc):
        def body(i, carry):
            at = pl.ds(pl.multiple_of((2 * yy + cc) * block + i * chunk, chunk), chunk)
            normed = layer_norm(r.hid_v[at, :].astype(f32), r.gain1[...], r.bias1[...])
            r.normed[at, :] = normed.astype(bf16)
            return carry

        lax.fori_loop(0, block // chunk, body, 0)
        at = rows_at(yy, cc)
        r.qkv_v[at, :] = mm(r.normed[at, :], r.w_v[...]).astype(bf16)

    keep(0).wait()
    for n in range(3):
        weight(n).wait()
    result(0).start()
    project(y, core)
    across(0).wait_recv()
    project(y, 1 - core)
    along(0).wait_send()
    along(1).start()
    along(0).wait_recv()
    onward(0).start()
    project(1 - y, core)
    onward(0).wait_recv()
    project(1 - y, 1 - core)
    result(1).start()
    result(2).start()
    result(3).start()

    allowed = causal_block(QB)
    blocks = tokens // QB

    def lanes_of(i, j):
        return pl.ds(pl.multiple_of(i * 128 + j * wide, 128), 128)

    def causal_pair(i, carry):
        q_ref, k_ref, v_ref = (r.qkv_v.at[:, lanes_of(i, j)] for j in range(3))
        r.v_t[...] = turn(v_ref[...]).astype(bf16)
        def causal_head(h, carry):
            mask = head_mask(h)
            rows = head_rows(h)
            for qb in range(blocks):
                cols = slice(qb * QB, qb * QB + QB)
                q = jnp.where(mask, q_ref[cols, :].astype(f32) * 0.125, 0.0).astype(bf16)
                top = None
                for kb in range(qb + 1):
                    keys = slice(kb * QB, kb * QB + QB)
                    s = mm(k_ref[keys, :], q, NT)
                    if kb == qb:
                        s = jnp.where(allowed, s, masked_score)
                    r.s[keys, :] = s
                    best = jnp.max(s, axis=0, keepdims=True)
                    top = best if top is None else jnp.maximum(top, best)
                denom = jnp.zeros_like(top)
                out = jnp.zeros((64, QB), f32)
                for kb in range(qb + 1):
                    keys = slice(kb * QB, kb * QB + QB)
                    e = jnp.exp(r.s[keys, :] - top)
                    denom = denom + jnp.sum(e, axis=0, keepdims=True)
                    out = out + mm(r.v_t[rows, keys], e.astype(bf16))
                r.att_v[i, rows, cols] = out / denom
                r.lse[i, pl.ds(h, 1), cols] = top + jnp.log(denom)
            return carry

        lax.fori_loop(0, 2, causal_head, 0)
        return carry

    lax.fori_loop(0, pairs - 1, causal_pair, 0)
    along(1).wait_send()
    along(2).start()
    along(1).wait_recv()
    onward(1).start()
    lax.fori_loop(pairs - 1, pairs, causal_pair, 0)
    result(6).start()
    index = lax.broadcasted_iota(jnp.int32, (tokens, r.picks.shape[1]), 0)
    chosen = jnp.where(index == r.picks[pl.ds(y, 1), :], 1.0, 0.0).astype(bf16)
    shares = mm(features, chosen, NT)
    high = shares.astype(bf16)
    rest = shares - high.astype(f32)
    middle = rest.astype(bf16)
    r.shares[0] = high
    r.shares[1] = middle
    r.shares[2] = (rest - middle.astype(f32)).astype(bf16)

    across(1).wait_recv()
    keep(1).wait()
    onward(1).wait_recv()
    prev = r.prev[...]
    side = mm(r.shares[0], prev) + (mm(r.shares[1], prev) + mm(r.shares[2], prev))
    low_part = mm(
        i_ref[1], side[half:] - mm(r.cross[...], side[:half], TN, precision=highest), precision=highest
    )
    r.coeff_v[half:, :] = low_part.astype(bf16)
    r.coeff_v[:half, :] = (
        mm(i_ref[0], side[:half], precision=highest) - mm(r.cross[...], low_part, precision=highest)
    ).astype(bf16)
    r.mkv_v[...] = mm(r.coeff_v[...], r.w_v[:, wide:]).astype(bf16)
    result(4).start()
    result(5).start()

    def memory_pair(i, carry):
        q_ref = r.qkv_v.at[:, lanes_of(i, 0)]
        mk_ref, mv_ref = (r.mkv_v.at[:, lanes_of(i, j)] for j in range(2))
        r.mv_t[...] = turn(mv_ref[...]).astype(bf16)
        def memory_head(h, carry):
            rows = head_rows(h)
            u, b, centre, total = place_params(q_ref[...], mk_ref[...], r.musg[2 * i + h], head_mask(h), basis)
            scale = spread * lax.rsqrt(total)
            fall = -0.5 / total
            for qb in range(blocks):
                cols = slice(qb * QB, qb * QB + QB)
                gap = centre[:, cols] - centers
                dens = (scale[:, cols] * jnp.exp(gap * gap * fall[:, cols])).astype(bf16)
                r.o[rows, cols] = r.att_v[i, rows, cols] + mm(r.mv_t[rows, :], dens)
            return carry

        lax.fori_loop(0, 2, memory_head, 0)
        r.ctx_v[:, lanes_of(i, 0)] = jnp.transpose(r.o[...]).astype(bf16)
        for j in range(2):
            context(i, j).start()
        return carry

    def half_at(j):
        return pl.ds(j * block, block)

    def context(i, j):
        src = r.ctx_v.at[rows_at(j, 1 - core), lanes_of(i, 0)]
        return remote(src, r.ctx_rx.at[half_at(j), lanes_of(i, 0)], ex, 9 + 2 * i + j, place.peer_core)

    def second(j):
        part = r.n2_v.at[half_at(j)]
        return remote(part, r.n2.at[rows_at(j, core)], ex, 9 + 2 * pairs + j, place.peer_core)

    def second_keep(j):
        return pltpu.make_async_copy(r.n2_v.at[half_at(j)], r.n2.at[rows_at(j, core)], loc.at[15 + j])

    lax.fori_loop(0, pairs - 1, memory_pair, 0)
    along(2).wait_recv()
    onward(2).start()
    lax.fori_loop(pairs - 1, pairs, memory_pair, 0)
    result(7).start()
    for n in range(2):
        projection(n).wait()

    for j in range(2):
        own = mm(r.ctx_v[rows_at(j, core), :], r.wo_v[0])
        r.mix_v[half_at(j), :] = r.hid_v[rows_at(j, core), :].astype(f32) + own
    for j in range(2):
        for i in range(pairs):
            context(i, j).wait_recv()
        r.mix_v[half_at(j), :] += mm(r.ctx_rx[half_at(j), :], r.wo_v[1])

        def norm_chunk(i, carry, j=j):
            at = pl.ds(pl.multiple_of(j * block + i * chunk, chunk), chunk)
            r.n2_v[at, :] = layer_norm(r.mix_v[at, :], r.gain2[...], r.bias2[...]).astype(bf16)
            return carry

        lax.fori_loop(0, block // chunk, norm_chunk, 0)
        second(j).start()
        second_keep(j).start()
    result(8).start()
    keep(2).wait()
    across(2).wait_recv()
    onward(2).wait_recv()
    for j in range(2):
        second(j).wait()
        second_keep(j).wait()
        for i in range(pairs):
            context(i, j).wait_send()
    along(2).wait_send()
    for n in range(3):
        across(n).wait_send()
        onward(n).wait_send()
    for n in range(len(results)):
        result(n).wait()


def front_call(held, given, basis):
    block, width = held[next(iter(held))].shape[1:]
    tokens = block * 4
    wide = width // 2
    pairs = wide // 128
    shape = jax.ShapeDtypeStruct
    outs = dict(
        hidden=shape((tokens, width), bf16),
        normed_out=shape((tokens, width), bf16),
        qkv=shape((tokens, 3 * wide), bf16),
        mkv=shape((basis, width), bf16),
        coeff=shape((basis, width), bf16),
        w_qkv=shape((width, 3 * wide), bf16),
        cot=shape((tokens, width), bf16),
        ctx=shape((tokens, wide), bf16),
        att=shape((pairs, 128, tokens), f32),
        mixed=shape((tokens // 2, width), f32),
        n2=shape((tokens, width), bf16),
    )
    near = dict(lse=shape((pairs, 2, tokens), f32))
    like = lambda a: pltpu.VMEM(a.shape, a.dtype)
    o = SimpleNamespace(**outs)
    scratch = dict(
        ex=pltpu.SemaphoreType.DMA((2, 11 + 2 * pairs)),
        loc=pltpu.SemaphoreType.DMA((19,)),
        hid_v=like(o.hidden),
        qkv_v=like(o.qkv),
        mkv_v=like(o.mkv),
        coeff_v=like(o.coeff),
        w_v=like(o.w_qkv),
        ctx_v=like(o.ctx),
        att_v=like(o.att),
        mix_v=like(o.mixed),
        n2_v=pltpu.VMEM((tokens // 2, width), bf16),
        ctx_rx=pltpu.VMEM((tokens // 2, wide), bf16),
        wo_v=pltpu.VMEM((2, wide, width), bf16),
        gain2=pltpu.VMEM((1, width), f32),
        bias2=pltpu.VMEM((1, width), f32),
        prev=pltpu.VMEM((tokens, width), bf16),
        normed=pltpu.VMEM((tokens, width), bf16),
        a=pltpu.VMEM((basis, basis), f32),
        i=pltpu.VMEM((2, basis // 2, basis // 2), f32),
        cross=pltpu.VMEM((basis // 2, basis // 2), f32),
        schur=pltpu.VMEM((basis // 2, basis // 2), f32),
        shares=pltpu.VMEM((3, basis, tokens), bf16),
        gain1=pltpu.VMEM((1, width), f32),
        bias1=pltpu.VMEM((1, width), f32),
        musg=pltpu.VMEM((2 * pairs, 8, basis), f32),
        s=pltpu.VMEM((tokens, QB), f32),
        v_t=pltpu.VMEM((128, tokens), bf16),
        mv_t=pltpu.VMEM((128, basis), bf16),
        o=pltpu.VMEM((128, tokens), f32),
    )
    hbm, vmem = pl.BlockSpec(memory_space=pl.ANY), pl.BlockSpec(memory_space=pltpu.VMEM)
    names = list(held) + list(given) + list(outs) + list(near) + list(scratch)
    return pl.pallas_call(
        functools.partial(front_kernel, names),
        in_specs=[hbm] * len(held) + [vmem] * len(given),
        out_specs=[hbm] * len(outs) + [vmem] * len(near),
        out_shape=list(outs.values()) + list(near.values()),
        scratch_shapes=list(scratch.values()),
        compiler_params=vmem_params(collective_id=2, has_side_effects=True),
        name="front",
    )(*held.values(), *given.values())


def finish(down, up, out_t, parts, small, basis):
    width = out_t.shape[1]
    per = basis // 128
    heads = width // 64
    steps = width // 128
    per_core = steps // 2
    tall = down.shape[1] // per_core
    wide = width // 2

    def body(down_ref, up_ref, t_ref, s_ref, *refs):
        o_down, o_up, o_q, o_k, o_v, o_o, o_mu, o_sg = refs[len(parts) :]
        for n, ref in enumerate((o_mu, o_sg)):
            for h in range(heads):
                for t in range(per):
                    row = n * (heads // 2) * per + h % (heads // 2) * per + t
                    here = slice(t * 128, t * 128 + 128)
                    ref[h : h + 1, here] = s_ref[h // (heads // 2), row : row + 1, :]
        o_down[...] = down_ref[0].astype(f32)
        n = up_ref.shape[2]
        for c in range(2):
            o_up[:, c * n : c * n + n] = up_ref[c].astype(f32)
            for i, ref in enumerate(refs[: len(parts)]):
                here = slice(c * wide + i * 128, c * wide + i * 128 + 128)
                o_q[:, here] = ref[c, :, 0:128].astype(f32)
                o_k[:, here] = ref[c, :, 128:256].astype(f32)
                o_v[:, here] = ref[c, :, 256:384].astype(f32)
        o_o[...] = jnp.transpose(t_ref[0].astype(f32))

    row = lambda n: pl.BlockSpec((128, n), lambda i: (i, 0))
    shape = jax.ShapeDtypeStruct
    return pl.pallas_call(
        body,
        grid=(steps,),
        in_specs=[
            pl.BlockSpec((1, tall, width), lambda i: (i // per_core, i % per_core, 0)),
            pl.BlockSpec((2, 128, up.shape[2]), lambda i: (0, i, 0)),
            pl.BlockSpec((1, width, 128), lambda i: (i // per_core, 0, i % per_core)),
            pl.BlockSpec(small.shape, lambda i: (0, 0, 0)),
        ]
        + [pl.BlockSpec((2, 128, 384), lambda i: (0, i, 0))] * len(parts),
        out_specs=[pl.BlockSpec((tall, width), lambda i: (i, 0)), row(2 * up.shape[2])]
        + [row(width)] * 4
        + [pl.BlockSpec((heads, basis), lambda i: (0, 0))] * 2,
        out_shape=[
            shape((2 * down.shape[1], width), f32),
            shape((width, 2 * up.shape[2]), f32),
        ]
        + [shape((width, width), f32)] * 4
        + [shape((heads, basis), f32)] * 2,
        compiler_params=vmem_params(),
        name="finish",
    )(down, up, out_t, small, *parts)


def chip_local(
    inputs,
    previous,
    memory_rows,
    sticky_positions,
    cotangent,
    ln1_gain,
    ln1_bias,
    query_weight,
    key_weight,
    value_weight,
    out_weight,
    mu_weight,
    sigma_weight,
    ln2_gain,
    ln2_bias,
    expand_weight,
    up_bias,
    down_weight,
    down_bias,
):
    width = inputs.shape[2]
    heads, basis = mu_weight.shape
    ff = up_bias.shape[0]
    params = dict(ln1_gain=ln1_gain, ln2_gain=ln2_gain, mu=mu_weight, sigma=sigma_weight)
    hidden, normed, qkv, mkv, coeff, w_qkv, cot, ctx, att, mixed, n2, lse = front_call(
        dict(
            inputs=inputs,
            previous=previous,
            cotangent=cotangent,
            wq=query_weight,
            wk=key_weight,
            wv=value_weight,
            wo=out_weight,
        ),
        dict(picks=memory_rows, sticky=sticky_positions, ln1_bias=ln1_bias, ln2_bias=ln2_bias, **params),
        basis,
    )
    o_down, o_up, o_out, o_0, o_1, o_2, o_s, block_output, grad_inputs = tail_call(
        dict(
            cot=cot,
            n2_in=n2,
            mixed_in=mixed,
            hidden=hidden,
            ctx=ctx,
            expand=expand_weight,
            down=down_weight,
            w_out=out_weight,
            qkv=qkv,
            mkv=mkv,
            att=att,
            normed=normed,
            coeff=coeff,
            w_qkv=w_qkv,
        ),
        dict(lse=lse, up_bias=up_bias, down_bias=down_bias, **params),
    )
    g_down, g_up, g_q, g_k, g_v, g_o, g_mu, g_sigma = finish(
        o_down, o_up, o_out, (o_0, o_1, o_2), o_s, basis
    )
    s = o_s.reshape(2, -1)
    start = heads * basis
    cuts = [ff // 2, width, width, width, width, width]
    parts = []
    for n in cuts:
        parts.append(s[:, start : start + n])
        start += n
    both = [a[0] + a[1] for a in parts[2:]]
    return (
        block_output,
        grad_inputs,
        both[2],
        both[3],
        g_q,
        g_k,
        g_v,
        g_o,
        g_mu,
        g_sigma,
        both[0],
        both[1],
        g_up,
        parts[0].reshape(ff),
        g_down,
        parts[1][0],
    )


def pick(mesh):
    def step(*arrays):
        inputs, mu = arrays[0], arrays[11]
        fits = (
            mesh.shape[BATCH] == 8
            and mesh.shape[BLK] == 4
            and inputs.shape[0] == 2
            and inputs.shape[1] % QB == 0
            and mu.shape[0] % 4 == 0
            and inputs.shape[2] == mu.shape[0] * 64
        )
        return (chip_local if fits else general)(*arrays)

    return step


def solution(mesh):
    return jax.shard_map(
        pick(mesh),
        mesh=mesh,
        in_specs=(
            P(BATCH, BLK, None),
            P(BATCH, BLK, None),
            P(BATCH, None),
            P(BATCH, None),
            P(BATCH, BLK, None),
            P(),
            P(),
            P(),
            P(),
            P(),
            P(),
            P(),
            P(),
            P(),
            P(),
            P(),
            P(),
            P(),
            P(),
        ),
        out_specs=(
            P(BATCH, BLK, None),
            P(BATCH, BLK, None),
            P(),
            P(),
            P(),
            P(),
            P(),
            P(),
            P(),
            P(),
            P(),
            P(),
            P(),
            P(),
            P(),
            P(),
        ),
        check_vma=False,
    )
```

```python
import functools
from types import SimpleNamespace

import jax
import jax.numpy as jnp
from jax import lax
from jax.experimental import pallas as pl
from jax.experimental.pallas import tpu as pltpu
from jax.sharding import PartitionSpec as P

epsilon = 1e-05
ridge_weight = 1.0
var_scale = 0.01
masked_score = -1e30
BLK = "blk"
BATCH = "batch"
highest = lax.Precision.HIGHEST


def layer_norm(values, gain, bias):
    center = jnp.mean(values, axis=-1, keepdims=True)
    shifted = values - center
    spread_sq = jnp.mean(shifted * shifted, axis=-1, keepdims=True)
    return shifted * lax.rsqrt(spread_sq + epsilon) * gain + bias


def density(scores, mu_row, sigma_row):
    count = scores.shape[-1]
    centers = (jnp.arange(count, dtype=scores.dtype) + 0.5) / count
    spread = 1.0 / count
    centre = jax.nn.sigmoid(jnp.dot(scores, mu_row, precision=highest))
    variance = var_scale * jax.nn.softplus(jnp.dot(scores, sigma_row, precision=highest))
    total = spread * spread + variance
    return (spread * lax.rsqrt(total))[..., None] * jnp.exp(
        -((centre[..., None] - centers) ** 2) / (2.0 * total[..., None])
    )


def project(source, weight):
    return jnp.einsum("std,de->ste", source, weight, preferred_element_type=jnp.float32)


def weight_grad(source, grads):
    return jnp.einsum("std,ste->de", source, grads, preferred_element_type=jnp.float32)


def back_project(grads, weight):
    return jnp.einsum("ste,de->std", grads, weight, preferred_element_type=jnp.float32)


def gelu_tanh(values):
    return jax.nn.gelu(values, approximate=True)


def general(
    inputs,
    previous,
    memory_rows,
    sticky_positions,
    cotangent,
    ln1_gain,
    ln1_bias,
    query_weight,
    key_weight,
    value_weight,
    out_weight,
    mu_weight,
    sigma_weight,
    ln2_gain,
    ln2_bias,
    expand_weight,
    up_bias,
    down_weight,
    down_bias,
):
    seg_count, tok_rows, model_width = inputs.shape
    blocks = lax.axis_size(BLK)
    length = tok_rows * blocks
    first_row = lax.axis_index(BLK) * tok_rows
    head_count, basis_count = mu_weight.shape
    head_width = model_width // head_count
    centers = (jnp.arange(basis_count, dtype=jnp.float32) + 0.5) / basis_count
    spread = 1.0 / basis_count
    places = (sticky_positions.astype(jnp.float32) + 0.5) / length
    features = jnp.exp(-((places[..., None] - centers) ** 2) / (2.0 * spread * spread)).astype(
        jnp.bfloat16
    )
    local_index = memory_rows - first_row
    owned_rows = (local_index >= 0) & (local_index < tok_rows)
    picked = jax.vmap(lambda shard_rows, row_index: shard_rows[row_index])(
        previous, jnp.clip(local_index, 0, tok_rows - 1)
    )
    picked = jnp.where(owned_rows[..., None], picked, jnp.zeros_like(picked))
    own_features = jnp.where(owned_rows[..., None], features, jnp.zeros_like(features))
    side_part = jnp.einsum("smn,smd->snd", own_features, picked, preferred_element_type=jnp.float32)
    gram_part = jnp.einsum(
        "smn,smk->snk", own_features, own_features, preferred_element_type=jnp.float32
    )
    gram_sum, right_side = lax.psum((gram_part, side_part), BLK)
    system = gram_sum + ridge_weight * jnp.eye(basis_count, dtype=jnp.float32)
    factor = jnp.linalg.cholesky(system)
    coefficients = jax.scipy.linalg.cho_solve((factor, True), right_side)
    coeff_low = coefficients.astype(jnp.bfloat16)
    hidden_in = inputs.astype(jnp.float32)
    normed_low = layer_norm(hidden_in, ln1_gain, ln1_bias).astype(jnp.bfloat16)
    queries = project(normed_low, query_weight).astype(jnp.bfloat16)
    keys_local = project(normed_low, key_weight).astype(jnp.bfloat16)
    values_local = project(normed_low, value_weight).astype(jnp.bfloat16)
    mem_keys = project(coeff_low, key_weight).astype(jnp.bfloat16)
    mem_values = project(coeff_low, value_weight).astype(jnp.bfloat16)
    all_keys, all_values = (
        lax.all_gather(keys_local, BLK, axis=1, tiled=True),
        lax.all_gather(values_local, BLK, axis=1, tiled=True),
    )

    def split_heads(array):
        return array.reshape(array.shape[0], array.shape[1], head_count, head_width).transpose(
            2, 0, 1, 3
        )

    def merge_heads(array):
        return array.transpose(1, 2, 0, 3).reshape(array.shape[1], array.shape[2], model_width)

    query_pos = first_row + jnp.arange(tok_rows)
    key_pos = jnp.arange(length)
    causal = key_pos[None, :] <= query_pos[:, None]

    def forward_head(operands):
        query_h, key_h, value_h, memkey_h, memval_h, mu_row, sigma_row = operands
        scores = (
            jnp.einsum("sqd,skd->sqk", query_h, key_h, preferred_element_type=jnp.float32) * 0.125
        )
        scores = jnp.where(causal, scores, masked_score)
        top = jnp.max(scores, axis=-1, keepdims=True)
        raised = jnp.exp(scores - top)
        total = jnp.sum(raised, axis=-1, keepdims=True)
        probs = raised / total
        log_total = (top + jnp.log(total))[..., 0]
        attended = jnp.einsum(
            "sqk,skd->sqd", probs.astype(jnp.bfloat16), value_h, preferred_element_type=jnp.float32
        )
        memory_scores = (
            jnp.einsum("sqd,snd->sqn", query_h, memkey_h, preferred_element_type=jnp.float32)
            * 0.125
        )
        weights_mem = density(memory_scores, mu_row, sigma_row)
        recalled = jnp.einsum(
            "sqn,snd->sqd",
            weights_mem.astype(jnp.bfloat16),
            memval_h,
            preferred_element_type=jnp.float32,
        )
        return (attended + recalled, log_total)

    head_queries = split_heads(queries)
    head_keys = split_heads(all_keys)
    value_per_head = split_heads(all_values)
    head_memkeys = split_heads(mem_keys)
    head_memvals = split_heads(mem_values)
    heads_ctx, log_totals = lax.map(
        forward_head,
        (
            head_queries,
            head_keys,
            value_per_head,
            head_memkeys,
            head_memvals,
            mu_weight,
            sigma_weight,
        ),
    )
    context_low = merge_heads(heads_ctx).astype(jnp.bfloat16)
    mixed = hidden_in + project(context_low, out_weight)
    normed_two_low = layer_norm(mixed, ln2_gain, ln2_bias).astype(jnp.bfloat16)
    hidden_up = (
        jnp.einsum("std,df->stf", normed_two_low, expand_weight, preferred_element_type=jnp.float32)
        + up_bias
    )
    active_low = gelu_tanh(hidden_up).astype(jnp.bfloat16)
    result = (
        mixed
        + jnp.einsum("stf,fd->std", active_low, down_weight, preferred_element_type=jnp.float32)
        + down_bias
    )
    block_output = result.astype(jnp.bfloat16)
    grad_result = cotangent.astype(jnp.float32)
    grad_down_bias = jnp.sum(grad_result, axis=(0, 1))
    grad_down_weight = jnp.einsum(
        "stf,std->fd", active_low, cotangent, preferred_element_type=jnp.float32
    )
    grad_active = jnp.einsum(
        "std,fd->stf", cotangent, down_weight, preferred_element_type=jnp.float32
    )
    gelu_value, gelu_pull = jax.vjp(gelu_tanh, hidden_up)
    grad_up_low = gelu_pull(grad_active)[0].astype(jnp.bfloat16)
    grad_up_bias = jnp.sum(grad_up_low.astype(jnp.float32), axis=(0, 1))
    grad_up_weight = jnp.einsum(
        "std,stf->df", normed_two_low, grad_up_low, preferred_element_type=jnp.float32
    )
    grad_normed_two = jnp.einsum(
        "stf,df->std", grad_up_low, expand_weight, preferred_element_type=jnp.float32
    )
    norm_two_value, norm_two_pull = jax.vjp(layer_norm, mixed, ln2_gain, ln2_bias)
    grad_mixed_norm, grad_ln2_gain, grad_ln2_bias = norm_two_pull(grad_normed_two)
    grad_mixed = grad_result + grad_mixed_norm
    grad_mixed_low = grad_mixed.astype(jnp.bfloat16)
    grad_out_weight = weight_grad(context_low, grad_mixed_low)
    grad_context_low = back_project(grad_mixed_low, out_weight).astype(jnp.bfloat16)

    def backward_head(operands):
        query_h, key_h, value_h, memkey_h, memval_h, mu_row, sigma_row, grad_h, log_total = operands
        scores = (
            jnp.einsum("sqd,skd->sqk", query_h, key_h, preferred_element_type=jnp.float32) * 0.125
        )
        probs = jnp.where(causal, jnp.exp(scores - log_total[..., None]), 0.0)
        grad_probs = jnp.einsum("sqd,skd->sqk", grad_h, value_h, preferred_element_type=jnp.float32)
        row_dot = jnp.sum(probs * grad_probs, axis=-1, keepdims=True)
        grad_scores = (probs * (grad_probs - row_dot)).astype(jnp.bfloat16)
        grad_query = (
            jnp.einsum("sqk,skd->sqd", grad_scores, key_h, preferred_element_type=jnp.float32)
            * 0.125
        )
        memory_scores = (
            jnp.einsum("sqd,snd->sqn", query_h, memkey_h, preferred_element_type=jnp.float32)
            * 0.125
        )
        weights_mem, density_pull = jax.vjp(density, memory_scores, mu_row, sigma_row)
        weights_low = weights_mem.astype(jnp.bfloat16)
        grad_weights = jnp.einsum(
            "sqd,snd->sqn", grad_h, memval_h, preferred_element_type=jnp.float32
        )
        grad_memval = jnp.einsum(
            "sqn,sqd->snd", weights_low, grad_h, preferred_element_type=jnp.float32
        )
        grad_memscores, grad_mu, grad_sigma = density_pull(grad_weights)
        grad_memscores_low = grad_memscores.astype(jnp.bfloat16)
        grad_query = (
            grad_query
            + jnp.einsum(
                "sqn,snd->sqd", grad_memscores_low, memkey_h, preferred_element_type=jnp.float32
            )
            * 0.125
        )
        grad_memkey = (
            jnp.einsum(
                "sqn,sqd->snd", grad_memscores_low, query_h, preferred_element_type=jnp.float32
            )
            * 0.125
        )
        grad_key = (
            jnp.einsum("sqk,sqd->skd", grad_scores, query_h, preferred_element_type=jnp.float32)
            * 0.125
        )
        grad_value = jnp.einsum(
            "sqk,sqd->skd", probs.astype(jnp.bfloat16), grad_h, preferred_element_type=jnp.float32
        )
        return (grad_query, grad_memkey, grad_memval, grad_mu, grad_sigma, grad_key, grad_value)

    head_grads = split_heads(grad_context_low)
    outcome = lax.map(
        backward_head,
        (
            head_queries,
            head_keys,
            value_per_head,
            head_memkeys,
            head_memvals,
            mu_weight,
            sigma_weight,
            head_grads,
            log_totals,
        ),
    )
    grad_query_heads, grad_memkey_heads, grad_memval_heads, grad_mu_weight, grad_sigma_weight = (
        outcome[:5]
    )
    terms = (
        jnp.stack((outcome[5], outcome[6]))
        .transpose(3, 2, 0, 1, 4)
        .reshape(length, seg_count, 2 * model_width)
    )
    own_terms = lax.psum_scatter(
        terms.astype(jnp.bfloat16), BLK, scatter_dimension=0, tiled=True
    ).astype(jnp.float32)
    own_terms = own_terms.reshape(tok_rows, seg_count, 2, model_width).transpose(2, 1, 0, 3)
    grad_keys = own_terms[0]
    grad_values = own_terms[1]
    grad_queries_low = merge_heads(grad_query_heads).astype(jnp.bfloat16)
    grad_keys_low = grad_keys.astype(jnp.bfloat16)
    grad_values_low = grad_values.astype(jnp.bfloat16)
    memkey_sum, memval_sum = (
        lax.psum(grad_memkey_heads.astype(jnp.bfloat16), BLK).astype(jnp.float32),
        lax.psum(grad_memval_heads.astype(jnp.bfloat16), BLK).astype(jnp.float32),
    )
    gradient_memory_keys_reduced = merge_heads(memkey_sum).astype(jnp.bfloat16)
    gradient_memory_values_reduced = merge_heads(memval_sum).astype(jnp.bfloat16)
    grad_query_weight = weight_grad(normed_low, grad_queries_low)
    grad_key_weight = weight_grad(normed_low, grad_keys_low)
    grad_value_weight = weight_grad(normed_low, grad_values_low)
    grad_normed = (
        back_project(grad_queries_low, query_weight)
        + back_project(grad_keys_low, key_weight)
        + back_project(grad_values_low, value_weight)
    )
    norm_one_value, norm_one_pull = jax.vjp(layer_norm, hidden_in, ln1_gain, ln1_bias)
    grad_in_norm, grad_ln1_gain, grad_ln1_bias = norm_one_pull(grad_normed)
    grad_inputs = grad_mixed + grad_in_norm
    shares = (
        lax.psum_scatter(
            grad_ln1_gain.astype(jnp.bfloat16), BLK, scatter_dimension=0, tiled=True
        ).astype(jnp.float32),
        lax.psum_scatter(
            grad_ln1_bias.astype(jnp.bfloat16), BLK, scatter_dimension=0, tiled=True
        ).astype(jnp.float32),
        lax.psum_scatter(
            grad_query_weight.astype(jnp.bfloat16), BLK, scatter_dimension=0, tiled=True
        ).astype(jnp.float32),
        lax.psum_scatter(
            grad_key_weight.astype(jnp.bfloat16), BLK, scatter_dimension=0, tiled=True
        ).astype(jnp.float32),
        lax.psum_scatter(
            grad_value_weight.astype(jnp.bfloat16), BLK, scatter_dimension=0, tiled=True
        ).astype(jnp.float32),
        lax.psum_scatter(
            grad_out_weight.astype(jnp.bfloat16), BLK, scatter_dimension=0, tiled=True
        ).astype(jnp.float32),
        lax.psum_scatter(
            grad_mu_weight.astype(jnp.bfloat16), BLK, scatter_dimension=1, tiled=True
        ).astype(jnp.float32),
        lax.psum_scatter(
            grad_sigma_weight.astype(jnp.bfloat16), BLK, scatter_dimension=1, tiled=True
        ).astype(jnp.float32),
        lax.psum_scatter(
            grad_ln2_gain.astype(jnp.bfloat16), BLK, scatter_dimension=0, tiled=True
        ).astype(jnp.float32),
        lax.psum_scatter(
            grad_ln2_bias.astype(jnp.bfloat16), BLK, scatter_dimension=0, tiled=True
        ).astype(jnp.float32),
        lax.psum_scatter(
            grad_up_weight.astype(jnp.bfloat16), BLK, scatter_dimension=0, tiled=True
        ).astype(jnp.float32),
        lax.psum_scatter(
            grad_up_bias.astype(jnp.bfloat16), BLK, scatter_dimension=0, tiled=True
        ).astype(jnp.float32),
        lax.psum_scatter(
            grad_down_weight.astype(jnp.bfloat16), BLK, scatter_dimension=0, tiled=True
        ).astype(jnp.float32),
        lax.psum_scatter(
            grad_down_bias.astype(jnp.bfloat16), BLK, scatter_dimension=0, tiled=True
        ).astype(jnp.float32),
    )
    share_width = model_width // blocks
    coefficient_part = lax.dynamic_slice_in_dim(
        coeff_low, lax.axis_index(BLK) * share_width, share_width, 2
    )
    key_share = shares[3] + jnp.einsum(
        "wrc,wrt->ct",
        coefficient_part,
        gradient_memory_keys_reduced,
        preferred_element_type=jnp.float32,
    )
    value_share = shares[4] + jnp.einsum(
        "wrc,wrt->ct",
        coefficient_part,
        gradient_memory_values_reduced,
        preferred_element_type=jnp.float32,
    )
    totals = (
        lax.psum(shares[0].astype(jnp.bfloat16), BATCH).astype(jnp.float32),
        lax.psum(shares[1].astype(jnp.bfloat16), BATCH).astype(jnp.float32),
        lax.psum(shares[2].astype(jnp.bfloat16), BATCH).astype(jnp.float32),
        lax.psum(key_share.astype(jnp.bfloat16), BATCH).astype(jnp.float32),
        lax.psum(value_share.astype(jnp.bfloat16), BATCH).astype(jnp.float32),
        lax.psum(shares[5].astype(jnp.bfloat16), BATCH).astype(jnp.float32),
        lax.psum(shares[6].astype(jnp.bfloat16), BATCH).astype(jnp.float32),
        lax.psum(shares[7].astype(jnp.bfloat16), BATCH).astype(jnp.float32),
        lax.psum(shares[8].astype(jnp.bfloat16), BATCH).astype(jnp.float32),
        lax.psum(shares[9].astype(jnp.bfloat16), BATCH).astype(jnp.float32),
        lax.psum(shares[10].astype(jnp.bfloat16), BATCH).astype(jnp.float32),
        lax.psum(shares[11].astype(jnp.bfloat16), BATCH).astype(jnp.float32),
        lax.psum(shares[12].astype(jnp.bfloat16), BATCH).astype(jnp.float32),
        lax.psum(shares[13].astype(jnp.bfloat16), BATCH).astype(jnp.float32),
    )
    whole = (
        lax.all_gather(totals[0].astype(jnp.bfloat16), BLK, axis=0, tiled=True).astype(
            jnp.float32
        ),
        lax.all_gather(totals[1].astype(jnp.bfloat16), BLK, axis=0, tiled=True).astype(
            jnp.float32
        ),
        lax.all_gather(totals[2].astype(jnp.bfloat16), BLK, axis=0, tiled=True).astype(
            jnp.float32
        ),
        lax.all_gather(totals[3].astype(jnp.bfloat16), BLK, axis=0, tiled=True).astype(
            jnp.float32
        ),
        lax.all_gather(totals[4].astype(jnp.bfloat16), BLK, axis=0, tiled=True).astype(
            jnp.float32
        ),
        lax.all_gather(totals[5].astype(jnp.bfloat16), BLK, axis=0, tiled=True).astype(
            jnp.float32
        ),
        lax.all_gather(totals[6].astype(jnp.bfloat16), BLK, axis=1, tiled=True).astype(
            jnp.float32
        ),
        lax.all_gather(totals[7].astype(jnp.bfloat16), BLK, axis=1, tiled=True).astype(
            jnp.float32
        ),
        lax.all_gather(totals[8].astype(jnp.bfloat16), BLK, axis=0, tiled=True).astype(
            jnp.float32
        ),
        lax.all_gather(totals[9].astype(jnp.bfloat16), BLK, axis=0, tiled=True).astype(
            jnp.float32
        ),
        lax.all_gather(totals[10].astype(jnp.bfloat16), BLK, axis=0, tiled=True).astype(
            jnp.float32
        ),
        lax.all_gather(totals[11].astype(jnp.bfloat16), BLK, axis=0, tiled=True).astype(
            jnp.float32
        ),
        lax.all_gather(totals[12].astype(jnp.bfloat16), BLK, axis=0, tiled=True).astype(
            jnp.float32
        ),
        lax.all_gather(totals[13].astype(jnp.bfloat16), BLK, axis=0, tiled=True).astype(
            jnp.float32
        ),
    )
    return (
        block_output,
        grad_inputs,
        whole[0],
        whole[1],
        whole[2],
        whole[3],
        whole[4],
        whole[5],
        whole[6],
        whole[7],
        whole[8],
        whole[9],
        whole[10],
        whole[11],
        whole[12],
        whole[13],
    )


f32 = jnp.float32
bf16 = jnp.bfloat16
NN = (((1,), (0,)), ((), ()))
NT = (((1,), (1,)), ((), ()))
TN = (((0,), (0,)), ((), ()))
QB = 256


def mm(a, b, dims=NN, precision=None):
    return lax.dot_general(a, b, dims, precision=precision, preferred_element_type=f32)


def vmem_params(**more):
    return pltpu.CompilerParams(vmem_limit_bytes=56 * 1024 * 1024, **more)


def head_mask(h):
    lane = lax.broadcasted_iota(jnp.int32, (1, 128), 1)
    return lane // 64 == h


def head_rows(h):
    return pl.ds(pl.multiple_of(h * 64, 64), 64)


def turn(a):
    return jnp.transpose(a.astype(f32))


def parts_of(rows):
    index = lax.broadcasted_iota(jnp.int32, (8, 1), 0)
    out = jnp.zeros_like(rows)
    for n in range(2):
        rest = rows[n : n + 1]
        for t in range(3):
            part = rest.astype(bf16).astype(f32)
            out = jnp.where(index == 3 * n + t, part, out)
            rest = rest - part
    return out.astype(bf16)


def gather_parts(rows):
    index = lax.broadcasted_iota(jnp.int32, (8, 1), 0)
    first = rows[2:3] + rows[1:2] + rows[0:1]
    second = rows[5:6] + rows[4:5] + rows[3:4]
    return jnp.where(index == 0, first, jnp.where(index == 1, second, 0.0))


def place_params(q, mk, musg, mask, basis):
    u = jnp.where(mask, gather_parts(mm(parts_of(musg), mk)) * 0.125, 0.0)
    ab = gather_parts(mm(parts_of(u), q, NT))
    spread = 1.0 / basis
    a = ab[0:1]
    b = ab[1:2]
    centre = 1.0 / (1.0 + jnp.exp(-a))
    soft = jnp.maximum(b, 0.0) + jnp.log1p(jnp.exp(-jnp.abs(b)))
    total = spread * spread + var_scale * soft
    return u, b, centre, total


def causal_block(n):
    key = lax.broadcasted_iota(jnp.int32, (n, n), 0)
    query = lax.broadcasted_iota(jnp.int32, (n, n), 1)
    return key <= query


class Place:
    def __init__(self):
        b, k = lax.axis_index(BATCH), lax.axis_index(BLK)
        z, x = b // 2, b % 2
        y, core = k // 2, k % 2
        self.z, self.x, self.y, self.core = z, x, y, core
        self.peer_x = (z * 2 + 1 - x, k)
        self.peer_y = (b, (1 - y) * 2 + core)
        self.peer_core = (b, y * 2 + 1 - core)
        self.peer_z = [(((z + d) % 4) * 2 + x, k) for d in (1, 2, 3)]

    def announce(self):
        peers = [self.peer_x, self.peer_y, self.peer_core] + self.peer_z
        barrier = pltpu.get_barrier_semaphore()
        for peer in peers:
            pl.semaphore_signal(barrier, inc=1, device_id=peer, device_id_type=pl.DeviceIdType.MESH)

    def wait(self):
        pl.semaphore_wait(pltpu.get_barrier_semaphore(), 6)


def remote(src, dst, sems, n, peer):
    return pltpu.make_async_remote_copy(
        src_ref=src,
        dst_ref=dst,
        send_sem=sems.at[0, n],
        recv_sem=sems.at[1, n],
        device_id=peer,
        device_id_type=pl.DeviceIdType.MESH,
    )


class Reducer:
    copies = 13

    def __init__(self, place, first, src, out, scratch, window=(0, 0), target=(0, 0)):
        self.place = place
        self.f, self.s = (place.x, place.y) if first == "x" else (place.y, place.x)
        x, y = place.peer_x, place.peer_y
        self.peer_f, self.peer_s = (x, y) if first == "x" else (y, x)
        self.src, self.out = src, out
        self.r1, self.send2, self.r2, self.acc, self.r3, self.done, self.sems, self.own = scratch
        self.rows, self.cols = self.r1.shape[0] * 2, self.r1.shape[1]
        self.step = self.rows // 16
        self.window, self.target = window, target

    @staticmethod
    def scratch(rows, cols, dtype):
        return [
            pltpu.VMEM((rows // 2, cols), dtype),
            pltpu.VMEM((rows // 4, cols), dtype),
            pltpu.VMEM((rows // 4, cols), dtype),
            pltpu.VMEM((rows // 4, cols), dtype),
            pltpu.VMEM((3, rows // 16, cols), dtype),
            pltpu.VMEM((rows // 16, cols), dtype),
            pltpu.SemaphoreType.DMA((2, Reducer.copies)),
            pltpu.SemaphoreType.DMA((1,)),
        ]

    def at(self, row, count):
        return pl.ds(pl.multiple_of(row, self.step), count)

    def taken(self, row, count):
        return self.at(self.window[0] + row, count), pl.ds(self.window[1], self.cols)

    def home(self, row, count):
        rows = self.at(self.target[0] + row, count)
        return self.out.at[self.place.core, rows, pl.ds(self.target[1], self.cols)]

    def copy(self, n):
        f, s, z = self.f, self.s, self.place.z
        half, quarter, step = self.rows // 2, self.rows // 4, self.step
        mine = f * half + s * quarter
        if n == 0:
            return remote(self.src.at[*self.taken((1 - f) * half, half)], self.r1, self.sems, n, self.peer_f)
        if n == 1:
            return remote(self.send2, self.r2, self.sems, n, self.peer_s)
        if n < 5:
            d = n - 2
            part = self.acc.at[self.at(((z + d + 1) % 4) * step, step)]
            return remote(part, self.r3.at[d], self.sems, n, self.place.peer_z[d])
        if n < 8:
            part = self.home(mine + z * step, step)
            return remote(self.done, part, self.sems, n, self.place.peer_z[n - 5])
        if n == 8:
            part, peer = self.home(mine, quarter), self.peer_s
        elif n == 9:
            part, peer = self.home(f * half, half), self.peer_f
        elif n == 10:
            part, peer = self.home(mine, quarter), self.place.peer_core
        elif n == 11:
            part, peer = self.home(f * half + (1 - s) * quarter, quarter), self.place.peer_core
        else:
            part, peer = self.home((1 - f) * half, half), self.place.peer_core
        return remote(part, part, self.sems, n, peer)

    def keep(self):
        mine = self.f * (self.rows // 2) + self.s * (self.rows // 4)
        part = self.home(mine + self.place.z * self.step, self.step)
        return pltpu.make_async_copy(self.done, part, self.own.at[0])

    def start(self, *numbers):
        for n in numbers:
            self.copy(n).start()

    def arrive(self, *numbers):
        for n in numbers:
            self.copy(n).wait_recv()

    def sum_into(self, dst, row, *more):
        def body(i, carry):
            at = i * self.step
            total = self.src[self.taken(row + at, self.step)].astype(f32)
            for ref, start in more:
                total = total + ref[self.at(start + at, self.step)].astype(f32)
            dst[self.at(at, self.step)] = total.astype(dst.dtype)
            return carry

        lax.fori_loop(0, 4, body, 0)

    def run(self, stage):
        f, s, z = self.f, self.s, self.place.z
        half, quarter, step = self.rows // 2, self.rows // 4, self.step
        if stage == 0:
            self.start(0)
        elif stage == 1:
            self.arrive(0)
            self.sum_into(self.send2, f * half + (1 - s) * quarter, (self.r1, (1 - s) * quarter))
            self.start(1)
        elif stage == 2:
            self.arrive(1)
            self.sum_into(self.acc, f * half + s * quarter, (self.r1, s * quarter), (self.r2, 0))
            self.start(2, 3, 4)
        elif stage == 3:
            self.arrive(2, 3, 4)
            total = self.acc[self.at(z * step, step)].astype(f32)
            for d in range(3):
                total = total + self.r3[d].astype(f32)
            self.done[...] = total.astype(self.done.dtype)
            self.start(5, 6, 7)
            self.keep().start()
        elif stage == 4:
            self.arrive(5, 6, 7)
            self.keep().wait()
            self.start(8, 10)
        elif stage == 5:
            self.arrive(8)
            self.start(9, 11)
        elif stage == 6:
            self.arrive(9)
            self.start(12)
        elif stage == 7:
            self.arrive(10, 11, 12)
            for n in range(self.copies):
                self.copy(n).wait_send()


def norm_back(x, gy, gain):
    center = jnp.mean(x, axis=-1, keepdims=True)
    shifted = x - center
    rstd = lax.rsqrt(jnp.mean(shifted * shifted, axis=-1, keepdims=True) + epsilon)
    hat = shifted * rstd
    g = gy * gain
    mean_g = jnp.mean(g, axis=-1, keepdims=True)
    mean_gh = jnp.mean(g * hat, axis=-1, keepdims=True)
    gx = rstd * (g - mean_g - hat * mean_gh)
    return gx, jnp.sum(gy * hat, axis=0, keepdims=True), jnp.sum(gy, axis=0, keepdims=True)


def gelu_both(v):
    root = 0.7978845608028654
    sq = v * v
    t = jnp.tanh(root * v * (1.0 + 0.044715 * sq))
    up = 0.5 + 0.5 * t
    slope = up + (0.5 * v) * (1.0 - t * t) * (root + (3.0 * 0.044715 * root) * sq)
    return v * up, slope


SPANS = (256, 512, 768)
STARTS = (0, 256, 768)
AFTER = 3
FIRST = "yyxyxxyxyxy"
PLAN = {
    0: [(1, 0), (0, 0)],
    1: [(3, 0), (2, 0)],
    2: [(1, 1), (5, 0), (0, 1), (4, 0)],
    3: [(2, 1)],
    4: [(6, 0)],
    5: [(11, 0), (1, 2), (2, 2)],
    9: [(0, 2)],
    10: [(1, 3), (5, 1)],
    11: [(6, 1)],
    12: [(2, 3), (0, 3)],
    13: [(1, 4), (4, 1)],
    14: [(3, 1), (6, 2)],
    15: [(5, 2)],
    17: [(2, 4), (7, 0)],
    19: [(0, 4)],
    20: [(1, 5), (4, 2)],
    22: [(2, 5)],
    23: [(8, 0)],
    25: [(5, 3)],
    26: [(7, 1)],
    29: [(8, 1), (6, 3), (0, 5), (9, 0)],
    30: [(5, 4), (4, 3), (8, 2), (6, 4)],
    31: [(10, 0), (5, 5), (7, 2), (4, 4), (8, 3), (9, 1), (3, 2), (10, 1), (7, 3), (6, 5), (8, 4), (4, 5), (3, 3), (9, 2), (3, 4), (10, 2), (7, 4), (9, 3), (8, 5), (7, 5), (5, 6), (9, 4), (1, 6), (5, 7), (0, 6), (0, 7), (2, 6), (4, 6), (10, 3), (6, 6), (3, 5), (10, 4), (1, 7), (8, 6), (9, 5), (7, 6), (10, 5), (2, 7), (3, 6), (9, 6), (10, 6), (4, 7), (10, 7), (3, 7), (6, 7), (7, 7), (8, 7), (9, 7)],
}


def tail_kernel(names, *refs):
    r = SimpleNamespace(**dict(zip(names, refs)))
    jobs_scratch = refs[len(names) :]
    place = Place()
    y, core = place.y, place.core
    tokens, width = r.cot_v.shape
    wide = width // 2
    ff = r.e_v.shape[1]
    pairs = wide // 128
    basis = r.mkv_v.shape[0]
    spread = 1.0 / basis
    block = tokens // 4
    chunk = 64
    n_sem = 8
    take = lambda i: jobs_scratch[n_sem * i : n_sem * i + n_sem]
    ex, loc = r.ex, r.loc
    small_rows = pairs * 2 * basis // 128
    up_rows = ff // 128
    width_rows = width // 128
    base_up = 2 * small_rows
    base_down = base_up + up_rows
    base_ln2 = base_down + width_rows
    base_ln1 = base_ln2 + 2 * width_rows
    third = lambda n: (0, n * wide)
    jobs = []
    for n, lo in enumerate(STARTS):
        jobs += [(r.g_down, r.o_down, (lo, 0), (lo, 0)), (r.g_up, r.o_up, (0, lo), (0, lo))]
    jobs += [(r.gup, r.o_out, third(3)), (r.gup, r.o_0, third(0)), (r.gup, r.o_1, third(1)), (r.gup, r.o_2, third(2))]
    jobs += [(r.sv, r.o_s)]
    jobs = [
        Reducer(place, FIRST[n], src, out, take(n), *windows)
        for n, (src, out, *windows) in enumerate(jobs)
    ]

    def act(step):
        for job, stage in PLAN.get(step, ()):
            if job < len(jobs):
                jobs[job].run(stage)
            else:
                out_copy().start()

    def rows_at(j, c):
        return pl.ds(pl.multiple_of((2 * j + c) * block, block), block)

    def half_at(j):
        return pl.ds(j * block, block)

    def half_dyn(j):
        return pl.ds(pl.multiple_of(j * block, block), block)

    def small_at(j, i):
        return pl.ds(pl.multiple_of((2 * j + core) * block + i * chunk, chunk), chunk)

    def expand_part(lo, count):
        return r.expand.at[:, pl.ds(pl.multiple_of(core * ff + lo, 128), count)]

    def down_part(lo, count):
        return r.down.at[pl.ds(pl.multiple_of(core * ff + lo, 128), count), :]

    def rows_from(ref, n, c):
        return ref.at[pl.ds(pl.multiple_of(c * n, 128), n), :]

    loads = [
        (r.n2_in, r.n2),
        (expand_part(0, SPANS[0]), r.e_v.at[:, pl.ds(0, SPANS[0])]),
        (down_part(0, SPANS[0]), r.d_v.at[pl.ds(0, SPANS[0])]),
        (r.cot, r.cot_v),
        (r.mixed_in, r.mixed),
        (rows_from(r.w_out, wide, core), r.wo_own),
        (r.ctx, r.ctx_v),
        (r.qkv, r.qkv_v),
        (r.mkv, r.mkv_v),
        (r.att, r.att_v),
        (r.normed, r.norm_v),
        (r.coeff, r.coeff_v),
        (r.w_qkv, r.wqkv_v),
        (r.hidden.at[rows_at(0, core)], r.hid_own.at[half_at(0)]),
        (r.hidden.at[rows_at(1, core)], r.hid_own.at[half_at(1)]),
        (expand_part(SPANS[0], ff - SPANS[0]), r.e_v.at[:, pl.ds(SPANS[0], ff - SPANS[0])]),
        (down_part(SPANS[0], ff - SPANS[0]), r.d_v.at[pl.ds(SPANS[0], ff - SPANS[0])]),
    ]

    def load(n):
        return pltpu.make_async_copy(*loads[n], loc.at[n])

    def ready(*numbers):
        for n in numbers:
            load(n).wait()

    def swap(n, j):
        if n == 2 or n == 5:
            src, dst = r.tx.at[half_at(j)], r.rx.at[half_at(j)]
        elif n == 3:
            src = dst = r.gml.at[rows_at(j, core)]
        else:
            src, dst = r.tx.at[half_at(j)], r.rx_out.at[half_at(j)]
        return remote(src, dst, ex, 2 * n + j, place.peer_core)

    def out_copy():
        return remote(r.bo.at[half_dyn(1 - y)], r.out.at[y], ex, 12, place.peer_y)

    def out_keep():
        return pltpu.make_async_copy(r.bo.at[half_dyn(y)], r.out.at[y], loc.at[17])

    def gin_copy():
        return remote(r.n2.at[half_dyn(1 - y)], r.gi_rx, ex, 13, place.peer_y)

    def gin_keep():
        return pltpu.make_async_copy(r.gm.at[half_dyn(y)], r.gin.at[y], loc.at[18])

    def gin_place():
        return pltpu.make_async_copy(r.rx.at[half_at(0)], r.gin.at[1 - y], loc.at[19])

    for n in (0, 1, 2, 3, 15, 16, *range(4, 15)):
        load(n).start()
    place.announce()
    r.sv[...] = jnp.zeros_like(r.sv)
    r.gain1[...] = as_row(r.ln1_gain)
    r.gain2[...] = as_row(r.ln2_gain)
    r.bias_d[...] = as_row(r.down_bias)
    both_up = as_row(r.up_bias)
    r.bias_u[...] = jnp.where(core == 0, both_up[:, :ff], both_up[:, ff:])
    fill_heads(r.musg, r.mu, r.sigma, core)

    def put(row, vec):
        for t in range(vec.shape[1] // 128):
            r.sv[pl.ds(row + t, 1), :] = vec[:, t * 128 : t * 128 + 128]

    ready(0, 1, 2, 3)
    tall = tokens // 2
    for part, (lo, span) in enumerate(zip(STARTS, SPANS)):
        if part == 1:
            ready(15, 16)

        def tile(i, carry, lo=lo):
            rows = pl.ds(pl.multiple_of((i % 2) * tall, tall), tall)
            col = pl.multiple_of(lo + (i // 2) * 256, 256)
            cols = pl.ds(col, 256)
            hidden_up = mm(r.n2[rows, :], r.e_v[:, cols]) + r.bias_u[:, cols]
            value, slope = gelu_both(hidden_up)
            r.active[rows, cols] = value.astype(bf16)
            grad = (mm(r.cot_v[rows, :], r.d_v[cols, :], NT) * slope).astype(bf16)
            r.gup[rows, cols] = grad
            sums = jnp.sum(grad.astype(f32), axis=0, keepdims=True)
            at = base_up + col // 128
            for t in range(2):
                r.sv[pl.ds(at + t, 1), :] += sums[:, t * 128 : t * 128 + 128]
            return carry

        lax.fori_loop(0, 2 * (span // 256), tile, 0)
        for m in range(span // 256):
            here = slice(lo + m * 256, lo + m * 256 + 256)
            r.g_down[here, :] = mm(r.active[:, here], r.cot_v[...], TN).astype(bf16)
        for m in range(width // 256):
            cols = slice(m * 256, m * 256 + 256)
            r.g_up[cols, lo : lo + span] = mm(r.n2[:, cols], r.gup[:, lo : lo + span], TN).astype(bf16)
        if part == 0:
            place.wait()
        act(part)

    ready(4, 5, 6)
    for j in range(2):
        r.tx[half_at(j), :] = mm(r.gup[rows_at(j, 1 - core), :], r.e_v[...], NT)
        swap(2, j).start()

    def norm_two(j, carry):
        def body(i, carry):
            at = pl.ds(pl.multiple_of(j * block + i * chunk, chunk), chunk)
            gy = r.gm[at, :] + r.rx[at, :]
            gx, dg, db = norm_back(r.mixed[at, :], gy, r.gain2[...])
            cot = r.cot_v[small_at(j, i), :].astype(f32)
            gm = cot + gx
            r.gm[at, :] = gm
            r.gml[small_at(j, i), :] = gm.astype(bf16)
            return carry[0] + dg, carry[1] + db

        return lax.fori_loop(0, block // chunk, body, carry)

    sums = (jnp.zeros((1, width), f32), jnp.zeros((1, width), f32))
    for j in range(2):
        r.gm[half_at(j), :] = mm(r.gup[rows_at(j, core), :], r.e_v[...], NT)
        swap(2, j).wait_recv()
        sums = norm_two(j, sums)
        swap(3, j).start()
    put(base_ln2, sums[0])
    put(base_ln2 + width_rows, sums[1])
    put(base_down, jnp.sum(r.cot_v[...].astype(f32), axis=0, keepdims=True))
    act(AFTER + 0)
    for c in (0, 1):
        for j in range(2):
            if c:
                swap(3, j).wait_recv()
            there = rows_at(j, core if c == 0 else 1 - core)
            r.do[there, :] = mm(r.gml[there, :], r.wo_own[...], NT).astype(bf16)
    for m in range(width // 256):
        cols = slice(m * 256, m * 256 + 256)
        r.gup[cols, pairs * wide : pairs * wide + wide] = mm(r.gml[:, cols], r.ctx_v[...], TN).astype(bf16)
    act(AFTER + 1)

    for j in range(2):
        swap(2, j).wait_send()
        r.tx[half_at(j), :] = mm(r.active[rows_at(j, 1 - core), :], r.d_v[...])
        swap(4, j).start()
    for j in range(2):
        own = mm(r.active[rows_at(j, core), :], r.d_v[...])
        swap(4, j).wait_recv()
        total = r.mixed[half_at(j), :] + (own + r.rx_out[half_at(j), :]) + r.bias_d[...]
        r.bo[half_at(j), :] = total.astype(bf16)
    out_keep().start()
    act(AFTER + 2)

    centers = (lax.broadcasted_iota(jnp.int32, (basis, 1), 0).astype(f32) + 0.5) / basis
    allowed = causal_block(QB)
    pick_row = lax.broadcasted_iota(jnp.int32, (8, 1), 0)
    blocks = tokens // QB
    per_pair = 2 * blocks
    ready(7, 8, 9, 10, 11)
    for n in range(4):
        at = slice(n * block, n * block + block)
        r.normed_v[:, at] = turn(r.norm_v[at, :]).astype(bf16)

    def pair_step(i, carry):
        lanes = pl.ds(pl.multiple_of(i * 128, 128), 128)

        def lanes_of(j):
            return pl.ds(pl.multiple_of(i * 128 + j * wide, 128), 128)

        q_ref, k_ref, v_ref = (r.qkv_v.at[:, lanes_of(j)] for j in range(3))
        mk_ref, mv_ref = (r.mkv_v.at[:, lanes_of(j)] for j in range(2))
        do_ref = r.do.at[:, lanes]
        dka, dva, dqt, gmva, k_t, do_t = r.dka, r.dva, r.dqt, r.gmva, r.k_t, r.do_t
        k_t[...] = turn(k_ref[...]).astype(bf16)
        do_t[...] = turn(do_ref[...])
        dka[...] = jnp.zeros_like(dka)
        dva[...] = jnp.zeros_like(dva)
        gmva[...] = jnp.zeros_like(gmva)
        r.gmk[...] = jnp.zeros_like(r.gmk)

        def finish_pair():
            r.active[:, lanes] = jnp.transpose(dqt[...]).astype(bf16)
            r.active[:, lanes_of(1)] = dka[...].astype(bf16)
            r.active[:, lanes_of(2)] = dva[...].astype(bf16)
            r.part[:, 0:128] = r.active[:, lanes]
            r.part[:, 128:256] = r.active[:, lanes_of(1)]
            r.part[:, 256:384] = r.active[:, lanes_of(2)]
            r.part_mem[:, 0:128] = r.gmk[...].astype(bf16)
            r.part_mem[:, 128:256] = gmva[...].astype(bf16)
            spot = pl.multiple_of(i * wide, 128)
            for m in range(width // 256):
                here = slice(m * 256, m * 256 + 256)
                g = mm(r.normed_v[here, :], r.part[...])
                cg = mm(r.coeff_v[:, here], r.part_mem[...], TN)
                r.gup[here, pl.ds(spot, 128)] = g[:, :128].astype(bf16)
                r.gup[here, pl.ds(spot + 128, 256)] = (g[:, 128:] + cg).astype(bf16)

        def head_step(h, carry):
            mask = head_mask(h)
            rows = head_rows(h)
            musg = r.musg[2 * i + h]
            u, b, centre, total = place_params(q_ref[...], mk_ref[...], musg, mask, basis)
            scale = spread * lax.rsqrt(total)
            inv = 1.0 / total
            dot_rows = jnp.sum(do_t[rows, :] * r.att_v[i, rows, :], axis=0, keepdims=True)
            z = jnp.zeros((8, 128), f32)
            for qb in range(blocks):
                cols = slice(qb * QB, qb * QB + QB)
                q = jnp.where(mask, q_ref[cols, :].astype(f32) * 0.125, 0.0).astype(bf16)
                do = jnp.where(mask, do_ref[cols, :].astype(f32), 0.0).astype(bf16)
                lse = r.lse[i, pl.ds(h, 1), cols]
                dot_row = dot_rows[:, cols]
                dq_t = jnp.zeros((64, QB), f32)
                for kb in range(qb + 1):
                    keys = slice(kb * QB, kb * QB + QB)
                    p = jnp.exp(mm(k_ref[keys, :], q, NT) - lse)
                    if kb == qb:
                        p = jnp.where(allowed, p, 0.0)
                    dva[keys, :] += mm(p.astype(bf16), do)
                    ds = (p * (mm(v_ref[keys, :], do, NT) - dot_row)).astype(bf16)
                    dka[keys, :] += mm(ds, q)
                    dq_t = dq_t + mm(k_t[rows, keys], ds)
                dqt[rows, cols] = dq_t * 0.125
                gap = centre[:, cols] - centers
                gap2 = gap * gap
                inv_b = inv[:, cols]
                dens = scale[:, cols] * jnp.exp(gap2 * (-0.5 * inv_b))
                gmva[...] += mm(dens.astype(bf16), do)
                e = mm(mv_ref[...], do, NT) * dens
                sum0 = jnp.sum(e, axis=0, keepdims=True)
                sum1 = jnp.sum(e * gap, axis=0, keepdims=True)
                sum2 = jnp.sum(e * gap2, axis=0, keepdims=True)
                c = centre[:, cols]
                da = -sum1 * inv_b * c * (1.0 - c)
                dtotal = 0.5 * inv_b * (sum2 * inv_b - sum0)
                db = dtotal * var_scale / (1.0 + jnp.exp(-b[:, cols]))
                dab = jnp.where(pick_row == 0, da, jnp.where(pick_row == 1, db, 0.0))
                dqt[:, cols] += mm(u, dab, TN, precision=highest)
                z = z + gather_parts(mm(parts_of(dab), q))
                if qb == blocks - 1:
                    r.gmk[...] += mm(musg, z, TN, precision=highest)
                    grads = gather_parts(mm(parts_of(z), mk_ref[...], NT))
                    at = (2 * i + h) * (basis // 128)
                    put(at, grads[0:1])
                    put(small_rows + at, grads[1:2])
                    pl.when(h == 1)(finish_pair)
                for step in range(2 * pairs):
                    at_step = AFTER + 3 + step * blocks + qb
                    if at_step in PLAN:

                        @pl.when(2 * i + h == step)
                        def _(at_step=at_step):
                            act(at_step)

            return carry

        lax.fori_loop(0, 2, head_step, 0)
        return carry

    lax.fori_loop(0, pairs, pair_step, 0)

    ready(12, 13, 14)
    for j in range(2):
        swap(4, j).wait_send()
        r.tx[half_at(j), :] = mm(r.active[rows_at(j, 1 - core), : 3 * wide], r.wqkv_v[...], NT)
        swap(5, j).start()
    for j in range(2):
        r.mixed[half_at(j), :] = mm(r.active[rows_at(j, core), : 3 * wide], r.wqkv_v[...], NT)

    act(AFTER + 27)
    def norm_one(i, carry):
        at = pl.ds(pl.multiple_of(i * chunk, chunk), chunk)
        gy = r.mixed[at, :] + r.rx[at, :]
        gx, dg, db = norm_back(r.hid_own[at, :].astype(f32), gy, r.gain1[...])
        total = r.gm[at, :] + gx
        r.gm[at, :] = total
        r.n2[at, :] = total.astype(bf16)
        return carry[0] + dg, carry[1] + db

    for j in range(2):
        swap(5, j).wait_recv()
    sums = lax.fori_loop(
        0, 2 * block // chunk, norm_one, (jnp.zeros((1, width), f32), jnp.zeros((1, width), f32))
    )
    put(base_ln1, sums[0])
    put(base_ln1 + width_rows, sums[1])
    gin_keep().start()
    gin_copy().start()
    act(AFTER + 28)
    gin_copy().wait()
    r.rx[half_at(0), :] = r.gi_rx[...].astype(f32)
    gin_place().start()
    out_copy().wait()
    out_keep().wait()
    gin_keep().wait()
    gin_place().wait()
    for j in range(2):
        for n in (3, 5):
            swap(n, j).wait_send()


def tail_call(held, given):
    g = SimpleNamespace(**held, **given)
    tokens, width = g.cot.shape
    wide = width // 2
    ff = g.expand.shape[1] // 2
    heads = wide // 64
    basis = g.mkv.shape[0]
    half, block = tokens // 2, tokens // 4
    used = 2 * (wide // 64) * basis // 128 + ff // 128 + 5 * (width // 128)
    sv_rows = -(-used // 128) * 128
    shape = jax.ShapeDtypeStruct
    like = lambda a: pltpu.VMEM(a.shape, a.dtype)
    outs = dict(
        o_down=shape((2, ff, width), bf16),
        o_up=shape((2, width, ff), bf16),
        o_out=shape((2, width, wide), bf16),
        o_0=shape((2, width, wide), bf16),
        o_1=shape((2, width, wide), bf16),
        o_2=shape((2, width, wide), bf16),
        o_s=shape((2, sv_rows, 128), f32),
        out=shape((2, block, width), bf16),
        gin=shape((2, block, width), f32),
    )
    scratch = dict(
        ex=pltpu.SemaphoreType.DMA((2, 14)),
        loc=pltpu.SemaphoreType.DMA((20,)),
        ctx_v=like(g.ctx),
        wo_own=pltpu.VMEM((wide, width), bf16),
        hid_own=pltpu.VMEM((half, width), bf16),
        e_v=pltpu.VMEM((width, ff), bf16),
        d_v=pltpu.VMEM((ff, width), bf16),
        cot_v=like(g.cot),
        qkv_v=like(g.qkv),
        mkv_v=like(g.mkv),
        att_v=like(g.att),
        norm_v=like(g.normed),
        normed_v=pltpu.VMEM((width, tokens), bf16),
        coeff_v=like(g.coeff),
        wqkv_v=like(g.w_qkv),
        mixed=pltpu.VMEM((half, width), f32),
        n2=pltpu.VMEM((tokens, width), bf16),
        active=pltpu.VMEM((tokens, ff), bf16),
        gup=pltpu.VMEM((tokens, ff), bf16),
        g_down=pltpu.VMEM((ff, width), bf16),
        g_up=pltpu.VMEM((width, ff), bf16),
        tx=pltpu.VMEM((half, width), f32),
        rx=pltpu.VMEM((half, width), f32),
        rx_out=pltpu.VMEM((half, width), f32),
        gm=pltpu.VMEM((half, width), f32),
        gml=pltpu.VMEM((tokens, width), bf16),
        bo=pltpu.VMEM((half, width), bf16),
        gi_rx=pltpu.VMEM((block, width), bf16),
        do=pltpu.VMEM((tokens, wide), bf16),
        part=pltpu.VMEM((tokens, 384), bf16),
        part_mem=pltpu.VMEM((basis, 256), bf16),
        dka=pltpu.VMEM((tokens, 128), f32),
        dva=pltpu.VMEM((tokens, 128), f32),
        dqt=pltpu.VMEM((128, tokens), f32),
        gmva=pltpu.VMEM((basis, 128), f32),
        gmk=pltpu.VMEM((basis, 128), f32),
        k_t=pltpu.VMEM((128, tokens), bf16),
        do_t=pltpu.VMEM((128, tokens), f32),
        sv=pltpu.VMEM((sv_rows, 128), f32),
        gain1=pltpu.VMEM((1, width), f32),
        gain2=pltpu.VMEM((1, width), f32),
        bias_d=pltpu.VMEM((1, width), f32),
        bias_u=pltpu.VMEM((1, ff), f32),
        musg=pltpu.VMEM((heads, 8, basis), f32),
    )
    more = []
    shapes = []
    for span in SPANS:
        shapes += [(span, width, bf16), (width, span, bf16)]
    shapes += [(width, wide, bf16)] * 4 + [(sv_rows, 128, f32)]
    for item in shapes:
        more += Reducer.scratch(*item)
    hbm, vmem = pl.BlockSpec(memory_space=pl.ANY), pl.BlockSpec(memory_space=pltpu.VMEM)
    names = list(held) + list(given) + list(outs) + list(scratch)
    return pl.pallas_call(
        functools.partial(tail_kernel, names),
        in_specs=[hbm] * len(held) + [vmem] * len(given),
        out_specs=[hbm] * len(outs),
        out_shape=list(outs.values()),
        scratch_shapes=list(scratch.values()) + more,
        compiler_params=pltpu.CompilerParams(
            vmem_limit_bytes=60 * 1024 * 1024, collective_id=1, has_side_effects=True
        ),
        name="tail",
    )(*held.values(), *given.values())


def as_row(ref):
    return ref[...].reshape(1, ref.shape[0])


def fill_heads(dst, mu, sigma, core):
    heads = dst.shape[0]
    dst[...] = jnp.zeros_like(dst)
    for h in range(heads):
        for n, src in enumerate((mu, sigma)):
            dst[h, n : n + 1, :] = src[pl.ds(core * heads + h, 1), :]


def sweep_inverse(a):
    n = a.shape[0]
    lane = lax.broadcasted_iota(jnp.int32, (8, n), 1)
    sub = lax.broadcasted_iota(jnp.int32, (8, n), 0)
    groups = [a[8 * g : 8 * g + 8, :] for g in range(n // 8)]

    def inverse_two(p, q, t):
        inv = 1.0 / (p * t - q * q)
        return t * inv, -q * inv, p * inv

    for k in range(0, n, 4):
        own, at = groups[k // 8], k % 8
        rows = [jnp.broadcast_to(own[at + i : at + i + 1, :], (8, n)) for i in range(4)]
        d = {
            (i, j): jnp.broadcast_to(rows[i][:, k + j : k + j + 1], (8, n))
            for i in range(4)
            for j in range(i, 4)
        }
        a0, a1, a2 = inverse_two(d[0, 0], d[0, 1], d[1, 1])
        w = [
            [a0 * d[0, 2] + a1 * d[1, 2], a0 * d[0, 3] + a1 * d[1, 3]],
            [a1 * d[0, 2] + a2 * d[1, 2], a1 * d[0, 3] + a2 * d[1, 3]],
        ]
        s0 = d[2, 2] - (d[0, 2] * w[0][0] + d[1, 2] * w[1][0])
        s1 = d[2, 3] - (d[0, 2] * w[0][1] + d[1, 2] * w[1][1])
        s2 = d[3, 3] - (d[0, 3] * w[0][1] + d[1, 3] * w[1][1])
        s0, s1, s2 = inverse_two(s0, s1, s2)
        v = [[w[i][0] * s0 + w[i][1] * s1, w[i][0] * s1 + w[i][1] * s2] for i in range(2)]
        p00 = a0 + v[0][0] * w[0][0] + v[0][1] * w[0][1]
        p01 = a1 + v[0][0] * w[1][0] + v[0][1] * w[1][1]
        p11 = a2 + v[1][0] * w[1][0] + v[1][1] * w[1][1]
        p = [
            [p00, p01, -v[0][0], -v[0][1]],
            [p01, p11, -v[1][0], -v[1][1]],
            [-v[0][0], -v[1][0], s0, s1],
            [-v[0][1], -v[1][1], s1, s2],
        ]
        new = []
        for i in range(4):
            row = p[i][0] * rows[0] + p[i][1] * rows[1] + p[i][2] * rows[2] + p[i][3] * rows[3]
            for j in range(4):
                row = jnp.where(lane == k + j, p[i][j], row)
            new.append(row)
        inside = (lane >= k) & (lane < k + 4)
        for g in range(n // 8):
            old = groups[g]
            cols = [jnp.broadcast_to(old[:, k + j : k + j + 1], (8, n)) for j in range(4)]
            part = (cols[0] * new[0] + cols[1] * new[1]) + (cols[2] * new[2] + cols[3] * new[3])
            fresh = jnp.where(inside, 0.0, old) - part
            if g == k // 8:
                for i in range(4):
                    fresh = jnp.where(sub == at + i, new[i], fresh)
            groups[g] = fresh
    return jnp.concatenate(groups, 0)


KB = 128


def front_kernel(names, *refs):
    r = SimpleNamespace(**dict(zip(names, refs)))
    place = Place()
    y, core = place.y, place.core
    tokens, width = r.hid_v.shape
    block = tokens // 4
    wide = width // 2
    pairs = wide // 128
    basis = r.mkv_v.shape[0]
    half = basis // 2
    ex, loc = r.ex, r.loc
    flows = [(r.inputs, r.hid_v), (r.previous, r.prev), (r.cotangent, r.cot)]

    def rows_at(yy, cc):
        return pl.ds(pl.multiple_of((2 * yy + cc) * block, block), block)

    def along(n):
        src, dst = flows[n]
        return remote(src.at[1 - y], dst.at[rows_at(y, core)], ex, n, place.peer_y)

    def across(n):
        src, dst = flows[n]
        return remote(src.at[y], dst.at[rows_at(y, core)], ex, 3 + n, place.peer_core)

    def onward(n):
        part = flows[n][1].at[rows_at(1 - y, core)]
        return remote(part, part, ex, 6 + n, place.peer_core)

    def keep(n):
        src, dst = flows[n]
        return pltpu.make_async_copy(src.at[y], dst.at[rows_at(y, core)], loc.at[n])

    def weight(n):
        src = (r.wq, r.wk, r.wv)[n].at[:, pl.ds(pl.multiple_of(core * wide, 128), wide)]
        return pltpu.make_async_copy(src, r.w_v.at[:, n * wide : n * wide + wide], loc.at[3 + n])

    def projection(n):
        c = core if n == 0 else 1 - core
        src = r.wo.at[pl.ds(pl.multiple_of(c * wide, 128), wide)]
        return pltpu.make_async_copy(src, r.wo_v.at[n], loc.at[17 + n])

    results = [
        (r.w_v, r.w_qkv),
        (r.hid_v, r.hidden),
        (r.normed, r.normed_out),
        (r.qkv_v, r.qkv),
        (r.mkv_v, r.mkv),
        (r.coeff_v, r.coeff),
        (r.att_v, r.att),
        (r.ctx_v, r.ctx),
        (r.mix_v, r.mixed),
    ]

    def result(n):
        return pltpu.make_async_copy(*results[n], loc.at[6 + n])

    barrier = pltpu.get_barrier_semaphore()
    for peer in (place.peer_y, place.peer_core):
        pl.semaphore_signal(barrier, inc=1, device_id=peer, device_id_type=pl.DeviceIdType.MESH)
    r.gain1[...] = as_row(r.ln1_gain)
    r.bias1[...] = as_row(r.ln1_bias)
    r.gain2[...] = as_row(r.ln2_gain)
    r.bias2[...] = as_row(r.ln2_bias)
    fill_heads(r.musg, r.mu, r.sigma, core)

    spread = 1.0 / basis
    centers = (lax.broadcasted_iota(jnp.int32, (basis, 1), 0).astype(f32) + 0.5) / basis
    places = (r.sticky[pl.ds(y, 1), :].astype(f32) + 0.5) / tokens
    features = jnp.exp(-((places - centers) ** 2) / (2.0 * spread * spread)).astype(bf16)
    same = lax.broadcasted_iota(jnp.int32, (basis, basis), 0) == lax.broadcasted_iota(
        jnp.int32, (basis, basis), 1
    )
    a_ref, i_ref = r.a, r.i
    a_ref[...] = mm(features, features, NT) + jnp.where(same, ridge_weight, 0.0)
    pl.semaphore_wait(barrier, 2)
    along(0).start()
    across(0).start()
    keep(0).start()
    along(1).start()
    for n in range(3):
        weight(n).start()
    for n in range(2):
        projection(n).start()
    across(1).start()
    keep(1).start()
    along(2).start()
    across(2).start()
    keep(2).start()

    r.schur[...] = a_ref[:half, :half]

    def eliminate(n, carry):
        i_ref[n] = sweep_inverse(r.schur[...])

        @pl.when(n == 0)
        def _():
            cross = a_ref[:half, half:]
            r.cross[...] = mm(i_ref[0], cross, precision=highest)
            r.schur[...] = a_ref[half:, half:] - mm(cross, r.cross[...], TN, precision=highest)

        return carry

    lax.fori_loop(0, 2, eliminate, 0)

    chunk = 64

    def project(yy, cc):
        def body(i, carry):
            at = pl.ds(pl.multiple_of((2 * yy + cc) * block + i * chunk, chunk), chunk)
            normed = layer_norm(r.hid_v[at, :].astype(f32), r.gain1[...], r.bias1[...])
            r.normed[at, :] = normed.astype(bf16)
            return carry

        lax.fori_loop(0, block // chunk, body, 0)
        at = rows_at(yy, cc)
        r.qkv_v[at, :] = mm(r.normed[at, :], r.w_v[...]).astype(bf16)

    keep(0).wait()
    for n in range(3):
        weight(n).wait()
    result(0).start()
    project(y, core)
    across(0).wait_recv()
    project(y, 1 - core)
    index = lax.broadcasted_iota(jnp.int32, (tokens, r.picks.shape[1]), 0)
    chosen = jnp.where(index == r.picks[pl.ds(y, 1), :], 1.0, 0.0).astype(bf16)
    shares = mm(features, chosen, NT)
    high = shares.astype(bf16)
    rest = shares - high.astype(f32)
    middle = rest.astype(bf16)
    r.shares[0] = high
    r.shares[1] = middle
    r.shares[2] = (rest - middle.astype(f32)).astype(bf16)

    along(0).wait_recv()
    onward(0).start()
    project(1 - y, core)
    onward(0).wait_recv()
    project(1 - y, 1 - core)
    result(1).start()
    result(2).start()
    result(3).start()

    allowed = causal_block(QB)
    blocks = tokens // QB
    split = QB // KB

    def lanes_of(i, j):
        return pl.ds(pl.multiple_of(i * 128 + j * wide, 128), 128)

    def causal_pair(i, carry):
        q_ref, k_ref, v_ref = (r.qkv_v.at[:, lanes_of(i, j)] for j in range(3))
        r.v_t[...] = turn(v_ref[...]).astype(bf16)
        def causal_head(h, carry):
            mask = head_mask(h)
            rows = head_rows(h)
            for qb in range(blocks):
                cols = slice(qb * QB, qb * QB + QB)
                q = jnp.where(mask, q_ref[cols, :].astype(f32) * 0.125, 0.0).astype(bf16)
                top = None
                for kb in range((qb + 1) * split):
                    keys = slice(kb * KB, kb * KB + KB)
                    s = mm(k_ref[keys, :], q, NT)
                    if kb >= qb * split:
                        at = (kb - qb * split) * KB
                        s = jnp.where(allowed[at : at + KB], s, masked_score)
                    r.s[keys, :] = s
                    best = jnp.max(s, axis=0, keepdims=True)
                    top = best if top is None else jnp.maximum(top, best)
                denom = jnp.zeros_like(top)
                out = jnp.zeros((64, QB), f32)
                for kb in range((qb + 1) * split):
                    keys = slice(kb * KB, kb * KB + KB)
                    e = jnp.exp(r.s[keys, :] - top)
                    denom = denom + jnp.sum(e, axis=0, keepdims=True)
                    out = out + mm(r.v_t[rows, keys], e.astype(bf16))
                r.att_v[i, rows, cols] = out / denom
                r.lse[i, pl.ds(h, 1), cols] = top + jnp.log(denom)
            return carry

        lax.fori_loop(0, 2, causal_head, 0)
        return carry

    lax.fori_loop(0, pairs - 1, causal_pair, 0)
    along(1).wait_recv()
    onward(1).start()
    lax.fori_loop(pairs - 1, pairs, causal_pair, 0)
    result(6).start()
    across(1).wait_recv()
    keep(1).wait()
    onward(1).wait_recv()
    prev = r.prev[...]
    side = mm(r.shares[0], prev) + (mm(r.shares[1], prev) + mm(r.shares[2], prev))
    low_part = mm(
        i_ref[1], side[half:] - mm(r.cross[...], side[:half], TN, precision=highest), precision=highest
    )
    r.coeff_v[half:, :] = low_part.astype(bf16)
    r.coeff_v[:half, :] = (
        mm(i_ref[0], side[:half], precision=highest) - mm(r.cross[...], low_part, precision=highest)
    ).astype(bf16)
    r.mkv_v[...] = mm(r.coeff_v[...], r.w_v[:, wide:]).astype(bf16)
    result(4).start()
    result(5).start()

    def memory_pair(i, carry):
        q_ref = r.qkv_v.at[:, lanes_of(i, 0)]
        mk_ref, mv_ref = (r.mkv_v.at[:, lanes_of(i, j)] for j in range(2))
        r.mv_t[...] = turn(mv_ref[...]).astype(bf16)
        def memory_head(h, carry):
            rows = head_rows(h)
            u, b, centre, total = place_params(q_ref[...], mk_ref[...], r.musg[2 * i + h], head_mask(h), basis)
            scale = spread * lax.rsqrt(total)
            fall = -0.5 / total
            for qb in range(blocks):
                cols = slice(qb * QB, qb * QB + QB)
                gap = centre[:, cols] - centers
                dens = (scale[:, cols] * jnp.exp(gap * gap * fall[:, cols])).astype(bf16)
                r.o[rows, cols] = r.att_v[i, rows, cols] + mm(r.mv_t[rows, :], dens)
            return carry

        lax.fori_loop(0, 2, memory_head, 0)
        r.ctx_v[:, lanes_of(i, 0)] = jnp.transpose(r.o[...]).astype(bf16)
        for j in range(2):
            context(i, j).start()
        return carry

    def half_at(j):
        return pl.ds(j * block, block)

    def context(i, j):
        src = r.ctx_v.at[rows_at(j, 1 - core), lanes_of(i, 0)]
        return remote(src, r.ctx_rx.at[half_at(j), lanes_of(i, 0)], ex, 9 + 2 * i + j, place.peer_core)

    def second(j):
        part = r.n2_v.at[half_at(j)]
        return remote(part, r.n2.at[rows_at(j, core)], ex, 9 + 2 * pairs + j, place.peer_core)

    def second_keep(j):
        return pltpu.make_async_copy(r.n2_v.at[half_at(j)], r.n2.at[rows_at(j, core)], loc.at[15 + j])

    lax.fori_loop(0, pairs - 1, memory_pair, 0)
    along(2).wait_recv()
    onward(2).start()
    lax.fori_loop(pairs - 1, pairs, memory_pair, 0)
    result(7).start()
    for n in range(2):
        projection(n).wait()

    for j in range(2):
        own = mm(r.ctx_v[rows_at(j, core), :], r.wo_v[0])
        r.mix_v[half_at(j), :] = r.hid_v[rows_at(j, core), :].astype(f32) + own
    for j in range(2):
        for i in range(pairs):
            context(i, j).wait_recv()
        r.mix_v[half_at(j), :] += mm(r.ctx_rx[half_at(j), :], r.wo_v[1])

        def norm_chunk(i, carry, j=j):
            at = pl.ds(pl.multiple_of(j * block + i * chunk, chunk), chunk)
            r.n2_v[at, :] = layer_norm(r.mix_v[at, :], r.gain2[...], r.bias2[...]).astype(bf16)
            return carry

        lax.fori_loop(0, block // chunk, norm_chunk, 0)
        second(j).start()
        second_keep(j).start()
    result(8).start()
    keep(2).wait()
    across(2).wait_recv()
    onward(2).wait_recv()
    for j in range(2):
        second(j).wait()
        second_keep(j).wait()
        for i in range(pairs):
            context(i, j).wait_send()
    for n in range(3):
        along(n).wait_send()
        across(n).wait_send()
        onward(n).wait_send()
    for n in range(len(results)):
        result(n).wait()


def front_call(held, given, basis):
    block, width = held[next(iter(held))].shape[1:]
    tokens = block * 4
    wide = width // 2
    pairs = wide // 128
    shape = jax.ShapeDtypeStruct
    outs = dict(
        hidden=shape((tokens, width), bf16),
        normed_out=shape((tokens, width), bf16),
        qkv=shape((tokens, 3 * wide), bf16),
        mkv=shape((basis, width), bf16),
        coeff=shape((basis, width), bf16),
        w_qkv=shape((width, 3 * wide), bf16),
        cot=shape((tokens, width), bf16),
        ctx=shape((tokens, wide), bf16),
        att=shape((pairs, 128, tokens), f32),
        mixed=shape((tokens // 2, width), f32),
        n2=shape((tokens, width), bf16),
    )
    near = dict(lse=shape((pairs, 2, tokens), f32))
    like = lambda a: pltpu.VMEM(a.shape, a.dtype)
    o = SimpleNamespace(**outs)
    scratch = dict(
        ex=pltpu.SemaphoreType.DMA((2, 11 + 2 * pairs)),
        loc=pltpu.SemaphoreType.DMA((19,)),
        hid_v=like(o.hidden),
        qkv_v=like(o.qkv),
        mkv_v=like(o.mkv),
        coeff_v=like(o.coeff),
        w_v=like(o.w_qkv),
        ctx_v=like(o.ctx),
        att_v=like(o.att),
        mix_v=like(o.mixed),
        n2_v=pltpu.VMEM((tokens // 2, width), bf16),
        ctx_rx=pltpu.VMEM((tokens // 2, wide), bf16),
        wo_v=pltpu.VMEM((2, wide, width), bf16),
        gain2=pltpu.VMEM((1, width), f32),
        bias2=pltpu.VMEM((1, width), f32),
        prev=pltpu.VMEM((tokens, width), bf16),
        normed=pltpu.VMEM((tokens, width), bf16),
        a=pltpu.VMEM((basis, basis), f32),
        i=pltpu.VMEM((2, basis // 2, basis // 2), f32),
        cross=pltpu.VMEM((basis // 2, basis // 2), f32),
        schur=pltpu.VMEM((basis // 2, basis // 2), f32),
        shares=pltpu.VMEM((3, basis, tokens), bf16),
        gain1=pltpu.VMEM((1, width), f32),
        bias1=pltpu.VMEM((1, width), f32),
        musg=pltpu.VMEM((2 * pairs, 8, basis), f32),
        s=pltpu.VMEM((tokens, QB), f32),
        v_t=pltpu.VMEM((128, tokens), bf16),
        mv_t=pltpu.VMEM((128, basis), bf16),
        o=pltpu.VMEM((128, tokens), f32),
    )
    hbm, vmem = pl.BlockSpec(memory_space=pl.ANY), pl.BlockSpec(memory_space=pltpu.VMEM)
    names = list(held) + list(given) + list(outs) + list(near) + list(scratch)
    return pl.pallas_call(
        functools.partial(front_kernel, names),
        in_specs=[hbm] * len(held) + [vmem] * len(given),
        out_specs=[hbm] * len(outs) + [vmem] * len(near),
        out_shape=list(outs.values()) + list(near.values()),
        scratch_shapes=list(scratch.values()),
        compiler_params=vmem_params(collective_id=2, has_side_effects=True),
        name="front",
    )(*held.values(), *given.values())


def finish(down, up, out_t, parts, small, basis):
    ff = 2 * up.shape[2]
    width = out_t.shape[1]
    per = basis // 128
    heads = width // 64
    steps = width // 128
    per_core = steps // 2
    tall = down.shape[1] // per_core
    wide = width // 2

    def body(down_ref, up_ref, t_ref, s_ref, *refs):
        o_down, o_up, o_q, o_k, o_v, o_o, o_mu, o_sg, o_bias, *o_rows = refs[len(parts) :]
        start = heads * per
        count = ff // 256
        for c in range(2):
            row = [s_ref[c, start + t : start + t + 1, :] for t in range(count)]
            o_bias[c * (ff // 2) : (c + 1) * (ff // 2)] = jnp.concatenate(row, 1).reshape(ff // 2)
        start = start + count
        for n, ref in enumerate(o_rows):
            row = []
            for t in range(width // 128):
                first = s_ref[0, start + t : start + t + 1, :]
                row.append(first + s_ref[1, start + t : start + t + 1, :] if n else first)
            ref[...] = jnp.concatenate(row, 1).reshape(width)
            start = start + width // 128
        for n, ref in enumerate((o_mu, o_sg)):
            for h in range(heads):
                for t in range(per):
                    row = n * (heads // 2) * per + h % (heads // 2) * per + t
                    here = slice(t * 128, t * 128 + 128)
                    ref[h : h + 1, here] = s_ref[h // (heads // 2), row : row + 1, :]
        o_down[...] = down_ref[0].astype(f32)
        n = up_ref.shape[2]
        for c in range(2):
            o_up[:, c * n : c * n + n] = up_ref[c].astype(f32)
            for i, ref in enumerate(refs[: len(parts)]):
                here = slice(c * wide + i * 128, c * wide + i * 128 + 128)
                o_q[:, here] = ref[c, :, 0:128].astype(f32)
                o_k[:, here] = ref[c, :, 128:256].astype(f32)
                o_v[:, here] = ref[c, :, 256:384].astype(f32)
        o_o[...] = jnp.transpose(t_ref[0].astype(f32))

    row = lambda n: pl.BlockSpec((128, n), lambda i: (i, 0))
    shape = jax.ShapeDtypeStruct
    return pl.pallas_call(
        body,
        grid=(steps,),
        in_specs=[
            pl.BlockSpec((1, tall, width), lambda i: (i // per_core, i % per_core, 0)),
            pl.BlockSpec((2, 128, up.shape[2]), lambda i: (0, i, 0)),
            pl.BlockSpec((1, width, 128), lambda i: (i // per_core, 0, i % per_core)),
            pl.BlockSpec(small.shape, lambda i: (0, 0, 0)),
        ]
        + [pl.BlockSpec((2, 128, 384), lambda i: (0, i, 0))] * len(parts),
        out_specs=[pl.BlockSpec((tall, width), lambda i: (i, 0)), row(2 * up.shape[2])]
        + [row(width)] * 4
        + [pl.BlockSpec((heads, basis), lambda i: (0, 0))] * 2
        + [pl.BlockSpec((ff,), lambda i: (0,))]
        + [pl.BlockSpec((width,), lambda i: (0,))] * 5,
        out_shape=[
            shape((2 * down.shape[1], width), f32),
            shape((width, 2 * up.shape[2]), f32),
        ]
        + [shape((width, width), f32)] * 4
        + [shape((heads, basis), f32)] * 2
        + [shape((ff,), f32)]
        + [shape((width,), f32)] * 5,
        compiler_params=vmem_params(),
        name="finish",
    )(down, up, out_t, small, *parts)


def chip_local(
    inputs,
    previous,
    memory_rows,
    sticky_positions,
    cotangent,
    ln1_gain,
    ln1_bias,
    query_weight,
    key_weight,
    value_weight,
    out_weight,
    mu_weight,
    sigma_weight,
    ln2_gain,
    ln2_bias,
    expand_weight,
    up_bias,
    down_weight,
    down_bias,
):
    width = inputs.shape[2]
    heads, basis = mu_weight.shape
    ff = up_bias.shape[0]
    params = dict(ln1_gain=ln1_gain, ln2_gain=ln2_gain, mu=mu_weight, sigma=sigma_weight)
    hidden, normed, qkv, mkv, coeff, w_qkv, cot, ctx, att, mixed, n2, lse = front_call(
        dict(
            inputs=inputs,
            previous=previous,
            cotangent=cotangent,
            wq=query_weight,
            wk=key_weight,
            wv=value_weight,
            wo=out_weight,
        ),
        dict(picks=memory_rows, sticky=sticky_positions, ln1_bias=ln1_bias, ln2_bias=ln2_bias, **params),
        basis,
    )
    o_down, o_up, o_out, o_0, o_1, o_2, o_s, block_output, grad_inputs = tail_call(
        dict(
            cot=cot,
            n2_in=n2,
            mixed_in=mixed,
            hidden=hidden,
            ctx=ctx,
            expand=expand_weight,
            down=down_weight,
            w_out=out_weight,
            qkv=qkv,
            mkv=mkv,
            att=att,
            normed=normed,
            coeff=coeff,
            w_qkv=w_qkv,
        ),
        dict(lse=lse, up_bias=up_bias, down_bias=down_bias, **params),
    )
    g_down, g_up, g_q, g_k, g_v, g_o, g_mu, g_sigma, g_bias, g_db, g_g2, g_b2, g_g1, g_b1 = finish(
        o_down, o_up, o_out, (o_0, o_1, o_2), o_s, basis
    )
    return (
        block_output,
        grad_inputs,
        g_g1,
        g_b1,
        g_q,
        g_k,
        g_v,
        g_o,
        g_mu,
        g_sigma,
        g_g2,
        g_b2,
        g_up,
        g_bias,
        g_down,
        g_db,
    )


def pick(mesh):
    def step(*arrays):
        inputs, mu = arrays[0], arrays[11]
        fits = (
            mesh.shape[BATCH] == 8
            and mesh.shape[BLK] == 4
            and inputs.shape[0] == 2
            and inputs.shape[1] % QB == 0
            and mu.shape[0] % 4 == 0
            and inputs.shape[2] == mu.shape[0] * 64
        )
        return (chip_local if fits else general)(*arrays)

    return step


def solution(mesh):
    return jax.shard_map(
        pick(mesh),
        mesh=mesh,
        in_specs=(
            P(BATCH, BLK, None),
            P(BATCH, BLK, None),
            P(BATCH, None),
            P(BATCH, None),
            P(BATCH, BLK, None),
            P(),
            P(),
            P(),
            P(),
            P(),
            P(),
            P(),
            P(),
            P(),
            P(),
            P(),
            P(),
            P(),
            P(),
        ),
        out_specs=(
            P(BATCH, BLK, None),
            P(BATCH, BLK, None),
            P(),
            P(),
            P(),
            P(),
            P(),
            P(),
            P(),
            P(),
            P(),
            P(),
            P(),
            P(),
            P(),
            P(),
        ),
        check_vma=False,
    )
```

```python
import functools
from types import SimpleNamespace

import jax
import jax.numpy as jnp
from jax import lax
from jax.experimental import pallas as pl
from jax.experimental.pallas import tpu as pltpu
from jax.sharding import PartitionSpec as P

epsilon = 1e-05
ridge_weight = 1.0
var_scale = 0.01
masked_score = -1e30
BLK = "blk"
BATCH = "batch"
highest = lax.Precision.HIGHEST


def layer_norm(values, gain, bias):
    center = jnp.mean(values, axis=-1, keepdims=True)
    shifted = values - center
    spread_sq = jnp.mean(shifted * shifted, axis=-1, keepdims=True)
    return shifted * lax.rsqrt(spread_sq + epsilon) * gain + bias


def density(scores, mu_row, sigma_row):
    count = scores.shape[-1]
    centers = (jnp.arange(count, dtype=scores.dtype) + 0.5) / count
    spread = 1.0 / count
    centre = jax.nn.sigmoid(jnp.dot(scores, mu_row, precision=highest))
    variance = var_scale * jax.nn.softplus(jnp.dot(scores, sigma_row, precision=highest))
    total = spread * spread + variance
    return (spread * lax.rsqrt(total))[..., None] * jnp.exp(
        -((centre[..., None] - centers) ** 2) / (2.0 * total[..., None])
    )


def project(source, weight):
    return jnp.einsum("std,de->ste", source, weight, preferred_element_type=jnp.float32)


def weight_grad(source, grads):
    return jnp.einsum("std,ste->de", source, grads, preferred_element_type=jnp.float32)


def back_project(grads, weight):
    return jnp.einsum("ste,de->std", grads, weight, preferred_element_type=jnp.float32)


def gelu_tanh(values):
    return jax.nn.gelu(values, approximate=True)


def general(
    inputs,
    previous,
    memory_rows,
    sticky_positions,
    cotangent,
    ln1_gain,
    ln1_bias,
    query_weight,
    key_weight,
    value_weight,
    out_weight,
    mu_weight,
    sigma_weight,
    ln2_gain,
    ln2_bias,
    expand_weight,
    up_bias,
    down_weight,
    down_bias,
):
    seg_count, tok_rows, model_width = inputs.shape
    blocks = lax.axis_size(BLK)
    length = tok_rows * blocks
    first_row = lax.axis_index(BLK) * tok_rows
    head_count, basis_count = mu_weight.shape
    head_width = model_width // head_count
    centers = (jnp.arange(basis_count, dtype=jnp.float32) + 0.5) / basis_count
    spread = 1.0 / basis_count
    places = (sticky_positions.astype(jnp.float32) + 0.5) / length
    features = jnp.exp(-((places[..., None] - centers) ** 2) / (2.0 * spread * spread)).astype(
        jnp.bfloat16
    )
    local_index = memory_rows - first_row
    owned_rows = (local_index >= 0) & (local_index < tok_rows)
    picked = jax.vmap(lambda shard_rows, row_index: shard_rows[row_index])(
        previous, jnp.clip(local_index, 0, tok_rows - 1)
    )
    picked = jnp.where(owned_rows[..., None], picked, jnp.zeros_like(picked))
    own_features = jnp.where(owned_rows[..., None], features, jnp.zeros_like(features))
    side_part = jnp.einsum("smn,smd->snd", own_features, picked, preferred_element_type=jnp.float32)
    gram_part = jnp.einsum(
        "smn,smk->snk", own_features, own_features, preferred_element_type=jnp.float32
    )
    gram_sum, right_side = lax.psum((gram_part, side_part), BLK)
    system = gram_sum + ridge_weight * jnp.eye(basis_count, dtype=jnp.float32)
    factor = jnp.linalg.cholesky(system)
    coefficients = jax.scipy.linalg.cho_solve((factor, True), right_side)
    coeff_low = coefficients.astype(jnp.bfloat16)
    hidden_in = inputs.astype(jnp.float32)
    normed_low = layer_norm(hidden_in, ln1_gain, ln1_bias).astype(jnp.bfloat16)
    queries = project(normed_low, query_weight).astype(jnp.bfloat16)
    keys_local = project(normed_low, key_weight).astype(jnp.bfloat16)
    values_local = project(normed_low, value_weight).astype(jnp.bfloat16)
    mem_keys = project(coeff_low, key_weight).astype(jnp.bfloat16)
    mem_values = project(coeff_low, value_weight).astype(jnp.bfloat16)
    all_keys, all_values = (
        lax.all_gather(keys_local, BLK, axis=1, tiled=True),
        lax.all_gather(values_local, BLK, axis=1, tiled=True),
    )

    def split_heads(array):
        return array.reshape(array.shape[0], array.shape[1], head_count, head_width).transpose(
            2, 0, 1, 3
        )

    def merge_heads(array):
        return array.transpose(1, 2, 0, 3).reshape(array.shape[1], array.shape[2], model_width)

    query_pos = first_row + jnp.arange(tok_rows)
    key_pos = jnp.arange(length)
    causal = key_pos[None, :] <= query_pos[:, None]

    def forward_head(operands):
        query_h, key_h, value_h, memkey_h, memval_h, mu_row, sigma_row = operands
        scores = (
            jnp.einsum("sqd,skd->sqk", query_h, key_h, preferred_element_type=jnp.float32) * 0.125
        )
        scores = jnp.where(causal, scores, masked_score)
        top = jnp.max(scores, axis=-1, keepdims=True)
        raised = jnp.exp(scores - top)
        total = jnp.sum(raised, axis=-1, keepdims=True)
        probs = raised / total
        log_total = (top + jnp.log(total))[..., 0]
        attended = jnp.einsum(
            "sqk,skd->sqd", probs.astype(jnp.bfloat16), value_h, preferred_element_type=jnp.float32
        )
        memory_scores = (
            jnp.einsum("sqd,snd->sqn", query_h, memkey_h, preferred_element_type=jnp.float32)
            * 0.125
        )
        weights_mem = density(memory_scores, mu_row, sigma_row)
        recalled = jnp.einsum(
            "sqn,snd->sqd",
            weights_mem.astype(jnp.bfloat16),
            memval_h,
            preferred_element_type=jnp.float32,
        )
        return (attended + recalled, log_total)

    head_queries = split_heads(queries)
    head_keys = split_heads(all_keys)
    value_per_head = split_heads(all_values)
    head_memkeys = split_heads(mem_keys)
    head_memvals = split_heads(mem_values)
    heads_ctx, log_totals = lax.map(
        forward_head,
        (
            head_queries,
            head_keys,
            value_per_head,
            head_memkeys,
            head_memvals,
            mu_weight,
            sigma_weight,
        ),
    )
    context_low = merge_heads(heads_ctx).astype(jnp.bfloat16)
    mixed = hidden_in + project(context_low, out_weight)
    normed_two_low = layer_norm(mixed, ln2_gain, ln2_bias).astype(jnp.bfloat16)
    hidden_up = (
        jnp.einsum("std,df->stf", normed_two_low, expand_weight, preferred_element_type=jnp.float32)
        + up_bias
    )
    active_low = gelu_tanh(hidden_up).astype(jnp.bfloat16)
    result = (
        mixed
        + jnp.einsum("stf,fd->std", active_low, down_weight, preferred_element_type=jnp.float32)
        + down_bias
    )
    block_output = result.astype(jnp.bfloat16)
    grad_result = cotangent.astype(jnp.float32)
    grad_down_bias = jnp.sum(grad_result, axis=(0, 1))
    grad_down_weight = jnp.einsum(
        "stf,std->fd", active_low, cotangent, preferred_element_type=jnp.float32
    )
    grad_active = jnp.einsum(
        "std,fd->stf", cotangent, down_weight, preferred_element_type=jnp.float32
    )
    gelu_value, gelu_pull = jax.vjp(gelu_tanh, hidden_up)
    grad_up_low = gelu_pull(grad_active)[0].astype(jnp.bfloat16)
    grad_up_bias = jnp.sum(grad_up_low.astype(jnp.float32), axis=(0, 1))
    grad_up_weight = jnp.einsum(
        "std,stf->df", normed_two_low, grad_up_low, preferred_element_type=jnp.float32
    )
    grad_normed_two = jnp.einsum(
        "stf,df->std", grad_up_low, expand_weight, preferred_element_type=jnp.float32
    )
    norm_two_value, norm_two_pull = jax.vjp(layer_norm, mixed, ln2_gain, ln2_bias)
    grad_mixed_norm, grad_ln2_gain, grad_ln2_bias = norm_two_pull(grad_normed_two)
    grad_mixed = grad_result + grad_mixed_norm
    grad_mixed_low = grad_mixed.astype(jnp.bfloat16)
    grad_out_weight = weight_grad(context_low, grad_mixed_low)
    grad_context_low = back_project(grad_mixed_low, out_weight).astype(jnp.bfloat16)

    def backward_head(operands):
        query_h, key_h, value_h, memkey_h, memval_h, mu_row, sigma_row, grad_h, log_total = operands
        scores = (
            jnp.einsum("sqd,skd->sqk", query_h, key_h, preferred_element_type=jnp.float32) * 0.125
        )
        probs = jnp.where(causal, jnp.exp(scores - log_total[..., None]), 0.0)
        grad_probs = jnp.einsum("sqd,skd->sqk", grad_h, value_h, preferred_element_type=jnp.float32)
        row_dot = jnp.sum(probs * grad_probs, axis=-1, keepdims=True)
        grad_scores = (probs * (grad_probs - row_dot)).astype(jnp.bfloat16)
        grad_query = (
            jnp.einsum("sqk,skd->sqd", grad_scores, key_h, preferred_element_type=jnp.float32)
            * 0.125
        )
        memory_scores = (
            jnp.einsum("sqd,snd->sqn", query_h, memkey_h, preferred_element_type=jnp.float32)
            * 0.125
        )
        weights_mem, density_pull = jax.vjp(density, memory_scores, mu_row, sigma_row)
        weights_low = weights_mem.astype(jnp.bfloat16)
        grad_weights = jnp.einsum(
            "sqd,snd->sqn", grad_h, memval_h, preferred_element_type=jnp.float32
        )
        grad_memval = jnp.einsum(
            "sqn,sqd->snd", weights_low, grad_h, preferred_element_type=jnp.float32
        )
        grad_memscores, grad_mu, grad_sigma = density_pull(grad_weights)
        grad_memscores_low = grad_memscores.astype(jnp.bfloat16)
        grad_query = (
            grad_query
            + jnp.einsum(
                "sqn,snd->sqd", grad_memscores_low, memkey_h, preferred_element_type=jnp.float32
            )
            * 0.125
        )
        grad_memkey = (
            jnp.einsum(
                "sqn,sqd->snd", grad_memscores_low, query_h, preferred_element_type=jnp.float32
            )
            * 0.125
        )
        grad_key = (
            jnp.einsum("sqk,sqd->skd", grad_scores, query_h, preferred_element_type=jnp.float32)
            * 0.125
        )
        grad_value = jnp.einsum(
            "sqk,sqd->skd", probs.astype(jnp.bfloat16), grad_h, preferred_element_type=jnp.float32
        )
        return (grad_query, grad_memkey, grad_memval, grad_mu, grad_sigma, grad_key, grad_value)

    head_grads = split_heads(grad_context_low)
    outcome = lax.map(
        backward_head,
        (
            head_queries,
            head_keys,
            value_per_head,
            head_memkeys,
            head_memvals,
            mu_weight,
            sigma_weight,
            head_grads,
            log_totals,
        ),
    )
    grad_query_heads, grad_memkey_heads, grad_memval_heads, grad_mu_weight, grad_sigma_weight = (
        outcome[:5]
    )
    terms = (
        jnp.stack((outcome[5], outcome[6]))
        .transpose(3, 2, 0, 1, 4)
        .reshape(length, seg_count, 2 * model_width)
    )
    own_terms = lax.psum_scatter(
        terms.astype(jnp.bfloat16), BLK, scatter_dimension=0, tiled=True
    ).astype(jnp.float32)
    own_terms = own_terms.reshape(tok_rows, seg_count, 2, model_width).transpose(2, 1, 0, 3)
    grad_keys = own_terms[0]
    grad_values = own_terms[1]
    grad_queries_low = merge_heads(grad_query_heads).astype(jnp.bfloat16)
    grad_keys_low = grad_keys.astype(jnp.bfloat16)
    grad_values_low = grad_values.astype(jnp.bfloat16)
    memkey_sum, memval_sum = (
        lax.psum(grad_memkey_heads.astype(jnp.bfloat16), BLK).astype(jnp.float32),
        lax.psum(grad_memval_heads.astype(jnp.bfloat16), BLK).astype(jnp.float32),
    )
    gradient_memory_keys_reduced = merge_heads(memkey_sum).astype(jnp.bfloat16)
    gradient_memory_values_reduced = merge_heads(memval_sum).astype(jnp.bfloat16)
    grad_query_weight = weight_grad(normed_low, grad_queries_low)
    grad_key_weight = weight_grad(normed_low, grad_keys_low)
    grad_value_weight = weight_grad(normed_low, grad_values_low)
    grad_normed = (
        back_project(grad_queries_low, query_weight)
        + back_project(grad_keys_low, key_weight)
        + back_project(grad_values_low, value_weight)
    )
    norm_one_value, norm_one_pull = jax.vjp(layer_norm, hidden_in, ln1_gain, ln1_bias)
    grad_in_norm, grad_ln1_gain, grad_ln1_bias = norm_one_pull(grad_normed)
    grad_inputs = grad_mixed + grad_in_norm
    shares = (
        lax.psum_scatter(
            grad_ln1_gain.astype(jnp.bfloat16), BLK, scatter_dimension=0, tiled=True
        ).astype(jnp.float32),
        lax.psum_scatter(
            grad_ln1_bias.astype(jnp.bfloat16), BLK, scatter_dimension=0, tiled=True
        ).astype(jnp.float32),
        lax.psum_scatter(
            grad_query_weight.astype(jnp.bfloat16), BLK, scatter_dimension=0, tiled=True
        ).astype(jnp.float32),
        lax.psum_scatter(
            grad_key_weight.astype(jnp.bfloat16), BLK, scatter_dimension=0, tiled=True
        ).astype(jnp.float32),
        lax.psum_scatter(
            grad_value_weight.astype(jnp.bfloat16), BLK, scatter_dimension=0, tiled=True
        ).astype(jnp.float32),
        lax.psum_scatter(
            grad_out_weight.astype(jnp.bfloat16), BLK, scatter_dimension=0, tiled=True
        ).astype(jnp.float32),
        lax.psum_scatter(
            grad_mu_weight.astype(jnp.bfloat16), BLK, scatter_dimension=1, tiled=True
        ).astype(jnp.float32),
        lax.psum_scatter(
            grad_sigma_weight.astype(jnp.bfloat16), BLK, scatter_dimension=1, tiled=True
        ).astype(jnp.float32),
        lax.psum_scatter(
            grad_ln2_gain.astype(jnp.bfloat16), BLK, scatter_dimension=0, tiled=True
        ).astype(jnp.float32),
        lax.psum_scatter(
            grad_ln2_bias.astype(jnp.bfloat16), BLK, scatter_dimension=0, tiled=True
        ).astype(jnp.float32),
        lax.psum_scatter(
            grad_up_weight.astype(jnp.bfloat16), BLK, scatter_dimension=0, tiled=True
        ).astype(jnp.float32),
        lax.psum_scatter(
            grad_up_bias.astype(jnp.bfloat16), BLK, scatter_dimension=0, tiled=True
        ).astype(jnp.float32),
        lax.psum_scatter(
            grad_down_weight.astype(jnp.bfloat16), BLK, scatter_dimension=0, tiled=True
        ).astype(jnp.float32),
        lax.psum_scatter(
            grad_down_bias.astype(jnp.bfloat16), BLK, scatter_dimension=0, tiled=True
        ).astype(jnp.float32),
    )
    share_width = model_width // blocks
    coefficient_part = lax.dynamic_slice_in_dim(
        coeff_low, lax.axis_index(BLK) * share_width, share_width, 2
    )
    key_share = shares[3] + jnp.einsum(
        "wrc,wrt->ct",
        coefficient_part,
        gradient_memory_keys_reduced,
        preferred_element_type=jnp.float32,
    )
    value_share = shares[4] + jnp.einsum(
        "wrc,wrt->ct",
        coefficient_part,
        gradient_memory_values_reduced,
        preferred_element_type=jnp.float32,
    )
    totals = (
        lax.psum(shares[0].astype(jnp.bfloat16), BATCH).astype(jnp.float32),
        lax.psum(shares[1].astype(jnp.bfloat16), BATCH).astype(jnp.float32),
        lax.psum(shares[2].astype(jnp.bfloat16), BATCH).astype(jnp.float32),
        lax.psum(key_share.astype(jnp.bfloat16), BATCH).astype(jnp.float32),
        lax.psum(value_share.astype(jnp.bfloat16), BATCH).astype(jnp.float32),
        lax.psum(shares[5].astype(jnp.bfloat16), BATCH).astype(jnp.float32),
        lax.psum(shares[6].astype(jnp.bfloat16), BATCH).astype(jnp.float32),
        lax.psum(shares[7].astype(jnp.bfloat16), BATCH).astype(jnp.float32),
        lax.psum(shares[8].astype(jnp.bfloat16), BATCH).astype(jnp.float32),
        lax.psum(shares[9].astype(jnp.bfloat16), BATCH).astype(jnp.float32),
        lax.psum(shares[10].astype(jnp.bfloat16), BATCH).astype(jnp.float32),
        lax.psum(shares[11].astype(jnp.bfloat16), BATCH).astype(jnp.float32),
        lax.psum(shares[12].astype(jnp.bfloat16), BATCH).astype(jnp.float32),
        lax.psum(shares[13].astype(jnp.bfloat16), BATCH).astype(jnp.float32),
    )
    whole = (
        lax.all_gather(totals[0].astype(jnp.bfloat16), BLK, axis=0, tiled=True).astype(
            jnp.float32
        ),
        lax.all_gather(totals[1].astype(jnp.bfloat16), BLK, axis=0, tiled=True).astype(
            jnp.float32
        ),
        lax.all_gather(totals[2].astype(jnp.bfloat16), BLK, axis=0, tiled=True).astype(
            jnp.float32
        ),
        lax.all_gather(totals[3].astype(jnp.bfloat16), BLK, axis=0, tiled=True).astype(
            jnp.float32
        ),
        lax.all_gather(totals[4].astype(jnp.bfloat16), BLK, axis=0, tiled=True).astype(
            jnp.float32
        ),
        lax.all_gather(totals[5].astype(jnp.bfloat16), BLK, axis=0, tiled=True).astype(
            jnp.float32
        ),
        lax.all_gather(totals[6].astype(jnp.bfloat16), BLK, axis=1, tiled=True).astype(
            jnp.float32
        ),
        lax.all_gather(totals[7].astype(jnp.bfloat16), BLK, axis=1, tiled=True).astype(
            jnp.float32
        ),
        lax.all_gather(totals[8].astype(jnp.bfloat16), BLK, axis=0, tiled=True).astype(
            jnp.float32
        ),
        lax.all_gather(totals[9].astype(jnp.bfloat16), BLK, axis=0, tiled=True).astype(
            jnp.float32
        ),
        lax.all_gather(totals[10].astype(jnp.bfloat16), BLK, axis=0, tiled=True).astype(
            jnp.float32
        ),
        lax.all_gather(totals[11].astype(jnp.bfloat16), BLK, axis=0, tiled=True).astype(
            jnp.float32
        ),
        lax.all_gather(totals[12].astype(jnp.bfloat16), BLK, axis=0, tiled=True).astype(
            jnp.float32
        ),
        lax.all_gather(totals[13].astype(jnp.bfloat16), BLK, axis=0, tiled=True).astype(
            jnp.float32
        ),
    )
    return (
        block_output,
        grad_inputs,
        whole[0],
        whole[1],
        whole[2],
        whole[3],
        whole[4],
        whole[5],
        whole[6],
        whole[7],
        whole[8],
        whole[9],
        whole[10],
        whole[11],
        whole[12],
        whole[13],
    )


f32 = jnp.float32
bf16 = jnp.bfloat16
NN = (((1,), (0,)), ((), ()))
NT = (((1,), (1,)), ((), ()))
TN = (((0,), (0,)), ((), ()))
QB = 256


def mm(a, b, dims=NN, precision=None):
    return lax.dot_general(a, b, dims, precision=precision, preferred_element_type=f32)


def vmem_params(**more):
    return pltpu.CompilerParams(vmem_limit_bytes=56 * 1024 * 1024, **more)


def head_mask(h):
    lane = lax.broadcasted_iota(jnp.int32, (1, 128), 1)
    return lane // 64 == h


def head_rows(h):
    return pl.ds(pl.multiple_of(h * 64, 64), 64)


def turn(a):
    return jnp.transpose(a.astype(f32))


def parts_of(rows):
    index = lax.broadcasted_iota(jnp.int32, (8, 1), 0)
    out = jnp.zeros_like(rows)
    for n in range(2):
        rest = rows[n : n + 1]
        for t in range(3):
            part = rest.astype(bf16).astype(f32)
            out = jnp.where(index == 3 * n + t, part, out)
            rest = rest - part
    return out.astype(bf16)


def gather_parts(rows):
    index = lax.broadcasted_iota(jnp.int32, (8, 1), 0)
    first = rows[2:3] + rows[1:2] + rows[0:1]
    second = rows[5:6] + rows[4:5] + rows[3:4]
    return jnp.where(index == 0, first, jnp.where(index == 1, second, 0.0))


def place_params(q, mk, musg, mask, basis):
    u = jnp.where(mask, gather_parts(mm(parts_of(musg), mk)) * 0.125, 0.0)
    ab = gather_parts(mm(parts_of(u), q, NT))
    spread = 1.0 / basis
    a = ab[0:1]
    b = ab[1:2]
    centre = 1.0 / (1.0 + jnp.exp(-a))
    soft = jnp.maximum(b, 0.0) + jnp.log1p(jnp.exp(-jnp.abs(b)))
    total = spread * spread + var_scale * soft
    return u, b, centre, total


def causal_block(n):
    key = lax.broadcasted_iota(jnp.int32, (n, n), 0)
    query = lax.broadcasted_iota(jnp.int32, (n, n), 1)
    return key <= query


class Place:
    def __init__(self):
        b, k = lax.axis_index(BATCH), lax.axis_index(BLK)
        z, x = b // 2, b % 2
        y, core = k // 2, k % 2
        self.z, self.x, self.y, self.core = z, x, y, core
        self.peer_x = (z * 2 + 1 - x, k)
        self.peer_y = (b, (1 - y) * 2 + core)
        self.peer_core = (b, y * 2 + 1 - core)
        self.peer_z = [(((z + d) % 4) * 2 + x, k) for d in (1, 2, 3)]

    def announce(self):
        peers = [self.peer_x, self.peer_y, self.peer_core] + self.peer_z
        barrier = pltpu.get_barrier_semaphore()
        for peer in peers:
            pl.semaphore_signal(barrier, inc=1, device_id=peer, device_id_type=pl.DeviceIdType.MESH)

    def wait(self):
        pl.semaphore_wait(pltpu.get_barrier_semaphore(), 6)


def remote(src, dst, sems, n, peer):
    return pltpu.make_async_remote_copy(
        src_ref=src,
        dst_ref=dst,
        send_sem=sems.at[0, n],
        recv_sem=sems.at[1, n],
        device_id=peer,
        device_id_type=pl.DeviceIdType.MESH,
    )


class Reducer:
    copies = 13

    def __init__(self, place, first, src, out, scratch, window=(0, 0), target=(0, 0)):
        self.place = place
        self.f, self.s = (place.x, place.y) if first == "x" else (place.y, place.x)
        x, y = place.peer_x, place.peer_y
        self.peer_f, self.peer_s = (x, y) if first == "x" else (y, x)
        self.src, self.out = src, out
        self.r1, self.send2, self.r2, self.acc, self.r3, self.done, self.sems, self.own = scratch
        self.rows, self.cols = self.r1.shape[0] * 2, self.r1.shape[1]
        self.step = self.rows // 16
        self.window, self.target = window, target

    @staticmethod
    def scratch(rows, cols, dtype):
        return [
            pltpu.VMEM((rows // 2, cols), dtype),
            pltpu.VMEM((rows // 4, cols), dtype),
            pltpu.VMEM((rows // 4, cols), dtype),
            pltpu.VMEM((rows // 4, cols), dtype),
            pltpu.VMEM((3, rows // 16, cols), dtype),
            pltpu.VMEM((rows // 16, cols), dtype),
            pltpu.SemaphoreType.DMA((2, Reducer.copies)),
            pltpu.SemaphoreType.DMA((1,)),
        ]

    def at(self, row, count):
        return pl.ds(pl.multiple_of(row, self.step), count)

    def taken(self, row, count):
        return self.at(self.window[0] + row, count), pl.ds(self.window[1], self.cols)

    def home(self, row, count):
        rows = self.at(self.target[0] + row, count)
        return self.out.at[self.place.core, rows, pl.ds(self.target[1], self.cols)]

    def copy(self, n):
        f, s, z = self.f, self.s, self.place.z
        half, quarter, step = self.rows // 2, self.rows // 4, self.step
        mine = f * half + s * quarter
        if n == 0:
            return remote(self.src.at[*self.taken((1 - f) * half, half)], self.r1, self.sems, n, self.peer_f)
        if n == 1:
            return remote(self.send2, self.r2, self.sems, n, self.peer_s)
        if n < 5:
            d = n - 2
            part = self.acc.at[self.at(((z + d + 1) % 4) * step, step)]
            return remote(part, self.r3.at[d], self.sems, n, self.place.peer_z[d])
        if n < 8:
            part = self.home(mine + z * step, step)
            return remote(self.done, part, self.sems, n, self.place.peer_z[n - 5])
        if n == 8:
            part, peer = self.home(mine, quarter), self.peer_s
        elif n == 9:
            part, peer = self.home(f * half, half), self.peer_f
        elif n == 10:
            part, peer = self.home(mine, quarter), self.place.peer_core
        elif n == 11:
            part, peer = self.home(f * half + (1 - s) * quarter, quarter), self.place.peer_core
        else:
            part, peer = self.home((1 - f) * half, half), self.place.peer_core
        return remote(part, part, self.sems, n, peer)

    def keep(self):
        mine = self.f * (self.rows // 2) + self.s * (self.rows // 4)
        part = self.home(mine + self.place.z * self.step, self.step)
        return pltpu.make_async_copy(self.done, part, self.own.at[0])

    def start(self, *numbers):
        for n in numbers:
            self.copy(n).start()

    def arrive(self, *numbers):
        for n in numbers:
            self.copy(n).wait_recv()

    def sum_into(self, dst, row, *more):
        def body(i, carry):
            at = i * self.step
            total = self.src[self.taken(row + at, self.step)].astype(f32)
            for ref, start in more:
                total = total + ref[self.at(start + at, self.step)].astype(f32)
            dst[self.at(at, self.step)] = total.astype(dst.dtype)
            return carry

        lax.fori_loop(0, 4, body, 0)

    def run(self, stage):
        f, s, z = self.f, self.s, self.place.z
        half, quarter, step = self.rows // 2, self.rows // 4, self.step
        if stage == 0:
            self.start(0)
        elif stage == 1:
            self.arrive(0)
            self.sum_into(self.send2, f * half + (1 - s) * quarter, (self.r1, (1 - s) * quarter))
            self.start(1)
        elif stage == 2:
            self.arrive(1)
            self.sum_into(self.acc, f * half + s * quarter, (self.r1, s * quarter), (self.r2, 0))
            self.start(2, 3, 4)
        elif stage == 3:
            self.arrive(2, 3, 4)
            total = self.acc[self.at(z * step, step)].astype(f32)
            for d in range(3):
                total = total + self.r3[d].astype(f32)
            self.done[...] = total.astype(self.done.dtype)
            self.start(5, 6, 7)
            self.keep().start()
        elif stage == 4:
            self.arrive(5, 6, 7)
            self.keep().wait()
            self.start(8, 10)
        elif stage == 5:
            self.arrive(8)
            self.start(9, 11)
        elif stage == 6:
            self.arrive(9)
            self.start(12)
        elif stage == 7:
            self.arrive(10, 11, 12)
            for n in range(self.copies):
                self.copy(n).wait_send()


def norm_back(x, gy, gain):
    center = jnp.mean(x, axis=-1, keepdims=True)
    shifted = x - center
    rstd = lax.rsqrt(jnp.mean(shifted * shifted, axis=-1, keepdims=True) + epsilon)
    hat = shifted * rstd
    g = gy * gain
    mean_g = jnp.mean(g, axis=-1, keepdims=True)
    mean_gh = jnp.mean(g * hat, axis=-1, keepdims=True)
    gx = rstd * (g - mean_g - hat * mean_gh)
    return gx, jnp.sum(gy * hat, axis=0, keepdims=True), jnp.sum(gy, axis=0, keepdims=True)


def gelu_both(v):
    root = 0.7978845608028654
    sq = v * v
    t = jnp.tanh(root * v * (1.0 + 0.044715 * sq))
    up = 0.5 + 0.5 * t
    slope = up + (0.5 * v) * (1.0 - t * t) * (root + (3.0 * 0.044715 * root) * sq)
    return v * up, slope


SPANS = (256, 512, 768)
STARTS = (0, 256, 768)
AFTER = 3
FIRST = "yyxyxxyxyxy"
PLAN = {
    0: [(1, 0), (0, 0)],
    1: [(3, 0), (2, 0)],
    2: [(1, 1), (5, 0), (0, 1), (4, 0)],
    3: [(2, 1)],
    4: [(6, 0)],
    5: [(11, 0), (1, 2), (2, 2)],
    9: [(0, 2)],
    10: [(1, 3), (5, 1)],
    11: [(6, 1)],
    12: [(2, 3), (0, 3)],
    13: [(1, 4), (4, 1)],
    14: [(3, 1), (6, 2)],
    15: [(5, 2)],
    17: [(2, 4), (7, 0)],
    19: [(0, 4)],
    20: [(1, 5), (4, 2)],
    22: [(2, 5)],
    23: [(8, 0)],
    25: [(5, 3)],
    26: [(7, 1)],
    29: [(8, 1), (6, 3), (0, 5), (9, 0)],
    30: [(5, 4), (4, 3), (8, 2), (6, 4)],
    31: [(10, 0), (5, 5), (7, 2), (4, 4), (8, 3), (9, 1), (3, 2), (10, 1), (7, 3), (6, 5), (8, 4), (4, 5), (3, 3), (9, 2), (3, 4), (10, 2), (7, 4), (9, 3), (8, 5), (7, 5), (5, 6), (9, 4), (1, 6), (5, 7), (0, 6), (0, 7), (2, 6), (4, 6), (10, 3), (6, 6), (3, 5), (10, 4), (1, 7), (8, 6), (9, 5), (7, 6), (10, 5), (2, 7), (3, 6), (9, 6), (10, 6), (4, 7), (10, 7), (3, 7), (6, 7), (7, 7), (8, 7), (9, 7)],
}


def tail_kernel(names, *refs):
    r = SimpleNamespace(**dict(zip(names, refs)))
    jobs_scratch = refs[len(names) :]
    place = Place()
    y, core = place.y, place.core
    tokens, width = r.cot_v.shape
    wide = width // 2
    ff = r.e_v.shape[1]
    pairs = wide // 128
    basis = r.mkv_v.shape[0]
    spread = 1.0 / basis
    block = tokens // 4
    chunk = 64
    n_sem = 8
    take = lambda i: jobs_scratch[n_sem * i : n_sem * i + n_sem]
    ex, loc = r.ex, r.loc
    small_rows = pairs * 2 * basis // 128
    up_rows = ff // 128
    width_rows = width // 128
    base_up = 2 * small_rows
    base_down = base_up + up_rows
    base_ln2 = base_down + width_rows
    base_ln1 = base_ln2 + 2 * width_rows
    third = lambda n: (0, n * wide)
    jobs = []
    for n, lo in enumerate(STARTS):
        jobs += [(r.g_down, r.o_down, (lo, 0), (lo, 0)), (r.g_up, r.o_up, (0, lo), (0, lo))]
    jobs += [(r.gup, r.o_out, third(3)), (r.gup, r.o_0, third(0)), (r.gup, r.o_1, third(1)), (r.gup, r.o_2, third(2))]
    jobs += [(r.sv, r.o_s)]
    jobs = [
        Reducer(place, FIRST[n], src, out, take(n), *windows)
        for n, (src, out, *windows) in enumerate(jobs)
    ]

    def act(step):
        for job, stage in PLAN.get(step, ()):
            if job < len(jobs):
                jobs[job].run(stage)
            else:
                out_copy().start()

    def rows_at(j, c):
        return pl.ds(pl.multiple_of((2 * j + c) * block, block), block)

    def half_at(j):
        return pl.ds(j * block, block)

    def half_dyn(j):
        return pl.ds(pl.multiple_of(j * block, block), block)

    def small_at(j, i):
        return pl.ds(pl.multiple_of((2 * j + core) * block + i * chunk, chunk), chunk)

    def expand_part(lo, count):
        return r.expand.at[:, pl.ds(pl.multiple_of(core * ff + lo, 128), count)]

    def down_part(lo, count):
        return r.down.at[pl.ds(pl.multiple_of(core * ff + lo, 128), count), :]

    def rows_from(ref, n, c):
        return ref.at[pl.ds(pl.multiple_of(c * n, 128), n), :]

    loads = [
        (r.n2_in, r.n2),
        (expand_part(0, SPANS[0]), r.e_v.at[:, pl.ds(0, SPANS[0])]),
        (down_part(0, SPANS[0]), r.d_v.at[pl.ds(0, SPANS[0])]),
        (r.cot, r.cot_v),
        (r.mixed_in, r.mixed),
        (rows_from(r.w_out, wide, core), r.wo_own),
        (r.ctx, r.ctx_v),
        (r.qkv, r.qkv_v),
        (r.mkv, r.mkv_v),
        (r.att, r.att_v),
        (r.normed, r.norm_v),
        (r.coeff, r.coeff_v),
        (r.w_qkv, r.wqkv_v),
        (r.hidden.at[rows_at(0, core)], r.hid_own.at[half_at(0)]),
        (r.hidden.at[rows_at(1, core)], r.hid_own.at[half_at(1)]),
        (expand_part(SPANS[0], ff - SPANS[0]), r.e_v.at[:, pl.ds(SPANS[0], ff - SPANS[0])]),
        (down_part(SPANS[0], ff - SPANS[0]), r.d_v.at[pl.ds(SPANS[0], ff - SPANS[0])]),
    ]

    def load(n):
        return pltpu.make_async_copy(*loads[n], loc.at[n])

    def ready(*numbers):
        for n in numbers:
            load(n).wait()

    def swap(n, j):
        if n == 2 or n == 5:
            src, dst = r.tx.at[half_at(j)], r.rx.at[half_at(j)]
        elif n == 3:
            src = dst = r.gml.at[rows_at(j, core)]
        else:
            src, dst = r.tx.at[half_at(j)], r.rx_out.at[half_at(j)]
        return remote(src, dst, ex, 2 * n + j, place.peer_core)

    def out_copy():
        return remote(r.bo.at[half_dyn(1 - y)], r.out.at[y], ex, 12, place.peer_y)

    def out_keep():
        return pltpu.make_async_copy(r.bo.at[half_dyn(y)], r.out.at[y], loc.at[17])

    def gin_copy():
        return remote(r.n2.at[half_dyn(1 - y)], r.gi_rx, ex, 13, place.peer_y)

    def gin_keep():
        return pltpu.make_async_copy(r.gm.at[half_dyn(y)], r.gin.at[y], loc.at[18])

    def gin_place():
        return pltpu.make_async_copy(r.rx.at[half_at(0)], r.gin.at[1 - y], loc.at[19])

    for n in (0, 1, 2, 3, 15, 16, *range(4, 15)):
        load(n).start()
    place.announce()
    r.sv[...] = jnp.zeros_like(r.sv)
    r.gain1[...] = as_row(r.ln1_gain)
    r.gain2[...] = as_row(r.ln2_gain)
    r.bias_d[...] = as_row(r.down_bias)
    both_up = as_row(r.up_bias)
    r.bias_u[...] = jnp.where(core == 0, both_up[:, :ff], both_up[:, ff:])
    fill_heads(r.musg, r.mu, r.sigma, core)

    def put(row, vec):
        for t in range(vec.shape[1] // 128):
            r.sv[pl.ds(row + t, 1), :] = vec[:, t * 128 : t * 128 + 128]

    ready(0, 1, 2, 3)
    tall = tokens // 2
    for part, (lo, span) in enumerate(zip(STARTS, SPANS)):
        if part == 1:
            ready(15, 16)

        def tile(i, carry, lo=lo):
            rows = pl.ds(pl.multiple_of((i % 2) * tall, tall), tall)
            col = pl.multiple_of(lo + (i // 2) * 256, 256)
            cols = pl.ds(col, 256)
            hidden_up = mm(r.n2[rows, :], r.e_v[:, cols]) + r.bias_u[:, cols]
            value, slope = gelu_both(hidden_up)
            r.active[rows, cols] = value.astype(bf16)
            grad = (mm(r.cot_v[rows, :], r.d_v[cols, :], NT) * slope).astype(bf16)
            r.gup[rows, cols] = grad
            sums = jnp.sum(grad.astype(f32), axis=0, keepdims=True)
            at = base_up + col // 128
            for t in range(2):
                r.sv[pl.ds(at + t, 1), :] += sums[:, t * 128 : t * 128 + 128]
            return carry

        lax.fori_loop(0, 2 * (span // 256), tile, 0)
        for m in range(span // 256):
            here = slice(lo + m * 256, lo + m * 256 + 256)
            r.g_down[here, :] = mm(r.active[:, here], r.cot_v[...], TN).astype(bf16)
        for m in range(width // 256):
            cols = slice(m * 256, m * 256 + 256)
            r.g_up[cols, lo : lo + span] = mm(r.n2[:, cols], r.gup[:, lo : lo + span], TN).astype(bf16)
        if part == 0:
            place.wait()
        act(part)

    ready(4, 5, 6)
    for j in range(2):
        r.tx[half_at(j), :] = mm(r.gup[rows_at(j, 1 - core), :], r.e_v[...], NT)
        swap(2, j).start()

    def norm_two(j, carry):
        def body(i, carry):
            at = pl.ds(pl.multiple_of(j * block + i * chunk, chunk), chunk)
            gy = r.gm[at, :] + r.rx[at, :]
            gx, dg, db = norm_back(r.mixed[at, :], gy, r.gain2[...])
            cot = r.cot_v[small_at(j, i), :].astype(f32)
            gm = cot + gx
            r.gm[at, :] = gm
            r.gml[small_at(j, i), :] = gm.astype(bf16)
            return carry[0] + dg, carry[1] + db

        return lax.fori_loop(0, block // chunk, body, carry)

    sums = (jnp.zeros((1, width), f32), jnp.zeros((1, width), f32))
    for j in range(2):
        r.gm[half_at(j), :] = mm(r.gup[rows_at(j, core), :], r.e_v[...], NT)
        swap(2, j).wait_recv()
        sums = norm_two(j, sums)
        swap(3, j).start()
    put(base_ln2, sums[0])
    put(base_ln2 + width_rows, sums[1])
    put(base_down, jnp.sum(r.cot_v[...].astype(f32), axis=0, keepdims=True))
    act(AFTER + 0)
    for c in (0, 1):
        for j in range(2):
            if c:
                swap(3, j).wait_recv()
            there = rows_at(j, core if c == 0 else 1 - core)
            r.do[there, :] = mm(r.gml[there, :], r.wo_own[...], NT).astype(bf16)
    for m in range(width // 256):
        cols = slice(m * 256, m * 256 + 256)
        r.gup[cols, pairs * wide : pairs * wide + wide] = mm(r.gml[:, cols], r.ctx_v[...], TN).astype(bf16)
    act(AFTER + 1)

    for j in range(2):
        swap(2, j).wait_send()
        r.tx[half_at(j), :] = mm(r.active[rows_at(j, 1 - core), :], r.d_v[...])
        swap(4, j).start()
    for j in range(2):
        own = mm(r.active[rows_at(j, core), :], r.d_v[...])
        swap(4, j).wait_recv()
        total = r.mixed[half_at(j), :] + (own + r.rx_out[half_at(j), :]) + r.bias_d[...]
        r.bo[half_at(j), :] = total.astype(bf16)
    out_keep().start()
    act(AFTER + 2)

    centers = (lax.broadcasted_iota(jnp.int32, (basis, 1), 0).astype(f32) + 0.5) / basis
    allowed = causal_block(QB)
    pick_row = lax.broadcasted_iota(jnp.int32, (8, 1), 0)
    blocks = tokens // QB
    per_pair = 2 * blocks
    ready(7, 8, 9, 10, 11)
    for n in range(4):
        at = slice(n * block, n * block + block)
        r.normed_v[:, at] = turn(r.norm_v[at, :]).astype(bf16)

    def pair_step(i, carry):
        lanes = pl.ds(pl.multiple_of(i * 128, 128), 128)

        def lanes_of(j):
            return pl.ds(pl.multiple_of(i * 128 + j * wide, 128), 128)

        q_ref, k_ref, v_ref = (r.qkv_v.at[:, lanes_of(j)] for j in range(3))
        mk_ref, mv_ref = (r.mkv_v.at[:, lanes_of(j)] for j in range(2))
        do_ref = r.do.at[:, lanes]
        dka, dva, dqt, gmva, k_t, do_t = r.dka, r.dva, r.dqt, r.gmva, r.k_t, r.do_t
        k_t[...] = turn(k_ref[...]).astype(bf16)
        do_t[...] = turn(do_ref[...])
        dka[...] = jnp.zeros_like(dka)
        dva[...] = jnp.zeros_like(dva)
        gmva[...] = jnp.zeros_like(gmva)
        r.gmk[...] = jnp.zeros_like(r.gmk)

        def finish_pair():
            r.active[:, lanes] = jnp.transpose(dqt[...]).astype(bf16)
            r.active[:, lanes_of(1)] = dka[...].astype(bf16)
            r.active[:, lanes_of(2)] = dva[...].astype(bf16)
            r.part[:, 0:128] = r.active[:, lanes]
            r.part[:, 128:256] = r.active[:, lanes_of(1)]
            r.part[:, 256:384] = r.active[:, lanes_of(2)]
            r.part_mem[:, 0:128] = r.gmk[...].astype(bf16)
            r.part_mem[:, 128:256] = gmva[...].astype(bf16)
            spot = pl.multiple_of(i * wide, 128)
            for m in range(width // 256):
                here = slice(m * 256, m * 256 + 256)
                g = mm(r.normed_v[here, :], r.part[...])
                cg = mm(r.coeff_v[:, here], r.part_mem[...], TN)
                r.gup[here, pl.ds(spot, 128)] = g[:, :128].astype(bf16)
                r.gup[here, pl.ds(spot + 128, 256)] = (g[:, 128:] + cg).astype(bf16)

        def head_step(h, carry):
            mask = head_mask(h)
            rows = head_rows(h)
            musg = r.musg[2 * i + h]
            u, b, centre, total = place_params(q_ref[...], mk_ref[...], musg, mask, basis)
            scale = spread * lax.rsqrt(total)
            inv = 1.0 / total
            dot_rows = jnp.sum(do_t[rows, :] * r.att_v[i, rows, :], axis=0, keepdims=True)
            z = jnp.zeros((8, 128), f32)
            for qb in range(blocks):
                cols = slice(qb * QB, qb * QB + QB)
                q = jnp.where(mask, q_ref[cols, :].astype(f32) * 0.125, 0.0).astype(bf16)
                do = jnp.where(mask, do_ref[cols, :].astype(f32), 0.0).astype(bf16)
                lse = r.lse[i, pl.ds(h, 1), cols]
                dot_row = dot_rows[:, cols]
                dq_t = jnp.zeros((64, QB), f32)
                for kb in range(qb + 1):
                    keys = slice(kb * QB, kb * QB + QB)
                    p = jnp.exp(mm(k_ref[keys, :], q, NT) - lse)
                    if kb == qb:
                        p = jnp.where(allowed, p, 0.0)
                    dva[keys, :] += mm(p.astype(bf16), do)
                    ds = (p * (mm(v_ref[keys, :], do, NT) - dot_row)).astype(bf16)
                    dka[keys, :] += mm(ds, q)
                    dq_t = dq_t + mm(k_t[rows, keys], ds)
                dqt[rows, cols] = dq_t * 0.125
                gap = centre[:, cols] - centers
                gap2 = gap * gap
                inv_b = inv[:, cols]
                dens = scale[:, cols] * jnp.exp(gap2 * (-0.5 * inv_b))
                gmva[...] += mm(dens.astype(bf16), do)
                e = mm(mv_ref[...], do, NT) * dens
                sum0 = jnp.sum(e, axis=0, keepdims=True)
                sum1 = jnp.sum(e * gap, axis=0, keepdims=True)
                sum2 = jnp.sum(e * gap2, axis=0, keepdims=True)
                c = centre[:, cols]
                da = -sum1 * inv_b * c * (1.0 - c)
                dtotal = 0.5 * inv_b * (sum2 * inv_b - sum0)
                db = dtotal * var_scale / (1.0 + jnp.exp(-b[:, cols]))
                dab = jnp.where(pick_row == 0, da, jnp.where(pick_row == 1, db, 0.0))
                dqt[:, cols] += mm(u, dab, TN, precision=highest)
                z = z + gather_parts(mm(parts_of(dab), q))
                if qb == blocks - 1:
                    r.gmk[...] += mm(musg, z, TN, precision=highest)
                    grads = gather_parts(mm(parts_of(z), mk_ref[...], NT))
                    at = (2 * i + h) * (basis // 128)
                    put(at, grads[0:1])
                    put(small_rows + at, grads[1:2])
                    pl.when(h == 1)(finish_pair)
                for step in range(2 * pairs):
                    at_step = AFTER + 3 + step * blocks + qb
                    if at_step in PLAN:

                        @pl.when(2 * i + h == step)
                        def _(at_step=at_step):
                            act(at_step)

            return carry

        lax.fori_loop(0, 2, head_step, 0)
        return carry

    lax.fori_loop(0, pairs, pair_step, 0)

    ready(12, 13, 14)
    for j in range(2):
        swap(4, j).wait_send()
        r.tx[half_at(j), :] = mm(r.active[rows_at(j, 1 - core), : 3 * wide], r.wqkv_v[...], NT)
        swap(5, j).start()
    for j in range(2):
        r.mixed[half_at(j), :] = mm(r.active[rows_at(j, core), : 3 * wide], r.wqkv_v[...], NT)

    act(AFTER + 27)
    def norm_one(i, carry):
        at = pl.ds(pl.multiple_of(i * chunk, chunk), chunk)
        gy = r.mixed[at, :] + r.rx[at, :]
        gx, dg, db = norm_back(r.hid_own[at, :].astype(f32), gy, r.gain1[...])
        total = r.gm[at, :] + gx
        r.gm[at, :] = total
        r.n2[at, :] = total.astype(bf16)
        return carry[0] + dg, carry[1] + db

    for j in range(2):
        swap(5, j).wait_recv()
    sums = lax.fori_loop(
        0, 2 * block // chunk, norm_one, (jnp.zeros((1, width), f32), jnp.zeros((1, width), f32))
    )
    put(base_ln1, sums[0])
    put(base_ln1 + width_rows, sums[1])
    gin_keep().start()
    gin_copy().start()
    act(AFTER + 28)
    gin_copy().wait()
    r.rx[half_at(0), :] = r.gi_rx[...].astype(f32)
    gin_place().start()
    out_copy().wait()
    out_keep().wait()
    gin_keep().wait()
    gin_place().wait()
    for j in range(2):
        for n in (3, 5):
            swap(n, j).wait_send()


def tail_call(held, given):
    g = SimpleNamespace(**held, **given)
    tokens, width = g.cot.shape
    wide = width // 2
    ff = g.expand.shape[1] // 2
    heads = wide // 64
    basis = g.mkv.shape[0]
    half, block = tokens // 2, tokens // 4
    used = 2 * (wide // 64) * basis // 128 + ff // 128 + 5 * (width // 128)
    sv_rows = -(-used // 128) * 128
    shape = jax.ShapeDtypeStruct
    like = lambda a: pltpu.VMEM(a.shape, a.dtype)
    outs = dict(
        o_down=shape((2, ff, width), bf16),
        o_up=shape((2, width, ff), bf16),
        o_out=shape((2, width, wide), bf16),
        o_0=shape((2, width, wide), bf16),
        o_1=shape((2, width, wide), bf16),
        o_2=shape((2, width, wide), bf16),
        o_s=shape((2, sv_rows, 128), f32),
        out=shape((2, block, width), bf16),
        gin=shape((2, block, width), f32),
    )
    scratch = dict(
        ex=pltpu.SemaphoreType.DMA((2, 14)),
        loc=pltpu.SemaphoreType.DMA((20,)),
        ctx_v=like(g.ctx),
        wo_own=pltpu.VMEM((wide, width), bf16),
        hid_own=pltpu.VMEM((half, width), bf16),
        e_v=pltpu.VMEM((width, ff), bf16),
        d_v=pltpu.VMEM((ff, width), bf16),
        cot_v=like(g.cot),
        qkv_v=like(g.qkv),
        mkv_v=like(g.mkv),
        att_v=like(g.att),
        norm_v=like(g.normed),
        normed_v=pltpu.VMEM((width, tokens), bf16),
        coeff_v=like(g.coeff),
        wqkv_v=like(g.w_qkv),
        mixed=pltpu.VMEM((half, width), f32),
        n2=pltpu.VMEM((tokens, width), bf16),
        active=pltpu.VMEM((tokens, ff), bf16),
        gup=pltpu.VMEM((tokens, ff), bf16),
        g_down=pltpu.VMEM((ff, width), bf16),
        g_up=pltpu.VMEM((width, ff), bf16),
        tx=pltpu.VMEM((half, width), f32),
        rx=pltpu.VMEM((half, width), f32),
        rx_out=pltpu.VMEM((half, width), f32),
        gm=pltpu.VMEM((half, width), f32),
        gml=pltpu.VMEM((tokens, width), bf16),
        bo=pltpu.VMEM((half, width), bf16),
        gi_rx=pltpu.VMEM((block, width), bf16),
        do=pltpu.VMEM((tokens, wide), bf16),
        part=pltpu.VMEM((tokens, 384), bf16),
        part_mem=pltpu.VMEM((basis, 256), bf16),
        dka=pltpu.VMEM((tokens, 128), f32),
        dva=pltpu.VMEM((tokens, 128), f32),
        dqt=pltpu.VMEM((128, tokens), f32),
        gmva=pltpu.VMEM((basis, 128), f32),
        gmk=pltpu.VMEM((basis, 128), f32),
        k_t=pltpu.VMEM((128, tokens), bf16),
        do_t=pltpu.VMEM((128, tokens), f32),
        sv=pltpu.VMEM((sv_rows, 128), f32),
        gain1=pltpu.VMEM((1, width), f32),
        gain2=pltpu.VMEM((1, width), f32),
        bias_d=pltpu.VMEM((1, width), f32),
        bias_u=pltpu.VMEM((1, ff), f32),
        musg=pltpu.VMEM((heads, 8, basis), f32),
    )
    more = []
    shapes = []
    for span in SPANS:
        shapes += [(span, width, bf16), (width, span, bf16)]
    shapes += [(width, wide, bf16)] * 4 + [(sv_rows, 128, f32)]
    for item in shapes:
        more += Reducer.scratch(*item)
    hbm, vmem = pl.BlockSpec(memory_space=pl.ANY), pl.BlockSpec(memory_space=pltpu.VMEM)
    names = list(held) + list(given) + list(outs) + list(scratch)
    return pl.pallas_call(
        functools.partial(tail_kernel, names),
        in_specs=[hbm] * len(held) + [vmem] * len(given),
        out_specs=[hbm] * len(outs),
        out_shape=list(outs.values()),
        scratch_shapes=list(scratch.values()) + more,
        compiler_params=pltpu.CompilerParams(
            vmem_limit_bytes=60 * 1024 * 1024, collective_id=1, has_side_effects=True
        ),
        name="tail",
    )(*held.values(), *given.values())


def as_row(ref):
    return ref[...].reshape(1, ref.shape[0])


def fill_heads(dst, mu, sigma, core):
    heads = dst.shape[0]
    dst[...] = jnp.zeros_like(dst)
    for h in range(heads):
        for n, src in enumerate((mu, sigma)):
            dst[h, n : n + 1, :] = src[pl.ds(core * heads + h, 1), :]


def sweep_inverse(a):
    n = a.shape[0]
    lane = lax.broadcasted_iota(jnp.int32, (8, n), 1)
    sub = lax.broadcasted_iota(jnp.int32, (8, n), 0)
    groups = [a[8 * g : 8 * g + 8, :] for g in range(n // 8)]

    def inverse_two(p, q, t):
        inv = 1.0 / (p * t - q * q)
        return t * inv, -q * inv, p * inv

    for k in range(0, n, 4):
        own, at = groups[k // 8], k % 8
        rows = [jnp.broadcast_to(own[at + i : at + i + 1, :], (8, n)) for i in range(4)]
        d = {
            (i, j): jnp.broadcast_to(rows[i][:, k + j : k + j + 1], (8, n))
            for i in range(4)
            for j in range(i, 4)
        }
        a0, a1, a2 = inverse_two(d[0, 0], d[0, 1], d[1, 1])
        w = [
            [a0 * d[0, 2] + a1 * d[1, 2], a0 * d[0, 3] + a1 * d[1, 3]],
            [a1 * d[0, 2] + a2 * d[1, 2], a1 * d[0, 3] + a2 * d[1, 3]],
        ]
        s0 = d[2, 2] - (d[0, 2] * w[0][0] + d[1, 2] * w[1][0])
        s1 = d[2, 3] - (d[0, 2] * w[0][1] + d[1, 2] * w[1][1])
        s2 = d[3, 3] - (d[0, 3] * w[0][1] + d[1, 3] * w[1][1])
        s0, s1, s2 = inverse_two(s0, s1, s2)
        v = [[w[i][0] * s0 + w[i][1] * s1, w[i][0] * s1 + w[i][1] * s2] for i in range(2)]
        p00 = a0 + v[0][0] * w[0][0] + v[0][1] * w[0][1]
        p01 = a1 + v[0][0] * w[1][0] + v[0][1] * w[1][1]
        p11 = a2 + v[1][0] * w[1][0] + v[1][1] * w[1][1]
        p = [
            [p00, p01, -v[0][0], -v[0][1]],
            [p01, p11, -v[1][0], -v[1][1]],
            [-v[0][0], -v[1][0], s0, s1],
            [-v[0][1], -v[1][1], s1, s2],
        ]
        new = []
        for i in range(4):
            row = p[i][0] * rows[0] + p[i][1] * rows[1] + p[i][2] * rows[2] + p[i][3] * rows[3]
            for j in range(4):
                row = jnp.where(lane == k + j, p[i][j], row)
            new.append(row)
        inside = (lane >= k) & (lane < k + 4)
        for g in range(n // 8):
            old = groups[g]
            cols = [jnp.broadcast_to(old[:, k + j : k + j + 1], (8, n)) for j in range(4)]
            part = (cols[0] * new[0] + cols[1] * new[1]) + (cols[2] * new[2] + cols[3] * new[3])
            fresh = jnp.where(inside, 0.0, old) - part
            if g == k // 8:
                for i in range(4):
                    fresh = jnp.where(sub == at + i, new[i], fresh)
            groups[g] = fresh
    return jnp.concatenate(groups, 0)


KB = 128


def front_kernel(names, *refs):
    r = SimpleNamespace(**dict(zip(names, refs)))
    place = Place()
    y, core = place.y, place.core
    tokens, width = r.hid_v.shape
    block = tokens // 4
    wide = width // 2
    pairs = wide // 128
    basis = r.mkv_v.shape[0]
    half = basis // 2
    ex, loc = r.ex, r.loc
    flows = [(r.inputs, r.hid_v), (r.previous, r.prev), (r.cotangent, r.cot)]

    def rows_at(yy, cc):
        return pl.ds(pl.multiple_of((2 * yy + cc) * block, block), block)

    def along(n):
        src, dst = flows[n]
        return remote(src.at[1 - y], dst.at[rows_at(y, core)], ex, n, place.peer_y)

    def across(n):
        src, dst = flows[n]
        return remote(src.at[y], dst.at[rows_at(y, core)], ex, 3 + n, place.peer_core)

    def onward(n):
        part = flows[n][1].at[rows_at(1 - y, core)]
        return remote(part, part, ex, 6 + n, place.peer_core)

    def keep(n):
        src, dst = flows[n]
        return pltpu.make_async_copy(src.at[y], dst.at[rows_at(y, core)], loc.at[n])

    def weight(n):
        src = (r.wq, r.wk, r.wv)[n].at[:, pl.ds(pl.multiple_of(core * wide, 128), wide)]
        return pltpu.make_async_copy(src, r.w_v.at[:, n * wide : n * wide + wide], loc.at[3 + n])

    def projection(n):
        c = core if n == 0 else 1 - core
        src = r.wo.at[pl.ds(pl.multiple_of(c * wide, 128), wide)]
        return pltpu.make_async_copy(src, r.wo_v.at[n], loc.at[17 + n])

    results = [
        (r.w_v, r.w_qkv),
        (r.hid_v, r.hidden),
        (r.normed, r.normed_out),
        (r.qkv_v, r.qkv),
        (r.mkv_v, r.mkv),
        (r.coeff_v, r.coeff),
        (r.att_v, r.att),
        (r.ctx_v, r.ctx),
        (r.mix_v, r.mixed),
    ]

    def result(n):
        return pltpu.make_async_copy(*results[n], loc.at[6 + n])

    barrier = pltpu.get_barrier_semaphore()
    for peer in (place.peer_y, place.peer_core):
        pl.semaphore_signal(barrier, inc=1, device_id=peer, device_id_type=pl.DeviceIdType.MESH)
    r.gain1[...] = as_row(r.ln1_gain)
    r.bias1[...] = as_row(r.ln1_bias)
    r.gain2[...] = as_row(r.ln2_gain)
    r.bias2[...] = as_row(r.ln2_bias)
    fill_heads(r.musg, r.mu, r.sigma, core)

    spread = 1.0 / basis
    centers = (lax.broadcasted_iota(jnp.int32, (basis, 1), 0).astype(f32) + 0.5) / basis
    places = (r.sticky[pl.ds(y, 1), :].astype(f32) + 0.5) / tokens
    features = jnp.exp(-((places - centers) ** 2) / (2.0 * spread * spread)).astype(bf16)
    same = lax.broadcasted_iota(jnp.int32, (basis, basis), 0) == lax.broadcasted_iota(
        jnp.int32, (basis, basis), 1
    )
    a_ref, i_ref = r.a, r.i
    a_ref[...] = mm(features, features, NT) + jnp.where(same, ridge_weight, 0.0)
    pl.semaphore_wait(barrier, 2)
    along(0).start()
    across(0).start()
    keep(0).start()
    along(1).start()
    for n in range(3):
        weight(n).start()
    for n in range(2):
        projection(n).start()
    across(1).start()
    keep(1).start()
    along(2).start()
    across(2).start()
    keep(2).start()

    r.schur[...] = a_ref[:half, :half]

    def eliminate(n, carry):
        i_ref[n] = sweep_inverse(r.schur[...])

        @pl.when(n == 0)
        def _():
            cross = a_ref[:half, half:]
            r.cross[...] = mm(i_ref[0], cross, precision=highest)
            r.schur[...] = a_ref[half:, half:] - mm(cross, r.cross[...], TN, precision=highest)

        return carry

    lax.fori_loop(0, 2, eliminate, 0)

    chunk = 64

    def project(yy, cc):
        def body(i, carry):
            at = pl.ds(pl.multiple_of((2 * yy + cc) * block + i * chunk, chunk), chunk)
            normed = layer_norm(r.hid_v[at, :].astype(f32), r.gain1[...], r.bias1[...])
            r.normed[at, :] = normed.astype(bf16)
            return carry

        lax.fori_loop(0, block // chunk, body, 0)
        at = rows_at(yy, cc)
        r.qkv_v[at, :] = mm(r.normed[at, :], r.w_v[...]).astype(bf16)

    keep(0).wait()
    for n in range(3):
        weight(n).wait()
    result(0).start()
    project(y, core)
    across(0).wait_recv()
    project(y, 1 - core)
    index = lax.broadcasted_iota(jnp.int32, (tokens, r.picks.shape[1]), 0)
    chosen = jnp.where(index == r.picks[pl.ds(y, 1), :], 1.0, 0.0).astype(bf16)
    shares = mm(features, chosen, NT)
    high = shares.astype(bf16)
    rest = shares - high.astype(f32)
    middle = rest.astype(bf16)
    r.shares[0] = high
    r.shares[1] = middle
    r.shares[2] = (rest - middle.astype(f32)).astype(bf16)

    along(0).wait_recv()
    onward(0).start()
    project(1 - y, core)
    onward(0).wait_recv()
    project(1 - y, 1 - core)
    result(1).start()
    result(2).start()
    result(3).start()

    allowed = causal_block(QB)
    blocks = tokens // QB
    split = QB // KB

    def lanes_of(i, j):
        return pl.ds(pl.multiple_of(i * 128 + j * wide, 128), 128)

    def causal_pair(i, carry):
        q_ref, k_ref, v_ref = (r.qkv_v.at[:, lanes_of(i, j)] for j in range(3))
        r.v_t[...] = turn(v_ref[...]).astype(bf16)
        def causal_head(h, carry):
            mask = head_mask(h)
            rows = head_rows(h)
            for qb in range(blocks):
                cols = slice(qb * QB, qb * QB + QB)
                q = jnp.where(mask, q_ref[cols, :].astype(f32) * 0.125, 0.0).astype(bf16)
                top = None
                for kb in range((qb + 1) * split):
                    keys = slice(kb * KB, kb * KB + KB)
                    s = mm(k_ref[keys, :], q, NT)
                    if kb >= qb * split:
                        at = (kb - qb * split) * KB
                        s = jnp.where(allowed[at : at + KB], s, masked_score)
                    r.s[keys, :] = s
                    best = jnp.max(s, axis=0, keepdims=True)
                    top = best if top is None else jnp.maximum(top, best)
                denom = jnp.zeros_like(top)
                out = jnp.zeros((64, QB), f32)
                for kb in range((qb + 1) * split):
                    keys = slice(kb * KB, kb * KB + KB)
                    e = jnp.exp(r.s[keys, :] - top)
                    denom = denom + jnp.sum(e, axis=0, keepdims=True)
                    out = out + mm(r.v_t[rows, keys], e.astype(bf16))
                r.att_v[i, rows, cols] = out / denom
                r.lse[i, pl.ds(h, 1), cols] = top + jnp.log(denom)
            return carry

        lax.fori_loop(0, 2, causal_head, 0)
        return carry

    lax.fori_loop(0, pairs - 1, causal_pair, 0)
    along(1).wait_recv()
    onward(1).start()
    lax.fori_loop(pairs - 1, pairs, causal_pair, 0)
    result(6).start()
    across(1).wait_recv()
    keep(1).wait()
    onward(1).wait_recv()
    prev = r.prev[...]
    side = mm(r.shares[0], prev) + (mm(r.shares[1], prev) + mm(r.shares[2], prev))
    low_part = mm(
        i_ref[1], side[half:] - mm(r.cross[...], side[:half], TN, precision=highest), precision=highest
    )
    r.coeff_v[half:, :] = low_part.astype(bf16)
    r.coeff_v[:half, :] = (
        mm(i_ref[0], side[:half], precision=highest) - mm(r.cross[...], low_part, precision=highest)
    ).astype(bf16)
    r.mkv_v[...] = mm(r.coeff_v[...], r.w_v[:, wide:]).astype(bf16)
    result(4).start()
    result(5).start()

    def memory_pair(i, carry):
        q_ref = r.qkv_v.at[:, lanes_of(i, 0)]
        mk_ref, mv_ref = (r.mkv_v.at[:, lanes_of(i, j)] for j in range(2))
        r.mv_t[...] = turn(mv_ref[...]).astype(bf16)
        def memory_head(h, carry):
            rows = head_rows(h)
            u, b, centre, total = place_params(q_ref[...], mk_ref[...], r.musg[2 * i + h], head_mask(h), basis)
            scale = spread * lax.rsqrt(total)
            fall = -0.5 / total
            for qb in range(blocks):
                cols = slice(qb * QB, qb * QB + QB)
                gap = centre[:, cols] - centers
                dens = (scale[:, cols] * jnp.exp(gap * gap * fall[:, cols])).astype(bf16)
                r.o[rows, cols] = r.att_v[i, rows, cols] + mm(r.mv_t[rows, :], dens)
            return carry

        lax.fori_loop(0, 2, memory_head, 0)
        r.ctx_v[:, lanes_of(i, 0)] = jnp.transpose(r.o[...]).astype(bf16)
        for j in range(2):
            context(i, j).start()
        return carry

    def half_at(j):
        return pl.ds(j * block, block)

    def context(i, j):
        src = r.ctx_v.at[rows_at(j, 1 - core), lanes_of(i, 0)]
        return remote(src, r.ctx_rx.at[half_at(j), lanes_of(i, 0)], ex, 9 + 2 * i + j, place.peer_core)

    def second(j):
        part = r.n2_v.at[half_at(j)]
        return remote(part, r.n2.at[rows_at(j, core)], ex, 9 + 2 * pairs + j, place.peer_core)

    def second_keep(j):
        return pltpu.make_async_copy(r.n2_v.at[half_at(j)], r.n2.at[rows_at(j, core)], loc.at[15 + j])

    lax.fori_loop(0, pairs - 1, memory_pair, 0)
    along(2).wait_recv()
    onward(2).start()
    lax.fori_loop(pairs - 1, pairs, memory_pair, 0)
    result(7).start()
    for n in range(2):
        projection(n).wait()

    for j in range(2):
        own = mm(r.ctx_v[rows_at(j, core), :], r.wo_v[0])
        r.mix_v[half_at(j), :] = r.hid_v[rows_at(j, core), :].astype(f32) + own
    for j in range(2):
        for i in range(pairs):
            context(i, j).wait_recv()
        r.mix_v[half_at(j), :] += mm(r.ctx_rx[half_at(j), :], r.wo_v[1])

        def norm_chunk(i, carry, j=j):
            at = pl.ds(pl.multiple_of(j * block + i * chunk, chunk), chunk)
            r.n2_v[at, :] = layer_norm(r.mix_v[at, :], r.gain2[...], r.bias2[...]).astype(bf16)
            return carry

        lax.fori_loop(0, block // chunk, norm_chunk, 0)
        second(j).start()
        second_keep(j).start()
    result(8).start()
    keep(2).wait()
    across(2).wait_recv()
    onward(2).wait_recv()
    for j in range(2):
        second(j).wait()
        second_keep(j).wait()
        for i in range(pairs):
            context(i, j).wait_send()
    for n in range(3):
        along(n).wait_send()
        across(n).wait_send()
        onward(n).wait_send()
    for n in range(len(results)):
        result(n).wait()


def front_call(held, given, basis):
    block, width = held[next(iter(held))].shape[1:]
    tokens = block * 4
    wide = width // 2
    pairs = wide // 128
    shape = jax.ShapeDtypeStruct
    outs = dict(
        hidden=shape((tokens, width), bf16),
        normed_out=shape((tokens, width), bf16),
        qkv=shape((tokens, 3 * wide), bf16),
        mkv=shape((basis, width), bf16),
        coeff=shape((basis, width), bf16),
        w_qkv=shape((width, 3 * wide), bf16),
        cot=shape((tokens, width), bf16),
        ctx=shape((tokens, wide), bf16),
        att=shape((pairs, 128, tokens), f32),
        mixed=shape((tokens // 2, width), f32),
        n2=shape((tokens, width), bf16),
    )
    near = dict(lse=shape((pairs, 2, tokens), f32))
    like = lambda a: pltpu.VMEM(a.shape, a.dtype)
    o = SimpleNamespace(**outs)
    scratch = dict(
        ex=pltpu.SemaphoreType.DMA((2, 11 + 2 * pairs)),
        loc=pltpu.SemaphoreType.DMA((19,)),
        hid_v=like(o.hidden),
        qkv_v=like(o.qkv),
        mkv_v=like(o.mkv),
        coeff_v=like(o.coeff),
        w_v=like(o.w_qkv),
        ctx_v=like(o.ctx),
        att_v=like(o.att),
        mix_v=like(o.mixed),
        n2_v=pltpu.VMEM((tokens // 2, width), bf16),
        ctx_rx=pltpu.VMEM((tokens // 2, wide), bf16),
        wo_v=pltpu.VMEM((2, wide, width), bf16),
        gain2=pltpu.VMEM((1, width), f32),
        bias2=pltpu.VMEM((1, width), f32),
        prev=pltpu.VMEM((tokens, width), bf16),
        normed=pltpu.VMEM((tokens, width), bf16),
        a=pltpu.VMEM((basis, basis), f32),
        i=pltpu.VMEM((2, basis // 2, basis // 2), f32),
        cross=pltpu.VMEM((basis // 2, basis // 2), f32),
        schur=pltpu.VMEM((basis // 2, basis // 2), f32),
        shares=pltpu.VMEM((3, basis, tokens), bf16),
        gain1=pltpu.VMEM((1, width), f32),
        bias1=pltpu.VMEM((1, width), f32),
        musg=pltpu.VMEM((2 * pairs, 8, basis), f32),
        s=pltpu.VMEM((tokens, QB), f32),
        v_t=pltpu.VMEM((128, tokens), bf16),
        mv_t=pltpu.VMEM((128, basis), bf16),
        o=pltpu.VMEM((128, tokens), f32),
    )
    hbm, vmem = pl.BlockSpec(memory_space=pl.ANY), pl.BlockSpec(memory_space=pltpu.VMEM)
    names = list(held) + list(given) + list(outs) + list(near) + list(scratch)
    return pl.pallas_call(
        functools.partial(front_kernel, names),
        in_specs=[hbm] * len(held) + [vmem] * len(given),
        out_specs=[hbm] * len(outs) + [vmem] * len(near),
        out_shape=list(outs.values()) + list(near.values()),
        scratch_shapes=list(scratch.values()),
        compiler_params=vmem_params(collective_id=2, has_side_effects=True),
        name="front",
    )(*held.values(), *given.values())


def finish(down, up, out_t, parts, small, basis, ready):
    ff = 2 * up.shape[2]
    width = out_t.shape[1]
    per = basis // 128
    heads = width // 64
    steps = width // 128
    per_core = steps // 2
    tall = down.shape[1] // per_core
    wide = width // 2

    def body(down_ref, up_ref, t_ref, s_ref, *refs):
        *refs, kept_0, kept_1 = refs
        kept_0[...] = refs[len(parts)][...]
        kept_1[...] = refs[len(parts) + 1][...]
        o_down, o_up, o_q, o_k, o_v, o_o, o_mu, o_sg, o_bias, *o_rows = refs[len(parts) + 2 :]
        start = heads * per
        count = ff // 256
        for c in range(2):
            row = [s_ref[c, start + t : start + t + 1, :] for t in range(count)]
            o_bias[c * (ff // 2) : (c + 1) * (ff // 2)] = jnp.concatenate(row, 1).reshape(ff // 2)
        start = start + count
        for n, ref in enumerate(o_rows):
            row = []
            for t in range(width // 128):
                first = s_ref[0, start + t : start + t + 1, :]
                row.append(first + s_ref[1, start + t : start + t + 1, :] if n else first)
            ref[...] = jnp.concatenate(row, 1).reshape(width)
            start = start + width // 128
        for n, ref in enumerate((o_mu, o_sg)):
            for h in range(heads):
                for t in range(per):
                    row = n * (heads // 2) * per + h % (heads // 2) * per + t
                    here = slice(t * 128, t * 128 + 128)
                    ref[h : h + 1, here] = s_ref[h // (heads // 2), row : row + 1, :]
        o_down[...] = down_ref[0].astype(f32)
        n = up_ref.shape[2]
        for c in range(2):
            o_up[:, c * n : c * n + n] = up_ref[c].astype(f32)
            for i, ref in enumerate(refs[: len(parts)]):
                here = slice(c * wide + i * 128, c * wide + i * 128 + 128)
                o_q[:, here] = ref[c, :, 0:128].astype(f32)
                o_k[:, here] = ref[c, :, 128:256].astype(f32)
                o_v[:, here] = ref[c, :, 256:384].astype(f32)
        o_o[...] = jnp.transpose(t_ref[0].astype(f32))

    row = lambda n: pl.BlockSpec((128, n), lambda i: (i, 0))
    shape = jax.ShapeDtypeStruct
    return pl.pallas_call(
        body,
        grid=(steps,),
        in_specs=[
            pl.BlockSpec((1, tall, width), lambda i: (i // per_core, i % per_core, 0)),
            pl.BlockSpec((2, 128, up.shape[2]), lambda i: (0, i, 0)),
            pl.BlockSpec((1, width, 128), lambda i: (i // per_core, 0, i % per_core)),
            pl.BlockSpec(small.shape, lambda i: (0, 0, 0)),
        ]
        + [pl.BlockSpec((2, 128, 384), lambda i: (0, i, 0))] * len(parts)
        + [pl.BlockSpec(ready[0].shape[:2] + (128,), lambda i: (0, 0, i))] * 2,
        out_specs=[pl.BlockSpec((tall, width), lambda i: (i, 0)), row(2 * up.shape[2])]
        + [row(width)] * 4
        + [pl.BlockSpec((heads, basis), lambda i: (0, 0))] * 2
        + [pl.BlockSpec((ff,), lambda i: (0,))]
        + [pl.BlockSpec((width,), lambda i: (0,))] * 5
        + [pl.BlockSpec(ready[0].shape[:2] + (128,), lambda i: (0, 0, i))] * 2,
        out_shape=[
            shape((2 * down.shape[1], width), f32),
            shape((width, 2 * up.shape[2]), f32),
        ]
        + [shape((width, width), f32)] * 4
        + [shape((heads, basis), f32)] * 2
        + [shape((ff,), f32)]
        + [shape((width,), f32)] * 5
        + [shape(a.shape, a.dtype) for a in ready],
        compiler_params=vmem_params(),
        name="finish",
    )(down, up, out_t, small, *parts, *ready)


def chip_local(
    inputs,
    previous,
    memory_rows,
    sticky_positions,
    cotangent,
    ln1_gain,
    ln1_bias,
    query_weight,
    key_weight,
    value_weight,
    out_weight,
    mu_weight,
    sigma_weight,
    ln2_gain,
    ln2_bias,
    expand_weight,
    up_bias,
    down_weight,
    down_bias,
):
    width = inputs.shape[2]
    heads, basis = mu_weight.shape
    ff = up_bias.shape[0]
    params = dict(ln1_gain=ln1_gain, ln2_gain=ln2_gain, mu=mu_weight, sigma=sigma_weight)
    hidden, normed, qkv, mkv, coeff, w_qkv, cot, ctx, att, mixed, n2, lse = front_call(
        dict(
            inputs=inputs,
            previous=previous,
            cotangent=cotangent,
            wq=query_weight,
            wk=key_weight,
            wv=value_weight,
            wo=out_weight,
        ),
        dict(picks=memory_rows, sticky=sticky_positions, ln1_bias=ln1_bias, ln2_bias=ln2_bias, **params),
        basis,
    )
    o_down, o_up, o_out, o_0, o_1, o_2, o_s, block_output, grad_inputs = tail_call(
        dict(
            cot=cot,
            n2_in=n2,
            mixed_in=mixed,
            hidden=hidden,
            ctx=ctx,
            expand=expand_weight,
            down=down_weight,
            w_out=out_weight,
            qkv=qkv,
            mkv=mkv,
            att=att,
            normed=normed,
            coeff=coeff,
            w_qkv=w_qkv,
        ),
        dict(lse=lse, up_bias=up_bias, down_bias=down_bias, **params),
    )
    g_down, g_up, g_q, g_k, g_v, g_o, g_mu, g_sigma, g_bias, g_db, g_g2, g_b2, g_g1, g_b1, *done = finish(
        o_down, o_up, o_out, (o_0, o_1, o_2), o_s, basis, (block_output, grad_inputs)
    )
    return (
        *done,
        g_g1,
        g_b1,
        g_q,
        g_k,
        g_v,
        g_o,
        g_mu,
        g_sigma,
        g_g2,
        g_b2,
        g_up,
        g_bias,
        g_down,
        g_db,
    )


def pick(mesh):
    def step(*arrays):
        inputs, mu = arrays[0], arrays[11]
        fits = (
            mesh.shape[BATCH] == 8
            and mesh.shape[BLK] == 4
            and inputs.shape[0] == 2
            and inputs.shape[1] % QB == 0
            and mu.shape[0] % 4 == 0
            and inputs.shape[2] == mu.shape[0] * 64
        )
        return (chip_local if fits else general)(*arrays)

    return step


def solution(mesh):
    return jax.shard_map(
        pick(mesh),
        mesh=mesh,
        in_specs=(
            P(BATCH, BLK, None),
            P(BATCH, BLK, None),
            P(BATCH, None),
            P(BATCH, None),
            P(BATCH, BLK, None),
            P(),
            P(),
            P(),
            P(),
            P(),
            P(),
            P(),
            P(),
            P(),
            P(),
            P(),
            P(),
            P(),
            P(),
        ),
        out_specs=(
            P(BATCH, BLK, None),
            P(BATCH, BLK, None),
            P(),
            P(),
            P(),
            P(),
            P(),
            P(),
            P(),
            P(),
            P(),
            P(),
            P(),
            P(),
            P(),
            P(),
        ),
        check_vma=False,
    )
```
